32 devices in a mesh: dp: 8 (over y, x, core), seq: 4 (over z).
Axes of the slice: x: 2, y: 2, z: 4, core: 2. Of those that a mesh axis runs over, the one named last changes fastest.
Arguments:
- audio: float32 [8, 163840], P(None, ('dp', 'seq')), may hold values from -0.4 to 0.4
- starts: int32 [8], replicated, may hold values from 0 to 81919, as said below
- lengths: int32 [8], replicated, may hold values from 40960 to 163840, as said below
- slots: int32 [8], replicated, may hold values from 0 to 7, each once
- conv1_weight: bfloat16 [9, 256], replicated, may hold values from -2 to 2
- conv2_weight: bfloat16 [2304, 256], replicated, may hold values from -0.125 to 0.125
- proj_weight: bfloat16 [5120, 1024], P('dp'), may hold values from -0.078125 to 0.078125
- qkv_weight: bfloat16 [1024, 3072], P('dp'), may hold values from -8 to 8
- out_weight: bfloat16 [1024, 1024], P(None, 'dp'), may hold values from -0.1875 to 0.1875
Outputs:
- regrouped: bfloat16 [8, 8, 4, 8, 1024], P('dp', None, 'seq')
- attended: bfloat16 [8, 8, 4, 8, 1024], P('dp', None, 'seq')
The draws below stay inside these ranges and needn't reach their ends.
Inputs may be any that keep to these rules, and one draw needn't show every extreme that they name: starts plus lengths is at most 163840 for every stream; some stream's utterance covers the whole stream, and some other stream's utterance starts at 81919. `lengths`: some stream's utterance has exactly 40960 samples. `slots`: every row number appears once.
All inputs are finite; a program needn't handle non-finite values.
Results may differ from the reference program's by a relative error of at most 0.013.
Values may be sent and summed in bfloat16 or wider, within the bound.
No kernel may reach another device: no remote copies, remote signals or barrier semaphores. Data moves between devices by JAX's collectives and lax.ppermute only.
A program may use at most 128 MiB of HBM per device.

```python
import functools
import math
import jax
import jax.numpy as jnp
import numpy as np
from jax import lax

D = 1024
HEADS = 8
HEAD_DIM = 128
MELS = 80
CH = 256
N_FFT = 512
HOP = 160
W = 8
ROWS = 8
BLOCKS = 8
FRAMES = 256
STREAM = 163840
FEAT = 5120
N_SEQ = 4


def utterance_bounds(key):
    base = jax.random.fold_in(key, 37)
    first_key, second_key, third_key, fourth_key = jax.random.split(base, 4)
    begins = jax.random.randint(first_key, (ROWS,), 0, STREAM // 2)
    spare = STREAM - STREAM // 4 - begins
    extra = jax.random.randint(second_key, (ROWS,), 0, 1 << 30) % (spare + 1)
    spans = STREAM // 4 + extra
    whole = jax.random.randint(third_key, (), 0, ROWS)
    latest = (whole + 1 + jax.random.randint(fourth_key, (), 0, ROWS - 1)) % ROWS
    index = jnp.arange(ROWS)
    begins = jnp.where(index == whole, 0, begins)
    spans = jnp.where(index == whole, STREAM, spans)
    begins = jnp.where(index == latest, STREAM // 2 - 1, begins)
    spans = jnp.where(index == latest, STREAM // 4, spans)
    return (begins.astype(jnp.int32), spans.astype(jnp.int32))


def draw_starts(key, part):
    return utterance_bounds(key)[0]


def draw_lengths(key, part):
    return utterance_bounds(key)[1]


def draw_qkv_weight(key, part):
    base = jax.random.fold_in(key, 101)
    first_key = jax.random.fold_in(base, 0)
    sigma = D ** (-0.5)
    values = jax.random.normal(first_key, (D, 3 * D), jnp.float32) * sigma
    column = jnp.arange(3 * D)
    values = values * jnp.where(column < D, 3.0, 1.0)[None, :]
    return jnp.clip(values, -8.0, 8.0).astype(jnp.bfloat16)


def steps_of(own_key, extent, cuts, least, high):
    loudness, own = 1.0, jax.random.fold_in(own_key, 6)
    for dim, shards_of in cuts:
        draws = jnp.exp(jax.random.uniform(jax.random.fold_in(own, dim), (shards_of,), jnp.float32, least / len(cuts), high / len(cuts)))
        loudness = loudness * jnp.repeat(draws, extent[dim] // shards_of).reshape([-1 if axis == dim else 1 for axis in range(len(extent))])
    return loudness


def bell_draw(rng, dims, scale, most, shards=(), kind=jnp.bfloat16):
    gain = steps_of(rng, dims, shards, -0.22, 0.18) if shards else 1.0
    values = jax.random.normal(rng, dims, jnp.float32) * scale * gain
    return jnp.minimum(jnp.maximum(values, -most), most).astype(kind)


def setup_inputs(seed: int = 0) -> dict:
    arg_keys = jax.random.split(jax.random.key(seed), 10)
    audio = bell_draw(arg_keys[0], (ROWS, STREAM), 0.05, 0.4, ((1, 32),), jnp.float32)
    starts = draw_starts(jax.random.fold_in(arg_keys[9], 71), 0)
    lengths = draw_lengths(jax.random.fold_in(arg_keys[9], 71), 0)
    slots = jax.random.permutation(arg_keys[3], ROWS).astype(jnp.int32)
    conv1_weight = bell_draw(arg_keys[4], (9, CH), 9 ** -0.5, 2.0)
    conv2_weight = bell_draw(arg_keys[5], (9 * CH, CH), (9 * CH) ** -0.5, 0.125)
    proj_weight = bell_draw(arg_keys[6], (FEAT, D), FEAT ** -0.5, 0.078125, ((0, 8),))
    qkv_weight = draw_qkv_weight(jax.random.fold_in(arg_keys[9], 71), 0)
    out_weight = bell_draw(arg_keys[8], (D, D), D ** -0.5, 0.1875, ((1, 8),))
    return dict(audio=audio, starts=starts, lengths=lengths, slots=slots, conv1_weight=conv1_weight, conv2_weight=conv2_weight, proj_weight=proj_weight, qkv_weight=qkv_weight, out_weight=out_weight)


SAMPLE_RATE = 16000.0
EPS_LOG = 1e-06
EPS_NORM = 1e-05
MASKED = -1e+30

def mel_table(size, bands):
    count = size // 2 + 1
    highest = 2595.0 * math.log10(1.0 + SAMPLE_RATE / 1400.0)
    points = np.linspace(0.0, highest, bands + 2)
    edges = 700.0 * (10.0 ** (points / 2595.0) - 1.0)
    edges[0] = 0.0
    edges[-1] = SAMPLE_RATE / 2.0
    frequency = np.arange(count) * (SAMPLE_RATE / size)
    lower = edges[:-2][None, :]
    middle = edges[1:-1][None, :]
    upper = edges[2:][None, :]
    rising = (frequency[:, None] - lower) / (middle - lower)
    falling = (upper - frequency[:, None]) / (upper - middle)
    return np.maximum(0.0, np.minimum(rising, falling)).astype(np.float32)

def first_conv(log_mel, weight):
    padded = jnp.pad(log_mel, ((0, 0), (0, 0), (1, 1)))
    outputs = (log_mel.shape[1] - 1) // 2
    width = log_mel.shape[2]
    tap_list = [padded[:, row_tap:row_tap + 2 * outputs - 1:2, col_tap:col_tap + width - 1:2] for row_tap in range(3) for col_tap in range(3)]
    patches = jnp.stack(tap_list, axis=-1)
    result = jnp.dot(patches.reshape(-1, 9), weight, preferred_element_type=jnp.float32)
    result = jax.nn.relu(result).astype(jnp.bfloat16)
    return result.reshape(log_mel.shape[0], outputs, width // 2, weight.shape[1])

def second_conv(first, weight):
    padded = jnp.pad(first, ((0, 0), (0, 0), (1, 1), (0, 0)))
    outputs = (first.shape[1] - 1) // 2
    width = first.shape[2]
    tap_list = [padded[:, row_tap:row_tap + 2 * outputs - 1:2, col_tap:col_tap + width - 1:2, :] for row_tap in range(3) for col_tap in range(3)]
    patches = jnp.concatenate(tap_list, axis=-1)
    result = jnp.dot(patches.reshape(-1, patches.shape[-1]), weight, preferred_element_type=jnp.float32)
    result = jax.nn.relu(result).astype(jnp.bfloat16)
    return result.reshape(first.shape[0] * outputs, width // 2 * weight.shape[1])

def front_stream(audio_row, conv1_weight, conv2_weight, proj_weight):
    rim_width = N_FFT + 2 * HOP
    frame_count = 4 * FRAMES + 3
    needed = (frame_count + 3) * HOP
    extended = jnp.concatenate([jnp.zeros((rim_width,), jnp.float32), audio_row, jnp.zeros((needed - rim_width - STREAM,), jnp.float32)])
    hop_rows = extended.reshape(frame_count + 3, HOP)
    frames = jnp.concatenate([hop_rows[offset:offset + frame_count] for offset in range(4)], axis=1)[:, :N_FFT]
    position = jnp.arange(N_FFT).astype(jnp.float32)
    window = 0.5 - 0.5 * jnp.cos(position * (2.0 * math.pi / N_FFT))
    spectrum = jnp.fft.rfft(frames * window[None, :], axis=1)
    power = (jnp.real(spectrum) ** 2 + jnp.imag(spectrum) ** 2).astype(jnp.float32)
    mel_power = jnp.dot(power, jnp.asarray(mel_table(N_FFT, MELS)), precision=lax.Precision.HIGHEST)
    log_mel = jnp.log(mel_power + EPS_LOG).astype(jnp.bfloat16)
    first = first_conv(log_mel[None], conv1_weight)
    features = second_conv(first, conv2_weight)
    return jnp.dot(features, proj_weight, preferred_element_type=jnp.float32).astype(jnp.bfloat16)

def attend_row(frames_x, valid, qkv_weight, out_weight):
    values = frames_x.astype(jnp.float32)
    mean = lax.optimization_barrier(jnp.mean(values, axis=1, keepdims=True))
    centered = values - mean
    variance = lax.optimization_barrier(jnp.mean(centered * centered, axis=1, keepdims=True))
    normed = (centered * lax.rsqrt(variance + EPS_NORM)).astype(jnp.bfloat16)
    mixed = jnp.dot(normed, qkv_weight, preferred_element_type=jnp.float32).astype(jnp.bfloat16)
    queries = mixed[:, :D].reshape(FRAMES, HEADS, HEAD_DIM).transpose(1, 0, 2)
    keys = mixed[:, D:2 * D].reshape(FRAMES, HEADS, HEAD_DIM).transpose(1, 0, 2)
    value_heads = mixed[:, 2 * D:].reshape(FRAMES, HEADS, HEAD_DIM).transpose(1, 0, 2)
    scale = HEAD_DIM ** (-0.5)

    def one_head(triple):
        query, key, value = triple
        scores = jnp.dot(query, key.T, preferred_element_type=jnp.float32) * scale
        masked = jnp.where(valid[None, :], scores, MASKED)
        peak = lax.optimization_barrier(jnp.max(masked, axis=1, keepdims=True))
        weights = jnp.where(valid[None, :], jnp.exp(masked - peak), 0.0)
        total = lax.optimization_barrier(jnp.sum(weights, axis=1, keepdims=True))
        summed = jnp.dot(weights.astype(jnp.bfloat16), value, preferred_element_type=jnp.float32)
        return (summed / total).astype(jnp.bfloat16)
    context = lax.map(one_head, (queries, keys, value_heads))
    context = context.transpose(1, 0, 2).reshape(FRAMES, D)
    output = jnp.dot(context, out_weight, preferred_element_type=jnp.float32)
    attended = jnp.where(valid[:, None], output, 0.0).astype(jnp.bfloat16)
    regrouped = jnp.where(valid[:, None], frames_x, jnp.zeros_like(frames_x))
    return (regrouped, attended)

def reference(audio, starts, lengths, slots, conv1_weight, conv2_weight, proj_weight, qkv_weight, out_weight):
    encode = functools.partial(front_stream, conv1_weight=conv1_weight, conv2_weight=conv2_weight, proj_weight=proj_weight)
    encoded = lax.map(encode, audio)
    row_index = jnp.arange(ROWS, dtype=jnp.int32)
    table = slots[None, :] == row_index[:, None]
    source = lax.optimization_barrier(jnp.sum(jnp.where(table, row_index[None, :], 0), axis=1)).astype(jnp.int32)
    ordered = jnp.take(encoded, source, axis=0)
    begins = jnp.take(starts, source)
    spans = jnp.take(lengths, source)
    position = jnp.arange(FRAMES, dtype=jnp.int32) * (4 * HOP)
    valid = (position[None, :] >= begins[:, None]) & (position[None, :] < (begins + spans)[:, None])

    def one_row(pair):
        return attend_row(pair[0], pair[1], qkv_weight, out_weight)
    regrouped, attended = lax.map(one_row, (ordered, valid))
    regrouped = regrouped.reshape(ROWS, BLOCKS, N_SEQ, W, D)
    attended = attended.reshape(ROWS, BLOCKS, N_SEQ, W, D)
    return (regrouped, attended)
```

```python
import functools
import math

import jax
import jax.numpy as jnp
import numpy as np
from jax import lax
from jax.experimental import pallas as pl
from jax.experimental.pallas import tpu as pltpu
from jax.sharding import PartitionSpec as P

HEADS = 8
HEAD_DIM = 128
MELS = 80
BANDS = MELS // 4
N_FFT = 512
HOP = 160
W = 8
RIM = 1024
SPAN = 4 * HOP
JS = W + 1
LANES = 128
SAMPLE_RATE = 16000.0
EPS_LOG = 1e-06
EPS_NORM = 1e-05
MASKED = -1e30
F32 = jnp.float32
BF16 = jnp.bfloat16
MIB = 1 << 20


def mel_table(size, bands):
    count = size // 2 + 1
    highest = 2595.0 * math.log10(1.0 + SAMPLE_RATE / 1400.0)
    points = np.linspace(0.0, highest, bands + 2)
    edges = 700.0 * (10.0 ** (points / 2595.0) - 1.0)
    edges[0] = 0.0
    edges[-1] = SAMPLE_RATE / 2.0
    frequency = np.arange(count) * (SAMPLE_RATE / size)
    lower = edges[:-2][None, :]
    middle = edges[1:-1][None, :]
    upper = edges[2:][None, :]
    rising = (frequency[:, None] - lower) / (middle - lower)
    falling = (upper - frequency[:, None]) / (upper - middle)
    return np.maximum(0.0, np.minimum(rising, falling)).astype(np.float32)


def filter_table():
    table = mel_table(N_FFT, MELS)[: N_FFT // 2]
    return np.pad(table, ((0, 0), (0, LANES - MELS)))


def spectrum_table(size):
    sample = np.arange(size)
    phase = sample[:, None] * np.arange(size // 2)[None, :] % size
    angle = phase * (2.0 * math.pi / size)
    window = 0.5 - 0.5 * np.cos(sample * (2.0 * math.pi / size))
    both = np.concatenate([np.cos(angle), np.sin(angle)], axis=1) * window[:, None]
    return both.astype(np.float32)


def band_selection(parts):
    share = BANDS // parts
    width = 4 * share + 4
    table = np.zeros((5 * LANES, parts * LANES), np.float32)
    for part in range(parts):
        for delta in range(5):
            for lane in range(width):
                band = 4 * share * part - 4 + lane
                if 0 <= band < MELS:
                    table[delta * LANES + band, part * LANES + delta * width + lane] = 1.0
    return table.astype(BF16)


def tap_selection(parts):
    share = BANDS // parts
    width = 4 * share + 4
    outs = 2 * share + 1
    table = np.zeros((outs, LANES, 16), np.float32)
    for g in range(outs):
        for row_tap in range(3):
            for col_tap in range(3):
                table[g, row_tap * width + 2 * g + 1 + col_tap, 3 * row_tap + col_tap] = 1.0
    return table.reshape(outs * LANES, 16).astype(BF16)


def swap_table(outer, inner):
    count = outer * inner
    table = np.zeros((count, count), np.float32)
    for o in range(outer):
        for i in range(inner):
            table[i * outer + o, o * inner + i] = 1.0
    return table.astype(BF16)


def frame_table(windows):
    count = windows * W
    table = np.zeros((count, count), np.float32)
    for k in range(windows):
        for t in range(W):
            table[k * W + t, (k // 8) * 8 * W + t * 8 + k % 8] = 1.0
    return table.astype(BF16)


def vmem():
    return pl.BlockSpec(memory_space=pltpu.VMEM)


def smem():
    return pl.BlockSpec(memory_space=pltpu.SMEM)


def anywhere():
    return pl.BlockSpec(memory_space=pl.ANY)


def params(mib):
    return pltpu.CompilerParams(vmem_limit_bytes=mib * MIB)


def cost(flops, moved):
    return pl.CostEstimate(flops=int(flops), bytes_accessed=int(moved), transcendentals=0)


def prep_kernel(
    columns, chips, width, proj_ref, qkv_ref, taps_ref, conv1_ref, proj_out, mix_out, banded_out, mix_buf, sems
):
    features = qkv_ref.shape[1] // 3
    first = pl.multiple_of(lax.axis_index("seq") * width, LANES)
    loads = [
        pltpu.make_async_copy(
            qkv_ref.at[:, pl.ds(part * features + first, width)],
            mix_buf.at[:, pl.ds(part * width, width)],
            sems.at[part],
        )
        for part in range(3)
    ]
    for copy in loads:
        copy.start()
    pieces = [
        pltpu.make_async_copy(proj_ref.at[:, pl.ds(n * columns, columns)], proj_out.at[n], sems.at[3 + n])
        for n in range(proj_out.shape[0])
    ]
    for copy in pieces:
        copy.start()
    outs = banded_out.shape[1] // conv1_ref.shape[1]
    channels = conv1_ref.shape[1]
    for copy in loads:
        copy.wait()
    base = 3 + proj_out.shape[0]
    stores = [pltpu.make_async_copy(mix_buf, mix_out.at[n], sems.at[base + n]) for n in range(chips)]
    for copy in stores:
        copy.start()
    for g in range(outs):
        banded_out[:, g * channels : (g + 1) * channels] = jnp.dot(
            taps_ref[g * LANES : (g + 1) * LANES, :], conv1_ref[...], preferred_element_type=F32
        ).astype(BF16)
    for copy in pieces + stores:
        copy.wait()


def mel_kernel(parts, rim_ref, audio_ref, table_ref, filter_ref, select_ref, slots_ref, out_ref, ext):
    streams = audio_ref.shape[0]
    rows = JS * streams
    ext[:, :RIM] = rim_ref[...]
    ext[:, RIM:] = audio_ref[...]
    phases = []
    for phase in range(4):
        start = HOP * phase + 32
        base, shift = start // LANES * LANES, start % LANES
        length = N_FFT + (LANES if shift else 0)
        block = jnp.concatenate(
            [ext[:, SPAN * j + base : SPAN * j + base + length] for j in range(JS)], axis=0
        )
        if shift:
            block = pltpu.roll(block, length - shift, 1)[:, :N_FFT]
        phases.append(block)
    frames = jnp.concatenate(phases, axis=0)
    spectrum = jnp.dot(frames, table_ref[...], precision=lax.Precision.HIGHEST, preferred_element_type=F32)
    half = N_FFT // 2
    real, imag = spectrum[:, :half], spectrum[:, half:]
    power = real * real + imag * imag
    mel_power = jnp.dot(power, filter_ref[...], precision=lax.Precision.HIGHEST, preferred_element_type=F32)
    log_mel = jnp.log(mel_power + EPS_LOG)
    by_phase = [log_mel[phase * rows : (phase + 1) * rows] for phase in range(4)]

    def later(block):
        return jnp.concatenate([block[streams:], jnp.zeros((streams, LANES), F32)], axis=0)

    taps = [by_phase[1], by_phase[2], by_phase[3], later(by_phase[0]), later(by_phase[1])]
    gathered = jnp.concatenate([tap.astype(BF16) for tap in taps], axis=1)
    placed = jnp.dot(gathered, select_ref[...], preferred_element_type=F32).astype(BF16)
    routing = (slots_ref[...] == lax.broadcasted_iota(jnp.int32, (rows, rows), 0)).astype(F32).astype(BF16)
    routed = jnp.dot(routing, placed, preferred_element_type=F32).astype(BF16)
    copies = out_ref.shape[0] // parts
    for part in range(parts):
        block = routed[:, part * LANES : (part + 1) * LANES]
        for copy in range(copies):
            out_ref[part * copies + copy] = block


def conv_kernel(
    width, mel_ref, swap_ref, banded_ref, conv2_ref, proj_ref, out_ref, even, odd, second, conv2, proj, sems
):
    streams = out_ref.shape[0]
    n = 8 * streams
    step = pl.program_id(0)
    load_conv2 = pltpu.make_async_copy(conv2_ref, conv2, sems.at[0])
    load_proj = pltpu.make_async_copy(proj_ref, proj, sems.at[1])

    @pl.when(step == 0)
    def _():
        load_conv2.start()
        load_proj.start()

    blocks = [mel_ref[d].astype(F32) for d in range(8)]
    ordered = jnp.concatenate(
        [
            jnp.concatenate([block[j * streams : (j + 1) * streams] for block in blocks], axis=0)
            for j in range(JS)
        ],
        axis=1,
    ).astype(BF16)
    swapped = jnp.dot(swap_ref[...], ordered, preferred_element_type=F32)
    by_j = [swapped[:, j * LANES : (j + 1) * LANES] for j in range(JS)]
    evens = jnp.concatenate(by_j, axis=0)
    odds = pltpu.roll(evens[: W * n], LANES - 2 * width, 1).astype(BF16)
    evens = evens.astype(BF16)
    channels = conv2_ref.shape[1]
    outs = banded_ref.shape[1] // channels
    for g in range(outs):
        lanes = slice(g * channels, (g + 1) * channels)
        weight = banded_ref[:, lanes]
        even[:, lanes] = jax.nn.relu(jnp.dot(evens, weight, preferred_element_type=F32)).astype(BF16)
        odd[:, lanes] = jax.nn.relu(jnp.dot(odds, weight, preferred_element_type=F32)).astype(BF16)

    @pl.when(step == 0)
    def _():
        load_conv2.wait()
        load_proj.wait()

    for h in range((outs - 1) // 2):
        lanes = slice(2 * h * channels, (2 * h + 3) * channels)
        depth = 3 * channels
        total = jnp.dot(even[: W * n, lanes], conv2[:depth], preferred_element_type=F32)
        total += jnp.dot(odd[:, lanes], conv2[depth : 2 * depth], preferred_element_type=F32)
        total += jnp.dot(even[n:, lanes], conv2[2 * depth :], preferred_element_type=F32)
        second[:, h * channels : (h + 1) * channels] = jax.nn.relu(total).astype(BF16)
    weights = proj[...].reshape(second.shape[1], proj.shape[2])
    partial = jnp.dot(second[...], weights, preferred_element_type=F32)
    for r in range(streams):
        out_ref[r, 0] = jnp.concatenate(
            [partial[t * n + r * 8 : t * n + r * 8 + 8] for t in range(W)], axis=0
        ).astype(BF16)


def bounds(slots_ref, starts_ref, lengths_ref):
    mine = lax.axis_index("dp")
    begin, span = jnp.int32(0), jnp.int32(0)
    for u in range(slots_ref.shape[0]):
        chosen = slots_ref[u] == mine
        begin = begin + jnp.where(chosen, starts_ref[u], 0)
        span = span + jnp.where(chosen, lengths_ref[u], 0)
    return begin, begin + span


def norm_kernel(parts, slots_ref, starts_ref, lengths_ref, part_ref, frames_ref, sample_ref, rows_out, normed_out):
    begin, end = bounds(slots_ref, starts_ref, lengths_ref)
    copies = part_ref.shape[0] // parts
    halves = []
    for copy in range(copies):
        total = part_ref[copy].astype(F32)
        for part in range(1, parts):
            total += part_ref[part * copies + copy].astype(F32)
        halves.append(total)
    encoded = jnp.concatenate(halves, axis=1).astype(BF16)
    values = jnp.dot(frames_ref[...], encoded, preferred_element_type=F32)
    sample = sample_ref[...] + lax.axis_index("seq") * (W * SPAN)
    valid = (sample >= begin) & (sample < end)
    rows_out[...] = jnp.where(valid, values, 0.0).astype(BF16)
    mean = jnp.mean(values, axis=-1, keepdims=True)
    centered = values - mean
    variance = jnp.mean(centered * centered, axis=-1, keepdims=True)
    normed = (centered * lax.rsqrt(variance + EPS_NORM)).astype(BF16)
    for copy in range(normed_out.shape[0]):
        normed_out[copy] = normed


def gathered_copies(mine_ref, other_ref, buffer, sems):
    core = lax.axis_index("dp") % 2
    copies = []
    for chip in range(mine_ref.shape[0]):
        copies.append(pltpu.make_async_copy(mine_ref.at[chip], buffer.at[2 * chip + core], sems.at[2 * chip]))
        copies.append(
            pltpu.make_async_copy(other_ref.at[chip], buffer.at[2 * chip + 1 - core], sems.at[2 * chip + 1])
        )
    return copies


def attention_kernel(
    slots_ref, starts_ref, lengths_ref, normed_ref, sample_ref, mine_ref, other_ref, out_ref, buffer, sems
):
    copies = gathered_copies(mine_ref, other_ref, buffer, sems)
    for copy in copies:
        copy.start()
    begin, end = bounds(slots_ref, starts_ref, lengths_ref)
    sample = sample_ref[...]
    valid = (sample >= begin) & (sample < end)
    group, local, features = normed_ref.shape
    normed = normed_ref[...].reshape(group * local, features)
    for copy in copies:
        copy.wait()
    weights = buffer[...].reshape(features, buffer.shape[2])
    mixed = jnp.dot(normed, weights, preferred_element_type=F32).astype(BF16)
    width = buffer.shape[2] // 3
    scale = HEAD_DIM ** (-0.5)
    for head in range(width // HEAD_DIM):
        at = head * HEAD_DIM
        query = mixed[:, at : at + HEAD_DIM]
        key = mixed[:, width + at : width + at + HEAD_DIM]
        value = mixed[:, 2 * width + at : 2 * width + at + HEAD_DIM]
        scores = lax.dot_general(query, key, (((1,), (1,)), ((), ())), preferred_element_type=F32) * scale
        masked = jnp.where(valid, scores, MASKED)
        peak = jnp.max(masked, axis=1, keepdims=True)
        weight = jnp.where(valid, jnp.exp(masked - peak), 0.0)
        total = jnp.sum(weight, axis=1, keepdims=True)
        summed = jnp.dot(weight.astype(BF16), value, preferred_element_type=F32)
        context = (summed / total).astype(BF16)
        for part in range(group):
            out_ref[part, :, at : at + HEAD_DIM] = context[part * local : (part + 1) * local]


def output_kernel(
    slots_ref, starts_ref, lengths_ref, context_ref, sample_ref, mine_ref, other_ref, out_ref, buffer, sems
):
    copies = gathered_copies(mine_ref, other_ref, buffer, sems)
    for copy in copies:
        copy.start()
    begin, end = bounds(slots_ref, starts_ref, lengths_ref)
    context = jnp.concatenate([context_ref[part] for part in range(context_ref.shape[0])], axis=1)
    sample = sample_ref[...] + lax.axis_index("seq") * (W * SPAN)
    valid = (sample >= begin) & (sample < end)
    for copy in copies:
        copy.wait()
    result = jnp.concatenate(
        [jnp.dot(context, buffer[d], preferred_element_type=F32) for d in range(buffer.shape[0])], axis=1
    )
    out_ref[...] = jnp.where(valid, result, 0.0).astype(BF16)


def on_device(
    audio, starts, lengths, slots, conv1_weight, conv2_weight, proj_weight, qkv_weight, out_weight
):
    streams = audio.shape[0]
    windows = lax.axis_size("dp")
    group = lax.axis_size("seq")
    parts = math.gcd(windows, BANDS)
    copies = windows // parts
    chips = windows // 2
    share = BANDS // parts
    width = 4 * share + 4
    channels = conv1_weight.shape[1]
    features = proj_weight.shape[1]
    columns = features // copies
    head_width = features // group
    local = windows * W
    rows = JS * streams
    n = 8 * streams

    route = [(i, i + 1) for i in range(windows * group - 1)]
    rim = lax.ppermute(audio[:, audio.shape[1] - RIM :], ("dp", "seq"), route)

    proj_parts, mix_parts, banded = pl.pallas_call(
        functools.partial(prep_kernel, columns, chips, head_width),
        out_shape=(
            jax.ShapeDtypeStruct((copies, proj_weight.shape[0], columns), BF16),
            jax.ShapeDtypeStruct((chips, qkv_weight.shape[0], 3 * head_width), BF16),
            jax.ShapeDtypeStruct((LANES, (2 * share + 1) * channels), BF16),
        ),
        in_specs=[anywhere(), anywhere(), vmem(), vmem()],
        out_specs=(anywhere(), anywhere(), vmem()),
        scratch_shapes=[
            pltpu.VMEM((qkv_weight.shape[0], 3 * head_width), BF16),
            pltpu.SemaphoreType.DMA((3 + copies + chips,)),
        ],
        compiler_params=params(16),
        cost_estimate=cost(1e8, 8e6),
        name="prep",
    )(proj_weight, qkv_weight, jnp.asarray(tap_selection(parts)), jnp.pad(conv1_weight, ((0, 7), (0, 0))))

    same_core = [list(range(core, windows, 2)) for core in range(2)]
    swap_cores = [(i, i ^ 1) for i in range(windows)]
    neighbours = [list(range(i, i + copies)) for i in range(0, windows, copies)]
    proj_here = lax.all_to_all(
        proj_parts, "dp", split_axis=0, concat_axis=0, axis_index_groups=neighbours, tiled=True
    )
    mix_mine = lax.all_to_all(
        mix_parts, "dp", split_axis=0, concat_axis=0, axis_index_groups=same_core, tiled=True
    )
    mix_other = lax.ppermute(mix_mine, "dp", swap_cores)

    targets = (jnp.arange(JS, dtype=jnp.int32)[:, None] * streams + slots[None, :]).reshape(1, rows)
    mel = pl.pallas_call(
        functools.partial(mel_kernel, parts),
        out_shape=jax.ShapeDtypeStruct((windows, rows, LANES), BF16),
        in_specs=[vmem()] * 6,
        out_specs=vmem(),
        scratch_shapes=[pltpu.VMEM((streams, RIM + audio.shape[1]), F32)],
        compiler_params=params(24),
        cost_estimate=cost(2e9, 2e6),
        name="log_mel",
    )(
        rim,
        audio,
        jnp.asarray(spectrum_table(N_FFT)),
        jnp.asarray(filter_table()),
        jnp.asarray(band_selection(parts)),
        targets,
    )
    mel = lax.all_to_all(mel, "dp", split_axis=0, concat_axis=0, tiled=True)

    partial = pl.pallas_call(
        functools.partial(conv_kernel, width),
        grid=(windows // 8,),
        out_shape=jax.ShapeDtypeStruct((streams, windows // 8, 8 * W, columns), BF16),
        in_specs=[
            pl.BlockSpec((8, rows, LANES), lambda i: (i, 0, 0)),
            vmem(),
            vmem(),
            anywhere(),
            anywhere(),
        ],
        out_specs=pl.BlockSpec((streams, 1, 8 * W, columns), lambda i: (0, i, 0, 0)),
        scratch_shapes=[
            pltpu.VMEM((JS * n, banded.shape[1]), BF16),
            pltpu.VMEM((W * n, banded.shape[1]), BF16),
            pltpu.VMEM((W * n, share * channels), BF16),
            pltpu.VMEM(conv2_weight.shape, BF16),
            pltpu.VMEM(proj_parts.shape, BF16),
            pltpu.SemaphoreType.DMA((2,)),
        ],
        compiler_params=params(56),
        cost_estimate=cost(8e9, 4e6),
        name="conv",
    )(mel, jnp.asarray(swap_table(8, streams)), banded, conv2_weight, proj_here)
    partial = lax.all_to_all(partial, "dp", split_axis=0, concat_axis=0, tiled=True)
    partial, out_here = lax.optimization_barrier((partial, out_weight))

    index = np.arange(local)
    local_sample = ((index // W) * group * W + index % W) * SPAN
    all_sample = (local_sample[None, :] + np.arange(group)[:, None] * W * SPAN).reshape(1, -1)
    local_sample = jnp.asarray(local_sample.reshape(-1, 1).astype(np.int32))
    regrouped, normed = pl.pallas_call(
        functools.partial(norm_kernel, parts),
        out_shape=(
            jax.ShapeDtypeStruct((local, features), BF16),
            jax.ShapeDtypeStruct((group, local, features), BF16),
        ),
        in_specs=[smem()] * 3 + [vmem()] * 3,
        out_specs=(vmem(), vmem()),
        compiler_params=params(24),
        cost_estimate=cost(1e8, 1e6),
        name="layer_norm",
    )(
        slots,
        starts,
        lengths,
        partial.reshape(windows, local, columns),
        jnp.asarray(frame_table(windows)),
        local_sample,
    )
    normed = lax.all_to_all(normed, "seq", split_axis=0, concat_axis=0, tiled=True)

    out_mine = lax.all_to_all(
        jnp.broadcast_to(out_here[None], (chips,) + out_here.shape),
        "dp",
        split_axis=0,
        concat_axis=0,
        axis_index_groups=same_core,
        tiled=True,
    )
    out_other = lax.ppermute(out_mine, "dp", swap_cores)

    context = pl.pallas_call(
        attention_kernel,
        out_shape=jax.ShapeDtypeStruct((group, local, head_width), BF16),
        in_specs=[smem()] * 3 + [vmem()] * 2 + [anywhere()] * 2,
        out_specs=vmem(),
        scratch_shapes=[
            pltpu.VMEM((windows, qkv_weight.shape[0], 3 * head_width), BF16),
            pltpu.SemaphoreType.DMA((windows,)),
        ],
        compiler_params=params(48),
        cost_estimate=cost(1e9, 2e6),
        name="attention",
    )(
        slots,
        starts,
        lengths,
        normed,
        jnp.asarray(all_sample.astype(np.int32)),
        mix_mine,
        mix_other,
    )
    context = lax.all_to_all(context, "seq", split_axis=0, concat_axis=0, tiled=True)

    attended = pl.pallas_call(
        output_kernel,
        out_shape=jax.ShapeDtypeStruct((local, features), BF16),
        in_specs=[smem()] * 3 + [vmem()] * 2 + [anywhere()] * 2,
        out_specs=vmem(),
        scratch_shapes=[
            pltpu.VMEM((windows,) + out_weight.shape, BF16),
            pltpu.SemaphoreType.DMA((windows,)),
        ],
        compiler_params=params(24),
        cost_estimate=cost(1e8, 3e6),
        name="output",
    )(slots, starts, lengths, context, local_sample, out_mine, out_other)
    shape = (1, windows, 1, W, features)
    return (regrouped.reshape(shape), attended.reshape(shape))


def solution(mesh):
    in_specs = (
        P(None, ("dp", "seq")),
        P(),
        P(),
        P(),
        P(),
        P(),
        P("dp", None),
        P("dp", None),
        P(None, "dp"),
    )
    out_specs = (P("dp", None, "seq", None, None), P("dp", None, "seq", None, None))
    return jax.shard_map(
        on_device, mesh=mesh, in_specs=in_specs, out_specs=out_specs, check_vma=False
    )
```

```python
import functools
import math

import jax
import jax.numpy as jnp
import numpy as np
from jax import lax
from jax.experimental import pallas as pl
from jax.experimental.pallas import tpu as pltpu
from jax.sharding import PartitionSpec as P

HEADS = 8
HEAD_DIM = 128
MELS = 80
BANDS = MELS // 4
N_FFT = 512
HOP = 160
W = 8
RIM = 384
SPAN = 4 * HOP
JS = W + 1
LANES = 128
SAMPLE_RATE = 16000.0
EPS_LOG = 1e-06
EPS_NORM = 1e-05
MASKED = -1e30
F32 = jnp.float32
BF16 = jnp.bfloat16
MIB = 1 << 20


def mel_table(size, bands):
    count = size // 2 + 1
    highest = 2595.0 * math.log10(1.0 + SAMPLE_RATE / 1400.0)
    points = np.linspace(0.0, highest, bands + 2)
    edges = 700.0 * (10.0 ** (points / 2595.0) - 1.0)
    edges[0] = 0.0
    edges[-1] = SAMPLE_RATE / 2.0
    frequency = np.arange(count) * (SAMPLE_RATE / size)
    lower = edges[:-2][None, :]
    middle = edges[1:-1][None, :]
    upper = edges[2:][None, :]
    rising = (frequency[:, None] - lower) / (middle - lower)
    falling = (upper - frequency[:, None]) / (upper - middle)
    return np.maximum(0.0, np.minimum(rising, falling)).astype(np.float32)


def filter_table():
    table = mel_table(N_FFT, MELS)[: N_FFT // 2]
    return np.pad(table, ((0, 0), (0, LANES - MELS)))


def spectrum_table(size):
    sample = np.arange(size)
    phase = sample[:, None] * np.arange(size // 2)[None, :] % size
    angle = phase * (2.0 * math.pi / size)
    window = 0.5 - 0.5 * np.cos(sample * (2.0 * math.pi / size))
    both = np.concatenate([np.cos(angle), np.sin(angle)], axis=1) * window[:, None]
    return both.astype(np.float32)


def band_selection(parts):
    share = BANDS // parts
    width = 4 * share + 4
    table = np.zeros((4 * LANES, parts * LANES), np.float32)
    for part in range(parts):
        for delta in range(4):
            for lane in range(width):
                band = 4 * share * part - 4 + lane
                if 0 <= band < MELS:
                    table[delta * LANES + band, part * LANES + delta * width + lane] = 1.0
    return table.astype(BF16)


def shift_selection(width):
    table = np.zeros((LANES, 2 * LANES), np.float32)
    lane = np.arange(width)
    for delta in range(3):
        table[(delta + 1) * width + lane, delta * width + lane] = 1.0
    for delta in range(2):
        table[delta * width + lane, LANES + (delta + 3) * width + lane] = 1.0
    return table.astype(BF16)


def row_selection(windows, group):
    count = windows * group
    earlier = np.zeros((JS * count, W * count), np.float32)
    same = np.zeros((JS * count, W * count), np.float32)
    for j in range(JS):
        for s in range(group):
            for k in range(windows):
                row = j * count + s * windows + k
                window = k * group + s
                if j:
                    earlier[row, window * W + j - 1] = 1.0
                elif window:
                    earlier[row, (window - 1) * W + W - 1] = 1.0
                if j < W:
                    same[row, window * W + j] = 1.0
    return np.concatenate([earlier, same], axis=1).astype(BF16)


def frame_table(windows):
    count = windows * W
    table = np.zeros((count, count), np.float32)
    for k in range(windows):
        for t in range(W):
            table[k * W + t, t * windows + k] = 1.0
    return table.astype(BF16)


def vmem():
    return pl.BlockSpec(memory_space=pltpu.VMEM)


def smem():
    return pl.BlockSpec(memory_space=pltpu.SMEM)


def anywhere():
    return pl.BlockSpec(memory_space=pl.ANY)


def params(mib):
    return pltpu.CompilerParams(vmem_limit_bytes=mib * MIB)


def cost(flops, moved):
    return pl.CostEstimate(flops=int(flops), bytes_accessed=int(moved), transcendentals=0)


def place(parts):
    mine = lax.axis_index("dp")
    copies = lax.axis_size("dp") // parts
    return mine // copies, mine % copies


def later(index, step, count):
    return lax.rem(index + step, count)


def prep_kernel(parts, width, qkv_ref, conv1_ref, *refs):
    mix_outs, banded_out, sems = refs[:parts], refs[parts], refs[parts + 1]
    part, _ = place(parts)
    features = qkv_ref.shape[1] // 3
    head_width = features // parts
    copies = []
    for step in range(parts):
        first = pl.multiple_of(later(part, step, parts) * head_width, LANES)
        for kind in range(3):
            copies.append(
                pltpu.make_async_copy(
                    qkv_ref.at[:, pl.ds(kind * features + first, head_width)],
                    mix_outs[step].at[:, pl.ds(kind * head_width, head_width)],
                    sems.at[3 * step + kind],
                )
            )
    for copy in copies:
        copy.start()
    taps, channels = conv1_ref.shape
    outs = banded_out.shape[1] // channels
    row = lax.broadcasted_iota(jnp.int32, (LANES, taps), 0)
    tap = lax.broadcasted_iota(jnp.int32, (LANES, taps), 1)
    line = (tap >= 3).astype(jnp.int32) + (tap >= 6).astype(jnp.int32)
    target = line * (width - 3) + tap + 1
    weight = conv1_ref[...]
    for g in range(outs):
        select = (row == target + 2 * g).astype(F32).astype(BF16)
        banded_out[:, g * channels : (g + 1) * channels] = jnp.dot(
            select, weight, preferred_element_type=F32
        ).astype(BF16)
    for copy in copies:
        copy.wait()


def mel_kernel(parts, group, rim_ref, audio_ref, table_ref, filter_ref, select_ref, slots_ref, out_ref, ext):
    streams = audio_ref.shape[0]
    rows = W * streams
    ext[:, :RIM] = rim_ref[...]
    ext[:, RIM:] = audio_ref[...]
    phases = []
    for phase in range(4):
        start = HOP * phase + 32
        base, shift = start // LANES * LANES, start % LANES
        length = N_FFT + (LANES if shift else 0)
        block = jnp.concatenate(
            [ext[:, SPAN * j + base : SPAN * j + base + length] for j in range(W)], axis=0
        )
        if shift:
            block = pltpu.roll(block, length - shift, 1)[:, :N_FFT]
        phases.append(block)
    frames = jnp.concatenate(phases, axis=0)
    spectrum = jnp.dot(frames, table_ref[...], precision=lax.Precision.HIGHEST, preferred_element_type=F32)
    half = N_FFT // 2
    real, imag = spectrum[:, :half], spectrum[:, half:]
    power = real * real + imag * imag
    mel_power = jnp.dot(power, filter_ref[...], precision=lax.Precision.HIGHEST, preferred_element_type=F32)
    log_mel = jnp.log(mel_power + EPS_LOG).astype(BF16)
    gathered = jnp.concatenate([log_mel[phase * rows : (phase + 1) * rows] for phase in range(4)], axis=1)
    placed = jnp.dot(gathered, select_ref[...], preferred_element_type=F32).astype(BF16)
    routing = (slots_ref[...] == lax.broadcasted_iota(jnp.int32, (rows, rows), 0)).astype(F32).astype(BF16)
    routed = jnp.dot(routing, placed, preferred_element_type=F32)
    copies = streams // group
    for part in range(parts):
        for copy in range(copies):
            for plane in range(group):
                row = plane * copies + copy
                out_ref[(part * copies + copy) * group + plane] = routed[
                    row * W : (row + 1) * W, part * LANES : (part + 1) * LANES
                ].astype(BF16)


def conv_kernel(parts, width, windows, mel_ref, shift_ref, rows_ref, banded_ref, conv2_ref, *refs):
    part, copy_index = place(parts)
    copies = lax.axis_size("dp") // parts
    proj_refs, refs = refs[:copies], refs[copies:]
    mix_refs, refs = refs[:parts], refs[parts:]
    outs_refs, refs = refs[:parts], refs[parts:]
    stack_out, even, odd, second, conv2, proj, partial, sems = refs
    load_conv2 = pltpu.make_async_copy(conv2_ref, conv2, sems.at[0])
    load_conv2.start()
    loads = []
    for step in range(copies):
        slot = later(copy_index, copies - step, copies)
        loads.append(pltpu.make_async_copy(proj_refs[step], proj.at[slot], sems.at[1 + step]))
    for step in range(parts):
        slot = later(part, parts - step, parts)
        loads.append(pltpu.make_async_copy(mix_refs[step], stack_out.at[slot], sems.at[1 + copies + step]))
    for load in loads:
        load.start()

    sources = mel_ref.shape[0]
    n = sources
    payload = mel_ref[...].astype(F32).reshape(sources * W, LANES).astype(BF16)
    shifted = jnp.dot(payload, shift_ref[...], preferred_element_type=F32).astype(BF16)
    both = jnp.concatenate([shifted[:, :LANES], shifted[:, LANES:]], axis=0)
    evens = jnp.dot(rows_ref[...], both, preferred_element_type=F32)
    row = lax.broadcasted_iota(jnp.int32, evens.shape, 0)
    lane = lax.broadcasted_iota(jnp.int32, evens.shape, 1)
    low = (lane >= width).astype(jnp.int32) + (lane >= 2 * width).astype(jnp.int32)
    band = lane - low * width - 4 + (width - 4) * part
    silent = (row == 0) & (lane < 3 * width) & (band >= 0)
    evens = jnp.where(silent, jnp.log(jnp.full(evens.shape, EPS_LOG, F32)), evens)
    odds = pltpu.roll(evens[: W * n], LANES - 2 * width, 1).astype(BF16)
    evens = evens.astype(BF16)
    channels = conv2_ref.shape[1]
    outs = banded_ref.shape[1] // channels
    for g in range(outs):
        lanes = slice(g * channels, (g + 1) * channels)
        weight = banded_ref[:, lanes]
        even[:, lanes] = jax.nn.relu(jnp.dot(evens, weight, preferred_element_type=F32)).astype(BF16)
        odd[:, lanes] = jax.nn.relu(jnp.dot(odds, weight, preferred_element_type=F32)).astype(BF16)

    load_conv2.wait()
    for h in range((outs - 1) // 2):
        lanes = slice(2 * h * channels, (2 * h + 3) * channels)
        depth = 3 * channels
        total = jnp.dot(even[: W * n, lanes], conv2[:depth], preferred_element_type=F32)
        total += jnp.dot(odd[:, lanes], conv2[depth : 2 * depth], preferred_element_type=F32)
        total += jnp.dot(even[n:, lanes], conv2[2 * depth :], preferred_element_type=F32)
        second[:, h * channels : (h + 1) * channels] = jax.nn.relu(total).astype(BF16)
    for load in loads:
        load.wait()
    weights = proj[...].reshape(second.shape[1], proj.shape[2])
    partial[...] = jnp.dot(second[...], weights, preferred_element_type=F32)
    for step in range(parts):
        plane = later(part, step, parts)
        outs_refs[step][...] = jnp.concatenate(
            [partial[pl.ds(pl.multiple_of(t * n + plane * windows, 8), windows), :] for t in range(W)], axis=0
        ).astype(BF16)


def bounds(row, slots_ref, starts_ref, lengths_ref):
    begin, span = jnp.int32(0), jnp.int32(0)
    for u in range(slots_ref.shape[0]):
        chosen = slots_ref[u] == row
        begin = begin + jnp.where(chosen, starts_ref[u], 0)
        span = span + jnp.where(chosen, lengths_ref[u], 0)
    return begin, begin + span


def stacked(parts, pieces, stack_out, sems):
    part, _ = place(parts)
    copies = []
    for step in range(parts):
        slot = later(part, parts - step, parts)
        copies.append(pltpu.make_async_copy(pieces[step], stack_out.at[slot], sems.at[step]))
    return copies


def norm_kernel(parts, slots_ref, starts_ref, lengths_ref, frames_ref, sample_ref, *refs):
    part, copy_index = place(parts)
    copies = lax.axis_size("dp") // parts
    part_refs, piece_refs, refs = refs[:parts], refs[parts : 2 * parts], refs[2 * parts :]
    rows_out, normed_out, stack_out, sems = refs
    loads = stacked(parts, piece_refs, stack_out, sems)
    for load in loads:
        load.start()
    row = lax.axis_index("seq") * copies + copy_index
    begin, end = bounds(row, slots_ref, starts_ref, lengths_ref)
    total = part_refs[0][...].astype(F32)
    for step in range(1, parts):
        total += part_refs[step][...].astype(F32)
    encoded = total.astype(BF16)
    values = encoded.astype(F32)
    mean = jnp.mean(values, axis=-1, keepdims=True)
    centered = values - mean
    variance = jnp.mean(centered * centered, axis=-1, keepdims=True)
    normed_out[...] = (centered * lax.rsqrt(variance + EPS_NORM)).astype(BF16)
    ordered = jnp.dot(frames_ref[...], encoded, preferred_element_type=F32)
    sample = sample_ref[...] + part * (W * SPAN)
    valid = (sample >= begin) & (sample < end)
    rows_out[...] = jnp.where(valid, ordered, 0.0).astype(BF16)
    for load in loads:
        load.wait()


def gathered_copies(parts, stack_refs, buffer, sems):
    _, copy_index = place(parts)
    copies = len(stack_refs)
    moves = []
    for step in range(copies):
        slot = later(copy_index, copies - step, copies)
        for piece in range(parts):
            moves.append(
                pltpu.make_async_copy(
                    stack_refs[step].at[piece], buffer.at[piece * copies + slot], sems.at[step * parts + piece]
                )
            )
    return moves


def attention_kernel(parts, slots_ref, starts_ref, lengths_ref, sample_ref, *refs):
    part, copy_index = place(parts)
    copies = lax.axis_size("dp") // parts
    normed_refs, refs = refs[:parts], refs[parts:]
    stack_refs, refs = refs[:copies], refs[copies:]
    outs_refs, (buffer, sems) = refs[:parts], refs[parts:]
    moves = gathered_copies(parts, stack_refs, buffer, sems)
    for move in moves:
        move.start()
    row = lax.axis_index("seq") * copies + copy_index
    begin, end = bounds(row, slots_ref, starts_ref, lengths_ref)
    masks = []
    for step in range(parts):
        plane = later(part, parts - step, parts)
        sample = sample_ref[...] + plane * (W * SPAN)
        masks.append(((sample >= begin) & (sample < end)).astype(F32))
    valid = jnp.concatenate(masks, axis=1) > 0.5
    normed = jnp.concatenate([ref[...] for ref in normed_refs], axis=0)
    local, features = normed_refs[0].shape
    for move in moves:
        move.wait()
    weights = buffer[...].reshape(features, buffer.shape[2])
    mixed = jnp.dot(normed, weights, preferred_element_type=F32).astype(BF16)
    width = buffer.shape[2] // 3
    scale = HEAD_DIM ** (-0.5)
    for head in range(width // HEAD_DIM):
        at = head * HEAD_DIM
        query = mixed[:, at : at + HEAD_DIM]
        key = mixed[:, width + at : width + at + HEAD_DIM]
        value = mixed[:, 2 * width + at : 2 * width + at + HEAD_DIM]
        scores = lax.dot_general(query, key, (((1,), (1,)), ((), ())), preferred_element_type=F32) * scale
        masked = jnp.where(valid, scores, MASKED)
        peak = jnp.max(masked, axis=1, keepdims=True)
        weight = jnp.where(valid, jnp.exp(masked - peak), 0.0)
        total = jnp.sum(weight, axis=1, keepdims=True)
        summed = jnp.dot(weight.astype(BF16), value, preferred_element_type=F32)
        context = (summed / total).astype(BF16)
        for step in range(parts):
            outs_refs[step][:, at : at + HEAD_DIM] = context[step * local : (step + 1) * local]


def output_kernel(parts, slots_ref, starts_ref, lengths_ref, frames_ref, sample_ref, *refs):
    copies = lax.axis_size("dp") // parts
    context_refs, refs = refs[:parts], refs[parts:]
    stack_refs, refs = refs[:copies], refs[copies:]
    out_ref, buffer, context, sems = refs
    moves = gathered_copies(parts, stack_refs, buffer, sems)
    for move in moves:
        move.start()
    plane = lax.axis_index("seq")
    begin, end = bounds(lax.axis_index("dp"), slots_ref, starts_ref, lengths_ref)
    head_width = context_refs[0].shape[1]
    for step in range(parts):
        at = pl.multiple_of(later(plane, step, parts) * head_width, LANES)
        context[:, pl.ds(at, head_width)] = context_refs[step][...]
    ordered = jnp.dot(frames_ref[...], context[...], preferred_element_type=F32).astype(BF16)
    sample = sample_ref[...] + plane * (W * SPAN)
    valid = (sample >= begin) & (sample < end)
    for move in moves:
        move.wait()
    result = jnp.concatenate(
        [jnp.dot(ordered, buffer[d], preferred_element_type=F32) for d in range(buffer.shape[0])], axis=1
    )
    out_ref[...] = jnp.where(valid, result, 0.0).astype(BF16)


def on_device(
    audio, starts, lengths, slots, conv1_weight, conv2_weight, proj_weight, qkv_weight, out_weight
):
    streams = audio.shape[0]
    windows = lax.axis_size("dp")
    group = lax.axis_size("seq")
    parts = group
    copies = windows // parts
    assert BANDS % parts == 0 and streams == copies * group and streams == windows
    share = BANDS // parts
    width = 4 * share + 4
    channels = conv1_weight.shape[1]
    features = proj_weight.shape[1]
    head_width = features // parts
    local = windows * W
    sources = windows * group
    n = sources
    outs = 2 * share + 1

    route = [(i, i + 1) for i in range(sources - 1)]
    rim = lax.ppermute(audio[:, audio.shape[1] - RIM :], ("dp", "seq"), route)

    def to_part(block, step):
        pairs = [(p * copies + c, (p + step) % parts * copies + c) for p in range(parts) for c in range(copies)]
        return lax.ppermute(block, "dp", pairs)

    def to_copy(block, step):
        pairs = [(p * copies + c, p * copies + (c + step) % copies) for p in range(parts) for c in range(copies)]
        return lax.ppermute(block, "dp", pairs)

    def to_owner(block, step):
        pairs = []
        for p in range(parts):
            for c in range(copies):
                for z in range(group):
                    pairs.append(((p * copies + c) * group + z, (z * copies + c) * group + (p - step) % parts))
        return lax.ppermute(block, ("dp", "seq"), pairs)

    proj_all = [proj_weight] + [to_copy(proj_weight, step) for step in range(1, copies)]

    *mix_parts, banded = pl.pallas_call(
        functools.partial(prep_kernel, parts, width),
        out_shape=tuple(
            [jax.ShapeDtypeStruct((qkv_weight.shape[0], 3 * head_width), BF16)] * parts
            + [jax.ShapeDtypeStruct((LANES, outs * channels), BF16)]
        ),
        in_specs=[anywhere(), vmem()],
        out_specs=tuple([anywhere()] * parts + [vmem()]),
        scratch_shapes=[pltpu.SemaphoreType.DMA((3 * parts,))],
        compiler_params=params(16),
        cost_estimate=cost(1e8, 4e6),
        name="prep",
    )(qkv_weight, conv1_weight)
    mix_all = [mix_parts[0]] + [to_part(mix_parts[step], step) for step in range(1, parts)]
    out_all = [out_weight] + [to_part(out_weight, step) for step in range(1, parts)]

    targets = (slots[None, :] * W + jnp.arange(W, dtype=jnp.int32)[:, None]).reshape(1, W * streams)
    mel = pl.pallas_call(
        functools.partial(mel_kernel, parts, group),
        out_shape=jax.ShapeDtypeStruct((sources, W, LANES), BF16),
        in_specs=[vmem()] * 6,
        out_specs=vmem(),
        scratch_shapes=[pltpu.VMEM((streams, RIM + audio.shape[1]), F32)],
        compiler_params=params(24),
        cost_estimate=cost(2e9, 2e6),
        name="log_mel",
    )(
        rim,
        audio,
        jnp.asarray(spectrum_table(N_FFT)),
        jnp.asarray(filter_table()),
        jnp.asarray(band_selection(parts)),
        targets,
    )
    mel = lax.all_to_all(mel, ("dp", "seq"), split_axis=0, concat_axis=0, tiled=True)

    block = jax.ShapeDtypeStruct((local, features), BF16)
    *partials, mix_stack = pl.pallas_call(
        functools.partial(conv_kernel, parts, width, windows),
        out_shape=tuple([block] * parts + [jax.ShapeDtypeStruct((parts,) + mix_parts[0].shape, BF16)]),
        in_specs=[vmem()] * 4 + [anywhere()] * (1 + copies + parts),
        out_specs=tuple([vmem()] * parts + [anywhere()]),
        scratch_shapes=[
            pltpu.VMEM((JS * n, banded.shape[1]), BF16),
            pltpu.VMEM((W * n, banded.shape[1]), BF16),
            pltpu.VMEM((W * n, share * channels), BF16),
            pltpu.VMEM(conv2_weight.shape, BF16),
            pltpu.VMEM((copies,) + proj_weight.shape, BF16),
            pltpu.VMEM((W * n, features), F32),
            pltpu.SemaphoreType.DMA((1 + copies + parts,)),
        ],
        compiler_params=params(48),
        cost_estimate=cost(8e9, 4e6),
        name="conv",
    )(
        mel,
        jnp.asarray(shift_selection(width)),
        jnp.asarray(row_selection(windows, group)),
        banded,
        conv2_weight,
        *proj_all,
        *mix_all,
    )
    mix_stacks = [mix_stack] + [to_copy(mix_stack, step) for step in range(1, copies)]
    partials = [partials[0]] + [to_part(partials[step], step) for step in range(1, parts)]

    index = np.arange(local)
    out_sample = ((index // W) * group * W + index % W) * SPAN
    key_sample = ((index % windows) * group * W + index // windows) * SPAN
    out_sample = jnp.asarray(out_sample.reshape(-1, 1).astype(np.int32))
    key_sample = jnp.asarray(key_sample.reshape(1, -1).astype(np.int32))
    frames = jnp.asarray(frame_table(windows))
    regrouped, normed, out_stack = pl.pallas_call(
        functools.partial(norm_kernel, parts),
        out_shape=(block, block, jax.ShapeDtypeStruct((parts,) + out_weight.shape, BF16)),
        in_specs=[smem()] * 3 + [vmem()] * (2 + parts) + [anywhere()] * parts,
        out_specs=(vmem(), vmem(), anywhere()),
        scratch_shapes=[pltpu.SemaphoreType.DMA((parts,))],
        compiler_params=params(24),
        cost_estimate=cost(1e8, 1e6),
        name="layer_norm",
    )(slots, starts, lengths, frames, out_sample, *partials, *out_all)
    normed = [normed] + [to_part(normed, step) for step in range(1, parts)]
    out_stacks = [out_stack] + [to_copy(out_stack, step) for step in range(1, copies)]
    regrouped = to_owner(regrouped, 0)

    context = pl.pallas_call(
        functools.partial(attention_kernel, parts),
        out_shape=tuple([jax.ShapeDtypeStruct((local, head_width), BF16)] * parts),
        in_specs=[smem()] * 3 + [vmem()] * (1 + parts) + [anywhere()] * copies,
        out_specs=tuple([vmem()] * parts),
        scratch_shapes=[
            pltpu.VMEM((windows,) + mix_parts[0].shape, BF16),
            pltpu.SemaphoreType.DMA((windows,)),
        ],
        compiler_params=params(48),
        cost_estimate=cost(1e9, 2e6),
        name="attention",
    )(slots, starts, lengths, key_sample, *normed, *mix_stacks)
    context = [to_owner(context[step], step) for step in range(parts)]

    attended = pl.pallas_call(
        functools.partial(output_kernel, parts),
        out_shape=block,
        in_specs=[smem()] * 3 + [vmem()] * (2 + parts) + [anywhere()] * copies,
        out_specs=vmem(),
        scratch_shapes=[
            pltpu.VMEM((windows,) + out_weight.shape, BF16),
            pltpu.VMEM((local, features), BF16),
            pltpu.SemaphoreType.DMA((windows,)),
        ],
        compiler_params=params(24),
        cost_estimate=cost(1e8, 3e6),
        name="output",
    )(slots, starts, lengths, frames, out_sample, *context, *out_stacks)
    shape = (1, windows, 1, W, features)
    return (regrouped.reshape(shape), attended.reshape(shape))


def solution(mesh):
    in_specs = (
        P(None, ("dp", "seq")),
        P(),
        P(),
        P(),
        P(),
        P(),
        P("dp", None),
        P("dp", None),
        P(None, "dp"),
    )
    out_specs = (P("dp", None, "seq", None, None), P("dp", None, "seq", None, None))
    return jax.shard_map(
        on_device, mesh=mesh, in_specs=in_specs, out_specs=out_specs, check_vma=False
    )
```

```python
import functools
import math

import jax
import jax.numpy as jnp
import numpy as np
from jax import lax
from jax.experimental import pallas as pl
from jax.experimental.pallas import tpu as pltpu
from jax.sharding import PartitionSpec as P

HEADS = 8
HEAD_DIM = 128
MELS = 80
BANDS = MELS // 4
N_FFT = 512
HOP = 160
W = 8
RIM = 384
SPAN = 4 * HOP
JS = W + 1
LANES = 128
SAMPLE_RATE = 16000.0
EPS_LOG = 1e-06
EPS_NORM = 1e-05
MASKED = -1e30
F32 = jnp.float32
BF16 = jnp.bfloat16
MIB = 1 << 20


def mel_table(size, bands):
    count = size // 2 + 1
    highest = 2595.0 * math.log10(1.0 + SAMPLE_RATE / 1400.0)
    points = np.linspace(0.0, highest, bands + 2)
    edges = 700.0 * (10.0 ** (points / 2595.0) - 1.0)
    edges[0] = 0.0
    edges[-1] = SAMPLE_RATE / 2.0
    frequency = np.arange(count) * (SAMPLE_RATE / size)
    lower = edges[:-2][None, :]
    middle = edges[1:-1][None, :]
    upper = edges[2:][None, :]
    rising = (frequency[:, None] - lower) / (middle - lower)
    falling = (upper - frequency[:, None]) / (upper - middle)
    return np.maximum(0.0, np.minimum(rising, falling)).astype(np.float32)


def filter_table():
    table = mel_table(N_FFT, MELS)[: N_FFT // 2]
    return np.pad(table, ((0, 0), (0, LANES - MELS)))


def spectrum_table(size):
    sample = np.arange(size)
    phase = sample[:, None] * np.arange(size // 2)[None, :] % size
    angle = phase * (2.0 * math.pi / size)
    window = 0.5 - 0.5 * np.cos(sample * (2.0 * math.pi / size))
    both = np.concatenate([np.cos(angle), np.sin(angle)], axis=1) * window[:, None]
    return both.astype(np.float32)


def band_selection(parts):
    share = BANDS // parts
    width = 4 * share + 4
    table = np.zeros((4 * LANES, parts * LANES), np.float32)
    for part in range(parts):
        for delta in range(4):
            for lane in range(width):
                band = 4 * share * part - 4 + lane
                if 0 <= band < MELS:
                    table[delta * LANES + band, part * LANES + delta * width + lane] = 1.0
    return table.astype(BF16)


def shift_selection(width):
    table = np.zeros((LANES, 2 * LANES), np.float32)
    lane = np.arange(width)
    for delta in range(3):
        table[(delta + 1) * width + lane, delta * width + lane] = 1.0
    for delta in range(2):
        table[delta * width + lane, LANES + (delta + 3) * width + lane] = 1.0
    return table.astype(BF16)


def row_selection(windows, group):
    count = windows * group
    earlier = np.zeros((JS * count, W * count), np.float32)
    same = np.zeros((JS * count, W * count), np.float32)
    for j in range(JS):
        for s in range(group):
            for k in range(windows):
                row = j * count + s * windows + k
                window = k * group + s
                if j:
                    earlier[row, window * W + j - 1] = 1.0
                elif window:
                    earlier[row, (window - 1) * W + W - 1] = 1.0
                if j < W:
                    same[row, window * W + j] = 1.0
    return np.concatenate([earlier, same], axis=1).astype(BF16)


def frame_table(windows):
    count = windows * W
    table = np.zeros((count, count), np.float32)
    for k in range(windows):
        for t in range(W):
            table[k * W + t, t * windows + k] = 1.0
    return table.astype(BF16)


def vmem():
    return pl.BlockSpec(memory_space=pltpu.VMEM)


def smem():
    return pl.BlockSpec(memory_space=pltpu.SMEM)


def anywhere():
    return pl.BlockSpec(memory_space=pl.ANY)


def hbm():
    return pl.BlockSpec(memory_space=pltpu.HBM)


def params(mib):
    return pltpu.CompilerParams(vmem_limit_bytes=mib * MIB)


def cost(flops, moved):
    return pl.CostEstimate(flops=int(flops), bytes_accessed=int(moved), transcendentals=0)


def place(parts):
    mine = lax.axis_index("dp")
    copies = lax.axis_size("dp") // parts
    return mine // copies, mine % copies


def later(index, step, count):
    return lax.rem(index + step, count)


def start_all(copies):
    for copy in copies:
        copy.start()


def wait_all(copies):
    for copy in copies:
        copy.wait()


def loads_of(sources, targets, sems, base):
    return [
        pltpu.make_async_copy(source, target, sems.at[base + i])
        for i, (source, target) in enumerate(zip(sources, targets))
    ]


def prep_kernel(parts, width, tables, conv1_ref, qkv_ref, out_ref, *refs):
    table_refs, refs = refs[:tables], refs[tables:]
    table_outs, refs = refs[:tables], refs[tables:]
    pack_outs, (banded_out, sems) = refs[:parts], refs[parts:]
    part, _ = place(parts)
    rows = qkv_ref.shape[0]
    features = qkv_ref.shape[1] // 3
    head_width = features // parts
    blocks = head_width // LANES
    copies = loads_of(table_refs, table_outs, sems, 0)
    for step in range(parts):
        first = pl.multiple_of(later(part, step, parts) * head_width, LANES)
        for kind in range(3):
            for piece in range(blocks):
                source = qkv_ref.at[:, pl.ds(kind * features + first + piece * LANES, LANES)]
                target = pack_outs[step].at[pl.ds((kind * blocks + piece) * rows, rows)]
                copies.append(pltpu.make_async_copy(source, target, sems.at[len(copies)]))
        target = pack_outs[step].at[pl.ds(3 * blocks * rows, out_ref.shape[0])]
        copies.append(pltpu.make_async_copy(out_ref, target, sems.at[len(copies)]))
    start_all(copies)
    taps, channels = conv1_ref.shape
    outs = banded_out.shape[1] // channels
    row = lax.broadcasted_iota(jnp.int32, (LANES, taps), 0)
    tap = lax.broadcasted_iota(jnp.int32, (LANES, taps), 1)
    line = (tap >= 3).astype(jnp.int32) + (tap >= 6).astype(jnp.int32)
    target = line * (width - 3) + tap + 1
    weight = conv1_ref[...]
    for g in range(outs):
        select = (row == target + 2 * g).astype(F32).astype(BF16)
        banded_out[:, g * channels : (g + 1) * channels] = jnp.dot(
            select, weight, preferred_element_type=F32
        ).astype(BF16)
    wait_all(copies)


def mel_kernel(
    parts, group, tables, slots_ref, rim_ref, audio_ref, table_ref, filter_ref, select_ref, *refs
):
    table_refs, refs = refs[:tables], refs[tables:]
    out_ref, refs = refs[0], refs[1:]
    table_outs, (ext, sems) = refs[:tables], refs[tables:]
    loads = loads_of(table_refs, table_outs, sems, 0)
    start_all(loads)
    streams = audio_ref.shape[0]
    rows = W * streams
    ext[:, :RIM] = rim_ref[...]
    ext[:, RIM:] = audio_ref[...]
    phases = []
    for phase in range(4):
        start = HOP * phase + 32
        base, shift = start // LANES * LANES, start % LANES
        length = N_FFT + (LANES if shift else 0)
        block = jnp.concatenate(
            [ext[:, SPAN * j + base : SPAN * j + base + length] for j in range(W)], axis=0
        )
        if shift:
            block = pltpu.roll(block, length - shift, 1)[:, :N_FFT]
        phases.append(block)
    frames = jnp.concatenate(phases, axis=0)
    spectrum = jnp.dot(frames, table_ref[...], precision=lax.Precision.HIGHEST, preferred_element_type=F32)
    half = N_FFT // 2
    real, imag = spectrum[:, :half], spectrum[:, half:]
    power = real * real + imag * imag
    mel_power = jnp.dot(power, filter_ref[...], precision=lax.Precision.HIGHEST, preferred_element_type=F32)
    log_mel = jnp.log(mel_power + EPS_LOG).astype(BF16)
    gathered = jnp.concatenate([log_mel[phase * rows : (phase + 1) * rows] for phase in range(4)], axis=1)
    placed = jnp.dot(gathered, select_ref[...], preferred_element_type=F32).astype(BF16)
    column = lax.broadcasted_iota(jnp.int32, (1, rows), 1)
    early = jnp.zeros((1, rows), jnp.int32)
    for j in range(1, W):
        early += (column >= j * streams).astype(jnp.int32)
    target = jnp.zeros((1, rows), jnp.int32)
    for u in range(streams):
        target = jnp.where(column - early * streams == u, slots_ref[u] * W + early, target)
    routing = (target == lax.broadcasted_iota(jnp.int32, (rows, rows), 0)).astype(F32).astype(BF16)
    routed = jnp.dot(routing, placed, preferred_element_type=F32)
    copies = streams // group
    for part in range(parts):
        for copy in range(copies):
            for plane in range(group):
                row = plane * copies + copy
                out_ref[(part * copies + copy) * group + plane] = routed[
                    row * W : (row + 1) * W, part * LANES : (part + 1) * LANES
                ].astype(BF16)
    wait_all(loads)


def conv_kernel(parts, width, windows, mel_ref, banded_ref, conv2, rows_ref, shift_ref, *refs):
    part, copy_index = place(parts)
    copies = lax.axis_size("dp") // parts
    proj_refs, refs = refs[:copies], refs[copies:]
    pack_refs, refs = refs[:parts], refs[parts:]
    outs_refs, refs = refs[:parts], refs[parts:]
    stack_out, even, odd, second, proj, partial, sems = refs
    loads = []
    for step in range(copies):
        slot = later(copy_index, copies - step, copies)
        loads.append(pltpu.make_async_copy(proj_refs[step], proj.at[slot], sems.at[step]))
    for step in range(parts):
        slot = later(part, parts - step, parts)
        loads.append(pltpu.make_async_copy(pack_refs[step], stack_out.at[slot], sems.at[copies + step]))
    start_all(loads)
    sources = mel_ref.shape[0]
    n = sources
    payload = mel_ref[...].astype(F32).reshape(sources * W, LANES).astype(BF16)
    shifted = jnp.dot(payload, shift_ref[...], preferred_element_type=F32).astype(BF16)
    both = jnp.concatenate([shifted[:, :LANES], shifted[:, LANES:]], axis=0)
    evens = jnp.dot(rows_ref[...], both, preferred_element_type=F32)
    row = lax.broadcasted_iota(jnp.int32, evens.shape, 0)
    lane = lax.broadcasted_iota(jnp.int32, evens.shape, 1)
    low = (lane >= width).astype(jnp.int32) + (lane >= 2 * width).astype(jnp.int32)
    band = lane - low * width - 4 + (width - 4) * part
    silent = (row == 0) & (lane < 3 * width) & (band >= 0)
    evens = jnp.where(silent, jnp.log(jnp.full(evens.shape, EPS_LOG, F32)), evens)
    odds = pltpu.roll(evens[: W * n], LANES - 2 * width, 1).astype(BF16)
    evens = evens.astype(BF16)
    channels = conv2.shape[1]
    outs = banded_ref.shape[1] // channels
    for g in range(outs):
        lanes = slice(g * channels, (g + 1) * channels)
        weight = banded_ref[:, lanes]
        even[:, lanes] = jax.nn.relu(jnp.dot(evens, weight, preferred_element_type=F32)).astype(BF16)
        odd[:, lanes] = jax.nn.relu(jnp.dot(odds, weight, preferred_element_type=F32)).astype(BF16)

    for h in range((outs - 1) // 2):
        lanes = slice(2 * h * channels, (2 * h + 3) * channels)
        depth = 3 * channels
        total = jnp.dot(even[: W * n, lanes], conv2[:depth], preferred_element_type=F32)
        total += jnp.dot(odd[:, lanes], conv2[depth : 2 * depth], preferred_element_type=F32)
        total += jnp.dot(even[n:, lanes], conv2[2 * depth :], preferred_element_type=F32)
        second[:, h * channels : (h + 1) * channels] = jax.nn.relu(total).astype(BF16)
    wait_all(loads)
    weights = proj[...].reshape(second.shape[1], proj.shape[2])
    partial[...] = jnp.dot(second[...], weights, preferred_element_type=F32)
    for step in range(parts):
        plane = later(part, step, parts)
        outs_refs[step][...] = jnp.concatenate(
            [partial[pl.ds(pl.multiple_of(t * n + plane * windows, 8), windows), :] for t in range(W)], axis=0
        ).astype(BF16)


def bounds(row, slots_ref, starts_ref, lengths_ref):
    begin, span = jnp.int32(0), jnp.int32(0)
    for u in range(slots_ref.shape[0]):
        chosen = slots_ref[u] == row
        begin = begin + jnp.where(chosen, starts_ref[u], 0)
        span = span + jnp.where(chosen, lengths_ref[u], 0)
    return begin, begin + span


def place_mix(parts, rows, stack_refs, buffer, sems, base):
    _, copy_index = place(parts)
    copies = len(stack_refs)
    moves = []
    for step in range(copies):
        slot = later(copy_index, copies - step, copies)
        for piece in range(parts):
            for block in range(buffer.shape[2] // LANES):
                source = stack_refs[step].at[piece, pl.ds(block * rows, rows)]
                target = buffer.at[piece * copies + slot, :, pl.ds(block * LANES, LANES)]
                moves.append(pltpu.make_async_copy(source, target, sems.at[base + len(moves)]))
    return moves


def place_out(parts, rows, stack_refs, buffer, sems, base):
    _, copy_index = place(parts)
    copies = len(stack_refs)
    moves = []
    for step in range(copies):
        slot = later(copy_index, copies - step, copies)
        for piece in range(parts):
            source = stack_refs[step].at[piece, pl.ds(rows, buffer.shape[1])]
            target = buffer.at[piece * copies + slot]
            moves.append(pltpu.make_async_copy(source, target, sems.at[base + len(moves)]))
    return moves


def norm_kernel(parts, slots_ref, starts_ref, lengths_ref, frames_ref, sample_ref, *refs):
    part, copy_index = place(parts)
    copies = lax.axis_size("dp") // parts
    part_refs, refs = refs[:parts], refs[parts:]
    stack_refs, refs = refs[:copies], refs[copies:]
    rows_out, normed_out, mix_out, sems = refs
    moves = place_mix(parts, mix_out.shape[1], stack_refs, mix_out, sems, 0)
    start_all(moves)
    row = lax.axis_index("seq") * copies + copy_index
    begin, end = bounds(row, slots_ref, starts_ref, lengths_ref)
    total = part_refs[0][...].astype(F32)
    for step in range(1, parts):
        total += part_refs[step][...].astype(F32)
    encoded = total.astype(BF16)
    values = encoded.astype(F32)
    mean = jnp.mean(values, axis=-1, keepdims=True)
    centered = values - mean
    variance = jnp.mean(centered * centered, axis=-1, keepdims=True)
    normed_out[...] = (centered * lax.rsqrt(variance + EPS_NORM)).astype(BF16)
    ordered = jnp.dot(frames_ref[...], encoded, preferred_element_type=F32)
    sample = sample_ref[...] + part * (W * SPAN)
    valid = (sample >= begin) & (sample < end)
    rows_out[...] = jnp.where(valid, ordered, 0.0).astype(BF16)
    wait_all(moves)


def attention_kernel(parts, mix_rows, slots_ref, starts_ref, lengths_ref, sample_ref, mix_ref, *refs):
    part, copy_index = place(parts)
    copies = lax.axis_size("dp") // parts
    normed_refs, refs = refs[:parts], refs[parts:]
    stack_refs, refs = refs[:copies], refs[copies:]
    outs_refs, (weights_out, sems) = refs[:parts], refs[parts:]
    moves = place_out(parts, mix_rows, stack_refs, weights_out, sems, 0)
    start_all(moves)
    row = lax.axis_index("seq") * copies + copy_index
    begin, end = bounds(row, slots_ref, starts_ref, lengths_ref)
    masks = []
    for step in range(parts):
        plane = later(part, parts - step, parts)
        sample = sample_ref[...] + plane * (W * SPAN)
        masks.append(((sample >= begin) & (sample < end)).astype(F32))
    valid = jnp.concatenate(masks, axis=1) > 0.5
    normed = jnp.concatenate([ref[...] for ref in normed_refs], axis=0)
    local, features = normed_refs[0].shape
    weights = mix_ref[...].reshape(features, mix_ref.shape[2])
    mixed = jnp.dot(normed, weights, preferred_element_type=F32).astype(BF16)
    width = mix_ref.shape[2] // 3
    scale = HEAD_DIM ** (-0.5)
    for head in range(width // HEAD_DIM):
        at = head * HEAD_DIM
        query = mixed[:, at : at + HEAD_DIM]
        key = mixed[:, width + at : width + at + HEAD_DIM]
        value = mixed[:, 2 * width + at : 2 * width + at + HEAD_DIM]
        scores = lax.dot_general(query, key, (((1,), (1,)), ((), ())), preferred_element_type=F32) * scale
        masked = jnp.where(valid, scores, MASKED)
        peak = jnp.max(masked, axis=1, keepdims=True)
        weight = jnp.where(valid, jnp.exp(masked - peak), 0.0)
        total = jnp.sum(weight, axis=1, keepdims=True)
        summed = jnp.dot(weight.astype(BF16), value, preferred_element_type=F32)
        context = (summed / total).astype(BF16)
        for step in range(parts):
            outs_refs[step][:, at : at + HEAD_DIM] = context[step * local : (step + 1) * local]
    wait_all(moves)


def output_kernel(parts, slots_ref, starts_ref, lengths_ref, frames_ref, sample_ref, weights_ref, rows_ref, *refs):
    context_refs, refs = refs[:parts], refs[parts:]
    rows_out, out_ref, context, sems = refs
    keep = pltpu.make_async_copy(rows_ref, rows_out, sems.at[0])
    keep.start()
    plane = lax.axis_index("seq")
    begin, end = bounds(lax.axis_index("dp"), slots_ref, starts_ref, lengths_ref)
    head_width = context_refs[0].shape[1]
    for step in range(parts):
        at = pl.multiple_of(later(plane, step, parts) * head_width, LANES)
        context[:, pl.ds(at, head_width)] = context_refs[step][...]
    ordered = jnp.dot(frames_ref[...], context[...], preferred_element_type=F32).astype(BF16)
    sample = sample_ref[...] + plane * (W * SPAN)
    valid = (sample >= begin) & (sample < end)
    result = jnp.concatenate(
        [jnp.dot(ordered, weights_ref[d], preferred_element_type=F32) for d in range(weights_ref.shape[0])], axis=1
    )
    out_ref[...] = jnp.where(valid, result, 0.0).astype(BF16)
    keep.wait()


def on_device(
    audio, starts, lengths, slots, conv1_weight, conv2_weight, proj_weight, qkv_weight, out_weight
):
    streams = audio.shape[0]
    windows = lax.axis_size("dp")
    group = lax.axis_size("seq")
    parts = group
    copies = windows // parts
    assert BANDS % parts == 0 and streams == copies * group and streams == windows
    share = BANDS // parts
    width = 4 * share + 4
    channels = conv1_weight.shape[1]
    features = proj_weight.shape[1]
    head_width = features // parts
    local = windows * W
    sources = windows * group
    n = sources
    outs = 2 * share + 1

    route = [(i, i + 1) for i in range(sources - 1)]
    rim = lax.ppermute(audio[:, audio.shape[1] - RIM :], ("dp", "seq"), route)

    def to_part(block, step):
        pairs = [(p * copies + c, (p + step) % parts * copies + c) for p in range(parts) for c in range(copies)]
        return lax.ppermute(block, "dp", pairs)

    def to_copy(block, step):
        pairs = [(p * copies + c, p * copies + (c + step) % copies) for p in range(parts) for c in range(copies)]
        return lax.ppermute(block, "dp", pairs)

    def to_owner(block, step):
        pairs = []
        for p in range(parts):
            for c in range(copies):
                for z in range(group):
                    pairs.append(((p * copies + c) * group + z, (z * copies + c) * group + (p - step) % parts))
        return lax.ppermute(block, ("dp", "seq"), pairs)

    scale = sources // 32
    proj_all = [proj_weight] + [to_copy(proj_weight, step) for step in range(1, copies)]

    def like(array):
        return jax.ShapeDtypeStruct(array.shape, array.dtype)

    tables = [
        audio,
        jnp.asarray(spectrum_table(N_FFT)),
        jnp.asarray(filter_table()),
        jnp.asarray(band_selection(parts)),
    ]
    mix_rows = 3 * head_width // LANES * qkv_weight.shape[0]
    out_packed = out_weight.reshape(-1, LANES)
    pack = jax.ShapeDtypeStruct((mix_rows + out_packed.shape[0], LANES), BF16)
    prepared = pl.pallas_call(
        functools.partial(prep_kernel, parts, width, len(tables)),
        out_shape=tuple(
            [like(table) for table in tables]
            + [pack] * parts
            + [jax.ShapeDtypeStruct((LANES, outs * channels), BF16)]
        ),
        in_specs=[vmem()] + [hbm()] * (2 + len(tables)),
        out_specs=tuple([vmem()] * len(tables) + [anywhere()] * parts + [vmem()]),
        scratch_shapes=[
            pltpu.SemaphoreType.DMA((len(tables) + parts * (3 * head_width // LANES + 1),))
        ],
        compiler_params=params(min(16 * scale, 32)),
        cost_estimate=cost(1e8, 4e6),
        name="prep",
    )(conv1_weight, qkv_weight, out_packed, *tables)
    tables, packs, banded = prepared[: len(tables)], prepared[len(tables) : -1], prepared[-1]

    later_tables = [
        conv2_weight,
        jnp.asarray(row_selection(windows, group)),
        jnp.asarray(shift_selection(width)),
    ]
    mel, *later_tables = pl.pallas_call(
        functools.partial(mel_kernel, parts, group, len(later_tables)),
        out_shape=tuple(
            [jax.ShapeDtypeStruct((sources, W, LANES), BF16)] + [like(table) for table in later_tables]
        ),
        in_specs=[smem()] + [vmem()] * (1 + len(tables)) + [hbm()] * len(later_tables),
        out_specs=tuple([vmem()] * (1 + len(later_tables))),
        scratch_shapes=[
            pltpu.VMEM((streams, RIM + audio.shape[1]), F32),
            pltpu.SemaphoreType.DMA((len(later_tables),)),
        ],
        compiler_params=params(min(20 * scale, 48)),
        cost_estimate=cost(2e9, 2e6),
        name="log_mel",
    )(slots, rim, *tables, *later_tables)
    mel, *packs = lax.optimization_barrier((mel, *packs))
    mel = lax.all_to_all(mel, ("dp", "seq"), split_axis=0, concat_axis=0, tiled=True)
    packs = [packs[0]] + [to_part(packs[step], step) for step in range(1, parts)]

    block = jax.ShapeDtypeStruct((local, features), BF16)
    *partials, stack = pl.pallas_call(
        functools.partial(conv_kernel, parts, width, windows),
        out_shape=tuple([block] * parts + [jax.ShapeDtypeStruct((parts,) + pack.shape, BF16)]),
        in_specs=[vmem()] * (2 + len(later_tables)) + [anywhere()] * (copies + parts),
        out_specs=tuple([vmem()] * parts + [anywhere()]),
        scratch_shapes=[
            pltpu.VMEM((JS * n, banded.shape[1]), BF16),
            pltpu.VMEM((W * n, banded.shape[1]), BF16),
            pltpu.VMEM((W * n, share * channels), BF16),
            pltpu.VMEM((copies,) + proj_weight.shape, BF16),
            pltpu.VMEM((W * n, features), F32),
            pltpu.SemaphoreType.DMA((copies + parts,)),
        ],
        compiler_params=params(min(24 * scale, 48)),
        cost_estimate=cost(8e9, 4e6),
        name="conv",
    )(mel, banded, *later_tables, *proj_all, *packs)
    stacks = [stack] + [to_copy(stack, step) for step in range(1, copies)]
    partials = [partials[0]] + [to_part(partials[step], step) for step in range(1, parts)]

    index = np.arange(local)
    out_sample = ((index // W) * group * W + index % W) * SPAN
    key_sample = ((index % windows) * group * W + index // windows) * SPAN
    out_sample = jnp.asarray(out_sample.reshape(-1, 1).astype(np.int32))
    key_sample = jnp.asarray(key_sample.reshape(1, -1).astype(np.int32))
    frames = jnp.asarray(frame_table(windows))
    mix = jax.ShapeDtypeStruct((windows, qkv_weight.shape[0], 3 * head_width), BF16)
    regrouped, normed, mix = pl.pallas_call(
        functools.partial(norm_kernel, parts),
        out_shape=(block, block, mix),
        in_specs=[smem()] * 3 + [vmem()] * (2 + parts) + [anywhere()] * copies,
        out_specs=(vmem(), vmem(), vmem()),
        scratch_shapes=[pltpu.SemaphoreType.DMA((windows * (3 * head_width // LANES),))],
        compiler_params=params(min(12 * scale, 32)),
        cost_estimate=cost(1e8, 1e6),
        name="layer_norm",
    )(slots, starts, lengths, frames, out_sample, *partials, *stacks)
    normed = [normed] + [to_part(normed, step) for step in range(1, parts)]
    regrouped = to_owner(regrouped, 0)

    out_columns = jax.ShapeDtypeStruct((windows,) + out_weight.shape, BF16)
    if out_packed.shape != out_weight.shape:
        stacks = [stack[:, mix_rows:].reshape((parts,) + out_weight.shape) for stack in stacks]
        mix_rows = 0
    *context, out_columns = pl.pallas_call(
        functools.partial(attention_kernel, parts, mix_rows),
        out_shape=tuple([jax.ShapeDtypeStruct((local, head_width), BF16)] * parts + [out_columns]),
        in_specs=[smem()] * 3 + [vmem()] * (2 + parts) + [anywhere()] * copies,
        out_specs=tuple([vmem()] * (parts + 1)),
        scratch_shapes=[pltpu.SemaphoreType.DMA((windows,))],
        compiler_params=params(min(16 * scale, 48)),
        cost_estimate=cost(1e9, 2e6),
        name="attention",
    )(slots, starts, lengths, key_sample, mix, *normed, *stacks)
    context = [to_owner(context[step], step) for step in range(parts)]

    regrouped, attended = pl.pallas_call(
        functools.partial(output_kernel, parts),
        out_shape=(block, block),
        in_specs=[smem()] * 3 + [vmem()] * 3 + [anywhere()] + [vmem()] * parts,
        out_specs=(anywhere(), vmem()),
        scratch_shapes=[pltpu.VMEM((local, features), BF16), pltpu.SemaphoreType.DMA((1,))],
        compiler_params=params(min(12 * scale, 32)),
        cost_estimate=cost(1e8, 3e6),
        name="output",
    )(slots, starts, lengths, frames, out_sample, out_columns, regrouped, *context)
    shape = (1, windows, 1, W, features)
    return (regrouped.reshape(shape), attended.reshape(shape))


def solution(mesh):
    in_specs = (
        P(None, ("dp", "seq")),
        P(),
        P(),
        P(),
        P(),
        P(),
        P("dp", None),
        P("dp", None),
        P(None, "dp"),
    )
    out_specs = (P("dp", None, "seq", None, None), P("dp", None, "seq", None, None))
    return jax.shard_map(
        on_device, mesh=mesh, in_specs=in_specs, out_specs=out_specs, check_vma=False
    )
```

```python
import functools
import math

import jax
import jax.numpy as jnp
import numpy as np
from jax import lax
from jax.experimental import pallas as pl
from jax.experimental.pallas import tpu as pltpu
from jax.sharding import PartitionSpec as P

HEADS = 8
HEAD_DIM = 128
MELS = 80
BANDS = MELS // 4
N_FFT = 512
HOP = 160
W = 8
RIM = 384
SPAN = 4 * HOP
JS = W + 1
LANES = 128
SAMPLE_RATE = 16000.0
EPS_LOG = 1e-06
EPS_NORM = 1e-05
MASKED = -1e30
F32 = jnp.float32
BF16 = jnp.bfloat16
MIB = 1 << 20


def mel_table(size, bands):
    count = size // 2 + 1
    highest = 2595.0 * math.log10(1.0 + SAMPLE_RATE / 1400.0)
    points = np.linspace(0.0, highest, bands + 2)
    edges = 700.0 * (10.0 ** (points / 2595.0) - 1.0)
    edges[0] = 0.0
    edges[-1] = SAMPLE_RATE / 2.0
    frequency = np.arange(count) * (SAMPLE_RATE / size)
    lower = edges[:-2][None, :]
    middle = edges[1:-1][None, :]
    upper = edges[2:][None, :]
    rising = (frequency[:, None] - lower) / (middle - lower)
    falling = (upper - frequency[:, None]) / (upper - middle)
    return np.maximum(0.0, np.minimum(rising, falling)).astype(np.float32)


def filter_table():
    table = mel_table(N_FFT, MELS)[: N_FFT // 2]
    return np.pad(table, ((0, 0), (0, LANES - MELS)))


def spectrum_table(size):
    sample = np.arange(size)
    phase = sample[:, None] * np.arange(size // 2)[None, :] % size
    angle = phase * (2.0 * math.pi / size)
    window = 0.5 - 0.5 * np.cos(sample * (2.0 * math.pi / size))
    both = np.concatenate([np.cos(angle), np.sin(angle)], axis=1) * window[:, None]
    return both.astype(np.float32)


def band_selection(parts):
    share = BANDS // parts
    width = 4 * share + 4
    table = np.zeros((4 * LANES, parts * LANES), np.float32)
    for part in range(parts):
        for delta in range(4):
            for lane in range(width):
                band = 4 * share * part - 4 + lane
                if 0 <= band < MELS:
                    table[delta * LANES + band, part * LANES + delta * width + lane] = 1.0
    return table.astype(BF16)


def shift_selection(width):
    table = np.zeros((LANES, 2 * LANES), np.float32)
    lane = np.arange(width)
    for delta in range(3):
        table[(delta + 1) * width + lane, delta * width + lane] = 1.0
    for delta in range(2):
        table[delta * width + lane, LANES + (delta + 3) * width + lane] = 1.0
    return table.astype(BF16)


def row_selection(windows, group):
    count = windows * group
    earlier = np.zeros((JS * count, W * count), np.float32)
    same = np.zeros((JS * count, W * count), np.float32)
    for j in range(JS):
        for s in range(group):
            for k in range(windows):
                row = j * count + s * windows + k
                window = k * group + s
                if j:
                    earlier[row, window * W + j - 1] = 1.0
                elif window:
                    earlier[row, (window - 1) * W + W - 1] = 1.0
                if j < W:
                    same[row, window * W + j] = 1.0
    return np.concatenate([earlier, same], axis=1).astype(BF16)


def frame_table(windows):
    count = windows * W
    table = np.zeros((count, count), np.float32)
    for k in range(windows):
        for t in range(W):
            table[k * W + t, t * windows + k] = 1.0
    return table.astype(BF16)


def vmem():
    return pl.BlockSpec(memory_space=pltpu.VMEM)


def smem():
    return pl.BlockSpec(memory_space=pltpu.SMEM)


def anywhere():
    return pl.BlockSpec(memory_space=pl.ANY)


def hbm():
    return pl.BlockSpec(memory_space=pltpu.HBM)


def params(mib):
    return pltpu.CompilerParams(vmem_limit_bytes=mib * MIB)


def cost(flops, moved):
    return pl.CostEstimate(flops=int(flops), bytes_accessed=int(moved), transcendentals=0)


def place(parts):
    mine = lax.axis_index("dp")
    copies = lax.axis_size("dp") // parts
    return mine // copies, mine % copies


def later(index, step, count):
    return lax.rem(index + step, count)


def start_all(copies):
    for copy in copies:
        copy.start()


def wait_all(copies):
    for copy in copies:
        copy.wait()


def loads_of(sources, targets, sems, base):
    return [
        pltpu.make_async_copy(source, target, sems.at[base + i])
        for i, (source, target) in enumerate(zip(sources, targets))
    ]


def prep_kernel(parts, qkv_ref, *refs):
    mix_outs, sems = refs[:parts], refs[parts]
    part, _ = place(parts)
    features = qkv_ref.shape[1] // 3
    head_width = features // parts
    copies = []
    for step in range(parts):
        first = pl.multiple_of(later(part, step, parts) * head_width, LANES)
        for kind in range(3):
            source = qkv_ref.at[:, pl.ds(kind * features + first, head_width)]
            target = mix_outs[step].at[:, pl.ds(kind * head_width, head_width)]
            copies.append(pltpu.make_async_copy(source, target, sems.at[len(copies)]))
    start_all(copies)
    wait_all(copies)


def banded_weights(width, conv1_ref, banded_out):
    taps, channels = conv1_ref.shape
    row = lax.broadcasted_iota(jnp.int32, (LANES, taps), 0)
    tap = lax.broadcasted_iota(jnp.int32, (LANES, taps), 1)
    line = (tap >= 3).astype(jnp.int32) + (tap >= 6).astype(jnp.int32)
    target = line * (width - 3) + tap + 1
    weight = conv1_ref[...]
    for g in range(banded_out.shape[1] // channels):
        select = (row == target + 2 * g).astype(F32).astype(BF16)
        banded_out[:, g * channels : (g + 1) * channels] = jnp.dot(
            select, weight, preferred_element_type=F32
        ).astype(BF16)


def mel_kernel(
    parts, group, width, tables, slots_ref, rim_ref, audio_ref, table_ref, filter_ref, select_ref, conv1_ref, *refs
):
    table_refs, refs = refs[:tables], refs[tables:]
    (out_ref, banded_out), refs = refs[:2], refs[2:]
    table_outs, (ext, sems) = refs[:tables], refs[tables:]
    loads = loads_of(table_refs, table_outs, sems, 0)
    start_all(loads)
    banded_weights(width, conv1_ref, banded_out)
    streams = audio_ref.shape[0]
    rows = W * streams
    ext[:, :RIM] = rim_ref[...]
    ext[:, RIM:] = audio_ref[...]
    phases = []
    for phase in range(4):
        start = HOP * phase + 32
        base, shift = start // LANES * LANES, start % LANES
        length = N_FFT + (LANES if shift else 0)
        block = jnp.concatenate(
            [ext[:, SPAN * j + base : SPAN * j + base + length] for j in range(W)], axis=0
        )
        if shift:
            block = pltpu.roll(block, length - shift, 1)[:, :N_FFT]
        phases.append(block)
    frames = jnp.concatenate(phases, axis=0)
    spectrum = jnp.dot(frames, table_ref[...], precision=lax.Precision.HIGHEST, preferred_element_type=F32)
    half = N_FFT // 2
    real, imag = spectrum[:, :half], spectrum[:, half:]
    power = real * real + imag * imag
    mel_power = jnp.dot(power, filter_ref[...], precision=lax.Precision.HIGHEST, preferred_element_type=F32)
    log_mel = jnp.log(mel_power + EPS_LOG).astype(BF16)
    gathered = jnp.concatenate([log_mel[phase * rows : (phase + 1) * rows] for phase in range(4)], axis=1)
    placed = jnp.dot(gathered, select_ref[...], preferred_element_type=F32).astype(BF16)
    column = lax.broadcasted_iota(jnp.int32, (1, rows), 1)
    early = jnp.zeros((1, rows), jnp.int32)
    for j in range(1, W):
        early += (column >= j * streams).astype(jnp.int32)
    target = jnp.zeros((1, rows), jnp.int32)
    for u in range(streams):
        target = jnp.where(column - early * streams == u, slots_ref[u] * W + early, target)
    routing = (target == lax.broadcasted_iota(jnp.int32, (rows, rows), 0)).astype(F32).astype(BF16)
    routed = jnp.dot(routing, placed, preferred_element_type=F32)
    copies = streams // group
    for part in range(parts):
        for copy in range(copies):
            for plane in range(group):
                row = plane * copies + copy
                out_ref[(part * copies + copy) * group + plane] = routed[
                    row * W : (row + 1) * W, part * LANES : (part + 1) * LANES
                ].astype(BF16)
    wait_all(loads)


def stacked(parts, pieces, stack_out, sems, base):
    part, _ = place(parts)
    return [
        pltpu.make_async_copy(pieces[step], stack_out.at[later(part, parts - step, parts)], sems.at[base + step])
        for step in range(parts)
    ]


def conv_kernel(parts, width, windows, mel_ref, banded_ref, conv2, rows_ref, shift_ref, *refs):
    part, copy_index = place(parts)
    copies = lax.axis_size("dp") // parts
    proj_refs, refs = refs[:copies], refs[copies:]
    weight_refs, refs = refs[:parts], refs[parts:]
    outs_refs, refs = refs[:parts], refs[parts:]
    stack_out, even, odd, second, proj, partial, sems = refs
    loads = []
    for step in range(copies):
        slot = later(copy_index, copies - step, copies)
        loads.append(pltpu.make_async_copy(proj_refs[step], proj.at[slot], sems.at[step]))
    loads += stacked(parts, weight_refs, stack_out, sems, copies)
    start_all(loads)
    sources = mel_ref.shape[0]
    n = sources
    payload = mel_ref[...].astype(F32).reshape(sources * W, LANES).astype(BF16)
    shifted = jnp.dot(payload, shift_ref[...], preferred_element_type=F32).astype(BF16)
    both = jnp.concatenate([shifted[:, :LANES], shifted[:, LANES:]], axis=0)
    evens = jnp.dot(rows_ref[...], both, preferred_element_type=F32)
    row = lax.broadcasted_iota(jnp.int32, evens.shape, 0)
    lane = lax.broadcasted_iota(jnp.int32, evens.shape, 1)
    low = (lane >= width).astype(jnp.int32) + (lane >= 2 * width).astype(jnp.int32)
    band = lane - low * width - 4 + (width - 4) * part
    silent = (row == 0) & (lane < 3 * width) & (band >= 0)
    evens = jnp.where(silent, jnp.log(jnp.full(evens.shape, EPS_LOG, F32)), evens)
    odds = pltpu.roll(evens[: W * n], LANES - 2 * width, 1).astype(BF16)
    evens = evens.astype(BF16)
    channels = conv2.shape[1]
    outs = banded_ref.shape[1] // channels
    for g in range(outs):
        lanes = slice(g * channels, (g + 1) * channels)
        weight = banded_ref[:, lanes]
        even[:, lanes] = jax.nn.relu(jnp.dot(evens, weight, preferred_element_type=F32)).astype(BF16)
        odd[:, lanes] = jax.nn.relu(jnp.dot(odds, weight, preferred_element_type=F32)).astype(BF16)

    for h in range((outs - 1) // 2):
        lanes = slice(2 * h * channels, (2 * h + 3) * channels)
        depth = 3 * channels
        total = jnp.dot(even[: W * n, lanes], conv2[:depth], preferred_element_type=F32)
        total += jnp.dot(odd[:, lanes], conv2[depth : 2 * depth], preferred_element_type=F32)
        total += jnp.dot(even[n:, lanes], conv2[2 * depth :], preferred_element_type=F32)
        second[:, h * channels : (h + 1) * channels] = jax.nn.relu(total).astype(BF16)
    wait_all(loads)
    weights = proj[...].reshape(second.shape[1], proj.shape[2])
    partial[...] = jnp.dot(second[...], weights, preferred_element_type=F32)
    for step in range(parts):
        plane = later(part, step, parts)
        outs_refs[step][...] = jnp.concatenate(
            [partial[pl.ds(pl.multiple_of(t * n + plane * windows, 8), windows), :] for t in range(W)], axis=0
        ).astype(BF16)


def bounds(row, slots_ref, starts_ref, lengths_ref):
    begin, span = jnp.int32(0), jnp.int32(0)
    for u in range(slots_ref.shape[0]):
        chosen = slots_ref[u] == row
        begin = begin + jnp.where(chosen, starts_ref[u], 0)
        span = span + jnp.where(chosen, lengths_ref[u], 0)
    return begin, begin + span


def placed(parts, stack_refs, buffer, sems, base):
    _, copy_index = place(parts)
    copies = len(stack_refs)
    moves = []
    for step in range(copies):
        slot = later(copy_index, copies - step, copies)
        for piece in range(parts):
            target = buffer.at[piece * copies + slot]
            moves.append(pltpu.make_async_copy(stack_refs[step].at[piece], target, sems.at[base + len(moves)]))
    return moves


def norm_kernel(parts, slots_ref, starts_ref, lengths_ref, frames_ref, sample_ref, *refs):
    part, copy_index = place(parts)
    copies = lax.axis_size("dp") // parts
    part_refs, refs = refs[:parts], refs[parts:]
    piece_refs, refs = refs[:parts], refs[parts:]
    rows_out, normed_out, stack_out, sems = refs
    moves = stacked(parts, piece_refs, stack_out, sems, 0)
    start_all(moves)
    row = lax.axis_index("seq") * copies + copy_index
    begin, end = bounds(row, slots_ref, starts_ref, lengths_ref)
    total = part_refs[0][...].astype(F32)
    for step in range(1, parts):
        total += part_refs[step][...].astype(F32)
    encoded = total.astype(BF16)
    values = encoded.astype(F32)
    mean = jnp.mean(values, axis=-1, keepdims=True)
    centered = values - mean
    variance = jnp.mean(centered * centered, axis=-1, keepdims=True)
    normed_out[...] = (centered * lax.rsqrt(variance + EPS_NORM)).astype(BF16)
    ordered = jnp.dot(frames_ref[...], encoded, preferred_element_type=F32)
    sample = sample_ref[...] + part * (W * SPAN)
    valid = (sample >= begin) & (sample < end)
    rows_out[...] = jnp.where(valid, ordered, 0.0).astype(BF16)
    wait_all(moves)


def attention_kernel(parts, slots_ref, starts_ref, lengths_ref, sample_ref, *refs):
    part, copy_index = place(parts)
    copies = lax.axis_size("dp") // parts
    normed_refs, refs = refs[:parts], refs[parts:]
    mix_refs, refs = refs[:copies], refs[copies:]
    stack_refs, refs = refs[:copies], refs[copies:]
    outs_refs, (weights_out, mix, sems) = refs[:parts], refs[parts:]
    loads = placed(parts, mix_refs, mix, sems, 0)
    start_all(loads)
    moves = placed(parts, stack_refs, weights_out, sems, len(loads))
    start_all(moves)
    row = lax.axis_index("seq") * copies + copy_index
    begin, end = bounds(row, slots_ref, starts_ref, lengths_ref)
    masks = []
    for step in range(parts):
        plane = later(part, parts - step, parts)
        sample = sample_ref[...] + plane * (W * SPAN)
        masks.append(((sample >= begin) & (sample < end)).astype(F32))
    valid = jnp.concatenate(masks, axis=1) > 0.5
    normed = jnp.concatenate([ref[...] for ref in normed_refs], axis=0)
    local, features = normed_refs[0].shape
    wait_all(loads)
    weights = mix[...].reshape(features, mix.shape[2])
    mixed = jnp.dot(normed, weights, preferred_element_type=F32).astype(BF16)
    width = mix.shape[2] // 3
    scale = HEAD_DIM ** (-0.5)
    for head in range(width // HEAD_DIM):
        at = head * HEAD_DIM
        query = mixed[:, at : at + HEAD_DIM]
        key = mixed[:, width + at : width + at + HEAD_DIM]
        value = mixed[:, 2 * width + at : 2 * width + at + HEAD_DIM]
        scores = lax.dot_general(query, key, (((1,), (1,)), ((), ())), preferred_element_type=F32) * scale
        masked = jnp.where(valid, scores, MASKED)
        peak = jnp.max(masked, axis=1, keepdims=True)
        weight = jnp.where(valid, jnp.exp(masked - peak), 0.0)
        total = jnp.sum(weight, axis=1, keepdims=True)
        summed = jnp.dot(weight.astype(BF16), value, preferred_element_type=F32)
        context = (summed / total).astype(BF16)
        for step in range(parts):
            outs_refs[step][:, at : at + HEAD_DIM] = context[step * local : (step + 1) * local]
    wait_all(moves)


def output_kernel(parts, slots_ref, starts_ref, lengths_ref, frames_ref, sample_ref, weights_ref, rows_ref, *refs):
    context_refs, refs = refs[:parts], refs[parts:]
    rows_out, out_ref, context, sems = refs
    keep = pltpu.make_async_copy(rows_ref, rows_out, sems.at[0])
    keep.start()
    plane = lax.axis_index("seq")
    begin, end = bounds(lax.axis_index("dp"), slots_ref, starts_ref, lengths_ref)
    head_width = context_refs[0].shape[1]
    for step in range(parts):
        at = pl.multiple_of(later(plane, step, parts) * head_width, LANES)
        context[:, pl.ds(at, head_width)] = context_refs[step][...]
    ordered = jnp.dot(frames_ref[...], context[...], preferred_element_type=F32).astype(BF16)
    sample = sample_ref[...] + plane * (W * SPAN)
    valid = (sample >= begin) & (sample < end)
    result = jnp.concatenate(
        [jnp.dot(ordered, weights_ref[d], preferred_element_type=F32) for d in range(weights_ref.shape[0])], axis=1
    )
    out_ref[...] = jnp.where(valid, result, 0.0).astype(BF16)
    keep.wait()


def on_device(
    audio, starts, lengths, slots, conv1_weight, conv2_weight, proj_weight, qkv_weight, out_weight
):
    streams = audio.shape[0]
    windows = lax.axis_size("dp")
    group = lax.axis_size("seq")
    parts = group
    copies = windows // parts
    assert BANDS % parts == 0 and streams == copies * group and streams == windows
    share = BANDS // parts
    width = 4 * share + 4
    channels = conv1_weight.shape[1]
    features = proj_weight.shape[1]
    head_width = features // parts
    local = windows * W
    sources = windows * group
    n = sources
    outs = 2 * share + 1

    route = [(i, i + 1) for i in range(sources - 1)]
    rim = lax.ppermute(audio[:, audio.shape[1] - RIM :], ("dp", "seq"), route)

    def to_part(block, step):
        pairs = [(p * copies + c, (p + step) % parts * copies + c) for p in range(parts) for c in range(copies)]
        return lax.ppermute(block, "dp", pairs)

    def to_copy(block, step):
        pairs = [(p * copies + c, p * copies + (c + step) % copies) for p in range(parts) for c in range(copies)]
        return lax.ppermute(block, "dp", pairs)

    def to_owner(block, step):
        pairs = []
        for p in range(parts):
            for c in range(copies):
                for z in range(group):
                    pairs.append(((p * copies + c) * group + z, (z * copies + c) * group + (p - step) % parts))
        return lax.ppermute(block, ("dp", "seq"), pairs)

    scale = sources // 32
    proj_all = [proj_weight] + [to_copy(proj_weight, step) for step in range(1, copies)]

    def like(array):
        return jax.ShapeDtypeStruct(array.shape, array.dtype)

    mix_piece = jax.ShapeDtypeStruct((qkv_weight.shape[0], 3 * head_width), BF16)
    mix_parts = pl.pallas_call(
        functools.partial(prep_kernel, parts),
        out_shape=tuple([mix_piece] * parts),
        in_specs=[anywhere()],
        out_specs=tuple([anywhere()] * parts),
        scratch_shapes=[pltpu.SemaphoreType.DMA((3 * parts,))],
        compiler_params=params(4),
        cost_estimate=cost(1e8, 2e7),
        name="prep",
    )(qkv_weight)
    mix_parts, rim, out_here = lax.optimization_barrier((mix_parts, rim, out_weight))
    out_all = [out_here] + [to_part(out_here, step) for step in range(1, parts)]
    mix_all = [mix_parts[0]] + [to_part(mix_parts[step], step) for step in range(1, parts)]

    tables = [
        conv2_weight,
        jnp.asarray(row_selection(windows, group)),
        jnp.asarray(shift_selection(width)),
    ]
    banded = jax.ShapeDtypeStruct((LANES, outs * channels), BF16)
    mel, banded, *tables = pl.pallas_call(
        functools.partial(mel_kernel, parts, group, width, len(tables)),
        out_shape=tuple(
            [jax.ShapeDtypeStruct((sources, W, LANES), BF16), banded] + [like(table) for table in tables]
        ),
        in_specs=[smem()] + [vmem()] * 6 + [hbm()] * len(tables),
        out_specs=tuple([vmem()] * (2 + len(tables))),
        scratch_shapes=[
            pltpu.VMEM((streams, RIM + audio.shape[1]), F32),
            pltpu.SemaphoreType.DMA((len(tables),)),
        ],
        compiler_params=params(min(20 * scale, 48)),
        cost_estimate=cost(2e9, 2e6),
        name="log_mel",
    )(
        slots,
        rim,
        audio,
        jnp.asarray(spectrum_table(N_FFT)),
        jnp.asarray(filter_table()),
        jnp.asarray(band_selection(parts)),
        conv1_weight,
        *tables,
    )
    mel = lax.all_to_all(mel, ("dp", "seq"), split_axis=0, concat_axis=0, tiled=True)

    block = jax.ShapeDtypeStruct((local, features), BF16)
    *partials, stack = pl.pallas_call(
        functools.partial(conv_kernel, parts, width, windows),
        out_shape=tuple([block] * parts + [jax.ShapeDtypeStruct((parts,) + out_weight.shape, BF16)]),
        in_specs=[vmem()] * (2 + len(tables)) + [anywhere()] * (copies + parts),
        out_specs=tuple([vmem()] * parts + [anywhere()]),
        scratch_shapes=[
            pltpu.VMEM((JS * n, banded.shape[1]), BF16),
            pltpu.VMEM((W * n, banded.shape[1]), BF16),
            pltpu.VMEM((W * n, share * channels), BF16),
            pltpu.VMEM((copies,) + proj_weight.shape, BF16),
            pltpu.VMEM((W * n, features), F32),
            pltpu.SemaphoreType.DMA((copies + parts,)),
        ],
        compiler_params=params(min(24 * scale, 48)),
        cost_estimate=cost(8e9, 4e6),
        name="conv",
    )(mel, banded, *tables, *proj_all, *out_all)
    out_stacks = [stack] + [to_copy(stack, step) for step in range(1, copies)]
    partials = [partials[0]] + [to_part(partials[step], step) for step in range(1, parts)]

    index = np.arange(local)
    out_sample = ((index // W) * group * W + index % W) * SPAN
    key_sample = ((index % windows) * group * W + index // windows) * SPAN
    out_sample = jnp.asarray(out_sample.reshape(-1, 1).astype(np.int32))
    key_sample = jnp.asarray(key_sample.reshape(1, -1).astype(np.int32))
    frames = jnp.asarray(frame_table(windows))
    regrouped, normed, stack = pl.pallas_call(
        functools.partial(norm_kernel, parts),
        out_shape=(block, block, jax.ShapeDtypeStruct((parts,) + mix_piece.shape, BF16)),
        in_specs=[smem()] * 3 + [vmem()] * (2 + parts) + [anywhere()] * parts,
        out_specs=(vmem(), vmem(), anywhere()),
        scratch_shapes=[pltpu.SemaphoreType.DMA((parts,))],
        compiler_params=params(min(12 * scale, 32)),
        cost_estimate=cost(1e8, 1e6),
        name="layer_norm",
    )(slots, starts, lengths, frames, out_sample, *partials, *mix_all)
    mix_stacks = [stack] + [to_copy(stack, step) for step in range(1, copies)]
    normed = [normed] + [to_part(normed, step) for step in range(1, parts)]
    regrouped = to_owner(regrouped, 0)

    out_columns = jax.ShapeDtypeStruct((windows,) + out_weight.shape, BF16)
    *context, out_columns = pl.pallas_call(
        functools.partial(attention_kernel, parts),
        out_shape=tuple([jax.ShapeDtypeStruct((local, head_width), BF16)] * parts + [out_columns]),
        in_specs=[smem()] * 3 + [vmem()] * (1 + parts) + [anywhere()] * (2 * copies),
        out_specs=tuple([vmem()] * (parts + 1)),
        scratch_shapes=[
            pltpu.VMEM((windows,) + mix_piece.shape, BF16),
            pltpu.SemaphoreType.DMA((2 * windows,)),
        ],
        compiler_params=params(min(16 * scale, 48)),
        cost_estimate=cost(1e9, 2e6),
        name="attention",
    )(slots, starts, lengths, key_sample, *normed, *mix_stacks, *out_stacks)
    context = [to_owner(context[step], step) for step in range(parts)]

    regrouped, attended = pl.pallas_call(
        functools.partial(output_kernel, parts),
        out_shape=(block, block),
        in_specs=[smem()] * 3 + [vmem()] * 3 + [anywhere()] + [vmem()] * parts,
        out_specs=(anywhere(), vmem()),
        scratch_shapes=[pltpu.VMEM((local, features), BF16), pltpu.SemaphoreType.DMA((1,))],
        compiler_params=params(min(12 * scale, 32)),
        cost_estimate=cost(1e8, 3e6),
        name="output",
    )(slots, starts, lengths, frames, out_sample, out_columns, regrouped, *context)
    shape = (1, windows, 1, W, features)
    return (regrouped.reshape(shape), attended.reshape(shape))


def solution(mesh):
    in_specs = (
        P(None, ("dp", "seq")),
        P(),
        P(),
        P(),
        P(),
        P(),
        P("dp", None),
        P("dp", None),
        P(None, "dp"),
    )
    out_specs = (P("dp", None, "seq", None, None), P("dp", None, "seq", None, None))
    return jax.shard_map(
        on_device, mesh=mesh, in_specs=in_specs, out_specs=out_specs, check_vma=False
    )
```

```python
import functools
import math

import jax
import jax.numpy as jnp
import numpy as np
from jax import lax
from jax.experimental import pallas as pl
from jax.experimental.pallas import tpu as pltpu
from jax.sharding import PartitionSpec as P

HEADS = 8
HEAD_DIM = 128
MELS = 80
BANDS = MELS // 4
N_FFT = 512
HOP = 160
W = 8
RIM = 384
SPAN = 4 * HOP
JS = W + 1
LANES = 128
SAMPLE_RATE = 16000.0
EPS_LOG = 1e-06
EPS_NORM = 1e-05
MASKED = -1e30
F32 = jnp.float32
BF16 = jnp.bfloat16
MIB = 1 << 20


def mel_table(size, bands):
    count = size // 2 + 1
    highest = 2595.0 * math.log10(1.0 + SAMPLE_RATE / 1400.0)
    points = np.linspace(0.0, highest, bands + 2)
    edges = 700.0 * (10.0 ** (points / 2595.0) - 1.0)
    edges[0] = 0.0
    edges[-1] = SAMPLE_RATE / 2.0
    frequency = np.arange(count) * (SAMPLE_RATE / size)
    lower = edges[:-2][None, :]
    middle = edges[1:-1][None, :]
    upper = edges[2:][None, :]
    rising = (frequency[:, None] - lower) / (middle - lower)
    falling = (upper - frequency[:, None]) / (upper - middle)
    return np.maximum(0.0, np.minimum(rising, falling)).astype(np.float32)


def spectrum_table(size):
    sample = np.arange(size)
    phase = sample[:, None] * np.arange(size // 2)[None, :] % size
    angle = phase * (2.0 * math.pi / size)
    window = 0.5 - 0.5 * np.cos(sample * (2.0 * math.pi / size))
    both = np.concatenate([np.cos(angle), np.sin(angle)], axis=1) * window[:, None]
    filters = np.zeros((size, LANES))
    filters[: size // 2, :MELS] = mel_table(size, MELS)[: size // 2]
    return np.concatenate([both, filters], axis=1).astype(np.float32)


def vmem():
    return pl.BlockSpec(memory_space=pltpu.VMEM)


def smem():
    return pl.BlockSpec(memory_space=pltpu.SMEM)


def anywhere():
    return pl.BlockSpec(memory_space=pl.ANY)


def params(mib):
    return pltpu.CompilerParams(vmem_limit_bytes=mib * MIB)


def cost(flops, moved):
    return pl.CostEstimate(flops=int(flops), bytes_accessed=int(moved), transcendentals=0)


def place(parts):
    mine = lax.axis_index("dp")
    copies = lax.axis_size("dp") // parts
    return mine // copies, mine % copies


def later(index, step, count):
    return lax.rem(index + step, count)


def start_all(copies):
    for copy in copies:
        copy.start()


def wait_all(copies):
    for copy in copies:
        copy.wait()


def iota(rows, columns, axis):
    return lax.broadcasted_iota(jnp.int32, (rows, columns), axis)


def quotient(index, step, count):
    result = jnp.zeros_like(index)
    for i in range(1, count):
        result += (index >= i * step).astype(jnp.int32)
    return result


def one_hot(target, count):
    return (iota(target.shape[0], count, 1) == target).astype(F32).astype(BF16)


def frame_order(windows):
    count = windows * W
    row = iota(count, 1, 0)
    k = quotient(row, W, windows)
    return one_hot((row - k * W) * windows + k, count)


def first_samples(windows, group):
    row = iota(windows * W, 1, 0)
    return (row + quotient(row, W, windows) * (group - 1) * W) * SPAN


def key_samples(windows, group):
    lane = iota(1, windows * W, 1)
    t = quotient(lane, windows, W)
    return ((lane - t * windows) * group * W + t) * SPAN


def prep_kernel(parts, qkv_ref, *refs):
    mix_outs, sems = refs[:parts], refs[parts]
    part, _ = place(parts)
    features = qkv_ref.shape[1] // 3
    head_width = features // parts
    copies = []
    for step in range(parts):
        first = pl.multiple_of(later(part, step, parts) * head_width, LANES)
        for kind in range(3):
            source = qkv_ref.at[:, pl.ds(kind * features + first, head_width)]
            target = mix_outs[step].at[:, pl.ds(kind * head_width, head_width)]
            copies.append(pltpu.make_async_copy(source, target, sems.at[len(copies)]))
    start_all(copies)
    wait_all(copies)


def banded_weights(width, conv1_ref, banded_out):
    taps, channels = conv1_ref.shape
    row = lax.broadcasted_iota(jnp.int32, (LANES, taps), 0)
    tap = lax.broadcasted_iota(jnp.int32, (LANES, taps), 1)
    line = (tap >= 3).astype(jnp.int32) + (tap >= 6).astype(jnp.int32)
    target = line * (width - 3) + tap + 1
    weight = conv1_ref[...]
    for g in range(banded_out.shape[1] // channels):
        select = (row == target + 2 * g).astype(F32).astype(BF16)
        banded_out[:, g * channels : (g + 1) * channels] = jnp.dot(
            select, weight, preferred_element_type=F32
        ).astype(BF16)


def mel_kernel(parts, group, slots_ref, rim_ref, audio_ref, table_ref, out_ref, ext, table, sems):
    load_audio = pltpu.make_async_copy(audio_ref, ext.at[:, pl.ds(RIM, audio_ref.shape[1])], sems.at[0])
    load_table = pltpu.make_async_copy(table_ref, table, sems.at[1])
    load_audio.start()
    load_table.start()
    streams = audio_ref.shape[0]
    rows = W * streams
    ext[:, :RIM] = rim_ref[...]
    column = iota(1, rows, 1)
    early = quotient(column, streams, W)
    target = jnp.zeros((1, rows), jnp.int32)
    for u in range(streams):
        target = jnp.where(column - early * streams == u, slots_ref[u] * W + early, target)
    routing = (target == iota(rows, rows, 0)).astype(F32).astype(BF16)
    load_audio.wait()
    phases = []
    for phase in range(4):
        start = HOP * phase + 32
        base, shift = start // LANES * LANES, start % LANES
        length = N_FFT + (LANES if shift else 0)
        block = jnp.concatenate(
            [ext[:, SPAN * j + base : SPAN * j + base + length] for j in range(W)], axis=0
        )
        if shift:
            block = pltpu.roll(block, length - shift, 1)[:, :N_FFT]
        phases.append(block)
    frames = jnp.concatenate(phases, axis=0)
    load_table.wait()
    spectrum = jnp.dot(
        frames, table[:, :N_FFT], precision=lax.Precision.HIGHEST, preferred_element_type=F32
    )
    half = N_FFT // 2
    real, imag = spectrum[:, :half], spectrum[:, half:]
    power = real * real + imag * imag
    mel_power = jnp.dot(
        power, table[:half, N_FFT:], precision=lax.Precision.HIGHEST, preferred_element_type=F32
    )
    log_mel = jnp.log(mel_power + EPS_LOG)
    share = BANDS // parts
    width = 4 * share + 4
    lane = iota(rows, LANES, 1)
    blocks = []
    for part in range(parts):
        first = 4 * share * part - 4
        block = jnp.zeros((rows, LANES), F32)
        for phase in range(4):
            band = lane - width * phase + first
            here = (lane >= width * phase) & (lane < width * (phase + 1)) & (band >= 0) & (band < MELS)
            shift = (width * phase - first) % LANES
            frame = log_mel[phase * rows : (phase + 1) * rows]
            block = jnp.where(here, pltpu.roll(frame, shift, 1) if shift else frame, block)
        blocks.append(block.astype(BF16))
    routed = jnp.dot(routing, jnp.concatenate(blocks, axis=1), preferred_element_type=F32)
    copies = streams // group
    for part in range(parts):
        for copy in range(copies):
            for plane in range(group):
                row = plane * copies + copy
                out_ref[(part * copies + copy) * group + plane] = routed[
                    row * W : (row + 1) * W, part * LANES : (part + 1) * LANES
                ].astype(BF16)


def stacked(parts, pieces, stack_out, sems, base):
    part, _ = place(parts)
    return [
        pltpu.make_async_copy(pieces[step], stack_out.at[later(part, parts - step, parts)], sems.at[base + step])
        for step in range(parts)
    ]


def five_frames(part, width, windows, group, payload):
    n = windows * group
    row = iota(JS * n, 1, 0)
    j = quotient(row, n, JS)
    s = quotient(row - j * n, windows, group)
    window = (row - j * n - s * windows) * group + s
    before = jnp.where(j > 0, window * W + j - 1, window * W - 1)
    same = jnp.where(j < W, window * W + j, -1)
    lane = iota(payload.shape[0], LANES, 1)
    first = jnp.where(lane < 3 * width, pltpu.roll(payload, LANES - width, 1), 0.0).astype(BF16)
    last = (lane >= 3 * width) & (lane < 5 * width)
    second = jnp.where(last, pltpu.roll(payload, 3 * width, 1), 0.0).astype(BF16)
    result = jnp.dot(one_hot(before, n * W), first, preferred_element_type=F32)
    result += jnp.dot(one_hot(same, n * W), second, preferred_element_type=F32)
    lane = iota(1, LANES, 1)
    band = lane - quotient(lane, width, 3) * width - 4 + (width - 4) * part
    silent = (row == 0) & ((lane < 3 * width) & (band >= 0))
    return jnp.where(silent, jnp.log(jnp.full(result.shape, EPS_LOG, F32)), result)


def conv_kernel(parts, width, windows, mel_ref, conv1_ref, conv2_ref, *refs):
    part, copy_index = place(parts)
    copies = lax.axis_size("dp") // parts
    proj_refs, refs = refs[:copies], refs[copies:]
    weight_refs, refs = refs[:parts], refs[parts:]
    outs_refs, refs = refs[:parts], refs[parts:]
    stack_out, banded_ref, even, odd, second, conv2, proj, partial, sems = refs
    load_conv2 = pltpu.make_async_copy(conv2_ref, conv2, sems.at[0])
    load_conv2.start()
    loads = []
    for step in range(copies):
        slot = later(copy_index, copies - step, copies)
        loads.append(pltpu.make_async_copy(proj_refs[step], proj.at[slot], sems.at[1 + step]))
    loads += stacked(parts, weight_refs, stack_out, sems, 1 + copies)
    start_all(loads)
    banded_weights(width, conv1_ref, banded_ref)
    n = mel_ref.shape[0]
    payload = mel_ref[...].astype(F32).reshape(n * W, LANES)
    evens = five_frames(part, width, windows, n // windows, payload)
    odds = pltpu.roll(evens[: W * n], LANES - 2 * width, 1).astype(BF16)
    evens = evens.astype(BF16)
    channels = conv2.shape[1]
    outs = banded_ref.shape[1] // channels
    for g in range(outs):
        lanes = slice(g * channels, (g + 1) * channels)
        weight = banded_ref[:, lanes]
        even[:, lanes] = jax.nn.relu(jnp.dot(evens, weight, preferred_element_type=F32)).astype(BF16)
        odd[:, lanes] = jax.nn.relu(jnp.dot(odds, weight, preferred_element_type=F32)).astype(BF16)

    load_conv2.wait()
    for h in range((outs - 1) // 2):
        lanes = slice(2 * h * channels, (2 * h + 3) * channels)
        depth = 3 * channels
        total = jnp.dot(even[: W * n, lanes], conv2[:depth], preferred_element_type=F32)
        total += jnp.dot(odd[:, lanes], conv2[depth : 2 * depth], preferred_element_type=F32)
        total += jnp.dot(even[n:, lanes], conv2[2 * depth :], preferred_element_type=F32)
        second[:, h * channels : (h + 1) * channels] = jax.nn.relu(total).astype(BF16)
    wait_all(loads)
    weights = proj[...].reshape(second.shape[1], proj.shape[2])
    partial[...] = jnp.dot(second[...], weights, preferred_element_type=F32)
    for step in range(parts):
        plane = later(part, step, parts)
        outs_refs[step][...] = jnp.concatenate(
            [partial[pl.ds(pl.multiple_of(t * n + plane * windows, 8), windows), :] for t in range(W)], axis=0
        ).astype(BF16)


def bounds(row, slots_ref, starts_ref, lengths_ref):
    begin, span = jnp.int32(0), jnp.int32(0)
    for u in range(slots_ref.shape[0]):
        chosen = slots_ref[u] == row
        begin = begin + jnp.where(chosen, starts_ref[u], 0)
        span = span + jnp.where(chosen, lengths_ref[u], 0)
    return begin, begin + span


def norm_kernel(parts, windows, group, slots_ref, starts_ref, lengths_ref, *refs):
    part, copy_index = place(parts)
    copies = lax.axis_size("dp") // parts
    part_refs, refs = refs[:parts], refs[parts:]
    piece_refs, refs = refs[:parts], refs[parts:]
    rows_out, normed_out, stack_out, sems = refs
    moves = stacked(parts, piece_refs, stack_out, sems, 0)
    start_all(moves)
    row = lax.axis_index("seq") * copies + copy_index
    begin, end = bounds(row, slots_ref, starts_ref, lengths_ref)
    total = part_refs[0][...].astype(F32)
    for step in range(1, parts):
        total += part_refs[step][...].astype(F32)
    encoded = total.astype(BF16)
    values = encoded.astype(F32)
    mean = jnp.mean(values, axis=-1, keepdims=True)
    centered = values - mean
    variance = jnp.mean(centered * centered, axis=-1, keepdims=True)
    normed_out[...] = (centered * lax.rsqrt(variance + EPS_NORM)).astype(BF16)
    ordered = jnp.dot(frame_order(windows), encoded, preferred_element_type=F32)
    sample = first_samples(windows, group) + part * (W * SPAN)
    valid = (sample >= begin) & (sample < end)
    rows_out[...] = jnp.where(valid, ordered, 0.0).astype(BF16)
    wait_all(moves)


def attention_kernel(parts, windows, group, slots_ref, starts_ref, lengths_ref, rows_ref, *refs):
    part, copy_index = place(parts)
    copies = lax.axis_size("dp") // parts
    normed_refs, refs = refs[:parts], refs[parts:]
    stack_refs, refs = refs[:copies], refs[copies:]
    outs_refs, (pieces,) = refs[:parts], refs[parts:]
    row = lax.axis_index("seq") * copies + copy_index
    begin, end = bounds(row, slots_ref, starts_ref, lengths_ref)
    masks = []
    for step in range(parts):
        plane = later(part, parts - step, parts)
        sample = key_samples(windows, group) + plane * (W * SPAN)
        masks.append(((sample >= begin) & (sample < end)).astype(F32))
    valid = jnp.concatenate(masks, axis=1) > 0.5
    local = normed_refs[0].shape[0]
    depth = pieces.shape[2]
    for step in range(parts):
        for piece in range(windows):
            pieces[piece, step * local : (step + 1) * local, :] = normed_refs[step][
                :, piece * depth : (piece + 1) * depth
            ]
    mixed = 0.0
    for step in range(copies):
        slot = later(copy_index, copies - step, copies)
        normed = jnp.concatenate([pieces[piece * copies + slot] for piece in range(parts)], axis=1)
        weights = stack_refs[step][...].reshape(parts * depth, stack_refs[step].shape[2])
        mixed += jnp.dot(normed, weights, preferred_element_type=F32)
    mixed = mixed.astype(BF16)
    width = mixed.shape[1] // 3
    scale = HEAD_DIM ** (-0.5)
    for head in range(width // HEAD_DIM):
        at = head * HEAD_DIM
        query = mixed[:, at : at + HEAD_DIM]
        key = mixed[:, width + at : width + at + HEAD_DIM]
        value = mixed[:, 2 * width + at : 2 * width + at + HEAD_DIM]
        scores = lax.dot_general(query, key, (((1,), (1,)), ((), ())), preferred_element_type=F32) * scale
        masked = jnp.where(valid, scores, MASKED)
        peak = jnp.max(masked, axis=1, keepdims=True)
        weight = jnp.where(valid, jnp.exp(masked - peak), 0.0)
        total = jnp.sum(weight, axis=1, keepdims=True)
        summed = jnp.dot(weight.astype(BF16), value, preferred_element_type=F32)
        context = (summed / total).astype(BF16)
        for step in range(parts):
            outs_refs[step][:, at : at + HEAD_DIM] = context[step * local : (step + 1) * local]
    outs_refs[0][:, width:] = rows_ref[...]


def output_kernel(parts, windows, group, slots_ref, starts_ref, lengths_ref, *refs):
    context_refs, refs = refs[:parts], refs[parts:]
    stack_refs, refs = refs[: windows // parts], refs[windows // parts :]
    rows_out, out_ref, context, pieces = refs
    _, copy_index = place(parts)
    copies = windows // parts
    plane = lax.axis_index("seq")
    begin, end = bounds(lax.axis_index("dp"), slots_ref, starts_ref, lengths_ref)
    head_width = context_refs[-1].shape[1]
    rows_out[...] = context_refs[0][:, head_width:]
    for step in range(parts):
        at = pl.multiple_of(later(plane, step, parts) * head_width, LANES)
        context[:, pl.ds(at, head_width)] = context_refs[step][:, :head_width]
    ordered = jnp.dot(frame_order(windows), context[...], preferred_element_type=F32).astype(BF16)
    sample = first_samples(windows, group) + plane * (W * SPAN)
    valid = (sample >= begin) & (sample < end)
    for step in range(copies):
        slot = later(copy_index, copies - step, copies)
        for piece in range(parts):
            pieces[piece * copies + slot] = jnp.dot(
                ordered, stack_refs[step][piece], preferred_element_type=F32
            )
    result = jnp.concatenate([pieces[d] for d in range(windows)], axis=1)
    out_ref[...] = jnp.where(valid, result, 0.0).astype(BF16)


def on_device(
    audio, starts, lengths, slots, conv1_weight, conv2_weight, proj_weight, qkv_weight, out_weight
):
    streams = audio.shape[0]
    windows = lax.axis_size("dp")
    group = lax.axis_size("seq")
    parts = group
    copies = windows // parts
    assert BANDS % parts == 0 and streams == copies * group and streams == windows
    share = BANDS // parts
    width = 4 * share + 4
    channels = conv1_weight.shape[1]
    features = proj_weight.shape[1]
    head_width = features // parts
    local = windows * W
    sources = windows * group
    n = sources
    outs = 2 * share + 1

    route = [(i, i + 1) for i in range(sources - 1)]
    rim = lax.ppermute(audio[:, audio.shape[1] - RIM :], ("dp", "seq"), route)

    def to_part(block, step):
        pairs = [(p * copies + c, (p + step) % parts * copies + c) for p in range(parts) for c in range(copies)]
        return lax.ppermute(block, "dp", pairs)

    def to_copy(block, step):
        pairs = [(p * copies + c, p * copies + (c + step) % copies) for p in range(parts) for c in range(copies)]
        return lax.ppermute(block, "dp", pairs)

    def to_owner(block, step):
        pairs = []
        for p in range(parts):
            for c in range(copies):
                for z in range(group):
                    pairs.append(((p * copies + c) * group + z, (z * copies + c) * group + (p - step) % parts))
        return lax.ppermute(block, ("dp", "seq"), pairs)

    scale = sources // 32
    proj_all = [proj_weight] + [to_copy(proj_weight, step) for step in range(1, copies)]

    mix_piece = jax.ShapeDtypeStruct((qkv_weight.shape[0], 3 * head_width), BF16)
    mix_parts = pl.pallas_call(
        functools.partial(prep_kernel, parts),
        out_shape=tuple([mix_piece] * parts),
        in_specs=[anywhere()],
        out_specs=tuple([anywhere()] * parts),
        scratch_shapes=[pltpu.SemaphoreType.DMA((3 * parts,))],
        compiler_params=params(60),
        cost_estimate=cost(1e8, 4e6),
        name="prep",
    )(qkv_weight)
    mix_all = [mix_parts[0]] + [to_part(mix_parts[step], step) for step in range(1, parts)]
    out_all = [out_weight] + [to_part(out_weight, step) for step in range(1, parts)]

    table = jnp.asarray(spectrum_table(N_FFT))
    mel = pl.pallas_call(
        functools.partial(mel_kernel, parts, group),
        out_shape=jax.ShapeDtypeStruct((sources, W, LANES), BF16),
        in_specs=[smem(), vmem(), anywhere(), anywhere()],
        out_specs=vmem(),
        scratch_shapes=[
            pltpu.VMEM((streams, RIM + audio.shape[1]), F32),
            pltpu.VMEM(table.shape, F32),
            pltpu.SemaphoreType.DMA((2,)),
        ],
        compiler_params=params(60),
        cost_estimate=cost(2e9, 2e6),
        name="log_mel",
    )(slots, rim, audio, table)
    mel = lax.all_to_all(mel, ("dp", "seq"), split_axis=0, concat_axis=0, tiled=True)

    block = jax.ShapeDtypeStruct((local, features), BF16)
    *partials, stack = pl.pallas_call(
        functools.partial(conv_kernel, parts, width, windows),
        out_shape=tuple([block] * parts + [jax.ShapeDtypeStruct((parts,) + mix_piece.shape, BF16)]),
        in_specs=[vmem()] * 2 + [anywhere()] * (1 + copies + parts),
        out_specs=tuple([vmem()] * parts + [anywhere()]),
        scratch_shapes=[
            pltpu.VMEM((LANES, outs * channels), BF16),
            pltpu.VMEM((JS * n, outs * channels), BF16),
            pltpu.VMEM((W * n, outs * channels), BF16),
            pltpu.VMEM((W * n, share * channels), BF16),
            pltpu.VMEM(conv2_weight.shape, BF16),
            pltpu.VMEM((copies,) + proj_weight.shape, BF16),
            pltpu.VMEM((W * n, features), F32),
            pltpu.SemaphoreType.DMA((1 + copies + parts,)),
        ],
        compiler_params=params(60),
        cost_estimate=cost(8e9, 4e6),
        name="conv",
    )(mel, conv1_weight, conv2_weight, *proj_all, *mix_all)
    mix_stacks = [stack] + [to_copy(stack, step) for step in range(1, copies)]
    partials = [partials[0]] + [to_part(partials[step], step) for step in range(1, parts)]

    regrouped, normed, stack = pl.pallas_call(
        functools.partial(norm_kernel, parts, windows, group),
        out_shape=(block, block, jax.ShapeDtypeStruct((parts,) + out_weight.shape, BF16)),
        in_specs=[smem()] * 3 + [vmem()] * parts + [anywhere()] * parts,
        out_specs=(vmem(), vmem(), anywhere()),
        scratch_shapes=[pltpu.SemaphoreType.DMA((parts,))],
        compiler_params=params(min(12 * scale, 32)),
        cost_estimate=cost(1e8, 1e6),
        name="layer_norm",
    )(slots, starts, lengths, *partials, *out_all)
    out_stacks = [stack] + [to_copy(stack, step) for step in range(1, copies)]
    normed = [normed] + [to_part(normed, step) for step in range(1, parts)]

    first = jax.ShapeDtypeStruct((local, head_width + features), BF16)
    context = pl.pallas_call(
        functools.partial(attention_kernel, parts, windows, group),
        out_shape=tuple([first] + [jax.ShapeDtypeStruct((local, head_width), BF16)] * (parts - 1)),
        in_specs=[smem()] * 3 + [vmem()] * (1 + parts + copies),
        out_specs=tuple([vmem()] * parts),
        scratch_shapes=[pltpu.VMEM((windows, group * local, mix_piece.shape[0]), BF16)],
        compiler_params=params(min(16 * scale, 48)),
        cost_estimate=cost(1e9, 2e6),
        name="attention",
    )(slots, starts, lengths, regrouped, *normed, *mix_stacks)
    context = [to_owner(context[step], step) for step in range(parts)]

    regrouped, attended = pl.pallas_call(
        functools.partial(output_kernel, parts, windows, group),
        out_shape=(block, block),
        in_specs=[smem()] * 3 + [vmem()] * (parts + copies),
        out_specs=(vmem(), vmem()),
        scratch_shapes=[
            pltpu.VMEM((local, features), BF16),
            pltpu.VMEM((windows, local, out_weight.shape[1]), F32),
        ],
        compiler_params=params(min(12 * scale, 32)),
        cost_estimate=cost(1e8, 3e6),
        name="output",
    )(slots, starts, lengths, *context, *out_stacks)
    shape = (1, windows, 1, W, features)
    return (regrouped.reshape(shape), attended.reshape(shape))


def solution(mesh):
    in_specs = (
        P(None, ("dp", "seq")),
        P(),
        P(),
        P(),
        P(),
        P(),
        P("dp", None),
        P("dp", None),
        P(None, "dp"),
    )
    out_specs = (P("dp", None, "seq", None, None), P("dp", None, "seq", None, None))
    return jax.shard_map(
        on_device, mesh=mesh, in_specs=in_specs, out_specs=out_specs, check_vma=False
    )
```

```python
import functools
import math

import jax
import jax.numpy as jnp
import numpy as np
from jax import lax
from jax.experimental import pallas as pl
from jax.experimental.pallas import tpu as pltpu
from jax.sharding import PartitionSpec as P

HEADS = 8
HEAD_DIM = 128
MELS = 80
BANDS = MELS // 4
N_FFT = 512
HOP = 160
W = 8
RIM = 384
SPAN = 4 * HOP
JS = W + 1
LANES = 128
SAMPLE_RATE = 16000.0
EPS_LOG = 1e-06
EPS_NORM = 1e-05
MASKED = -1e30
F32 = jnp.float32
BF16 = jnp.bfloat16
MIB = 1 << 20


def mel_table(size, bands):
    count = size // 2 + 1
    highest = 2595.0 * math.log10(1.0 + SAMPLE_RATE / 1400.0)
    points = np.linspace(0.0, highest, bands + 2)
    edges = 700.0 * (10.0 ** (points / 2595.0) - 1.0)
    edges[0] = 0.0
    edges[-1] = SAMPLE_RATE / 2.0
    frequency = np.arange(count) * (SAMPLE_RATE / size)
    lower = edges[:-2][None, :]
    middle = edges[1:-1][None, :]
    upper = edges[2:][None, :]
    rising = (frequency[:, None] - lower) / (middle - lower)
    falling = (upper - frequency[:, None]) / (upper - middle)
    return np.maximum(0.0, np.minimum(rising, falling)).astype(np.float32)


def spectrum_table(size):
    sample = np.arange(size)
    phase = sample[:, None] * np.arange(size // 2)[None, :] % size
    angle = phase * (2.0 * math.pi / size)
    window = 0.5 - 0.5 * np.cos(sample * (2.0 * math.pi / size))
    both = np.concatenate([np.cos(angle), np.sin(angle)], axis=1) * window[:, None]
    filters = np.zeros((size, LANES))
    filters[: size // 2, :MELS] = mel_table(size, MELS)[: size // 2]
    return np.concatenate([both, filters], axis=1).astype(np.float32)


def vmem():
    return pl.BlockSpec(memory_space=pltpu.VMEM)


def smem():
    return pl.BlockSpec(memory_space=pltpu.SMEM)


def anywhere():
    return pl.BlockSpec(memory_space=pl.ANY)


def params(mib):
    return pltpu.CompilerParams(vmem_limit_bytes=mib * MIB)


def cost(flops, moved):
    return pl.CostEstimate(flops=int(flops), bytes_accessed=int(moved), transcendentals=0)


def place(parts):
    mine = lax.axis_index("dp")
    copies = lax.axis_size("dp") // parts
    return mine // copies, mine % copies


def later(index, step, count):
    return lax.rem(index + step, count)


def start_all(copies):
    for copy in copies:
        copy.start()


def wait_all(copies):
    for copy in copies:
        copy.wait()


def iota(rows, columns, axis):
    return lax.broadcasted_iota(jnp.int32, (rows, columns), axis)


def quotient(index, step, count):
    result = jnp.zeros_like(index)
    for i in range(1, count):
        result += (index >= i * step).astype(jnp.int32)
    return result


def one_hot(target, count):
    return (iota(target.shape[0], count, 1) == target).astype(F32).astype(BF16)


def frame_order(windows):
    count = windows * W
    row = iota(count, 1, 0)
    k = quotient(row, W, windows)
    return one_hot((row - k * W) * windows + k, count)


def first_samples(windows, group):
    row = iota(windows * W, 1, 0)
    return (row + quotient(row, W, windows) * (group - 1) * W) * SPAN


def key_samples(windows, group):
    lane = iota(1, windows * W, 1)
    t = quotient(lane, windows, W)
    return ((lane - t * windows) * group * W + t) * SPAN


def prep_kernel(parts, qkv_ref, out_ref, *pack_outs):
    part, _ = place(parts)
    rows = qkv_ref.shape[0]
    features = qkv_ref.shape[1] // 3
    head_width = features // parts
    blocks = head_width // LANES
    for step in range(parts):
        first = pl.multiple_of(later(part, step, parts) * head_width, LANES)
        for kind in range(3):
            for piece in range(blocks):
                at = (kind * blocks + piece) * rows
                pack_outs[step][at : at + rows, :] = qkv_ref[
                    :, pl.ds(kind * features + first + piece * LANES, LANES)
                ]
        pack_outs[step][3 * blocks * rows :, :] = out_ref[...]


def banded_weights(width, conv1_ref, banded_out):
    taps, channels = conv1_ref.shape
    row = lax.broadcasted_iota(jnp.int32, (LANES, taps), 0)
    tap = lax.broadcasted_iota(jnp.int32, (LANES, taps), 1)
    line = (tap >= 3).astype(jnp.int32) + (tap >= 6).astype(jnp.int32)
    target = line * (width - 3) + tap + 1
    weight = conv1_ref[...]
    for g in range(banded_out.shape[1] // channels):
        select = (row == target + 2 * g).astype(F32).astype(BF16)
        banded_out[:, g * channels : (g + 1) * channels] = jnp.dot(
            select, weight, preferred_element_type=F32
        ).astype(BF16)


def mel_kernel(parts, group, slots_ref, rim_ref, audio_ref, table_ref, out_ref, ext, table, sems):
    load_audio = pltpu.make_async_copy(audio_ref, ext.at[:, pl.ds(RIM, audio_ref.shape[1])], sems.at[0])
    load_table = pltpu.make_async_copy(table_ref, table, sems.at[1])
    load_audio.start()
    load_table.start()
    streams = audio_ref.shape[0]
    rows = W * streams
    ext[:, :RIM] = rim_ref[...]
    column = iota(1, rows, 1)
    early = quotient(column, streams, W)
    target = jnp.zeros((1, rows), jnp.int32)
    for u in range(streams):
        target = jnp.where(column - early * streams == u, slots_ref[u] * W + early, target)
    routing = (target == iota(rows, rows, 0)).astype(F32).astype(BF16)
    load_audio.wait()
    phases = []
    for phase in range(4):
        start = HOP * phase + 32
        base, shift = start // LANES * LANES, start % LANES
        length = N_FFT + (LANES if shift else 0)
        block = jnp.concatenate(
            [ext[:, SPAN * j + base : SPAN * j + base + length] for j in range(W)], axis=0
        )
        if shift:
            block = pltpu.roll(block, length - shift, 1)[:, :N_FFT]
        phases.append(block)
    frames = jnp.concatenate(phases, axis=0)
    load_table.wait()
    spectrum = jnp.dot(
        frames, table[:, :N_FFT], precision=lax.Precision.HIGHEST, preferred_element_type=F32
    )
    half = N_FFT // 2
    real, imag = spectrum[:, :half], spectrum[:, half:]
    power = real * real + imag * imag
    mel_power = jnp.dot(
        power, table[:half, N_FFT:], precision=lax.Precision.HIGHEST, preferred_element_type=F32
    )
    log_mel = jnp.log(mel_power + EPS_LOG)
    share = BANDS // parts
    width = 4 * share + 4
    lane = iota(rows, LANES, 1)
    blocks = []
    for part in range(parts):
        first = 4 * share * part - 4
        block = jnp.zeros((rows, LANES), F32)
        for phase in range(4):
            band = lane - width * phase + first
            here = (lane >= width * phase) & (lane < width * (phase + 1)) & (band >= 0) & (band < MELS)
            shift = (width * phase - first) % LANES
            frame = log_mel[phase * rows : (phase + 1) * rows]
            block = jnp.where(here, pltpu.roll(frame, shift, 1) if shift else frame, block)
        blocks.append(block.astype(BF16))
    routed = jnp.dot(routing, jnp.concatenate(blocks, axis=1), preferred_element_type=F32)
    copies = streams // group
    for part in range(parts):
        for copy in range(copies):
            for plane in range(group):
                row = plane * copies + copy
                out_ref[(part * copies + copy) * group + plane] = routed[
                    row * W : (row + 1) * W, part * LANES : (part + 1) * LANES
                ].astype(BF16)


def stacked(parts, pieces, stack_out, sems, base):
    part, _ = place(parts)
    return [
        pltpu.make_async_copy(pieces[step], stack_out.at[later(part, parts - step, parts)], sems.at[base + step])
        for step in range(parts)
    ]


def five_frames(part, width, windows, group, payload):
    n = windows * group
    row = iota(JS * n, 1, 0)
    j = quotient(row, n, JS)
    s = quotient(row - j * n, windows, group)
    window = (row - j * n - s * windows) * group + s
    before = jnp.where(j > 0, window * W + j - 1, window * W - 1)
    same = jnp.where(j < W, window * W + j, -1)
    lane = iota(payload.shape[0], LANES, 1)
    first = jnp.where(lane < 3 * width, pltpu.roll(payload, LANES - width, 1), 0.0).astype(BF16)
    last = (lane >= 3 * width) & (lane < 5 * width)
    second = jnp.where(last, pltpu.roll(payload, 3 * width, 1), 0.0).astype(BF16)
    result = jnp.dot(one_hot(before, n * W), first, preferred_element_type=F32)
    result += jnp.dot(one_hot(same, n * W), second, preferred_element_type=F32)
    lane = iota(1, LANES, 1)
    band = lane - quotient(lane, width, 3) * width - 4 + (width - 4) * part
    silent = (row == 0) & ((lane < 3 * width) & (band >= 0))
    return jnp.where(silent, jnp.log(jnp.full(result.shape, EPS_LOG, F32)), result)


def conv_kernel(parts, width, windows, mel_ref, conv1_ref, conv2_ref, *refs):
    part, copy_index = place(parts)
    copies = lax.axis_size("dp") // parts
    proj_refs, refs = refs[:copies], refs[copies:]
    outs_refs, refs = refs[:parts], refs[parts:]
    banded_ref, even, odd, second, conv2, proj, partial, sems = refs
    load_conv2 = pltpu.make_async_copy(conv2_ref, conv2, sems.at[0])
    load_conv2.start()
    loads = []
    for step in range(copies):
        slot = later(copy_index, copies - step, copies)
        loads.append(pltpu.make_async_copy(proj_refs[step], proj.at[slot], sems.at[1 + step]))
    start_all(loads)
    banded_weights(width, conv1_ref, banded_ref)
    n = mel_ref.shape[0]
    payload = mel_ref[...].astype(F32).reshape(n * W, LANES)
    evens = five_frames(part, width, windows, n // windows, payload)
    odds = pltpu.roll(evens[: W * n], LANES - 2 * width, 1).astype(BF16)
    evens = evens.astype(BF16)
    channels = conv2.shape[1]
    outs = banded_ref.shape[1] // channels
    for g in range(outs):
        lanes = slice(g * channels, (g + 1) * channels)
        weight = banded_ref[:, lanes]
        even[:, lanes] = jax.nn.relu(jnp.dot(evens, weight, preferred_element_type=F32)).astype(BF16)
        odd[:, lanes] = jax.nn.relu(jnp.dot(odds, weight, preferred_element_type=F32)).astype(BF16)

    load_conv2.wait()
    for h in range((outs - 1) // 2):
        lanes = slice(2 * h * channels, (2 * h + 3) * channels)
        depth = 3 * channels
        total = jnp.dot(even[: W * n, lanes], conv2[:depth], preferred_element_type=F32)
        total += jnp.dot(odd[:, lanes], conv2[depth : 2 * depth], preferred_element_type=F32)
        total += jnp.dot(even[n:, lanes], conv2[2 * depth :], preferred_element_type=F32)
        second[:, h * channels : (h + 1) * channels] = jax.nn.relu(total).astype(BF16)
    wait_all(loads)
    weights = proj[...].reshape(second.shape[1], proj.shape[2])
    partial[...] = jnp.dot(second[...], weights, preferred_element_type=F32)
    for step in range(parts):
        plane = later(part, step, parts)
        outs_refs[step][...] = jnp.concatenate(
            [partial[pl.ds(pl.multiple_of(t * n + plane * windows, 8), windows), :] for t in range(W)], axis=0
        ).astype(BF16)


def bounds(row, slots_ref, starts_ref, lengths_ref):
    begin, span = jnp.int32(0), jnp.int32(0)
    for u in range(slots_ref.shape[0]):
        chosen = slots_ref[u] == row
        begin = begin + jnp.where(chosen, starts_ref[u], 0)
        span = span + jnp.where(chosen, lengths_ref[u], 0)
    return begin, begin + span


def norm_kernel(parts, windows, group, slots_ref, starts_ref, lengths_ref, *refs):
    part, copy_index = place(parts)
    copies = lax.axis_size("dp") // parts
    part_refs, refs = refs[:parts], refs[parts:]
    piece_refs, refs = refs[:parts], refs[parts:]
    rows_out, normed_out, stack_out, sems = refs
    moves = stacked(parts, piece_refs, stack_out, sems, 0)
    start_all(moves)
    row = lax.axis_index("seq") * copies + copy_index
    begin, end = bounds(row, slots_ref, starts_ref, lengths_ref)
    total = part_refs[0][...].astype(F32)
    for step in range(1, parts):
        total += part_refs[step][...].astype(F32)
    encoded = total.astype(BF16)
    values = encoded.astype(F32)
    mean = jnp.mean(values, axis=-1, keepdims=True)
    centered = values - mean
    variance = jnp.mean(centered * centered, axis=-1, keepdims=True)
    normed_out[...] = (centered * lax.rsqrt(variance + EPS_NORM)).astype(BF16)
    ordered = jnp.dot(frame_order(windows), encoded, preferred_element_type=F32)
    sample = first_samples(windows, group) + part * (W * SPAN)
    valid = (sample >= begin) & (sample < end)
    rows_out[...] = jnp.where(valid, ordered, 0.0).astype(BF16)
    wait_all(moves)


def attention_kernel(parts, windows, group, slots_ref, starts_ref, lengths_ref, rows_ref, *refs):
    part, copy_index = place(parts)
    copies = lax.axis_size("dp") // parts
    normed_refs, refs = refs[:parts], refs[parts:]
    stack_refs, refs = refs[:copies], refs[copies:]
    outs_refs, (pieces,) = refs[:parts], refs[parts:]
    row = lax.axis_index("seq") * copies + copy_index
    begin, end = bounds(row, slots_ref, starts_ref, lengths_ref)
    masks = []
    for step in range(parts):
        plane = later(part, parts - step, parts)
        sample = key_samples(windows, group) + plane * (W * SPAN)
        masks.append(((sample >= begin) & (sample < end)).astype(F32))
    valid = jnp.concatenate(masks, axis=1) > 0.5
    local = normed_refs[0].shape[0]
    depth = pieces.shape[2]
    blocks = 3 * outs_refs[-1].shape[1] // LANES
    for step in range(parts):
        for piece in range(windows):
            pieces[piece, step * local : (step + 1) * local, :] = normed_refs[step][
                :, piece * depth : (piece + 1) * depth
            ]
    mixed = 0.0
    for step in range(copies):
        slot = later(copy_index, copies - step, copies)
        normed = jnp.concatenate([pieces[piece * copies + slot] for piece in range(parts)], axis=1)
        weights = jnp.concatenate(
            [
                jnp.concatenate(
                    [stack_refs[step][piece, block * depth : (block + 1) * depth, :] for piece in range(parts)], axis=0
                )
                for block in range(blocks)
            ],
            axis=1,
        )
        mixed += jnp.dot(normed, weights, preferred_element_type=F32)
    mixed = mixed.astype(BF16)
    width = mixed.shape[1] // 3
    scale = HEAD_DIM ** (-0.5)
    for head in range(width // HEAD_DIM):
        at = head * HEAD_DIM
        query = mixed[:, at : at + HEAD_DIM]
        key = mixed[:, width + at : width + at + HEAD_DIM]
        value = mixed[:, 2 * width + at : 2 * width + at + HEAD_DIM]
        scores = lax.dot_general(query, key, (((1,), (1,)), ((), ())), preferred_element_type=F32) * scale
        masked = jnp.where(valid, scores, MASKED)
        peak = jnp.max(masked, axis=1, keepdims=True)
        weight = jnp.where(valid, jnp.exp(masked - peak), 0.0)
        total = jnp.sum(weight, axis=1, keepdims=True)
        summed = jnp.dot(weight.astype(BF16), value, preferred_element_type=F32)
        context = (summed / total).astype(BF16)
        for step in range(parts):
            outs_refs[step][:, at : at + HEAD_DIM] = context[step * local : (step + 1) * local]
    outs_refs[0][:, width:] = rows_ref[...]


def output_kernel(parts, windows, group, base, slots_ref, starts_ref, lengths_ref, *refs):
    context_refs, refs = refs[:parts], refs[parts:]
    stack_refs, refs = refs[: windows // parts], refs[windows // parts :]
    rows_out, out_ref, context, pieces = refs
    _, copy_index = place(parts)
    copies = windows // parts
    plane = lax.axis_index("seq")
    begin, end = bounds(lax.axis_index("dp"), slots_ref, starts_ref, lengths_ref)
    head_width = context_refs[-1].shape[1]
    rows_out[...] = context_refs[0][:, head_width:]
    for step in range(parts):
        at = pl.multiple_of(later(plane, step, parts) * head_width, LANES)
        context[:, pl.ds(at, head_width)] = context_refs[step][:, :head_width]
    ordered = jnp.dot(frame_order(windows), context[...], preferred_element_type=F32).astype(BF16)
    sample = first_samples(windows, group) + plane * (W * SPAN)
    valid = (sample >= begin) & (sample < end)
    for step in range(copies):
        slot = later(copy_index, copies - step, copies)
        for piece in range(parts):
            pieces[piece * copies + slot] = jnp.dot(
                ordered, stack_refs[step][piece, base:, :], preferred_element_type=F32
            )
    result = jnp.concatenate([pieces[d] for d in range(windows)], axis=1)
    out_ref[...] = jnp.where(valid, result, 0.0).astype(BF16)


def on_device(
    audio, starts, lengths, slots, conv1_weight, conv2_weight, proj_weight, qkv_weight, out_weight
):
    streams = audio.shape[0]
    windows = lax.axis_size("dp")
    group = lax.axis_size("seq")
    parts = group
    copies = windows // parts
    assert BANDS % parts == 0 and streams == copies * group and streams == windows
    share = BANDS // parts
    width = 4 * share + 4
    channels = conv1_weight.shape[1]
    features = proj_weight.shape[1]
    head_width = features // parts
    local = windows * W
    sources = windows * group
    n = sources
    outs = 2 * share + 1

    route = [(i, i + 1) for i in range(sources - 1)]
    rim = lax.ppermute(audio[:, audio.shape[1] - RIM :], ("dp", "seq"), route)

    def to_part(block, step):
        pairs = [(p * copies + c, (p + step) % parts * copies + c) for p in range(parts) for c in range(copies)]
        return lax.ppermute(block, "dp", pairs)

    def to_copy(block, step):
        pairs = [(p * copies + c, p * copies + (c + step) % copies) for p in range(parts) for c in range(copies)]
        return lax.ppermute(block, "dp", pairs)

    def to_owner(block, step):
        pairs = []
        for p in range(parts):
            for c in range(copies):
                for z in range(group):
                    pairs.append(((p * copies + c) * group + z, (z * copies + c) * group + (p - step) % parts))
        return lax.ppermute(block, ("dp", "seq"), pairs)

    scale = sources // 32
    proj_all = [proj_weight] + [to_copy(proj_weight, step) for step in range(1, copies)]

    mix_rows = 3 * head_width // LANES * qkv_weight.shape[0]
    out_rows = out_weight.reshape(-1, LANES)
    pack = jax.ShapeDtypeStruct((mix_rows + out_rows.shape[0], LANES), BF16)
    packs = pl.pallas_call(
        functools.partial(prep_kernel, parts),
        out_shape=tuple([pack] * parts),
        in_specs=[vmem(), vmem()],
        out_specs=tuple([vmem()] * parts),
        compiler_params=params(60),
        cost_estimate=cost(1e8, 4e6),
        name="prep",
    )(qkv_weight, out_rows)
    packs = [packs[0]] + [to_part(packs[step], step) for step in range(1, parts)]

    table = jnp.asarray(spectrum_table(N_FFT))
    mel = pl.pallas_call(
        functools.partial(mel_kernel, parts, group),
        out_shape=jax.ShapeDtypeStruct((sources, W, LANES), BF16),
        in_specs=[smem(), vmem(), anywhere(), anywhere()],
        out_specs=vmem(),
        scratch_shapes=[
            pltpu.VMEM((streams, RIM + audio.shape[1]), F32),
            pltpu.VMEM(table.shape, F32),
            pltpu.SemaphoreType.DMA((2,)),
        ],
        compiler_params=params(60),
        cost_estimate=cost(2e9, 2e6),
        name="log_mel",
    )(slots, rim, audio, table)
    mel = lax.all_to_all(mel, ("dp", "seq"), split_axis=0, concat_axis=0, tiled=True)

    block = jax.ShapeDtypeStruct((local, features), BF16)
    partials = pl.pallas_call(
        functools.partial(conv_kernel, parts, width, windows),
        out_shape=tuple([block] * parts),
        in_specs=[vmem()] * 2 + [anywhere()] * (1 + copies),
        out_specs=tuple([vmem()] * parts),
        scratch_shapes=[
            pltpu.VMEM((LANES, outs * channels), BF16),
            pltpu.VMEM((JS * n, outs * channels), BF16),
            pltpu.VMEM((W * n, outs * channels), BF16),
            pltpu.VMEM((W * n, share * channels), BF16),
            pltpu.VMEM(conv2_weight.shape, BF16),
            pltpu.VMEM((copies,) + proj_weight.shape, BF16),
            pltpu.VMEM((W * n, features), F32),
            pltpu.SemaphoreType.DMA((1 + copies,)),
        ],
        compiler_params=params(60),
        cost_estimate=cost(8e9, 4e6),
        name="conv",
    )(mel, conv1_weight, conv2_weight, *proj_all)
    partials = [partials[0]] + [to_part(partials[step], step) for step in range(1, parts)]

    regrouped, normed, stack = pl.pallas_call(
        functools.partial(norm_kernel, parts, windows, group),
        out_shape=(block, block, jax.ShapeDtypeStruct((parts,) + pack.shape, BF16)),
        in_specs=[smem()] * 3 + [vmem()] * parts + [anywhere()] * parts,
        out_specs=(vmem(), vmem(), vmem()),
        scratch_shapes=[pltpu.SemaphoreType.DMA((parts,))],
        compiler_params=params(min(12 * scale, 32)),
        cost_estimate=cost(1e8, 1e6),
        name="layer_norm",
    )(slots, starts, lengths, *partials, *packs)
    stacks = [stack] + [to_copy(stack, step) for step in range(1, copies)]
    normed = [normed] + [to_part(normed, step) for step in range(1, parts)]

    first = jax.ShapeDtypeStruct((local, head_width + features), BF16)
    context = pl.pallas_call(
        functools.partial(attention_kernel, parts, windows, group),
        out_shape=tuple([first] + [jax.ShapeDtypeStruct((local, head_width), BF16)] * (parts - 1)),
        in_specs=[smem()] * 3 + [vmem()] * (1 + parts + copies),
        out_specs=tuple([vmem()] * parts),
        scratch_shapes=[pltpu.VMEM((windows, group * local, qkv_weight.shape[0]), BF16)],
        compiler_params=params(min(16 * scale, 48)),
        cost_estimate=cost(1e9, 2e6),
        name="attention",
    )(slots, starts, lengths, regrouped, *normed, *stacks)
    context = [to_owner(context[step], step) for step in range(parts)]

    if out_rows.shape != out_weight.shape:
        stacks = [stack[:, mix_rows:].reshape((parts,) + out_weight.shape) for stack in stacks]
        mix_rows = 0
    regrouped, attended = pl.pallas_call(
        functools.partial(output_kernel, parts, windows, group, mix_rows),
        out_shape=(block, block),
        in_specs=[smem()] * 3 + [vmem()] * (parts + copies),
        out_specs=(vmem(), vmem()),
        scratch_shapes=[
            pltpu.VMEM((local, features), BF16),
            pltpu.VMEM((windows, local, out_weight.shape[1]), F32),
        ],
        compiler_params=params(min(12 * scale, 32)),
        cost_estimate=cost(1e8, 3e6),
        name="output",
    )(slots, starts, lengths, *context, *stacks)
    shape = (1, windows, 1, W, features)
    return (regrouped.reshape(shape), attended.reshape(shape))


def solution(mesh):
    in_specs = (
        P(None, ("dp", "seq")),
        P(),
        P(),
        P(),
        P(),
        P(),
        P("dp", None),
        P("dp", None),
        P(None, "dp"),
    )
    out_specs = (P("dp", None, "seq", None, None), P("dp", None, "seq", None, None))
    return jax.shard_map(
        on_device, mesh=mesh, in_specs=in_specs, out_specs=out_specs, check_vma=False
    )
```

```python
import functools
import math

import jax
import jax.numpy as jnp
import numpy as np
from jax import lax
from jax.experimental import pallas as pl
from jax.experimental.pallas import tpu as pltpu
from jax.sharding import PartitionSpec as P

HEADS = 8
HEAD_DIM = 128
MELS = 80
BANDS = MELS // 4
N_FFT = 512
HOP = 160
W = 8
RIM = 384
SPAN = 4 * HOP
JS = W + 1
LANES = 128
SAMPLE_RATE = 16000.0
EPS_LOG = 1e-06
EPS_NORM = 1e-05
MASKED = -1e30
F32 = jnp.float32
BF16 = jnp.bfloat16
MIB = 1 << 20


def mel_table(size, bands):
    count = size // 2 + 1
    highest = 2595.0 * math.log10(1.0 + SAMPLE_RATE / 1400.0)
    points = np.linspace(0.0, highest, bands + 2)
    edges = 700.0 * (10.0 ** (points / 2595.0) - 1.0)
    edges[0] = 0.0
    edges[-1] = SAMPLE_RATE / 2.0
    frequency = np.arange(count) * (SAMPLE_RATE / size)
    lower = edges[:-2][None, :]
    middle = edges[1:-1][None, :]
    upper = edges[2:][None, :]
    rising = (frequency[:, None] - lower) / (middle - lower)
    falling = (upper - frequency[:, None]) / (upper - middle)
    return np.maximum(0.0, np.minimum(rising, falling)).astype(np.float32)


def spectrum_table(size):
    sample = np.arange(size)
    phase = sample[:, None] * np.arange(size // 2)[None, :] % size
    angle = phase * (2.0 * math.pi / size)
    window = 0.5 - 0.5 * np.cos(sample * (2.0 * math.pi / size))
    both = np.concatenate([np.cos(angle), np.sin(angle)], axis=1) * window[:, None]
    filters = np.zeros((size, LANES))
    filters[: size // 2, :MELS] = mel_table(size, MELS)[: size // 2]
    return np.concatenate([both, filters], axis=1).astype(np.float32)


def vmem():
    return pl.BlockSpec(memory_space=pltpu.VMEM)


def smem():
    return pl.BlockSpec(memory_space=pltpu.SMEM)


def anywhere():
    return pl.BlockSpec(memory_space=pl.ANY)


def params(mib):
    return pltpu.CompilerParams(vmem_limit_bytes=mib * MIB)


def all_vmem():
    return pltpu.CompilerParams(vmem_limit_bytes=63_400_000)


def cost(flops, moved):
    return pl.CostEstimate(flops=int(flops), bytes_accessed=int(moved), transcendentals=0)


def place(parts):
    mine = lax.axis_index("dp")
    copies = lax.axis_size("dp") // parts
    return mine // copies, mine % copies


def later(index, step, count):
    return lax.rem(index + step, count)


def start_all(copies):
    for copy in copies:
        copy.start()


def wait_all(copies):
    for copy in copies:
        copy.wait()


def iota(rows, columns, axis):
    return lax.broadcasted_iota(jnp.int32, (rows, columns), axis)


def quotient(index, step, count):
    result = jnp.zeros_like(index)
    for i in range(1, count):
        result += (index >= i * step).astype(jnp.int32)
    return result


def one_hot(target, count):
    return (iota(target.shape[0], count, 1) == target).astype(F32).astype(BF16)


def frame_order(windows):
    count = windows * W
    row = iota(count, 1, 0)
    k = quotient(row, W, windows)
    return one_hot((row - k * W) * windows + k, count)


def first_samples(windows, group):
    row = iota(windows * W, 1, 0)
    return (row + quotient(row, W, windows) * (group - 1) * W) * SPAN


def key_samples(windows, group):
    lane = iota(1, windows * W, 1)
    t = quotient(lane, windows, W)
    return ((lane - t * windows) * group * W + t) * SPAN


def mix_columns(parts, qkv, mix_outs, sems):
    part, _ = place(parts)
    features = qkv.shape[1] // 3
    width = features // parts
    copies = []
    for step in range(parts):
        first = pl.multiple_of(later(part, step, parts) * width, LANES)
        for kind in range(3):
            source = qkv.at[:, pl.ds(kind * features + first, width)]
            target = mix_outs[step].at[:, pl.ds(kind * width, width)]
            copies.append(pltpu.make_async_copy(source, target, sems.at[len(copies)]))
    return copies


def banded_weights(width, conv1_ref, banded_out):
    taps, channels = conv1_ref.shape
    row = lax.broadcasted_iota(jnp.int32, (LANES, taps), 0)
    tap = lax.broadcasted_iota(jnp.int32, (LANES, taps), 1)
    line = (tap >= 3).astype(jnp.int32) + (tap >= 6).astype(jnp.int32)
    target = line * (width - 3) + tap + 1
    weight = conv1_ref[...]
    for g in range(banded_out.shape[1] // channels):
        select = (row == target + 2 * g).astype(F32).astype(BF16)
        banded_out[:, g * channels : (g + 1) * channels] = jnp.dot(
            select, weight, preferred_element_type=F32
        ).astype(BF16)


def mel_kernel(parts, group, slots_ref, rim_ref, audio_ref, table_ref, qkv_ref, out_ref, *refs):
    mix_outs, (ext, table, qkv, mix_sems, sems) = refs[:parts], refs[parts:]
    load_audio = pltpu.make_async_copy(audio_ref, ext.at[:, pl.ds(RIM, audio_ref.shape[1])], sems.at[0])
    load_table = pltpu.make_async_copy(table_ref, table, sems.at[1])
    load_audio.start()
    load_table.start()
    load_qkv = pltpu.make_async_copy(qkv_ref, qkv, sems.at[2])
    load_qkv.start()
    streams = audio_ref.shape[0]
    rows = W * streams
    ext[:, :RIM] = rim_ref[...]
    column = iota(1, rows, 1)
    early = quotient(column, streams, W)
    target = jnp.zeros((1, rows), jnp.int32)
    for u in range(streams):
        target = jnp.where(column - early * streams == u, slots_ref[u] * W + early, target)
    routing = (target == iota(rows, rows, 0)).astype(F32).astype(BF16)
    load_audio.wait()
    phases = []
    for phase in range(4):
        start = HOP * phase + 32
        base, shift = start // LANES * LANES, start % LANES
        length = N_FFT + (LANES if shift else 0)
        block = jnp.concatenate(
            [ext[:, SPAN * j + base : SPAN * j + base + length] for j in range(W)], axis=0
        )
        if shift:
            block = pltpu.roll(block, length - shift, 1)[:, :N_FFT]
        phases.append(block)
    frames = jnp.concatenate(phases, axis=0)
    load_table.wait()
    spectrum = jnp.dot(
        frames, table[:, :N_FFT], precision=lax.Precision.HIGHEST, preferred_element_type=F32
    )
    load_qkv.wait()
    pieces = mix_columns(parts, qkv, mix_outs, mix_sems)
    start_all(pieces)
    half = N_FFT // 2
    real, imag = spectrum[:, :half], spectrum[:, half:]
    power = real * real + imag * imag
    mel_power = jnp.dot(
        power, table[:half, N_FFT:], precision=lax.Precision.HIGHEST, preferred_element_type=F32
    )
    log_mel = jnp.log(mel_power + EPS_LOG)
    share = BANDS // parts
    width = 4 * share + 4
    lane = iota(rows, LANES, 1)
    blocks = []
    for part in range(parts):
        first = 4 * share * part - 4
        block = jnp.zeros((rows, LANES), F32)
        for phase in range(4):
            band = lane - width * phase + first
            here = (lane >= width * phase) & (lane < width * (phase + 1)) & (band >= 0) & (band < MELS)
            shift = (width * phase - first) % LANES
            frame = log_mel[phase * rows : (phase + 1) * rows]
            block = jnp.where(here, pltpu.roll(frame, shift, 1) if shift else frame, block)
        blocks.append(block.astype(BF16))
    routed = jnp.dot(routing, jnp.concatenate(blocks, axis=1), preferred_element_type=F32)
    copies = streams // group
    for part in range(parts):
        for copy in range(copies):
            for plane in range(group):
                row = plane * copies + copy
                out_ref[(part * copies + copy) * group + plane] = routed[
                    row * W : (row + 1) * W, part * LANES : (part + 1) * LANES
                ].astype(BF16)
    wait_all(pieces)


def stacked(parts, pieces, stack_out, sems, base):
    part, _ = place(parts)
    return [
        pltpu.make_async_copy(pieces[step], stack_out.at[later(part, parts - step, parts)], sems.at[base + step])
        for step in range(parts)
    ]


def five_frames(part, width, windows, group, payload):
    n = windows * group
    row = iota(JS * n, 1, 0)
    j = quotient(row, n, JS)
    s = quotient(row - j * n, windows, group)
    window = (row - j * n - s * windows) * group + s
    before = jnp.where(j > 0, window * W + j - 1, window * W - 1)
    same = jnp.where(j < W, window * W + j, -1)
    lane = iota(payload.shape[0], LANES, 1)
    first = jnp.where(lane < 3 * width, pltpu.roll(payload, LANES - width, 1), 0.0).astype(BF16)
    last = (lane >= 3 * width) & (lane < 5 * width)
    second = jnp.where(last, pltpu.roll(payload, 3 * width, 1), 0.0).astype(BF16)
    result = jnp.dot(one_hot(before, n * W), first, preferred_element_type=F32)
    result += jnp.dot(one_hot(same, n * W), second, preferred_element_type=F32)
    lane = iota(1, LANES, 1)
    band = lane - quotient(lane, width, 3) * width - 4 + (width - 4) * part
    silent = (row == 0) & ((lane < 3 * width) & (band >= 0))
    return jnp.where(silent, jnp.log(jnp.full(result.shape, EPS_LOG, F32)), result)


def conv_kernel(parts, width, windows, mel_ref, conv1_ref, conv2_ref, *refs):
    part, copy_index = place(parts)
    copies = lax.axis_size("dp") // parts
    proj_refs, refs = refs[:copies], refs[copies:]
    weight_refs, refs = refs[:parts], refs[parts:]
    outs_refs, refs = refs[:parts], refs[parts:]
    stack_out, banded_ref, even, odd, second, conv2, proj, partial, sems = refs
    load_conv2 = pltpu.make_async_copy(conv2_ref, conv2, sems.at[0])
    load_conv2.start()
    loads = []
    for step in range(copies):
        slot = later(copy_index, copies - step, copies)
        loads.append(pltpu.make_async_copy(proj_refs[step], proj.at[slot], sems.at[1 + step]))
    loads += stacked(parts, weight_refs, stack_out, sems, 1 + copies)
    start_all(loads)
    banded_weights(width, conv1_ref, banded_ref)
    n = mel_ref.shape[0]
    payload = mel_ref[...].astype(F32).reshape(n * W, LANES)
    evens = five_frames(part, width, windows, n // windows, payload)
    odds = pltpu.roll(evens[: W * n], LANES - 2 * width, 1).astype(BF16)
    evens = evens.astype(BF16)
    channels = conv2.shape[1]
    outs = banded_ref.shape[1] // channels
    for g in range(outs):
        lanes = slice(g * channels, (g + 1) * channels)
        weight = banded_ref[:, lanes]
        even[:, lanes] = jax.nn.relu(jnp.dot(evens, weight, preferred_element_type=F32)).astype(BF16)
        odd[:, lanes] = jax.nn.relu(jnp.dot(odds, weight, preferred_element_type=F32)).astype(BF16)

    load_conv2.wait()
    for h in range((outs - 1) // 2):
        lanes = slice(2 * h * channels, (2 * h + 3) * channels)
        depth = 3 * channels
        total = jnp.dot(even[: W * n, lanes], conv2[:depth], preferred_element_type=F32)
        total += jnp.dot(odd[:, lanes], conv2[depth : 2 * depth], preferred_element_type=F32)
        total += jnp.dot(even[n:, lanes], conv2[2 * depth :], preferred_element_type=F32)
        second[:, h * channels : (h + 1) * channels] = jax.nn.relu(total).astype(BF16)
    wait_all(loads)
    weights = proj[...].reshape(second.shape[1], proj.shape[2])
    partial[...] = jnp.dot(second[...], weights, preferred_element_type=F32)
    for step in range(parts):
        plane = later(part, step, parts)
        outs_refs[step][...] = jnp.concatenate(
            [partial[pl.ds(pl.multiple_of(t * n + plane * windows, 8), windows), :] for t in range(W)], axis=0
        ).astype(BF16)


def bounds(row, slots_ref, starts_ref, lengths_ref):
    begin, span = jnp.int32(0), jnp.int32(0)
    for u in range(slots_ref.shape[0]):
        chosen = slots_ref[u] == row
        begin = begin + jnp.where(chosen, starts_ref[u], 0)
        span = span + jnp.where(chosen, lengths_ref[u], 0)
    return begin, begin + span


def norm_kernel(parts, windows, group, slots_ref, starts_ref, lengths_ref, *refs):
    part, copy_index = place(parts)
    copies = lax.axis_size("dp") // parts
    part_refs, refs = refs[:parts], refs[parts:]
    piece_refs, refs = refs[:parts], refs[parts:]
    rows_out, normed_out, stack_out, sems = refs
    moves = stacked(parts, piece_refs, stack_out, sems, 0)
    start_all(moves)
    row = lax.axis_index("seq") * copies + copy_index
    begin, end = bounds(row, slots_ref, starts_ref, lengths_ref)
    total = part_refs[0][...].astype(F32)
    for step in range(1, parts):
        total += part_refs[step][...].astype(F32)
    encoded = total.astype(BF16)
    values = encoded.astype(F32)
    mean = jnp.mean(values, axis=-1, keepdims=True)
    centered = values - mean
    variance = jnp.mean(centered * centered, axis=-1, keepdims=True)
    normed_out[...] = (centered * lax.rsqrt(variance + EPS_NORM)).astype(BF16)
    ordered = jnp.dot(frame_order(windows), encoded, preferred_element_type=F32)
    sample = first_samples(windows, group) + part * (W * SPAN)
    valid = (sample >= begin) & (sample < end)
    rows_out[...] = jnp.where(valid, ordered, 0.0).astype(BF16)
    wait_all(moves)


def attention_kernel(parts, windows, group, slots_ref, starts_ref, lengths_ref, rows_ref, *refs):
    part, copy_index = place(parts)
    copies = lax.axis_size("dp") // parts
    normed_refs, refs = refs[:parts], refs[parts:]
    stack_refs, refs = refs[:copies], refs[copies:]
    outs_refs, (pieces,) = refs[:parts], refs[parts:]
    row = lax.axis_index("seq") * copies + copy_index
    begin, end = bounds(row, slots_ref, starts_ref, lengths_ref)
    masks = []
    for step in range(parts):
        plane = later(part, parts - step, parts)
        sample = key_samples(windows, group) + plane * (W * SPAN)
        masks.append(((sample >= begin) & (sample < end)).astype(F32))
    valid = jnp.concatenate(masks, axis=1) > 0.5
    local = normed_refs[0].shape[0]
    depth = pieces.shape[2]
    for step in range(parts):
        for piece in range(windows):
            pieces[piece, step * local : (step + 1) * local, :] = normed_refs[step][
                :, piece * depth : (piece + 1) * depth
            ]
    mixed = 0.0
    for step in range(copies):
        slot = later(copy_index, copies - step, copies)
        normed = jnp.concatenate([pieces[piece * copies + slot] for piece in range(parts)], axis=1)
        weights = stack_refs[step][...].reshape(parts * depth, stack_refs[step].shape[2])
        mixed += jnp.dot(normed, weights, preferred_element_type=F32)
    mixed = mixed.astype(BF16)
    width = mixed.shape[1] // 3
    scale = HEAD_DIM ** (-0.5)
    for head in range(width // HEAD_DIM):
        at = head * HEAD_DIM
        query = mixed[:, at : at + HEAD_DIM]
        key = mixed[:, width + at : width + at + HEAD_DIM]
        value = mixed[:, 2 * width + at : 2 * width + at + HEAD_DIM]
        scores = lax.dot_general(query, key, (((1,), (1,)), ((), ())), preferred_element_type=F32) * scale
        masked = jnp.where(valid, scores, MASKED)
        peak = jnp.max(masked, axis=1, keepdims=True)
        weight = jnp.where(valid, jnp.exp(masked - peak), 0.0)
        total = jnp.sum(weight, axis=1, keepdims=True)
        summed = jnp.dot(weight.astype(BF16), value, preferred_element_type=F32)
        context = (summed / total).astype(BF16)
        for step in range(parts):
            outs_refs[step][:, at : at + HEAD_DIM] = context[step * local : (step + 1) * local]
    outs_refs[0][:, width:] = rows_ref[...]


def output_kernel(parts, windows, group, slots_ref, starts_ref, lengths_ref, *refs):
    context_refs, refs = refs[:parts], refs[parts:]
    stack_refs, refs = refs[: windows // parts], refs[windows // parts :]
    rows_out, out_ref, context, pieces = refs
    _, copy_index = place(parts)
    copies = windows // parts
    plane = lax.axis_index("seq")
    begin, end = bounds(lax.axis_index("dp"), slots_ref, starts_ref, lengths_ref)
    head_width = context_refs[-1].shape[1]
    rows_out[...] = context_refs[0][:, head_width:]
    for step in range(parts):
        at = pl.multiple_of(later(plane, step, parts) * head_width, LANES)
        context[:, pl.ds(at, head_width)] = context_refs[step][:, :head_width]
    ordered = jnp.dot(frame_order(windows), context[...], preferred_element_type=F32).astype(BF16)
    sample = first_samples(windows, group) + plane * (W * SPAN)
    valid = (sample >= begin) & (sample < end)
    for step in range(copies):
        slot = later(copy_index, copies - step, copies)
        for piece in range(parts):
            pieces[piece * copies + slot] = jnp.dot(
                ordered, stack_refs[step][piece], preferred_element_type=F32
            )
    result = jnp.concatenate([pieces[d] for d in range(windows)], axis=1)
    out_ref[...] = jnp.where(valid, result, 0.0).astype(BF16)


def on_device(
    audio, starts, lengths, slots, conv1_weight, conv2_weight, proj_weight, qkv_weight, out_weight
):
    streams = audio.shape[0]
    windows = lax.axis_size("dp")
    group = lax.axis_size("seq")
    parts = group
    copies = windows // parts
    assert BANDS % parts == 0 and streams == copies * group and streams == windows
    share = BANDS // parts
    width = 4 * share + 4
    channels = conv1_weight.shape[1]
    features = proj_weight.shape[1]
    head_width = features // parts
    local = windows * W
    sources = windows * group
    n = sources
    outs = 2 * share + 1

    route = [(i, i + 1) for i in range(sources - 1)]
    rim = lax.ppermute(audio[:, audio.shape[1] - RIM :], ("dp", "seq"), route)

    def to_part(block, step):
        pairs = [(p * copies + c, (p + step) % parts * copies + c) for p in range(parts) for c in range(copies)]
        return lax.ppermute(block, "dp", pairs)

    def to_copy(block, step):
        pairs = [(p * copies + c, p * copies + (c + step) % copies) for p in range(parts) for c in range(copies)]
        return lax.ppermute(block, "dp", pairs)

    def to_owner(block, step):
        pairs = []
        for p in range(parts):
            for c in range(copies):
                for z in range(group):
                    pairs.append(((p * copies + c) * group + z, (z * copies + c) * group + (p - step) % parts))
        return lax.ppermute(block, ("dp", "seq"), pairs)

    scale = sources // 32
    proj_all = [proj_weight] + [to_copy(proj_weight, step) for step in range(1, copies)]

    out_all = [out_weight] + [to_part(out_weight, step) for step in range(1, parts)]
    mix_piece = jax.ShapeDtypeStruct((qkv_weight.shape[0], 3 * head_width), BF16)

    table = jnp.asarray(spectrum_table(N_FFT))
    mel, *mix_all = pl.pallas_call(
        functools.partial(mel_kernel, parts, group),
        out_shape=tuple([jax.ShapeDtypeStruct((sources, W, LANES), BF16)] + [mix_piece] * parts),
        in_specs=[smem(), vmem()] + [anywhere()] * 3,
        out_specs=tuple([vmem()] + [anywhere()] * parts),
        scratch_shapes=[
            pltpu.VMEM((streams, RIM + audio.shape[1]), F32),
            pltpu.VMEM(table.shape, F32),
            pltpu.VMEM(qkv_weight.shape, BF16),
            pltpu.SemaphoreType.DMA((3 * parts,)),
            pltpu.SemaphoreType.DMA((3,)),
        ],
        compiler_params=all_vmem(),
        cost_estimate=cost(2e9, 2e6),
        name="log_mel",
    )(slots, rim, audio, table, qkv_weight)
    mix_all = [mix_all[0]] + [to_part(mix_all[step], step) for step in range(1, parts)]
    mel = lax.all_to_all(mel, ("dp", "seq"), split_axis=0, concat_axis=0, tiled=True)

    block = jax.ShapeDtypeStruct((local, features), BF16)
    *partials, stack = pl.pallas_call(
        functools.partial(conv_kernel, parts, width, windows),
        out_shape=tuple([block] * parts + [jax.ShapeDtypeStruct((parts,) + out_weight.shape, BF16)]),
        in_specs=[vmem()] * 2 + [anywhere()] * (1 + copies + parts),
        out_specs=tuple([vmem()] * (parts + 1)),
        scratch_shapes=[
            pltpu.VMEM((LANES, outs * channels), BF16),
            pltpu.VMEM((JS * n, outs * channels), BF16),
            pltpu.VMEM((W * n, outs * channels), BF16),
            pltpu.VMEM((W * n, share * channels), BF16),
            pltpu.VMEM(conv2_weight.shape, BF16),
            pltpu.VMEM((copies,) + proj_weight.shape, BF16),
            pltpu.VMEM((W * n, features), F32),
            pltpu.SemaphoreType.DMA((1 + copies + parts,)),
        ],
        compiler_params=all_vmem(),
        cost_estimate=cost(2e9, 4e6),
        name="conv",
    )(mel, conv1_weight, conv2_weight, *proj_all, *out_all)
    out_stacks = [stack] + [to_copy(stack, step) for step in range(1, copies)]
    partials = [partials[0]] + [to_part(partials[step], step) for step in range(1, parts)]

    regrouped, normed, stack = pl.pallas_call(
        functools.partial(norm_kernel, parts, windows, group),
        out_shape=(block, block, jax.ShapeDtypeStruct((parts,) + mix_piece.shape, BF16)),
        in_specs=[smem()] * 3 + [vmem()] * parts + [anywhere()] * parts,
        out_specs=(vmem(), vmem(), vmem()),
        scratch_shapes=[pltpu.SemaphoreType.DMA((parts,))],
        compiler_params=params(min(12 * scale, 32)),
        cost_estimate=cost(1e8, 1e6),
        name="layer_norm",
    )(slots, starts, lengths, *partials, *mix_all)
    mix_stacks = [stack] + [to_copy(stack, step) for step in range(1, copies)]
    normed = [normed] + [to_part(normed, step) for step in range(1, parts)]

    first = jax.ShapeDtypeStruct((local, head_width + features), BF16)
    context = pl.pallas_call(
        functools.partial(attention_kernel, parts, windows, group),
        out_shape=tuple([first] + [jax.ShapeDtypeStruct((local, head_width), BF16)] * (parts - 1)),
        in_specs=[smem()] * 3 + [vmem()] * (1 + parts + copies),
        out_specs=tuple([vmem()] * parts),
        scratch_shapes=[pltpu.VMEM((windows, group * local, qkv_weight.shape[0]), BF16)],
        compiler_params=params(min(16 * scale, 48)),
        cost_estimate=cost(1e9, 2e6),
        name="attention",
    )(slots, starts, lengths, regrouped, *normed, *mix_stacks)
    context = [to_owner(context[step], step) for step in range(parts)]

    regrouped, attended = pl.pallas_call(
        functools.partial(output_kernel, parts, windows, group),
        out_shape=(block, block),
        in_specs=[smem()] * 3 + [vmem()] * (parts + copies),
        out_specs=(vmem(), vmem()),
        scratch_shapes=[
            pltpu.VMEM((local, features), BF16),
            pltpu.VMEM((windows, local, out_weight.shape[1]), F32),
        ],
        compiler_params=params(min(12 * scale, 32)),
        cost_estimate=cost(1e8, 3e6),
        name="output",
    )(slots, starts, lengths, *context, *out_stacks)
    shape = (1, windows, 1, W, features)
    return (regrouped.reshape(shape), attended.reshape(shape))


def solution(mesh):
    in_specs = (
        P(None, ("dp", "seq")),
        P(),
        P(),
        P(),
        P(),
        P(),
        P("dp", None),
        P("dp", None),
        P(None, "dp"),
    )
    out_specs = (P("dp", None, "seq", None, None), P("dp", None, "seq", None, None))
    return jax.shard_map(
        on_device, mesh=mesh, in_specs=in_specs, out_specs=out_specs, check_vma=False
    )
```

```python
import functools
import math

import jax
import jax.numpy as jnp
import numpy as np
from jax import lax
from jax.experimental import pallas as pl
from jax.experimental.pallas import tpu as pltpu
from jax.sharding import PartitionSpec as P

HEADS = 8
HEAD_DIM = 128
MELS = 80
BANDS = MELS // 4
N_FFT = 512
HOP = 160
W = 8
RIM = 384
SPAN = 4 * HOP
JS = W + 1
LANES = 128
SAMPLE_RATE = 16000.0
EPS_LOG = 1e-06
EPS_NORM = 1e-05
MASKED = -1e30
F32 = jnp.float32
BF16 = jnp.bfloat16
MIB = 1 << 20


def mel_table(size, bands):
    count = size // 2 + 1
    highest = 2595.0 * math.log10(1.0 + SAMPLE_RATE / 1400.0)
    points = np.linspace(0.0, highest, bands + 2)
    edges = 700.0 * (10.0 ** (points / 2595.0) - 1.0)
    edges[0] = 0.0
    edges[-1] = SAMPLE_RATE / 2.0
    frequency = np.arange(count) * (SAMPLE_RATE / size)
    lower = edges[:-2][None, :]
    middle = edges[1:-1][None, :]
    upper = edges[2:][None, :]
    rising = (frequency[:, None] - lower) / (middle - lower)
    falling = (upper - frequency[:, None]) / (upper - middle)
    return np.maximum(0.0, np.minimum(rising, falling)).astype(np.float32)


def spectrum_table(size):
    sample = np.arange(size)
    phase = sample[:, None] * np.arange(size // 2)[None, :] % size
    angle = phase * (2.0 * math.pi / size)
    window = 0.5 - 0.5 * np.cos(sample * (2.0 * math.pi / size))
    both = np.concatenate([np.cos(angle), np.sin(angle)], axis=1) * window[:, None]
    filters = np.zeros((size, LANES))
    filters[: size // 2, :MELS] = mel_table(size, MELS)[: size // 2]
    return np.concatenate([both, filters], axis=1).astype(np.float32)


def vmem():
    return pl.BlockSpec(memory_space=pltpu.VMEM)


def smem():
    return pl.BlockSpec(memory_space=pltpu.SMEM)


def anywhere():
    return pl.BlockSpec(memory_space=pl.ANY)


def params(mib):
    return pltpu.CompilerParams(vmem_limit_bytes=mib * MIB)


def cost(flops, moved):
    return pl.CostEstimate(flops=int(flops), bytes_accessed=int(moved), transcendentals=0)


def place(parts):
    mine = lax.axis_index("dp")
    copies = lax.axis_size("dp") // parts
    return mine // copies, mine % copies


def start_all(copies):
    for copy in copies:
        copy.start()


def wait_all(copies):
    for copy in copies:
        copy.wait()


def iota(rows, columns, axis):
    return lax.broadcasted_iota(jnp.int32, (rows, columns), axis)


def quotient(index, step, count):
    result = jnp.zeros_like(index)
    for i in range(1, count):
        result += (index >= i * step).astype(jnp.int32)
    return result


def one_hot(target, count):
    return (iota(target.shape[0], count, 1) == target).astype(F32).astype(BF16)


def frame_order(windows):
    count = windows * W
    row = iota(count, 1, 0)
    k = quotient(row, W, windows)
    return one_hot((row - k * W) * windows + k, count)


def first_samples(windows, group):
    row = iota(windows * W, 1, 0)
    return (row + quotient(row, W, windows) * (group - 1) * W) * SPAN


def key_samples(windows, group):
    lane = iota(1, windows * W, 1)
    t = quotient(lane, windows, W)
    return ((lane - t * windows) * group * W + t) * SPAN


def mix_columns(parts, qkv, mix_outs, sems):
    part, _ = place(parts)
    features = qkv.shape[1] // 3
    width = features // parts
    copies = []
    for step in range(parts):
        first = pl.multiple_of((part ^ step) * width, LANES)
        for kind in range(3):
            source = qkv.at[:, pl.ds(kind * features + first, width)]
            target = mix_outs[step].at[:, pl.ds(kind * width, width)]
            copies.append(pltpu.make_async_copy(source, target, sems.at[len(copies)]))
    return copies


def banded_weights(width, conv1_ref, banded_out):
    taps, channels = conv1_ref.shape
    row = lax.broadcasted_iota(jnp.int32, (LANES, taps), 0)
    tap = lax.broadcasted_iota(jnp.int32, (LANES, taps), 1)
    line = (tap >= 3).astype(jnp.int32) + (tap >= 6).astype(jnp.int32)
    target = line * (width - 3) + tap + 1
    weight = conv1_ref[...]
    for g in range(banded_out.shape[1] // channels):
        select = (row == target + 2 * g).astype(F32).astype(BF16)
        banded_out[:, g * channels : (g + 1) * channels] = jnp.dot(
            select, weight, preferred_element_type=F32
        ).astype(BF16)


def mel_kernel(parts, group, slots_ref, rim_ref, audio_ref, table_ref, qkv_ref, out_ref, *refs):
    mix_outs, (ext, table, qkv, mix_sems, sems) = refs[:parts], refs[parts:]
    load_audio = pltpu.make_async_copy(audio_ref, ext.at[:, pl.ds(RIM, audio_ref.shape[1])], sems.at[0])
    load_table = pltpu.make_async_copy(table_ref, table, sems.at[1])
    load_audio.start()
    load_table.start()
    load_qkv = pltpu.make_async_copy(qkv_ref, qkv, sems.at[2])
    load_qkv.start()
    streams = audio_ref.shape[0]
    rows = W * streams
    ext[:, :RIM] = rim_ref[...]
    column = iota(1, rows, 1)
    early = quotient(column, streams, W)
    target = jnp.zeros((1, rows), jnp.int32)
    for u in range(streams):
        target = jnp.where(column - early * streams == u, slots_ref[u] * W + early, target)
    routing = (target == iota(rows, rows, 0)).astype(F32).astype(BF16)
    load_audio.wait()
    phases = []
    for phase in range(4):
        start = HOP * phase + 32
        base, shift = start // LANES * LANES, start % LANES
        length = N_FFT + (LANES if shift else 0)
        block = jnp.concatenate(
            [ext[:, SPAN * j + base : SPAN * j + base + length] for j in range(W)], axis=0
        )
        if shift:
            block = pltpu.roll(block, length - shift, 1)[:, :N_FFT]
        phases.append(block)
    frames = jnp.concatenate(phases, axis=0)
    load_table.wait()
    spectrum = jnp.dot(
        frames, table[:, :N_FFT], precision=lax.Precision.HIGHEST, preferred_element_type=F32
    )
    load_qkv.wait()
    pieces = mix_columns(parts, qkv, mix_outs, mix_sems)
    start_all(pieces)
    half = N_FFT // 2
    real, imag = spectrum[:, :half], spectrum[:, half:]
    power = real * real + imag * imag
    mel_power = jnp.dot(
        power, table[:half, N_FFT:], precision=lax.Precision.HIGHEST, preferred_element_type=F32
    )
    log_mel = jnp.log(mel_power + EPS_LOG)
    share = BANDS // parts
    width = 4 * share + 4
    lane = iota(rows, LANES, 1)
    blocks = []
    for part in range(parts):
        first = 4 * share * part - 4
        block = jnp.zeros((rows, LANES), F32)
        for phase in range(4):
            band = lane - width * phase + first
            here = (lane >= width * phase) & (lane < width * (phase + 1)) & (band >= 0) & (band < MELS)
            shift = (width * phase - first) % LANES
            frame = log_mel[phase * rows : (phase + 1) * rows]
            block = jnp.where(here, pltpu.roll(frame, shift, 1) if shift else frame, block)
        blocks.append(block.astype(BF16))
    routed = jnp.dot(routing, jnp.concatenate(blocks, axis=1), preferred_element_type=F32)
    copies = streams // group
    for part in range(parts):
        for copy in range(copies):
            for plane in range(group):
                row = plane * copies + copy
                out_ref[(part * copies + copy) * group + plane] = routed[
                    row * W : (row + 1) * W, part * LANES : (part + 1) * LANES
                ].astype(BF16)
    wait_all(pieces)


def stacked(parts, pieces, stack_out, sems, base):
    part, _ = place(parts)
    return [
        pltpu.make_async_copy(pieces[step], stack_out.at[part ^ step], sems.at[base + step])
        for step in range(parts)
    ]


def five_frames(part, width, windows, group, payload):
    n = windows * group
    row = iota(JS * n, 1, 0)
    j = quotient(row, n, JS)
    s = quotient(row - j * n, windows, group)
    window = (row - j * n - s * windows) * group + s
    before = jnp.where(j > 0, window * W + j - 1, window * W - 1)
    same = jnp.where(j < W, window * W + j, -1)
    lane = iota(payload.shape[0], LANES, 1)
    first = jnp.where(lane < 3 * width, pltpu.roll(payload, LANES - width, 1), 0.0).astype(BF16)
    last = (lane >= 3 * width) & (lane < 5 * width)
    second = jnp.where(last, pltpu.roll(payload, 3 * width, 1), 0.0).astype(BF16)
    result = jnp.dot(one_hot(before, n * W), first, preferred_element_type=F32)
    result += jnp.dot(one_hot(same, n * W), second, preferred_element_type=F32)
    lane = iota(1, LANES, 1)
    band = lane - quotient(lane, width, 3) * width - 4 + (width - 4) * part
    silent = (row == 0) & ((lane < 3 * width) & (band >= 0))
    return jnp.where(silent, jnp.log(jnp.full(result.shape, EPS_LOG, F32)), result)


def conv_kernel(parts, width, windows, mel_ref, conv1_ref, conv2_ref, *refs):
    part, copy_index = place(parts)
    copies = lax.axis_size("dp") // parts
    proj_refs, refs = refs[:copies], refs[copies:]
    weight_refs, refs = refs[:parts], refs[parts:]
    outs_refs, refs = refs[:parts], refs[parts:]
    stack_out, banded_ref, even, odd, second, conv2, proj, partial, sems = refs
    load_conv2 = pltpu.make_async_copy(conv2_ref, conv2, sems.at[0])
    load_conv2.start()
    loads = []
    for step in range(copies):
        slot = copy_index ^ step
        loads.append(pltpu.make_async_copy(proj_refs[step], proj.at[slot], sems.at[1 + step]))
    loads += stacked(parts, weight_refs, stack_out, sems, 1 + copies)
    start_all(loads)
    banded_weights(width, conv1_ref, banded_ref)
    n = mel_ref.shape[0]
    payload = mel_ref[...].astype(F32).reshape(n * W, LANES)
    evens = five_frames(part, width, windows, n // windows, payload)
    odds = pltpu.roll(evens[: W * n], LANES - 2 * width, 1).astype(BF16)
    evens = evens.astype(BF16)
    channels = conv2.shape[1]
    outs = banded_ref.shape[1] // channels
    for g in range(outs):
        lanes = slice(g * channels, (g + 1) * channels)
        weight = banded_ref[:, lanes]
        even[:, lanes] = jax.nn.relu(jnp.dot(evens, weight, preferred_element_type=F32)).astype(BF16)
        odd[:, lanes] = jax.nn.relu(jnp.dot(odds, weight, preferred_element_type=F32)).astype(BF16)

    load_conv2.wait()
    for h in range((outs - 1) // 2):
        lanes = slice(2 * h * channels, (2 * h + 3) * channels)
        depth = 3 * channels
        total = jnp.dot(even[: W * n, lanes], conv2[:depth], preferred_element_type=F32)
        total += jnp.dot(odd[:, lanes], conv2[depth : 2 * depth], preferred_element_type=F32)
        total += jnp.dot(even[n:, lanes], conv2[2 * depth :], preferred_element_type=F32)
        second[:, h * channels : (h + 1) * channels] = jax.nn.relu(total).astype(BF16)
    wait_all(loads)
    weights = proj[...].reshape(second.shape[1], proj.shape[2])
    partial[...] = jnp.dot(second[...], weights, preferred_element_type=F32)
    for step in range(parts):
        plane = (part ^ step)
        outs_refs[step][...] = jnp.concatenate(
            [partial[pl.ds(pl.multiple_of(t * n + plane * windows, 8), windows), :] for t in range(W)], axis=0
        ).astype(BF16)


def bounds(row, slots_ref, starts_ref, lengths_ref):
    begin, span = jnp.int32(0), jnp.int32(0)
    for u in range(slots_ref.shape[0]):
        chosen = slots_ref[u] == row
        begin = begin + jnp.where(chosen, starts_ref[u], 0)
        span = span + jnp.where(chosen, lengths_ref[u], 0)
    return begin, begin + span


def norm_kernel(parts, windows, group, slots_ref, starts_ref, lengths_ref, *refs):
    part, copy_index = place(parts)
    copies = lax.axis_size("dp") // parts
    part_refs, refs = refs[:parts], refs[parts:]
    piece_refs, refs = refs[:parts], refs[parts:]
    rows_out, normed_out, stack_out, sems = refs
    moves = stacked(parts, piece_refs, stack_out, sems, 0)
    start_all(moves)
    row = lax.axis_index("seq") * copies + copy_index
    begin, end = bounds(row, slots_ref, starts_ref, lengths_ref)
    total = part_refs[0][...].astype(F32)
    for step in range(1, parts):
        total += part_refs[step][...].astype(F32)
    encoded = total.astype(BF16)
    values = encoded.astype(F32)
    mean = jnp.mean(values, axis=-1, keepdims=True)
    centered = values - mean
    variance = jnp.mean(centered * centered, axis=-1, keepdims=True)
    normed_out[...] = (centered * lax.rsqrt(variance + EPS_NORM)).astype(BF16)
    ordered = jnp.dot(frame_order(windows), encoded, preferred_element_type=F32)
    sample = first_samples(windows, group) + part * (W * SPAN)
    valid = (sample >= begin) & (sample < end)
    rows_out[...] = jnp.where(valid, ordered, 0.0).astype(BF16)
    wait_all(moves)


def attention_kernel(parts, windows, group, slots_ref, starts_ref, lengths_ref, rows_ref, *refs):
    part, copy_index = place(parts)
    copies = lax.axis_size("dp") // parts
    normed_refs, refs = refs[:parts], refs[parts:]
    stack_refs, refs = refs[:copies], refs[copies:]
    outs_refs, (pieces,) = refs[:parts], refs[parts:]
    row = lax.axis_index("seq") * copies + copy_index
    begin, end = bounds(row, slots_ref, starts_ref, lengths_ref)
    masks = []
    for step in range(parts):
        plane = part ^ step
        sample = key_samples(windows, group) + plane * (W * SPAN)
        masks.append(((sample >= begin) & (sample < end)).astype(F32))
    valid = jnp.concatenate(masks, axis=1) > 0.5
    local = normed_refs[0].shape[0]
    depth = pieces.shape[2]
    for step in range(parts):
        for piece in range(windows):
            pieces[piece, step * local : (step + 1) * local, :] = normed_refs[step][
                :, piece * depth : (piece + 1) * depth
            ]
    mixed = 0.0
    for step in range(copies):
        slot = copy_index ^ step
        normed = jnp.concatenate([pieces[piece * copies + slot] for piece in range(parts)], axis=1)
        weights = stack_refs[step][...].reshape(parts * depth, stack_refs[step].shape[2])
        mixed += jnp.dot(normed, weights, preferred_element_type=F32)
    mixed = mixed.astype(BF16)
    width = mixed.shape[1] // 3
    scale = HEAD_DIM ** (-0.5)
    for head in range(width // HEAD_DIM):
        at = head * HEAD_DIM
        query = mixed[:, at : at + HEAD_DIM]
        key = mixed[:, width + at : width + at + HEAD_DIM]
        value = mixed[:, 2 * width + at : 2 * width + at + HEAD_DIM]
        scores = lax.dot_general(query, key, (((1,), (1,)), ((), ())), preferred_element_type=F32) * scale
        masked = jnp.where(valid, scores, MASKED)
        peak = jnp.max(masked, axis=1, keepdims=True)
        weight = jnp.where(valid, jnp.exp(masked - peak), 0.0)
        total = jnp.sum(weight, axis=1, keepdims=True)
        summed = jnp.dot(weight.astype(BF16), value, preferred_element_type=F32)
        context = (summed / total).astype(BF16)
        for step in range(parts):
            outs_refs[step][:, at : at + HEAD_DIM] = context[step * local : (step + 1) * local]
    outs_refs[0][:, width:] = rows_ref[...]


def output_kernel(parts, windows, group, slots_ref, starts_ref, lengths_ref, *refs):
    context_refs, refs = refs[:parts], refs[parts:]
    stack_refs, refs = refs[: windows // parts], refs[windows // parts :]
    rows_out, out_ref, context, pieces = refs
    _, copy_index = place(parts)
    copies = windows // parts
    plane = lax.axis_index("seq")
    begin, end = bounds(lax.axis_index("dp"), slots_ref, starts_ref, lengths_ref)
    head_width = context_refs[-1].shape[1]
    rows_out[...] = context_refs[0][:, head_width:]
    for step in range(parts):
        at = pl.multiple_of((plane ^ step) * head_width, LANES)
        context[:, pl.ds(at, head_width)] = context_refs[step][:, :head_width]
    ordered = jnp.dot(frame_order(windows), context[...], preferred_element_type=F32).astype(BF16)
    sample = first_samples(windows, group) + plane * (W * SPAN)
    valid = (sample >= begin) & (sample < end)
    for step in range(copies):
        slot = copy_index ^ step
        for piece in range(parts):
            pieces[piece * copies + slot] = jnp.dot(
                ordered, stack_refs[step][piece], preferred_element_type=F32
            )
    result = jnp.concatenate([pieces[d] for d in range(windows)], axis=1)
    out_ref[...] = jnp.where(valid, result, 0.0).astype(BF16)


def on_device(
    audio, starts, lengths, slots, conv1_weight, conv2_weight, proj_weight, qkv_weight, out_weight
):
    streams = audio.shape[0]
    windows = lax.axis_size("dp")
    group = lax.axis_size("seq")
    parts = group
    copies = windows // parts
    assert BANDS % parts == 0 and streams == copies * group and streams == windows
    assert parts & (parts - 1) == 0 and copies & (copies - 1) == 0
    share = BANDS // parts
    width = 4 * share + 4
    channels = conv1_weight.shape[1]
    features = proj_weight.shape[1]
    head_width = features // parts
    local = windows * W
    sources = windows * group
    n = sources
    outs = 2 * share + 1

    route = [(i, i + 1) for i in range(sources - 1)]
    rim = lax.ppermute(audio[:, audio.shape[1] - RIM :], ("dp", "seq"), route)

    def to_part(block, step):
        pairs = [(p * copies + c, (p ^ step) * copies + c) for p in range(parts) for c in range(copies)]
        return lax.ppermute(block, "dp", pairs)

    def to_copy(block, step):
        pairs = [(p * copies + c, p * copies + (c ^ step)) for p in range(parts) for c in range(copies)]
        return lax.ppermute(block, "dp", pairs)

    def to_owner(block, step):
        pairs = []
        for p in range(parts):
            for c in range(copies):
                for z in range(group):
                    pairs.append(((p * copies + c) * group + z, (z * copies + c) * group + (p ^ step)))
        return lax.ppermute(block, ("dp", "seq"), pairs)

    scale = sources // 32
    proj_all = [proj_weight] + [to_copy(proj_weight, step) for step in range(1, copies)]

    out_all = [out_weight] + [to_part(out_weight, step) for step in range(1, parts)]
    mix_piece = jax.ShapeDtypeStruct((qkv_weight.shape[0], 3 * head_width), BF16)

    table = jnp.asarray(spectrum_table(N_FFT))
    mel, *mix_all = pl.pallas_call(
        functools.partial(mel_kernel, parts, group),
        out_shape=tuple([jax.ShapeDtypeStruct((sources, W, LANES), BF16)] + [mix_piece] * parts),
        in_specs=[smem(), vmem()] + [anywhere()] * 3,
        out_specs=tuple([vmem()] + [anywhere()] * parts),
        scratch_shapes=[
            pltpu.VMEM((streams, RIM + audio.shape[1]), F32),
            pltpu.VMEM(table.shape, F32),
            pltpu.VMEM(qkv_weight.shape, BF16),
            pltpu.SemaphoreType.DMA((3 * parts,)),
            pltpu.SemaphoreType.DMA((3,)),
        ],
        compiler_params=params(60),
        cost_estimate=cost(2e9, 2e6),
        name="log_mel",
    )(slots, rim, audio, table, qkv_weight)
    mix_all = [mix_all[0]] + [to_part(mix_all[step], step) for step in range(1, parts)]
    mel = lax.all_to_all(mel, ("dp", "seq"), split_axis=0, concat_axis=0, tiled=True)

    block = jax.ShapeDtypeStruct((local, features), BF16)
    *partials, stack = pl.pallas_call(
        functools.partial(conv_kernel, parts, width, windows),
        out_shape=tuple([block] * parts + [jax.ShapeDtypeStruct((parts,) + out_weight.shape, BF16)]),
        in_specs=[vmem()] * 2 + [anywhere()] * (1 + copies + parts),
        out_specs=tuple([vmem()] * (parts + 1)),
        scratch_shapes=[
            pltpu.VMEM((LANES, outs * channels), BF16),
            pltpu.VMEM((JS * n, outs * channels), BF16),
            pltpu.VMEM((W * n, outs * channels), BF16),
            pltpu.VMEM((W * n, share * channels), BF16),
            pltpu.VMEM(conv2_weight.shape, BF16),
            pltpu.VMEM((copies,) + proj_weight.shape, BF16),
            pltpu.VMEM((W * n, features), F32),
            pltpu.SemaphoreType.DMA((1 + copies + parts,)),
        ],
        compiler_params=params(min(40 + 4 * scale, 56)),
        cost_estimate=cost(2e9, 4e6),
        name="conv",
    )(mel, conv1_weight, conv2_weight, *proj_all, *out_all)
    out_stacks = [stack] + [to_copy(stack, step) for step in range(1, copies)]
    partials = [partials[0]] + [to_part(partials[step], step) for step in range(1, parts)]

    regrouped, normed, stack = pl.pallas_call(
        functools.partial(norm_kernel, parts, windows, group),
        out_shape=(block, block, jax.ShapeDtypeStruct((parts,) + mix_piece.shape, BF16)),
        in_specs=[smem()] * 3 + [vmem()] * parts + [anywhere()] * parts,
        out_specs=(vmem(), vmem(), vmem()),
        scratch_shapes=[pltpu.SemaphoreType.DMA((parts,))],
        compiler_params=params(min(12 * scale, 32)),
        cost_estimate=cost(1e8, 1e6),
        name="layer_norm",
    )(slots, starts, lengths, *partials, *mix_all)
    mix_stacks = [stack] + [to_copy(stack, step) for step in range(1, copies)]
    normed = [normed] + [to_part(normed, step) for step in range(1, parts)]

    first = jax.ShapeDtypeStruct((local, head_width + features), BF16)
    context = pl.pallas_call(
        functools.partial(attention_kernel, parts, windows, group),
        out_shape=tuple([first] + [jax.ShapeDtypeStruct((local, head_width), BF16)] * (parts - 1)),
        in_specs=[smem()] * 3 + [vmem()] * (1 + parts + copies),
        out_specs=tuple([vmem()] * parts),
        scratch_shapes=[pltpu.VMEM((windows, group * local, qkv_weight.shape[0]), BF16)],
        compiler_params=params(min(16 * scale, 48)),
        cost_estimate=cost(1e9, 2e6),
        name="attention",
    )(slots, starts, lengths, regrouped, *normed, *mix_stacks)
    context = [to_owner(context[step], step) for step in range(parts)]

    regrouped, attended = pl.pallas_call(
        functools.partial(output_kernel, parts, windows, group),
        out_shape=(block, block),
        in_specs=[smem()] * 3 + [vmem()] * (parts + copies),
        out_specs=(vmem(), vmem()),
        scratch_shapes=[
            pltpu.VMEM((local, features), BF16),
            pltpu.VMEM((windows, local, out_weight.shape[1]), F32),
        ],
        compiler_params=params(min(12 * scale, 32)),
        cost_estimate=cost(1e8, 3e6),
        name="output",
    )(slots, starts, lengths, *context, *out_stacks)
    shape = (1, windows, 1, W, features)
    return (regrouped.reshape(shape), attended.reshape(shape))


def solution(mesh):
    in_specs = (
        P(None, ("dp", "seq")),
        P(),
        P(),
        P(),
        P(),
        P(),
        P("dp", None),
        P("dp", None),
        P(None, "dp"),
    )
    out_specs = (P("dp", None, "seq", None, None), P("dp", None, "seq", None, None))
    return jax.shard_map(
        on_device, mesh=mesh, in_specs=in_specs, out_specs=out_specs, check_vma=False
    )
```

```python
import functools
import math

import jax
import jax.numpy as jnp
import numpy as np
from jax import lax
from jax.experimental import pallas as pl
from jax.experimental.pallas import tpu as pltpu
from jax.sharding import PartitionSpec as P

HEADS = 8
HEAD_DIM = 128
MELS = 80
BANDS = MELS // 4
N_FFT = 512
HOP = 160
W = 8
RIM = 1024
SPAN = 4 * HOP
JS = W + 1
LANES = 128
SAMPLE_RATE = 16000.0
EPS_LOG = 1e-06
EPS_NORM = 1e-05
MASKED = -1e30
F32 = jnp.float32
BF16 = jnp.bfloat16
MIB = 1 << 20


def mel_table(size, bands):
    count = size // 2 + 1
    highest = 2595.0 * math.log10(1.0 + SAMPLE_RATE / 1400.0)
    points = np.linspace(0.0, highest, bands + 2)
    edges = 700.0 * (10.0 ** (points / 2595.0) - 1.0)
    edges[0] = 0.0
    edges[-1] = SAMPLE_RATE / 2.0
    frequency = np.arange(count) * (SAMPLE_RATE / size)
    lower = edges[:-2][None, :]
    middle = edges[1:-1][None, :]
    upper = edges[2:][None, :]
    rising = (frequency[:, None] - lower) / (middle - lower)
    falling = (upper - frequency[:, None]) / (upper - middle)
    return np.maximum(0.0, np.minimum(rising, falling)).astype(np.float32)


def spectrum_table(size):
    sample = np.arange(size)
    phase = sample[:, None] * np.arange(size // 2)[None, :] % size
    angle = phase * (2.0 * math.pi / size)
    window = 0.5 - 0.5 * np.cos(sample * (2.0 * math.pi / size))
    both = np.concatenate([np.cos(angle), np.sin(angle)], axis=1) * window[:, None]
    filters = np.zeros((size, LANES))
    filters[: size // 2, :MELS] = mel_table(size, MELS)[: size // 2]
    return np.concatenate([both, filters], axis=1).astype(np.float32)


def vmem():
    return pl.BlockSpec(memory_space=pltpu.VMEM)


def smem():
    return pl.BlockSpec(memory_space=pltpu.SMEM)


def anywhere():
    return pl.BlockSpec(memory_space=pl.ANY)


def params(mib):
    return pltpu.CompilerParams(vmem_limit_bytes=mib * MIB)


def cost(flops, moved):
    return pl.CostEstimate(flops=int(flops), bytes_accessed=int(moved), transcendentals=0)


def place(parts):
    mine = lax.axis_index("dp")
    copies = lax.axis_size("dp") // parts
    return mine // copies, mine % copies


def start_all(copies):
    for copy in copies:
        copy.start()


def wait_all(copies):
    for copy in copies:
        copy.wait()


def iota(rows, columns, axis):
    return lax.broadcasted_iota(jnp.int32, (rows, columns), axis)


def quotient(index, step, count):
    result = jnp.zeros_like(index)
    for i in range(1, count):
        result += (index >= i * step).astype(jnp.int32)
    return result


def one_hot(target, count):
    return (iota(target.shape[0], count, 1) == target).astype(F32).astype(BF16)


def frame_order(parts, copies):
    count = parts * copies * W
    row = iota(count, 1, 0)
    k = quotient(row, W, parts * copies)
    p = quotient(k, copies, parts)
    return one_hot((k - p * copies) * W * parts + (row - k * W) * parts + p, count)


def row_order(parts, streams):
    count = W * parts * streams
    row = iota(count, 1, 0)
    r = quotient(row, W * parts, streams)
    rest = row - r * W * parts
    return one_hot(rest * streams + r, count)


def samples(index, windows, group):
    return (index + quotient(index, W, windows) * (group - 1) * W) * SPAN


def mix_columns(group, qkv_ref, mix_out, sems):
    features = qkv_ref.shape[1] // 3
    width = features // group
    first = pl.multiple_of(lax.axis_index("seq") * width, LANES)
    return [
        pltpu.make_async_copy(
            qkv_ref.at[:, pl.ds(kind * features + first, width)],
            mix_out.at[:, pl.ds(kind * width, width)],
            sems.at[kind],
        )
        for kind in range(3)
    ]


def banded_weights(width, conv1_ref, banded_out):
    taps, channels = conv1_ref.shape
    row = lax.broadcasted_iota(jnp.int32, (LANES, taps), 0)
    tap = lax.broadcasted_iota(jnp.int32, (LANES, taps), 1)
    line = (tap >= 3).astype(jnp.int32) + (tap >= 6).astype(jnp.int32)
    target = line * (width - 3) + tap + 1
    weight = conv1_ref[...]
    for g in range(banded_out.shape[1] // channels):
        select = (row == target + 2 * g).astype(F32).astype(BF16)
        banded_out[:, g * channels : (g + 1) * channels] = jnp.dot(
            select, weight, preferred_element_type=F32
        ).astype(BF16)


def mel_kernel(parts, group, slots_ref, rim_ref, audio_ref, table_ref, qkv_ref, *refs):
    outs_refs, (mix_out, ext, table, blocks, sems) = refs[:parts], refs[parts:]
    load_audio = pltpu.make_async_copy(audio_ref, ext.at[:, pl.ds(RIM, audio_ref.shape[1])], sems.at[3])
    load_table = pltpu.make_async_copy(table_ref, table, sems.at[4])
    load_audio.start()
    load_table.start()
    pieces = mix_columns(group, qkv_ref, mix_out, sems)
    start_all(pieces)
    streams = audio_ref.shape[0]
    rows = JS * streams
    ext[:, :RIM] = rim_ref[...]
    column = iota(1, rows, 1)
    early = quotient(column, streams, JS)
    target = jnp.zeros((1, rows), jnp.int32)
    for u in range(streams):
        target = jnp.where(column - early * streams == u, early * streams + slots_ref[u], target)
    routing = (target == iota(rows, rows, 0)).astype(F32).astype(BF16)
    load_audio.wait()
    phases = []
    for phase in range(4):
        start = HOP * phase + 32
        base, shift = start // LANES * LANES, start % LANES
        length = N_FFT + (LANES if shift else 0)
        block = jnp.concatenate(
            [ext[:, SPAN * j + base : SPAN * j + base + length] for j in range(JS)], axis=0
        )
        if shift:
            block = pltpu.roll(block, length - shift, 1)[:, :N_FFT]
        phases.append(block)
    frames = jnp.concatenate(phases, axis=0)
    load_table.wait()
    spectrum = jnp.dot(
        frames, table[:, :N_FFT], precision=lax.Precision.HIGHEST, preferred_element_type=F32
    )
    half = N_FFT // 2
    real, imag = spectrum[:, :half], spectrum[:, half:]
    power = real * real + imag * imag
    mel_power = jnp.dot(
        power, table[:half, N_FFT:], precision=lax.Precision.HIGHEST, preferred_element_type=F32
    )
    log_mel = jnp.log(mel_power + EPS_LOG)
    share = BANDS // parts
    width = 4 * share + 4
    lane = iota(rows, LANES, 1)
    by_phase = [log_mel[phase * rows : (phase + 1) * rows] for phase in range(4)]

    def next_four(frames):
        return jnp.concatenate([frames[streams:], jnp.zeros((streams, LANES), F32)], axis=0)

    taps = [by_phase[1], by_phase[2], by_phase[3], next_four(by_phase[0]), next_four(by_phase[1])]
    for part in range(parts):
        first = 4 * share * part - 4
        block = jnp.zeros((rows, LANES), F32)
        for delta, frames in enumerate(taps):
            band = lane - width * delta + first
            here = (lane >= width * delta) & (lane < width * (delta + 1)) & (band >= 0) & (band < MELS)
            shift = (width * delta - first) % LANES
            block = jnp.where(here, pltpu.roll(frames, shift, 1) if shift else frames, block)
        blocks[part] = jnp.dot(routing, block.astype(BF16), preferred_element_type=F32).astype(BF16)
    mine, _ = place(parts)
    for step in range(parts):
        outs_refs[step][...] = blocks[mine ^ step]
    wait_all(pieces)


def stacked(parts, pieces, stack_out, sems, base):
    part, _ = place(parts)
    return [
        pltpu.make_async_copy(pieces[step], stack_out.at[part ^ step], sems.at[base + step])
        for step in range(parts)
    ]


def conv_kernel(parts, width, conv1_ref, conv2_ref, *refs):
    part, copy_index = place(parts)
    mine = lax.axis_index("dp")
    windows = lax.axis_size("dp")
    copies = windows // parts
    mel_refs, refs = refs[:parts], refs[parts:]
    proj_refs, refs = refs[:copies], refs[copies:]
    outs_refs, refs = refs[:windows], refs[windows:]
    mel, banded_ref, even, odd, second, conv2, proj, partial, sems = refs
    load_conv2 = pltpu.make_async_copy(conv2_ref, conv2, sems.at[0])
    load_conv2.start()
    loads = []
    for step in range(copies):
        slot = copy_index ^ step
        loads.append(pltpu.make_async_copy(proj_refs[step], proj.at[slot], sems.at[1 + step]))
    start_all(loads)
    banded_weights(width, conv1_ref, banded_ref)
    streams = mel_refs[0].shape[0] // JS
    n = parts * streams
    for step in range(parts):
        mel[part ^ step] = mel_refs[step][...].astype(F32)
    evens = jnp.concatenate(
        [mel[p, j * streams : (j + 1) * streams, :] for j in range(JS) for p in range(parts)], axis=0
    )
    odds = pltpu.roll(evens[: W * n], LANES - 2 * width, 1).astype(BF16)
    evens = evens.astype(BF16)
    channels = conv2.shape[1]
    outs = banded_ref.shape[1] // channels
    for g in range(outs):
        lanes = slice(g * channels, (g + 1) * channels)
        weight = banded_ref[:, lanes]
        even[:, lanes] = jax.nn.relu(jnp.dot(evens, weight, preferred_element_type=F32)).astype(BF16)
        odd[:, lanes] = jax.nn.relu(jnp.dot(odds, weight, preferred_element_type=F32)).astype(BF16)

    load_conv2.wait()
    order = row_order(parts, streams)
    for h in range((outs - 1) // 2):
        lanes = slice(2 * h * channels, (2 * h + 3) * channels)
        depth = 3 * channels
        total = jnp.dot(even[: W * n, lanes], conv2[:depth], preferred_element_type=F32)
        total += jnp.dot(odd[:, lanes], conv2[depth : 2 * depth], preferred_element_type=F32)
        total += jnp.dot(even[n:, lanes], conv2[2 * depth :], preferred_element_type=F32)
        second[:, h * channels : (h + 1) * channels] = jnp.dot(
            order, jax.nn.relu(total).astype(BF16), preferred_element_type=F32
        ).astype(BF16)
    wait_all(loads)
    weights = proj[...].reshape(second.shape[1], proj.shape[2])
    partial[...] = jnp.dot(second[...], weights, preferred_element_type=F32)
    rows = W * parts
    for step in range(windows):
        at = pl.multiple_of((mine ^ step) * rows, rows)
        outs_refs[step][...] = partial[pl.ds(at, rows), :].astype(BF16)


def bounds(row, slots_ref, starts_ref, lengths_ref):
    begin, span = jnp.int32(0), jnp.int32(0)
    for u in range(slots_ref.shape[0]):
        chosen = slots_ref[u] == row
        begin = begin + jnp.where(chosen, starts_ref[u], 0)
        span = span + jnp.where(chosen, lengths_ref[u], 0)
    return begin, begin + span


def norm_kernel(parts, group, slots_ref, starts_ref, lengths_ref, *refs):
    _, copy_index = place(parts)
    windows = lax.axis_size("dp")
    copies = windows // parts
    part_refs, refs = refs[:windows], refs[windows:]
    piece_refs, refs = refs[:parts], refs[parts:]
    rows_out, normed_out, stack_out, encoded, sems = refs
    moves = stacked(parts, piece_refs, stack_out, sems, 0)
    start_all(moves)
    begin, end = bounds(lax.axis_index("dp"), slots_ref, starts_ref, lengths_ref)
    rows = W * parts
    for copy in range(copies):
        total = part_refs[copy][...].astype(F32)
        for step in range(1, parts):
            total += part_refs[step * copies + copy][...].astype(F32)
        at = pl.multiple_of((copy_index ^ copy) * rows, rows)
        encoded[pl.ds(at, rows), :] = total.astype(BF16)
    values = jnp.dot(frame_order(parts, copies), encoded[...], preferred_element_type=F32)
    mean = jnp.mean(values, axis=-1, keepdims=True)
    centered = values - mean
    variance = jnp.mean(centered * centered, axis=-1, keepdims=True)
    normed_out[...] = (centered * lax.rsqrt(variance + EPS_NORM)).astype(BF16)
    sample = samples(iota(windows * W, 1, 0), windows, group) + lax.axis_index("seq") * (W * SPAN)
    valid = (sample >= begin) & (sample < end)
    rows_out[...] = jnp.where(valid, values, 0.0).astype(BF16)
    wait_all(moves)


def attention_kernel(parts, windows, group, slots_ref, starts_ref, lengths_ref, *refs):
    _, copy_index = place(parts)
    plane = lax.axis_index("seq")
    copies = windows // parts
    normed_refs, refs = refs[:group], refs[group:]
    stack_refs, refs = refs[:copies], refs[copies:]
    weight_refs, refs = refs[:parts], refs[parts:]
    outs_refs, (stack_out, pieces, sems) = refs[:group], refs[group:]
    moves = stacked(parts, weight_refs, stack_out, sems, 0)
    start_all(moves)
    begin, end = bounds(lax.axis_index("dp"), slots_ref, starts_ref, lengths_ref)
    masks = []
    for step in range(group):
        sample = samples(iota(1, windows * W, 1), windows, group) + (plane ^ step) * (W * SPAN)
        masks.append(((sample >= begin) & (sample < end)).astype(F32))
    valid = jnp.concatenate(masks, axis=1) > 0.5
    local = normed_refs[0].shape[0]
    depth = pieces.shape[2]
    for step in range(group):
        for piece in range(windows):
            pieces[piece, step * local : (step + 1) * local, :] = normed_refs[step][
                :, piece * depth : (piece + 1) * depth
            ]
    mixed = 0.0
    for step in range(copies):
        slot = copy_index ^ step
        normed = jnp.concatenate([pieces[piece * copies + slot] for piece in range(parts)], axis=1)
        weights = stack_refs[step][...].reshape(parts * depth, stack_refs[step].shape[2])
        mixed += jnp.dot(normed, weights, preferred_element_type=F32)
    mixed = mixed.astype(BF16)
    width = mixed.shape[1] // 3
    scale = HEAD_DIM ** (-0.5)
    for head in range(width // HEAD_DIM):
        at = head * HEAD_DIM
        query = mixed[:, at : at + HEAD_DIM]
        key = mixed[:, width + at : width + at + HEAD_DIM]
        value = mixed[:, 2 * width + at : 2 * width + at + HEAD_DIM]
        scores = lax.dot_general(query, key, (((1,), (1,)), ((), ())), preferred_element_type=F32) * scale
        masked = jnp.where(valid, scores, MASKED)
        peak = jnp.max(masked, axis=1, keepdims=True)
        weight = jnp.where(valid, jnp.exp(masked - peak), 0.0)
        total = jnp.sum(weight, axis=1, keepdims=True)
        summed = jnp.dot(weight.astype(BF16), value, preferred_element_type=F32)
        context = (summed / total).astype(BF16)
        for step in range(group):
            outs_refs[step][:, at : at + HEAD_DIM] = context[step * local : (step + 1) * local]
    wait_all(moves)


def output_kernel(parts, windows, group, slots_ref, starts_ref, lengths_ref, *refs):
    context_refs, refs = refs[:group], refs[group:]
    stack_refs, refs = refs[: windows // parts], refs[windows // parts :]
    out_ref, context, pieces = refs
    _, copy_index = place(parts)
    copies = windows // parts
    plane = lax.axis_index("seq")
    begin, end = bounds(lax.axis_index("dp"), slots_ref, starts_ref, lengths_ref)
    head_width = context_refs[0].shape[1]
    for step in range(group):
        at = pl.multiple_of((plane ^ step) * head_width, LANES)
        context[:, pl.ds(at, head_width)] = context_refs[step][...]
    ordered = context[...]
    sample = samples(iota(windows * W, 1, 0), windows, group) + plane * (W * SPAN)
    valid = (sample >= begin) & (sample < end)
    for step in range(copies):
        slot = copy_index ^ step
        for piece in range(parts):
            pieces[piece * copies + slot] = jnp.dot(
                ordered, stack_refs[step][piece], preferred_element_type=F32
            )
    result = jnp.concatenate([pieces[d] for d in range(windows)], axis=1)
    out_ref[...] = jnp.where(valid, result, 0.0).astype(BF16)


def on_device(
    audio, starts, lengths, slots, conv1_weight, conv2_weight, proj_weight, qkv_weight, out_weight
):
    streams = audio.shape[0]
    windows = lax.axis_size("dp")
    group = lax.axis_size("seq")
    parts = math.gcd(windows, BANDS)
    copies = windows // parts
    assert streams == windows and all(count & (count - 1) == 0 for count in (parts, copies, group))
    share = BANDS // parts
    width = 4 * share + 4
    channels = conv1_weight.shape[1]
    features = proj_weight.shape[1]
    head_width = features // group
    local = windows * W
    rows = JS * streams
    n = parts * streams
    outs = 2 * share + 1
    scale = max(1, windows * group // 32)

    route = [(i, i + 1) for i in range(windows * group - 1)]
    rim = lax.ppermute(audio[:, audio.shape[1] - RIM :], ("dp", "seq"), route)

    def to_part(block, step):
        pairs = [(p * copies + c, (p ^ step) * copies + c) for p in range(parts) for c in range(copies)]
        return lax.ppermute(block, "dp", pairs)

    def to_copy(block, step):
        pairs = [(p * copies + c, p * copies + (c ^ step)) for p in range(parts) for c in range(copies)]
        return lax.ppermute(block, "dp", pairs)

    def to_window(block, step):
        return lax.ppermute(block, "dp", [(i, i ^ step) for i in range(windows)])

    def to_plane(block, step):
        return lax.ppermute(block, "seq", [(i, i ^ step) for i in range(group)])

    proj_all = [proj_weight] + [to_copy(proj_weight, step) for step in range(1, copies)]

    table = jnp.asarray(spectrum_table(N_FFT))
    mix_piece = jax.ShapeDtypeStruct((qkv_weight.shape[0], 3 * head_width), BF16)
    *mel_all, mix = pl.pallas_call(
        functools.partial(mel_kernel, parts, group),
        out_shape=tuple([jax.ShapeDtypeStruct((rows, LANES), BF16)] * parts + [mix_piece]),
        in_specs=[smem(), vmem()] + [anywhere()] * 3,
        out_specs=tuple([vmem()] * (parts + 1)),
        scratch_shapes=[
            pltpu.VMEM((streams, RIM + audio.shape[1]), F32),
            pltpu.VMEM(table.shape, F32),
            pltpu.VMEM((parts, rows, LANES), BF16),
            pltpu.SemaphoreType.DMA((5,)),
        ],
        compiler_params=params(60),
        cost_estimate=cost(2e9, 2e6),
        name="log_mel",
    )(slots, rim, audio, table, qkv_weight)
    mel_all = [mel_all[0]] + [to_part(mel_all[step], step) for step in range(1, parts)]
    mix_all = [mix] + [to_part(mix, step) for step in range(1, parts)]

    block = jax.ShapeDtypeStruct((local, features), BF16)
    partials = pl.pallas_call(
        functools.partial(conv_kernel, parts, width),
        out_shape=tuple([jax.ShapeDtypeStruct((W * parts, features), BF16)] * windows),
        in_specs=[vmem()] + [anywhere()] + [vmem()] * parts + [anywhere()] * copies,
        out_specs=tuple([vmem()] * windows),
        scratch_shapes=[
            pltpu.VMEM((parts, rows, LANES), F32),
            pltpu.VMEM((LANES, outs * channels), BF16),
            pltpu.VMEM((JS * n, outs * channels), BF16),
            pltpu.VMEM((W * n, outs * channels), BF16),
            pltpu.VMEM((W * n, share * channels), BF16),
            pltpu.VMEM(conv2_weight.shape, BF16),
            pltpu.VMEM((copies,) + proj_weight.shape, BF16),
            pltpu.VMEM((W * n, features), F32),
            pltpu.SemaphoreType.DMA((1 + copies,)),
        ],
        compiler_params=params(min(40 + 4 * scale, 56)),
        cost_estimate=cost(2e9, 4e6),
        name="conv",
    )(conv1_weight, conv2_weight, *mel_all, *proj_all)
    partials = [partials[0]] + [to_window(partials[step], step) for step in range(1, windows)]

    regrouped, normed, stack = pl.pallas_call(
        functools.partial(norm_kernel, parts, group),
        out_shape=(block, block, jax.ShapeDtypeStruct((parts,) + mix_piece.shape, BF16)),
        in_specs=[smem()] * 3 + [vmem()] * windows + [anywhere()] * parts,
        out_specs=(vmem(), vmem(), vmem()),
        scratch_shapes=[pltpu.VMEM((local, features), BF16), pltpu.SemaphoreType.DMA((parts,))],
        compiler_params=params(min(12 * scale, 32)),
        cost_estimate=cost(1e8, 1e6),
        name="layer_norm",
    )(slots, starts, lengths, *partials, *mix_all)
    mix_stacks = [stack] + [to_copy(stack, step) for step in range(1, copies)]
    normed, out_here = lax.optimization_barrier((normed, out_weight))
    normed = [normed] + [to_plane(normed, step) for step in range(1, group)]
    out_all = [out_here] + [to_part(out_here, step) for step in range(1, parts)]

    *context, stack = pl.pallas_call(
        functools.partial(attention_kernel, parts, windows, group),
        out_shape=tuple(
            [jax.ShapeDtypeStruct((local, head_width), BF16)] * group
            + [jax.ShapeDtypeStruct((parts,) + out_weight.shape, BF16)]
        ),
        in_specs=[smem()] * 3 + [vmem()] * (group + copies) + [anywhere()] * parts,
        out_specs=tuple([vmem()] * (group + 1)),
        scratch_shapes=[
            pltpu.VMEM((windows, group * local, qkv_weight.shape[0]), BF16),
            pltpu.SemaphoreType.DMA((parts,)),
        ],
        compiler_params=params(min(16 * scale, 48)),
        cost_estimate=cost(1e9, 2e6),
        name="attention",
    )(slots, starts, lengths, *normed, *mix_stacks, *out_all)
    context = [context[0]] + [to_plane(context[step], step) for step in range(1, group)]
    out_stacks = [stack] + [to_copy(stack, step) for step in range(1, copies)]

    attended = pl.pallas_call(
        functools.partial(output_kernel, parts, windows, group),
        out_shape=block,
        in_specs=[smem()] * 3 + [vmem()] * (group + copies),
        out_specs=vmem(),
        scratch_shapes=[
            pltpu.VMEM((local, features), BF16),
            pltpu.VMEM((windows, local, out_weight.shape[1]), F32),
        ],
        compiler_params=params(min(12 * scale, 32)),
        cost_estimate=cost(1e8, 3e6),
        name="output",
    )(slots, starts, lengths, *context, *out_stacks)
    shape = (1, windows, 1, W, features)
    return (regrouped.reshape(shape), attended.reshape(shape))


def solution(mesh):
    in_specs = (
        P(None, ("dp", "seq")),
        P(),
        P(),
        P(),
        P(),
        P(),
        P("dp", None),
        P("dp", None),
        P(None, "dp"),
    )
    out_specs = (P("dp", None, "seq", None, None), P("dp", None, "seq", None, None))
    return jax.shard_map(
        on_device, mesh=mesh, in_specs=in_specs, out_specs=out_specs, check_vma=False
    )
```

```python
import functools
import math

import jax
import jax.numpy as jnp
import numpy as np
from jax import lax
from jax.experimental import pallas as pl
from jax.experimental.pallas import tpu as pltpu
from jax.sharding import PartitionSpec as P

HEADS = 8
HEAD_DIM = 128
MELS = 80
BANDS = MELS // 4
N_FFT = 512
HOP = 160
W = 8
RIM = 1024
SPAN = 4 * HOP
JS = W + 1
LANES = 128
SAMPLE_RATE = 16000.0
EPS_LOG = 1e-06
EPS_NORM = 1e-05
MASKED = -1e30
F32 = jnp.float32
BF16 = jnp.bfloat16
MIB = 1 << 20


def mel_table(size, bands):
    count = size // 2 + 1
    highest = 2595.0 * math.log10(1.0 + SAMPLE_RATE / 1400.0)
    points = np.linspace(0.0, highest, bands + 2)
    edges = 700.0 * (10.0 ** (points / 2595.0) - 1.0)
    edges[0] = 0.0
    edges[-1] = SAMPLE_RATE / 2.0
    frequency = np.arange(count) * (SAMPLE_RATE / size)
    lower = edges[:-2][None, :]
    middle = edges[1:-1][None, :]
    upper = edges[2:][None, :]
    rising = (frequency[:, None] - lower) / (middle - lower)
    falling = (upper - frequency[:, None]) / (upper - middle)
    return np.maximum(0.0, np.minimum(rising, falling)).astype(np.float32)


def spectrum_table(size):
    sample = np.arange(size)
    phase = sample[:, None] * np.arange(size // 2)[None, :] % size
    angle = phase * (2.0 * math.pi / size)
    window = 0.5 - 0.5 * np.cos(sample * (2.0 * math.pi / size))
    both = np.concatenate([np.cos(angle), np.sin(angle)], axis=1) * window[:, None]
    filters = np.zeros((size, LANES))
    filters[: size // 2, :MELS] = mel_table(size, MELS)[: size // 2]
    return np.concatenate([both, filters], axis=1).astype(np.float32)


def vmem():
    return pl.BlockSpec(memory_space=pltpu.VMEM)


def smem():
    return pl.BlockSpec(memory_space=pltpu.SMEM)


def anywhere():
    return pl.BlockSpec(memory_space=pl.ANY)


def params(mib):
    return pltpu.CompilerParams(vmem_limit_bytes=mib * MIB)


def cost(flops, moved):
    return pl.CostEstimate(flops=int(flops), bytes_accessed=int(moved), transcendentals=0)


def place(parts):
    mine = lax.axis_index("dp")
    copies = lax.axis_size("dp") // parts
    return mine // copies, mine % copies


def start_all(copies):
    for copy in copies:
        copy.start()


def wait_all(copies):
    for copy in copies:
        copy.wait()


def iota(rows, columns, axis):
    return lax.broadcasted_iota(jnp.int32, (rows, columns), axis)


def quotient(index, step, count):
    result = jnp.zeros_like(index)
    for i in range(1, count):
        result += (index >= i * step).astype(jnp.int32)
    return result


def one_hot(target, count):
    return (iota(target.shape[0], count, 1) == target).astype(F32).astype(BF16)


def frame_order(parts, copies):
    count = parts * copies * W
    row = iota(count, 1, 0)
    k = quotient(row, W, parts * copies)
    p = quotient(k, copies, parts)
    return one_hot((k - p * copies) * W * parts + (row - k * W) * parts + p, count)


def row_order(parts, streams):
    count = W * parts * streams
    row = iota(count, 1, 0)
    r = quotient(row, W * parts, streams)
    rest = row - r * W * parts
    return one_hot(rest * streams + r, count)


def samples(index, windows, group):
    return (index + quotient(index, W, windows) * (group - 1) * W) * SPAN


def mix_columns(group, qkv_ref, mix_out, sems):
    features = qkv_ref.shape[1] // 3
    width = features // group
    first = pl.multiple_of(lax.axis_index("seq") * width, LANES)
    return [
        pltpu.make_async_copy(
            qkv_ref.at[:, pl.ds(kind * features + first, width)],
            mix_out.at[:, pl.ds(kind * width, width)],
            sems.at[kind],
        )
        for kind in range(3)
    ]


def banded_weights(width, conv1_ref, banded_out):
    taps, channels = conv1_ref.shape
    row = lax.broadcasted_iota(jnp.int32, (LANES, taps), 0)
    tap = lax.broadcasted_iota(jnp.int32, (LANES, taps), 1)
    line = (tap >= 3).astype(jnp.int32) + (tap >= 6).astype(jnp.int32)
    target = line * (width - 3) + tap + 1
    weight = conv1_ref[...]
    for g in range(banded_out.shape[1] // channels):
        select = (row == target + 2 * g).astype(F32).astype(BF16)
        banded_out[:, g * channels : (g + 1) * channels] = jnp.dot(
            select, weight, preferred_element_type=F32
        ).astype(BF16)


def mel_kernel(parts, group, slots_ref, rim_ref, audio_ref, table_ref, qkv_ref, *refs):
    outs_refs, (mix_out, ext, table, blocks, sems) = refs[:parts], refs[parts:]
    load_audio = pltpu.make_async_copy(audio_ref, ext.at[:, pl.ds(RIM, audio_ref.shape[1])], sems.at[3])
    load_table = pltpu.make_async_copy(table_ref, table, sems.at[4])
    load_audio.start()
    load_table.start()
    pieces = mix_columns(group, qkv_ref, mix_out, sems)
    start_all(pieces)
    streams = audio_ref.shape[0]
    rows = JS * streams
    ext[:, :RIM] = rim_ref[...]
    column = iota(1, rows, 1)
    early = quotient(column, streams, JS)
    target = jnp.zeros((1, rows), jnp.int32)
    for u in range(streams):
        target = jnp.where(column - early * streams == u, early * streams + slots_ref[u], target)
    routing = (target == iota(rows, rows, 0)).astype(F32).astype(BF16)
    load_audio.wait()
    phases = []
    for phase in range(4):
        start = HOP * phase + 32
        base, shift = start // LANES * LANES, start % LANES
        length = N_FFT + (LANES if shift else 0)
        block = jnp.concatenate(
            [ext[:, SPAN * j + base : SPAN * j + base + length] for j in range(JS)], axis=0
        )
        if shift:
            block = pltpu.roll(block, length - shift, 1)[:, :N_FFT]
        phases.append(block)
    frames = jnp.concatenate(phases, axis=0)
    load_table.wait()
    spectrum = jnp.dot(
        frames, table[:, :N_FFT], precision=lax.Precision.HIGHEST, preferred_element_type=F32
    )
    half = N_FFT // 2
    real, imag = spectrum[:, :half], spectrum[:, half:]
    power = real * real + imag * imag
    mel_power = jnp.dot(
        power, table[:half, N_FFT:], precision=lax.Precision.HIGHEST, preferred_element_type=F32
    )
    log_mel = jnp.log(mel_power + EPS_LOG)
    share = BANDS // parts
    width = 4 * share + 4
    lane = iota(rows, LANES, 1)
    by_phase = [log_mel[phase * rows : (phase + 1) * rows] for phase in range(4)]

    def next_four(frames):
        return jnp.concatenate([frames[streams:], jnp.zeros((streams, LANES), F32)], axis=0)

    taps = [by_phase[1], by_phase[2], by_phase[3], next_four(by_phase[0]), next_four(by_phase[1])]
    for part in range(parts):
        first = 4 * share * part - 4
        block = jnp.zeros((rows, LANES), F32)
        for delta, frames in enumerate(taps):
            band = lane - width * delta + first
            here = (lane >= width * delta) & (lane < width * (delta + 1)) & (band >= 0) & (band < MELS)
            shift = (width * delta - first) % LANES
            block = jnp.where(here, pltpu.roll(frames, shift, 1) if shift else frames, block)
        blocks[part] = jnp.dot(routing, block.astype(BF16), preferred_element_type=F32).astype(BF16)
    mine, _ = place(parts)
    for step in range(parts):
        outs_refs[step][...] = blocks[mine ^ step]
    wait_all(pieces)


def stacked(parts, pieces, stack_out, sems, base):
    part, _ = place(parts)
    return [
        pltpu.make_async_copy(pieces[step], stack_out.at[part ^ step], sems.at[base + step])
        for step in range(parts)
    ]


def conv_kernel(parts, width, conv1_ref, conv2_ref, *refs):
    part, copy_index = place(parts)
    mine = lax.axis_index("dp")
    windows = lax.axis_size("dp")
    copies = windows // parts
    mel_refs, refs = refs[:parts], refs[parts:]
    proj_refs, refs = refs[:copies], refs[copies:]
    weight_refs, refs = refs[:parts], refs[parts:]
    outs_refs, refs = refs[:windows], refs[windows:]
    stack_out, mel, banded_ref, even, odd, second, conv2, proj, partial, sems = refs
    load_conv2 = pltpu.make_async_copy(conv2_ref, conv2, sems.at[0])
    load_conv2.start()
    loads = []
    for step in range(copies):
        slot = copy_index ^ step
        loads.append(pltpu.make_async_copy(proj_refs[step], proj.at[slot], sems.at[1 + step]))
    loads += stacked(parts, weight_refs, stack_out, sems, 1 + copies)
    start_all(loads)
    banded_weights(width, conv1_ref, banded_ref)
    streams = mel_refs[0].shape[0] // JS
    n = parts * streams
    for step in range(parts):
        mel[part ^ step] = mel_refs[step][...].astype(F32)
    evens = jnp.concatenate(
        [mel[p, j * streams : (j + 1) * streams, :] for j in range(JS) for p in range(parts)], axis=0
    )
    odds = pltpu.roll(evens[: W * n], LANES - 2 * width, 1).astype(BF16)
    evens = evens.astype(BF16)
    channels = conv2.shape[1]
    outs = banded_ref.shape[1] // channels
    for g in range(outs):
        lanes = slice(g * channels, (g + 1) * channels)
        weight = banded_ref[:, lanes]
        even[:, lanes] = jax.nn.relu(jnp.dot(evens, weight, preferred_element_type=F32)).astype(BF16)
        odd[:, lanes] = jax.nn.relu(jnp.dot(odds, weight, preferred_element_type=F32)).astype(BF16)

    load_conv2.wait()
    order = row_order(parts, streams)
    for h in range((outs - 1) // 2):
        lanes = slice(2 * h * channels, (2 * h + 3) * channels)
        depth = 3 * channels
        total = jnp.dot(even[: W * n, lanes], conv2[:depth], preferred_element_type=F32)
        total += jnp.dot(odd[:, lanes], conv2[depth : 2 * depth], preferred_element_type=F32)
        total += jnp.dot(even[n:, lanes], conv2[2 * depth :], preferred_element_type=F32)
        second[:, h * channels : (h + 1) * channels] = jnp.dot(
            order, jax.nn.relu(total).astype(BF16), preferred_element_type=F32
        ).astype(BF16)
    wait_all(loads)
    weights = proj[...].reshape(second.shape[1], proj.shape[2])
    partial[...] = jnp.dot(second[...], weights, preferred_element_type=F32)
    rows = W * parts
    for step in range(windows):
        at = pl.multiple_of((mine ^ step) * rows, rows)
        outs_refs[step][...] = partial[pl.ds(at, rows), :].astype(BF16)


def bounds(row, slots_ref, starts_ref, lengths_ref):
    begin, span = jnp.int32(0), jnp.int32(0)
    for u in range(slots_ref.shape[0]):
        chosen = slots_ref[u] == row
        begin = begin + jnp.where(chosen, starts_ref[u], 0)
        span = span + jnp.where(chosen, lengths_ref[u], 0)
    return begin, begin + span


def norm_kernel(parts, group, slots_ref, starts_ref, lengths_ref, *refs):
    _, copy_index = place(parts)
    windows = lax.axis_size("dp")
    copies = windows // parts
    part_refs, refs = refs[:windows], refs[windows:]
    piece_refs, refs = refs[:parts], refs[parts:]
    rows_out, normed_out, stack_out, encoded, sems = refs
    moves = stacked(parts, piece_refs, stack_out, sems, 0)
    start_all(moves)
    begin, end = bounds(lax.axis_index("dp"), slots_ref, starts_ref, lengths_ref)
    rows = W * parts
    for copy in range(copies):
        total = part_refs[copy][...].astype(F32)
        for step in range(1, parts):
            total += part_refs[step * copies + copy][...].astype(F32)
        at = pl.multiple_of((copy_index ^ copy) * rows, rows)
        encoded[pl.ds(at, rows), :] = total.astype(BF16)
    values = jnp.dot(frame_order(parts, copies), encoded[...], preferred_element_type=F32)
    mean = jnp.mean(values, axis=-1, keepdims=True)
    centered = values - mean
    variance = jnp.mean(centered * centered, axis=-1, keepdims=True)
    normed_out[...] = (centered * lax.rsqrt(variance + EPS_NORM)).astype(BF16)
    sample = samples(iota(windows * W, 1, 0), windows, group) + lax.axis_index("seq") * (W * SPAN)
    valid = (sample >= begin) & (sample < end)
    rows_out[...] = jnp.where(valid, values, 0.0).astype(BF16)
    wait_all(moves)


def attention_kernel(parts, windows, group, slots_ref, starts_ref, lengths_ref, *refs):
    _, copy_index = place(parts)
    plane = lax.axis_index("seq")
    copies = windows // parts
    normed_refs, refs = refs[:group], refs[group:]
    stack_refs, refs = refs[:copies], refs[copies:]
    outs_refs, (pieces,) = refs[:group], refs[group:]
    begin, end = bounds(lax.axis_index("dp"), slots_ref, starts_ref, lengths_ref)
    masks = []
    for step in range(group):
        sample = samples(iota(1, windows * W, 1), windows, group) + (plane ^ step) * (W * SPAN)
        masks.append(((sample >= begin) & (sample < end)).astype(F32))
    valid = jnp.concatenate(masks, axis=1) > 0.5
    local = normed_refs[0].shape[0]
    depth = pieces.shape[2]
    for step in range(group):
        for piece in range(windows):
            pieces[piece, step * local : (step + 1) * local, :] = normed_refs[step][
                :, piece * depth : (piece + 1) * depth
            ]
    mixed = 0.0
    for step in range(copies):
        slot = copy_index ^ step
        normed = jnp.concatenate([pieces[piece * copies + slot] for piece in range(parts)], axis=1)
        weights = stack_refs[step][...].reshape(parts * depth, stack_refs[step].shape[2])
        mixed += jnp.dot(normed, weights, preferred_element_type=F32)
    mixed = mixed.astype(BF16)
    width = mixed.shape[1] // 3
    scale = HEAD_DIM ** (-0.5)
    for head in range(width // HEAD_DIM):
        at = head * HEAD_DIM
        query = mixed[:, at : at + HEAD_DIM]
        key = mixed[:, width + at : width + at + HEAD_DIM]
        value = mixed[:, 2 * width + at : 2 * width + at + HEAD_DIM]
        scores = lax.dot_general(query, key, (((1,), (1,)), ((), ())), preferred_element_type=F32) * scale
        masked = jnp.where(valid, scores, MASKED)
        peak = jnp.max(masked, axis=1, keepdims=True)
        weight = jnp.where(valid, jnp.exp(masked - peak), 0.0)
        total = jnp.sum(weight, axis=1, keepdims=True)
        summed = jnp.dot(weight.astype(BF16), value, preferred_element_type=F32)
        context = (summed / total).astype(BF16)
        for step in range(group):
            outs_refs[step][:, at : at + HEAD_DIM] = context[step * local : (step + 1) * local]


def output_kernel(parts, windows, group, slots_ref, starts_ref, lengths_ref, *refs):
    context_refs, refs = refs[:group], refs[group:]
    stack_refs, refs = refs[: windows // parts], refs[windows // parts :]
    out_ref, context, pieces = refs
    _, copy_index = place(parts)
    copies = windows // parts
    plane = lax.axis_index("seq")
    begin, end = bounds(lax.axis_index("dp"), slots_ref, starts_ref, lengths_ref)
    head_width = context_refs[0].shape[1]
    for step in range(group):
        at = pl.multiple_of((plane ^ step) * head_width, LANES)
        context[:, pl.ds(at, head_width)] = context_refs[step][...]
    ordered = context[...]
    sample = samples(iota(windows * W, 1, 0), windows, group) + plane * (W * SPAN)
    valid = (sample >= begin) & (sample < end)
    for step in range(copies):
        slot = copy_index ^ step
        for piece in range(parts):
            pieces[piece * copies + slot] = jnp.dot(
                ordered, stack_refs[step][piece], preferred_element_type=F32
            )
    result = jnp.concatenate([pieces[d] for d in range(windows)], axis=1)
    out_ref[...] = jnp.where(valid, result, 0.0).astype(BF16)


def on_device(
    audio, starts, lengths, slots, conv1_weight, conv2_weight, proj_weight, qkv_weight, out_weight
):
    streams = audio.shape[0]
    windows = lax.axis_size("dp")
    group = lax.axis_size("seq")
    parts = math.gcd(windows, BANDS)
    copies = windows // parts
    assert streams == windows and all(count & (count - 1) == 0 for count in (parts, copies, group))
    share = BANDS // parts
    width = 4 * share + 4
    channels = conv1_weight.shape[1]
    features = proj_weight.shape[1]
    head_width = features // group
    local = windows * W
    rows = JS * streams
    n = parts * streams
    outs = 2 * share + 1
    scale = max(1, windows * group // 32)

    route = [(i, i + 1) for i in range(windows * group - 1)]
    rim = lax.ppermute(audio[:, audio.shape[1] - RIM :], ("dp", "seq"), route)

    def to_part(block, step):
        pairs = [(p * copies + c, (p ^ step) * copies + c) for p in range(parts) for c in range(copies)]
        return lax.ppermute(block, "dp", pairs)

    def to_copy(block, step):
        pairs = [(p * copies + c, p * copies + (c ^ step)) for p in range(parts) for c in range(copies)]
        return lax.ppermute(block, "dp", pairs)

    def to_window(block, step):
        return lax.ppermute(block, "dp", [(i, i ^ step) for i in range(windows)])

    def to_plane(block, step):
        return lax.ppermute(block, "seq", [(i, i ^ step) for i in range(group)])

    proj_all = [proj_weight] + [to_copy(proj_weight, step) for step in range(1, copies)]

    table = jnp.asarray(spectrum_table(N_FFT))
    mix_piece = jax.ShapeDtypeStruct((qkv_weight.shape[0], 3 * head_width), BF16)
    *mel_all, mix = pl.pallas_call(
        functools.partial(mel_kernel, parts, group),
        out_shape=tuple([jax.ShapeDtypeStruct((rows, LANES), BF16)] * parts + [mix_piece]),
        in_specs=[smem(), vmem()] + [anywhere()] * 3,
        out_specs=tuple([vmem()] * (parts + 1)),
        scratch_shapes=[
            pltpu.VMEM((streams, RIM + audio.shape[1]), F32),
            pltpu.VMEM(table.shape, F32),
            pltpu.VMEM((parts, rows, LANES), BF16),
            pltpu.SemaphoreType.DMA((5,)),
        ],
        compiler_params=params(60),
        cost_estimate=cost(2e9, 2e6),
        name="log_mel",
    )(slots, rim, audio, table, qkv_weight)
    mel_all = [mel_all[0]] + [to_part(mel_all[step], step) for step in range(1, parts)]
    mix_all = [mix] + [to_part(mix, step) for step in range(1, parts)]

    block = jax.ShapeDtypeStruct((local, features), BF16)
    out_all = [out_weight] + [to_part(out_weight, step) for step in range(1, parts)]
    *partials, stack = pl.pallas_call(
        functools.partial(conv_kernel, parts, width),
        out_shape=tuple(
            [jax.ShapeDtypeStruct((W * parts, features), BF16)] * windows
            + [jax.ShapeDtypeStruct((parts,) + out_weight.shape, BF16)]
        ),
        in_specs=[vmem()] + [anywhere()] + [vmem()] * parts + [anywhere()] * (copies + parts),
        out_specs=tuple([vmem()] * (windows + 1)),
        scratch_shapes=[
            pltpu.VMEM((parts, rows, LANES), F32),
            pltpu.VMEM((LANES, outs * channels), BF16),
            pltpu.VMEM((JS * n, outs * channels), BF16),
            pltpu.VMEM((W * n, outs * channels), BF16),
            pltpu.VMEM((W * n, share * channels), BF16),
            pltpu.VMEM(conv2_weight.shape, BF16),
            pltpu.VMEM((copies,) + proj_weight.shape, BF16),
            pltpu.VMEM((W * n, features), F32),
            pltpu.SemaphoreType.DMA((1 + copies + parts,)),
        ],
        compiler_params=params(min(40 + 4 * scale, 56)),
        cost_estimate=cost(2e9, 4e6),
        name="conv",
    )(conv1_weight, conv2_weight, *mel_all, *proj_all, *out_all)
    out_stacks = [stack] + [to_copy(stack, step) for step in range(1, copies)]
    partials = [partials[0]] + [to_window(partials[step], step) for step in range(1, windows)]

    regrouped, normed, stack = pl.pallas_call(
        functools.partial(norm_kernel, parts, group),
        out_shape=(block, block, jax.ShapeDtypeStruct((parts,) + mix_piece.shape, BF16)),
        in_specs=[smem()] * 3 + [vmem()] * windows + [anywhere()] * parts,
        out_specs=(vmem(), vmem(), vmem()),
        scratch_shapes=[pltpu.VMEM((local, features), BF16), pltpu.SemaphoreType.DMA((parts,))],
        compiler_params=params(min(12 * scale, 32)),
        cost_estimate=cost(1e8, 1e6),
        name="layer_norm",
    )(slots, starts, lengths, *partials, *mix_all)
    mix_stacks = [stack] + [to_copy(stack, step) for step in range(1, copies)]
    normed = [normed] + [to_plane(normed, step) for step in range(1, group)]

    context = pl.pallas_call(
        functools.partial(attention_kernel, parts, windows, group),
        out_shape=tuple([jax.ShapeDtypeStruct((local, head_width), BF16)] * group),
        in_specs=[smem()] * 3 + [vmem()] * (group + copies),
        out_specs=tuple([vmem()] * group),
        scratch_shapes=[pltpu.VMEM((windows, group * local, qkv_weight.shape[0]), BF16)],
        compiler_params=params(min(16 * scale, 48)),
        cost_estimate=cost(1e9, 2e6),
        name="attention",
    )(slots, starts, lengths, *normed, *mix_stacks)
    context = [context[0]] + [to_plane(context[step], step) for step in range(1, group)]

    attended = pl.pallas_call(
        functools.partial(output_kernel, parts, windows, group),
        out_shape=block,
        in_specs=[smem()] * 3 + [vmem()] * (group + copies),
        out_specs=vmem(),
        scratch_shapes=[
            pltpu.VMEM((local, features), BF16),
            pltpu.VMEM((windows, local, out_weight.shape[1]), F32),
        ],
        compiler_params=params(min(12 * scale, 32)),
        cost_estimate=cost(1e8, 3e6),
        name="output",
    )(slots, starts, lengths, *context, *out_stacks)
    shape = (1, windows, 1, W, features)
    return (regrouped.reshape(shape), attended.reshape(shape))


def solution(mesh):
    in_specs = (
        P(None, ("dp", "seq")),
        P(),
        P(),
        P(),
        P(),
        P(),
        P("dp", None),
        P("dp", None),
        P(None, "dp"),
    )
    out_specs = (P("dp", None, "seq", None, None), P("dp", None, "seq", None, None))
    return jax.shard_map(
        on_device, mesh=mesh, in_specs=in_specs, out_specs=out_specs, check_vma=False
    )
```

```python
import functools
import math

import jax
import jax.numpy as jnp
import numpy as np
from jax import lax
from jax.experimental import pallas as pl
from jax.experimental.pallas import tpu as pltpu
from jax.sharding import PartitionSpec as P

HEADS = 8
HEAD_DIM = 128
MELS = 80
BANDS = MELS // 4
N_FFT = 512
HOP = 160
W = 8
RIM = 1024
SPAN = 4 * HOP
JS = W + 1
LANES = 128
SAMPLE_RATE = 16000.0
EPS_LOG = 1e-06
EPS_NORM = 1e-05
MASKED = -1e30
F32 = jnp.float32
BF16 = jnp.bfloat16
MIB = 1 << 20


def mel_table(size, bands):
    count = size // 2 + 1
    highest = 2595.0 * math.log10(1.0 + SAMPLE_RATE / 1400.0)
    points = np.linspace(0.0, highest, bands + 2)
    edges = 700.0 * (10.0 ** (points / 2595.0) - 1.0)
    edges[0] = 0.0
    edges[-1] = SAMPLE_RATE / 2.0
    frequency = np.arange(count) * (SAMPLE_RATE / size)
    lower = edges[:-2][None, :]
    middle = edges[1:-1][None, :]
    upper = edges[2:][None, :]
    rising = (frequency[:, None] - lower) / (middle - lower)
    falling = (upper - frequency[:, None]) / (upper - middle)
    return np.maximum(0.0, np.minimum(rising, falling)).astype(np.float32)


def spectrum_table(size):
    sample = np.arange(size)
    phase = sample[:, None] * np.arange(size // 2)[None, :] % size
    angle = phase * (2.0 * math.pi / size)
    window = 0.5 - 0.5 * np.cos(sample * (2.0 * math.pi / size))
    both = np.concatenate([np.cos(angle), np.sin(angle)], axis=1) * window[:, None]
    filters = np.zeros((size, LANES))
    filters[: size // 2, :MELS] = mel_table(size, MELS)[: size // 2]
    return np.concatenate([both, filters], axis=1).astype(np.float32)


def vmem():
    return pl.BlockSpec(memory_space=pltpu.VMEM)


def smem():
    return pl.BlockSpec(memory_space=pltpu.SMEM)


def anywhere():
    return pl.BlockSpec(memory_space=pl.ANY)


def params(mib):
    return pltpu.CompilerParams(vmem_limit_bytes=mib * MIB)


def cost(flops, moved):
    return pl.CostEstimate(flops=int(flops), bytes_accessed=int(moved), transcendentals=0)


def place(parts):
    mine = lax.axis_index("dp")
    copies = lax.axis_size("dp") // parts
    return mine // copies, mine % copies


def start_all(copies):
    for copy in copies:
        copy.start()


def wait_all(copies):
    for copy in copies:
        copy.wait()


def iota(rows, columns, axis):
    return lax.broadcasted_iota(jnp.int32, (rows, columns), axis)


def quotient(index, step, count):
    result = jnp.zeros_like(index)
    for i in range(1, count):
        result += (index >= i * step).astype(jnp.int32)
    return result


def one_hot(target, count):
    return (iota(target.shape[0], count, 1) == target).astype(F32).astype(BF16)


def frame_order(parts, copies):
    count = parts * copies * W
    row = iota(count, 1, 0)
    k = quotient(row, W, parts * copies)
    p = quotient(k, copies, parts)
    return one_hot((k - p * copies) * W * parts + (row - k * W) * parts + p, count)


def samples(index, windows, group):
    return (index + quotient(index, W, windows) * (group - 1) * W) * SPAN


def mix_columns(group, qkv_ref, mix_out, sems):
    features = qkv_ref.shape[1] // 3
    width = features // group
    first = pl.multiple_of(lax.axis_index("seq") * width, LANES)
    return [
        pltpu.make_async_copy(
            qkv_ref.at[:, pl.ds(kind * features + first, width)],
            mix_out.at[:, pl.ds(kind * width, width)],
            sems.at[kind],
        )
        for kind in range(3)
    ]


def banded_weights(width, conv1_ref, banded_out):
    taps, channels = conv1_ref.shape
    row = lax.broadcasted_iota(jnp.int32, (LANES, taps), 0)
    tap = lax.broadcasted_iota(jnp.int32, (LANES, taps), 1)
    line = (tap >= 3).astype(jnp.int32) + (tap >= 6).astype(jnp.int32)
    target = line * (width - 3) + tap + 1
    weight = conv1_ref[...]
    for g in range(banded_out.shape[1] // channels):
        select = (row == target + 2 * g).astype(F32).astype(BF16)
        banded_out[:, g * channels : (g + 1) * channels] = jnp.dot(
            select, weight, preferred_element_type=F32
        ).astype(BF16)


def mel_kernel(parts, group, slots_ref, rim_ref, audio_ref, table_ref, qkv_ref, *refs):
    outs_refs, (mix_out, ext, table, blocks, sems) = refs[:parts], refs[parts:]
    load_audio = pltpu.make_async_copy(audio_ref, ext.at[:, pl.ds(RIM, audio_ref.shape[1])], sems.at[3])
    load_table = pltpu.make_async_copy(table_ref, table, sems.at[4])
    load_audio.start()
    load_table.start()
    pieces = mix_columns(group, qkv_ref, mix_out, sems)
    start_all(pieces)
    streams = audio_ref.shape[0]
    rows = JS * streams
    ext[:, :RIM] = rim_ref[...]
    column = iota(1, rows, 1)
    early = quotient(column, streams, JS)
    target = jnp.zeros((1, rows), jnp.int32)
    for u in range(streams):
        target = jnp.where(column - early * streams == u, early * streams + slots_ref[u], target)
    routing = (target == iota(rows, rows, 0)).astype(F32).astype(BF16)
    load_audio.wait()
    phases = []
    for phase in range(4):
        start = HOP * phase + 32
        base, shift = start // LANES * LANES, start % LANES
        length = N_FFT + (LANES if shift else 0)
        block = jnp.concatenate(
            [ext[:, SPAN * j + base : SPAN * j + base + length] for j in range(JS)], axis=0
        )
        if shift:
            block = pltpu.roll(block, length - shift, 1)[:, :N_FFT]
        phases.append(block)
    frames = jnp.concatenate(phases, axis=0)
    load_table.wait()
    spectrum = jnp.dot(
        frames, table[:, :N_FFT], precision=lax.Precision.HIGHEST, preferred_element_type=F32
    )
    half = N_FFT // 2
    real, imag = spectrum[:, :half], spectrum[:, half:]
    power = real * real + imag * imag
    mel_power = jnp.dot(
        power, table[:half, N_FFT:], precision=lax.Precision.HIGHEST, preferred_element_type=F32
    )
    log_mel = jnp.log(mel_power + EPS_LOG)
    share = BANDS // parts
    width = 4 * share + 4
    lane = iota(rows, LANES, 1)
    by_phase = [log_mel[phase * rows : (phase + 1) * rows] for phase in range(4)]

    def next_four(frames):
        return jnp.concatenate([frames[streams:], jnp.zeros((streams, LANES), F32)], axis=0)

    taps = [by_phase[1], by_phase[2], by_phase[3], next_four(by_phase[0]), next_four(by_phase[1])]
    for part in range(parts):
        first = 4 * share * part - 4
        block = jnp.zeros((rows, LANES), F32)
        for delta, frames in enumerate(taps):
            band = lane - width * delta + first
            here = (lane >= width * delta) & (lane < width * (delta + 1)) & (band >= 0) & (band < MELS)
            shift = (width * delta - first) % LANES
            block = jnp.where(here, pltpu.roll(frames, shift, 1) if shift else frames, block)
        blocks[part] = jnp.dot(routing, block.astype(BF16), preferred_element_type=F32).astype(BF16)
    mine, _ = place(parts)
    for step in range(parts):
        outs_refs[step][...] = blocks[mine ^ step]
    wait_all(pieces)


def stacked(parts, pieces, stack_out, sems, base):
    part, _ = place(parts)
    return [
        pltpu.make_async_copy(pieces[step], stack_out.at[part ^ step], sems.at[base + step])
        for step in range(parts)
    ]


def conv_kernel(parts, width, conv1_ref, conv2_ref, *refs):
    part, copy_index = place(parts)
    mine = lax.axis_index("dp")
    windows = lax.axis_size("dp")
    copies = windows // parts
    mel_refs, refs = refs[:parts], refs[parts:]
    proj_refs, refs = refs[:copies], refs[copies:]
    outs_refs, refs = refs[:windows], refs[windows:]
    mel, banded_ref, even, odd, second, conv2, proj, partial, sems = refs
    load_conv2 = pltpu.make_async_copy(conv2_ref, conv2, sems.at[0])
    load_conv2.start()
    loads = []
    for step in range(copies):
        slot = copy_index ^ step
        loads.append(pltpu.make_async_copy(proj_refs[step], proj.at[slot], sems.at[1 + step]))
    start_all(loads)
    banded_weights(width, conv1_ref, banded_ref)
    streams = mel_refs[0].shape[0] // JS
    n = parts * streams
    for step in range(parts):
        mel[part ^ step] = mel_refs[step][...].astype(F32)
    evens = jnp.concatenate(
        [mel[p, j * streams : (j + 1) * streams, :] for j in range(JS) for p in range(parts)], axis=0
    )
    odds = pltpu.roll(evens[: W * n], LANES - 2 * width, 1).astype(BF16)
    evens = evens.astype(BF16)
    channels = conv2.shape[1]
    outs = banded_ref.shape[1] // channels
    for g in range(outs):
        lanes = slice(g * channels, (g + 1) * channels)
        weight = banded_ref[:, lanes]
        even[:, lanes] = jax.nn.relu(jnp.dot(evens, weight, preferred_element_type=F32)).astype(BF16)
        odd[:, lanes] = jax.nn.relu(jnp.dot(odds, weight, preferred_element_type=F32)).astype(BF16)

    load_conv2.wait()
    for h in range((outs - 1) // 2):
        lanes = slice(2 * h * channels, (2 * h + 3) * channels)
        depth = 3 * channels
        total = jnp.dot(even[: W * n, lanes], conv2[:depth], preferred_element_type=F32)
        total += jnp.dot(odd[:, lanes], conv2[depth : 2 * depth], preferred_element_type=F32)
        total += jnp.dot(even[n:, lanes], conv2[2 * depth :], preferred_element_type=F32)
        second[:, h * channels : (h + 1) * channels] = jax.nn.relu(total).astype(BF16)
    wait_all(loads)
    weights = proj[...].reshape(second.shape[1], proj.shape[2])
    sums = jnp.dot(second[...], weights, preferred_element_type=F32)
    for block in range(partial.shape[0]):
        partial[block] = sums[:, block * LANES : (block + 1) * LANES]
    for step in range(windows):
        for block in range(partial.shape[0]):
            rows = partial[block, pl.ds(mine ^ step, W * parts, stride=streams), :]
            outs_refs[step][:, block * LANES : (block + 1) * LANES] = rows.astype(BF16)


def bounds(row, slots_ref, starts_ref, lengths_ref):
    begin, span = jnp.int32(0), jnp.int32(0)
    for u in range(slots_ref.shape[0]):
        chosen = slots_ref[u] == row
        begin = begin + jnp.where(chosen, starts_ref[u], 0)
        span = span + jnp.where(chosen, lengths_ref[u], 0)
    return begin, begin + span


def norm_kernel(parts, group, slots_ref, starts_ref, lengths_ref, *refs):
    _, copy_index = place(parts)
    windows = lax.axis_size("dp")
    copies = windows // parts
    part_refs, refs = refs[:windows], refs[windows:]
    piece_refs, refs = refs[:parts], refs[parts:]
    rows_out, normed_out, stack_out, encoded, sems = refs
    moves = stacked(parts, piece_refs, stack_out, sems, 0)
    start_all(moves)
    begin, end = bounds(lax.axis_index("dp"), slots_ref, starts_ref, lengths_ref)
    rows = W * parts
    for copy in range(copies):
        total = part_refs[copy][...].astype(F32)
        for step in range(1, parts):
            total += part_refs[step * copies + copy][...].astype(F32)
        at = pl.multiple_of((copy_index ^ copy) * rows, rows)
        encoded[pl.ds(at, rows), :] = total.astype(BF16)
    values = jnp.dot(frame_order(parts, copies), encoded[...], preferred_element_type=F32)
    mean = jnp.mean(values, axis=-1, keepdims=True)
    centered = values - mean
    variance = jnp.mean(centered * centered, axis=-1, keepdims=True)
    normed_out[...] = (centered * lax.rsqrt(variance + EPS_NORM)).astype(BF16)
    sample = samples(iota(windows * W, 1, 0), windows, group) + lax.axis_index("seq") * (W * SPAN)
    valid = (sample >= begin) & (sample < end)
    rows_out[...] = jnp.where(valid, values, 0.0).astype(BF16)
    wait_all(moves)


def attention_kernel(parts, windows, group, slots_ref, starts_ref, lengths_ref, *refs):
    _, copy_index = place(parts)
    plane = lax.axis_index("seq")
    copies = windows // parts
    normed_refs, refs = refs[:group], refs[group:]
    stack_refs, refs = refs[:copies], refs[copies:]
    weight_refs, refs = refs[:parts], refs[parts:]
    outs_refs, (stack_out, pieces, sems) = refs[:group], refs[group:]
    moves = stacked(parts, weight_refs, stack_out, sems, 0)
    start_all(moves)
    begin, end = bounds(lax.axis_index("dp"), slots_ref, starts_ref, lengths_ref)
    masks = []
    for step in range(group):
        sample = samples(iota(1, windows * W, 1), windows, group) + (plane ^ step) * (W * SPAN)
        masks.append(((sample >= begin) & (sample < end)).astype(F32))
    valid = jnp.concatenate(masks, axis=1) > 0.5
    local = normed_refs[0].shape[0]
    depth = pieces.shape[2]
    for step in range(group):
        for piece in range(windows):
            pieces[piece, step * local : (step + 1) * local, :] = normed_refs[step][
                :, piece * depth : (piece + 1) * depth
            ]
    mixed = 0.0
    for step in range(copies):
        slot = copy_index ^ step
        normed = jnp.concatenate([pieces[piece * copies + slot] for piece in range(parts)], axis=1)
        weights = stack_refs[step][...].reshape(parts * depth, stack_refs[step].shape[2])
        mixed += jnp.dot(normed, weights, preferred_element_type=F32)
    mixed = mixed.astype(BF16)
    width = mixed.shape[1] // 3
    scale = HEAD_DIM ** (-0.5)
    for head in range(width // HEAD_DIM):
        at = head * HEAD_DIM
        query = mixed[:, at : at + HEAD_DIM]
        key = mixed[:, width + at : width + at + HEAD_DIM]
        value = mixed[:, 2 * width + at : 2 * width + at + HEAD_DIM]
        scores = lax.dot_general(query, key, (((1,), (1,)), ((), ())), preferred_element_type=F32) * scale
        masked = jnp.where(valid, scores, MASKED)
        peak = jnp.max(masked, axis=1, keepdims=True)
        weight = jnp.where(valid, jnp.exp(masked - peak), 0.0)
        total = jnp.sum(weight, axis=1, keepdims=True)
        summed = jnp.dot(weight.astype(BF16), value, preferred_element_type=F32)
        context = (summed / total).astype(BF16)
        for step in range(group):
            outs_refs[step][:, at : at + HEAD_DIM] = context[step * local : (step + 1) * local]
    wait_all(moves)


def output_kernel(parts, windows, group, slots_ref, starts_ref, lengths_ref, *refs):
    context_refs, refs = refs[:group], refs[group:]
    stack_refs, refs = refs[: windows // parts], refs[windows // parts :]
    out_ref, context, pieces = refs
    _, copy_index = place(parts)
    copies = windows // parts
    plane = lax.axis_index("seq")
    begin, end = bounds(lax.axis_index("dp"), slots_ref, starts_ref, lengths_ref)
    head_width = context_refs[0].shape[1]
    for step in range(group):
        at = pl.multiple_of((plane ^ step) * head_width, LANES)
        context[:, pl.ds(at, head_width)] = context_refs[step][...]
    ordered = context[...]
    sample = samples(iota(windows * W, 1, 0), windows, group) + plane * (W * SPAN)
    valid = (sample >= begin) & (sample < end)
    for step in range(copies):
        slot = copy_index ^ step
        for piece in range(parts):
            pieces[piece * copies + slot] = jnp.dot(
                ordered, stack_refs[step][piece], preferred_element_type=F32
            )
    result = jnp.concatenate([pieces[d] for d in range(windows)], axis=1)
    out_ref[...] = jnp.where(valid, result, 0.0).astype(BF16)


def on_device(
    audio, starts, lengths, slots, conv1_weight, conv2_weight, proj_weight, qkv_weight, out_weight
):
    streams = audio.shape[0]
    windows = lax.axis_size("dp")
    group = lax.axis_size("seq")
    parts = math.gcd(windows, BANDS)
    copies = windows // parts
    assert streams == windows and all(count & (count - 1) == 0 for count in (parts, copies, group))
    share = BANDS // parts
    width = 4 * share + 4
    channels = conv1_weight.shape[1]
    features = proj_weight.shape[1]
    head_width = features // group
    local = windows * W
    rows = JS * streams
    n = parts * streams
    outs = 2 * share + 1
    scale = max(1, windows * group // 32)

    route = [(i, i + 1) for i in range(windows * group - 1)]
    rim = lax.ppermute(audio[:, audio.shape[1] - RIM :], ("dp", "seq"), route)

    def to_part(block, step):
        pairs = [(p * copies + c, (p ^ step) * copies + c) for p in range(parts) for c in range(copies)]
        return lax.ppermute(block, "dp", pairs)

    def to_copy(block, step):
        pairs = [(p * copies + c, p * copies + (c ^ step)) for p in range(parts) for c in range(copies)]
        return lax.ppermute(block, "dp", pairs)

    def to_window(block, step):
        return lax.ppermute(block, "dp", [(i, i ^ step) for i in range(windows)])

    def to_plane(block, step):
        return lax.ppermute(block, "seq", [(i, i ^ step) for i in range(group)])

    proj_all = [proj_weight] + [to_copy(proj_weight, step) for step in range(1, copies)]

    table = jnp.asarray(spectrum_table(N_FFT))
    mix_piece = jax.ShapeDtypeStruct((qkv_weight.shape[0], 3 * head_width), BF16)
    *mel_all, mix = pl.pallas_call(
        functools.partial(mel_kernel, parts, group),
        out_shape=tuple([jax.ShapeDtypeStruct((rows, LANES), BF16)] * parts + [mix_piece]),
        in_specs=[smem(), vmem()] + [anywhere()] * 3,
        out_specs=tuple([vmem()] * (parts + 1)),
        scratch_shapes=[
            pltpu.VMEM((streams, RIM + audio.shape[1]), F32),
            pltpu.VMEM(table.shape, F32),
            pltpu.VMEM((parts, rows, LANES), BF16),
            pltpu.SemaphoreType.DMA((5,)),
        ],
        compiler_params=params(60),
        cost_estimate=cost(1e10, 2e6),
        name="log_mel",
    )(slots, rim, audio, table, qkv_weight)
    near = [to_part(out_weight, step) for step in range(1, parts - 1)]
    mel_all, proj_all, near = lax.optimization_barrier((mel_all, proj_all, near))
    mel_all = [mel_all[0]] + [to_part(mel_all[step], step) for step in range(1, parts)]
    mix_all = [mix] + [to_part(mix, step) for step in range(1, parts)]

    block = jax.ShapeDtypeStruct((local, features), BF16)
    partials = pl.pallas_call(
        functools.partial(conv_kernel, parts, width),
        out_shape=tuple([jax.ShapeDtypeStruct((W * parts, features), BF16)] * windows),
        in_specs=[vmem()] + [anywhere()] + [vmem()] * parts + [anywhere()] * copies,
        out_specs=tuple([vmem()] * windows),
        scratch_shapes=[
            pltpu.VMEM((parts, rows, LANES), F32),
            pltpu.VMEM((LANES, outs * channels), BF16),
            pltpu.VMEM((JS * n, outs * channels), BF16),
            pltpu.VMEM((W * n, outs * channels), BF16),
            pltpu.VMEM((W * n, share * channels), BF16),
            pltpu.VMEM(conv2_weight.shape, BF16),
            pltpu.VMEM((copies,) + proj_weight.shape, BF16),
            pltpu.VMEM((features // LANES, W * n, LANES), F32),
            pltpu.SemaphoreType.DMA((1 + copies,)),
        ],
        compiler_params=params(min(40 + 4 * scale, 56)),
        cost_estimate=cost(2e9, 4e6),
        name="conv",
    )(conv1_weight, conv2_weight, *mel_all, *proj_all)
    partials = [partials[0]] + [to_window(partials[step], step) for step in range(1, windows)]

    regrouped, normed, stack = pl.pallas_call(
        functools.partial(norm_kernel, parts, group),
        out_shape=(block, block, jax.ShapeDtypeStruct((parts,) + mix_piece.shape, BF16)),
        in_specs=[smem()] * 3 + [vmem()] * windows + [anywhere()] * parts,
        out_specs=(vmem(), vmem(), vmem()),
        scratch_shapes=[pltpu.VMEM((local, features), BF16), pltpu.SemaphoreType.DMA((parts,))],
        compiler_params=params(min(12 * scale, 32)),
        cost_estimate=cost(1e8, 1e6),
        name="layer_norm",
    )(slots, starts, lengths, *partials, *mix_all)
    mix_stacks = [stack] + [to_copy(stack, step) for step in range(1, copies)]
    normed, out_here = lax.optimization_barrier((normed, out_weight))
    normed = [normed] + [to_plane(normed, step) for step in range(1, group)]
    out_all = [out_here] + near + [to_part(out_here, parts - 1)]

    *context, stack = pl.pallas_call(
        functools.partial(attention_kernel, parts, windows, group),
        out_shape=tuple(
            [jax.ShapeDtypeStruct((local, head_width), BF16)] * group
            + [jax.ShapeDtypeStruct((parts,) + out_weight.shape, BF16)]
        ),
        in_specs=[smem()] * 3 + [vmem()] * (group + copies) + [anywhere()] * parts,
        out_specs=tuple([vmem()] * (group + 1)),
        scratch_shapes=[
            pltpu.VMEM((windows, group * local, qkv_weight.shape[0]), BF16),
            pltpu.SemaphoreType.DMA((parts,)),
        ],
        compiler_params=params(min(16 * scale, 48)),
        cost_estimate=cost(1e9, 2e6),
        name="attention",
    )(slots, starts, lengths, *normed, *mix_stacks, *out_all)
    context = [context[0]] + [to_plane(context[step], step) for step in range(1, group)]
    out_stacks = [stack] + [to_copy(stack, step) for step in range(1, copies)]

    attended = pl.pallas_call(
        functools.partial(output_kernel, parts, windows, group),
        out_shape=block,
        in_specs=[smem()] * 3 + [vmem()] * (group + copies),
        out_specs=vmem(),
        scratch_shapes=[
            pltpu.VMEM((local, features), BF16),
            pltpu.VMEM((windows, local, out_weight.shape[1]), F32),
        ],
        compiler_params=params(min(12 * scale, 32)),
        cost_estimate=cost(1e8, 3e6),
        name="output",
    )(slots, starts, lengths, *context, *out_stacks)
    shape = (1, windows, 1, W, features)
    return (regrouped.reshape(shape), attended.reshape(shape))


def solution(mesh):
    in_specs = (
        P(None, ("dp", "seq")),
        P(),
        P(),
        P(),
        P(),
        P(),
        P("dp", None),
        P("dp", None),
        P(None, "dp"),
    )
    out_specs = (P("dp", None, "seq", None, None), P("dp", None, "seq", None, None))
    return jax.shard_map(
        on_device, mesh=mesh, in_specs=in_specs, out_specs=out_specs, check_vma=False
    )
```

```python
import functools
import math

import jax
import jax.numpy as jnp
import numpy as np
from jax import lax
from jax.experimental import pallas as pl
from jax.experimental.pallas import tpu as pltpu
from jax.sharding import PartitionSpec as P

HEADS = 8
HEAD_DIM = 128
MELS = 80
BANDS = MELS // 4
N_FFT = 512
HOP = 160
W = 8
RIM = 1024
SPAN = 4 * HOP
JS = W + 1
LANES = 128
SAMPLE_RATE = 16000.0
EPS_LOG = 1e-06
EPS_NORM = 1e-05
MASKED = -1e30
F32 = jnp.float32
BF16 = jnp.bfloat16
MIB = 1 << 20


def mel_table(size, bands):
    count = size // 2 + 1
    highest = 2595.0 * math.log10(1.0 + SAMPLE_RATE / 1400.0)
    points = np.linspace(0.0, highest, bands + 2)
    edges = 700.0 * (10.0 ** (points / 2595.0) - 1.0)
    edges[0] = 0.0
    edges[-1] = SAMPLE_RATE / 2.0
    frequency = np.arange(count) * (SAMPLE_RATE / size)
    lower = edges[:-2][None, :]
    middle = edges[1:-1][None, :]
    upper = edges[2:][None, :]
    rising = (frequency[:, None] - lower) / (middle - lower)
    falling = (upper - frequency[:, None]) / (upper - middle)
    return np.maximum(0.0, np.minimum(rising, falling)).astype(np.float32)


def spectrum_table(size):
    sample = np.arange(size)
    phase = sample[:, None] * np.arange(size // 2)[None, :] % size
    angle = phase * (2.0 * math.pi / size)
    window = 0.5 - 0.5 * np.cos(sample * (2.0 * math.pi / size))
    both = np.concatenate([np.cos(angle), np.sin(angle)], axis=1) * window[:, None]
    filters = np.zeros((size, LANES))
    filters[: size // 2, :MELS] = mel_table(size, MELS)[: size // 2]
    return np.concatenate([both, filters], axis=1).astype(np.float32)


def vmem():
    return pl.BlockSpec(memory_space=pltpu.VMEM)


def smem():
    return pl.BlockSpec(memory_space=pltpu.SMEM)


def anywhere():
    return pl.BlockSpec(memory_space=pl.ANY)


def params(mib):
    return pltpu.CompilerParams(vmem_limit_bytes=mib * MIB)


def cost(flops, moved):
    return pl.CostEstimate(flops=int(flops), bytes_accessed=int(moved), transcendentals=0)


def place(parts):
    mine = lax.axis_index("dp")
    copies = lax.axis_size("dp") // parts
    return mine // copies, mine % copies


def start_all(copies):
    for copy in copies:
        copy.start()


def wait_all(copies):
    for copy in copies:
        copy.wait()


def iota(rows, columns, axis):
    return lax.broadcasted_iota(jnp.int32, (rows, columns), axis)


def quotient(index, step, count):
    result = jnp.zeros_like(index)
    for i in range(1, count):
        result += (index >= i * step).astype(jnp.int32)
    return result


def one_hot(target, count):
    return (iota(target.shape[0], count, 1) == target).astype(F32).astype(BF16)


def frame_order(parts, copies):
    count = parts * copies * W
    row = iota(count, 1, 0)
    k = quotient(row, W, parts * copies)
    p = quotient(k, copies, parts)
    return one_hot((k - p * copies) * W * parts + (row - k * W) * parts + p, count)


def samples(index, windows, group):
    return (index + quotient(index, W, windows) * (group - 1) * W) * SPAN


def mix_columns(group, qkv_ref, mix_out, sems):
    features = qkv_ref.shape[1] // 3
    width = features // group
    first = pl.multiple_of(lax.axis_index("seq") * width, LANES)
    return [
        pltpu.make_async_copy(
            qkv_ref.at[:, pl.ds(kind * features + first, width)],
            mix_out.at[:, pl.ds(kind * width, width)],
            sems.at[kind],
        )
        for kind in range(3)
    ]


def banded_weights(width, conv1_ref, banded_out):
    taps, channels = conv1_ref.shape
    row = lax.broadcasted_iota(jnp.int32, (LANES, taps), 0)
    tap = lax.broadcasted_iota(jnp.int32, (LANES, taps), 1)
    line = (tap >= 3).astype(jnp.int32) + (tap >= 6).astype(jnp.int32)
    target = line * (width - 3) + tap + 1
    weight = conv1_ref[...]
    for g in range(banded_out.shape[1] // channels):
        select = (row == target + 2 * g).astype(F32).astype(BF16)
        banded_out[:, g * channels : (g + 1) * channels] = jnp.dot(
            select, weight, preferred_element_type=F32
        ).astype(BF16)


def mel_kernel(parts, group, slots_ref, rim_ref, audio_ref, table_ref, qkv_ref, *refs):
    outs_refs, (mix_out, ext, table, blocks, sems) = refs[:parts], refs[parts:]
    load_audio = pltpu.make_async_copy(audio_ref, ext.at[:, pl.ds(RIM, audio_ref.shape[1])], sems.at[3])
    load_table = pltpu.make_async_copy(table_ref, table, sems.at[4])
    load_audio.start()
    load_table.start()
    pieces = mix_columns(group, qkv_ref, mix_out, sems)
    start_all(pieces)
    streams = audio_ref.shape[0]
    rows = JS * streams
    ext[:, :RIM] = rim_ref[...]
    column = iota(1, rows, 1)
    early = quotient(column, streams, JS)
    target = jnp.zeros((1, rows), jnp.int32)
    for u in range(streams):
        target = jnp.where(column - early * streams == u, early * streams + slots_ref[u], target)
    routing = (target == iota(rows, rows, 0)).astype(F32).astype(BF16)
    load_audio.wait()
    phases = []
    for phase in range(4):
        start = HOP * phase + 32
        base, shift = start // LANES * LANES, start % LANES
        length = N_FFT + (LANES if shift else 0)
        block = jnp.concatenate(
            [ext[:, SPAN * j + base : SPAN * j + base + length] for j in range(JS)], axis=0
        )
        if shift:
            block = pltpu.roll(block, length - shift, 1)[:, :N_FFT]
        phases.append(block)
    frames = jnp.concatenate(phases, axis=0)
    load_table.wait()
    spectrum = jnp.dot(
        frames, table[:, :N_FFT], precision=lax.Precision.HIGHEST, preferred_element_type=F32
    )
    half = N_FFT // 2
    real, imag = spectrum[:, :half], spectrum[:, half:]
    power = real * real + imag * imag
    mel_power = jnp.dot(
        power, table[:half, N_FFT:], precision=lax.Precision.HIGHEST, preferred_element_type=F32
    )
    log_mel = jnp.log(mel_power + EPS_LOG)
    share = BANDS // parts
    width = 4 * share + 4
    lane = iota(rows, LANES, 1)
    by_phase = [log_mel[phase * rows : (phase + 1) * rows] for phase in range(4)]

    def next_four(frames):
        return jnp.concatenate([frames[streams:], jnp.zeros((streams, LANES), F32)], axis=0)

    taps = [by_phase[1], by_phase[2], by_phase[3], next_four(by_phase[0]), next_four(by_phase[1])]
    for part in range(parts):
        first = 4 * share * part - 4
        block = jnp.zeros((rows, LANES), F32)
        for delta, frames in enumerate(taps):
            band = lane - width * delta + first
            here = (lane >= width * delta) & (lane < width * (delta + 1)) & (band >= 0) & (band < MELS)
            shift = (width * delta - first) % LANES
            block = jnp.where(here, pltpu.roll(frames, shift, 1) if shift else frames, block)
        blocks[part] = jnp.dot(routing, block.astype(BF16), preferred_element_type=F32).astype(BF16)
    mine, _ = place(parts)
    for step in range(parts):
        outs_refs[step][...] = blocks[mine ^ step]
    wait_all(pieces)


def stacked(parts, pieces, stack_out, sems, base):
    part, _ = place(parts)
    return [
        pltpu.make_async_copy(pieces[step], stack_out.at[part ^ step], sems.at[base + step])
        for step in range(parts)
    ]


def conv_kernel(parts, width, conv1_ref, conv2_ref, *refs):
    part, copy_index = place(parts)
    mine = lax.axis_index("dp")
    windows = lax.axis_size("dp")
    copies = windows // parts
    mel_refs, refs = refs[:parts], refs[parts:]
    proj_refs, refs = refs[:copies], refs[copies:]
    outs_refs, refs = refs[:windows], refs[windows:]
    mel, own, banded_ref, even, odd, second, conv2, proj, partial, sems = refs
    load_own = pltpu.make_async_copy(mel_refs[0], own, sems.at[1 + copies])
    load_own.start()
    load_conv2 = pltpu.make_async_copy(conv2_ref, conv2, sems.at[0])
    load_conv2.start()
    loads = []
    for step in range(copies):
        slot = copy_index ^ step
        loads.append(pltpu.make_async_copy(proj_refs[step], proj.at[slot], sems.at[1 + step]))
    start_all(loads)
    banded_weights(width, conv1_ref, banded_ref)
    streams = mel_refs[0].shape[0] // JS
    n = parts * streams
    load_own.wait()
    mel[part] = own[...].astype(F32)
    for step in range(1, parts):
        mel[part ^ step] = mel_refs[step][...].astype(F32)
    evens = jnp.concatenate(
        [mel[p, j * streams : (j + 1) * streams, :] for j in range(JS) for p in range(parts)], axis=0
    )
    odds = pltpu.roll(evens[: W * n], LANES - 2 * width, 1).astype(BF16)
    evens = evens.astype(BF16)
    channels = conv2.shape[1]
    outs = banded_ref.shape[1] // channels
    for g in range(outs):
        lanes = slice(g * channels, (g + 1) * channels)
        weight = banded_ref[:, lanes]
        even[:, lanes] = jax.nn.relu(jnp.dot(evens, weight, preferred_element_type=F32)).astype(BF16)
        odd[:, lanes] = jax.nn.relu(jnp.dot(odds, weight, preferred_element_type=F32)).astype(BF16)

    load_conv2.wait()
    for h in range((outs - 1) // 2):
        lanes = slice(2 * h * channels, (2 * h + 3) * channels)
        depth = 3 * channels
        total = jnp.dot(even[: W * n, lanes], conv2[:depth], preferred_element_type=F32)
        total += jnp.dot(odd[:, lanes], conv2[depth : 2 * depth], preferred_element_type=F32)
        total += jnp.dot(even[n:, lanes], conv2[2 * depth :], preferred_element_type=F32)
        second[:, h * channels : (h + 1) * channels] = jax.nn.relu(total).astype(BF16)
    wait_all(loads)
    weights = proj[...].reshape(second.shape[1], proj.shape[2])
    sums = jnp.dot(second[...], weights, preferred_element_type=F32)
    for block in range(partial.shape[0]):
        partial[block] = sums[:, block * LANES : (block + 1) * LANES]
    for step in range(windows):
        for block in range(partial.shape[0]):
            rows = partial[block, pl.ds(mine ^ step, W * parts, stride=streams), :]
            outs_refs[step][:, block * LANES : (block + 1) * LANES] = rows.astype(BF16)


def bounds(row, slots_ref, starts_ref, lengths_ref):
    begin, span = jnp.int32(0), jnp.int32(0)
    for u in range(slots_ref.shape[0]):
        chosen = slots_ref[u] == row
        begin = begin + jnp.where(chosen, starts_ref[u], 0)
        span = span + jnp.where(chosen, lengths_ref[u], 0)
    return begin, begin + span


def norm_kernel(parts, *refs):
    _, copy_index = place(parts)
    windows = lax.axis_size("dp")
    copies = windows // parts
    part_refs, refs = refs[:windows], refs[windows:]
    piece_refs, refs = refs[:parts], refs[parts:]
    rows_out, normed_out, stack_out, encoded, sems = refs
    moves = stacked(parts, piece_refs, stack_out, sems, 0)
    start_all(moves)
    rows = W * parts
    for copy in range(copies):
        total = part_refs[copy][...].astype(F32)
        for step in range(1, parts):
            total += part_refs[step * copies + copy][...].astype(F32)
        at = pl.multiple_of((copy_index ^ copy) * rows, rows)
        encoded[pl.ds(at, rows), :] = total.astype(BF16)
    values = jnp.dot(frame_order(parts, copies), encoded[...], preferred_element_type=F32)
    rows_out[...] = values.astype(BF16)
    mean = jnp.mean(values, axis=-1, keepdims=True)
    centered = values - mean
    variance = jnp.mean(centered * centered, axis=-1, keepdims=True)
    normed_out[...] = (centered * lax.rsqrt(variance + EPS_NORM)).astype(BF16)
    wait_all(moves)


def mask_kernel(windows, group, slots_ref, starts_ref, lengths_ref, rows_ref, rows_out, keys_out, valid_out):
    begin, end = bounds(lax.axis_index("dp"), slots_ref, starts_ref, lengths_ref)
    sample = samples(iota(windows * W, 1, 0), windows, group) + lax.axis_index("seq") * (W * SPAN)
    valid = (sample >= begin) & (sample < end)
    rows_out[...] = jnp.where(valid, rows_ref[...].astype(F32), 0.0).astype(BF16)
    valid_out[...] = valid.astype(F32)
    keys = samples(iota(group, windows * W, 1), windows, group) + iota(group, windows * W, 0) * (W * SPAN)
    keys_out[...] = ((keys >= begin) & (keys < end)).astype(F32)


def attention_kernel(parts, windows, group, keys_ref, *refs):
    _, copy_index = place(parts)
    plane = lax.axis_index("seq")
    copies = windows // parts
    normed_refs, refs = refs[:group], refs[group:]
    stack_refs, refs = refs[:copies], refs[copies:]
    weight_refs, refs = refs[:parts], refs[parts:]
    outs_refs, (stack_out, pieces, sems) = refs[:group], refs[group:]
    moves = stacked(parts, weight_refs, stack_out, sems, 0)
    start_all(moves)
    keys = [keys_ref[pl.ds(plane ^ step, 1), :] for step in range(group)]
    valid = jnp.concatenate(keys, axis=1) > 0.5
    local = normed_refs[0].shape[0]
    depth = pieces.shape[2]
    for step in range(group):
        for piece in range(windows):
            pieces[piece, step * local : (step + 1) * local, :] = normed_refs[step][
                :, piece * depth : (piece + 1) * depth
            ]
    mixed = 0.0
    for step in range(copies):
        slot = copy_index ^ step
        normed = jnp.concatenate([pieces[piece * copies + slot] for piece in range(parts)], axis=1)
        weights = stack_refs[step][...].reshape(parts * depth, stack_refs[step].shape[2])
        mixed += jnp.dot(normed, weights, preferred_element_type=F32)
    mixed = mixed.astype(BF16)
    width = mixed.shape[1] // 3
    scale = HEAD_DIM ** (-0.5)
    for head in range(width // HEAD_DIM):
        at = head * HEAD_DIM
        query = mixed[:, at : at + HEAD_DIM]
        key = mixed[:, width + at : width + at + HEAD_DIM]
        value = mixed[:, 2 * width + at : 2 * width + at + HEAD_DIM]
        scores = lax.dot_general(query, key, (((1,), (1,)), ((), ())), preferred_element_type=F32) * scale
        masked = jnp.where(valid, scores, MASKED)
        peak = jnp.max(masked, axis=1, keepdims=True)
        weight = jnp.where(valid, jnp.exp(masked - peak), 0.0)
        total = jnp.sum(weight, axis=1, keepdims=True)
        summed = jnp.dot(weight.astype(BF16), value, preferred_element_type=F32)
        context = (summed / total).astype(BF16)
        for step in range(group):
            outs_refs[step][:, at : at + HEAD_DIM] = context[step * local : (step + 1) * local]
    wait_all(moves)


def output_kernel(parts, windows, group, valid_ref, *refs):
    context_refs, refs = refs[:group], refs[group:]
    stack_refs, refs = refs[: windows // parts], refs[windows // parts :]
    out_ref, context, pieces = refs
    _, copy_index = place(parts)
    copies = windows // parts
    plane = lax.axis_index("seq")
    head_width = context_refs[0].shape[1]
    for step in range(group):
        at = pl.multiple_of((plane ^ step) * head_width, LANES)
        context[:, pl.ds(at, head_width)] = context_refs[step][...]
    ordered = context[...]
    for step in range(copies):
        slot = copy_index ^ step
        for piece in range(parts):
            pieces[piece * copies + slot] = jnp.dot(
                ordered, stack_refs[step][piece], preferred_element_type=F32
            )
    result = jnp.concatenate([pieces[d] for d in range(windows)], axis=1)
    out_ref[...] = jnp.where(valid_ref[...] > 0.5, result, 0.0).astype(BF16)


def on_device(
    audio, starts, lengths, slots, conv1_weight, conv2_weight, proj_weight, qkv_weight, out_weight
):
    streams = audio.shape[0]
    windows = lax.axis_size("dp")
    group = lax.axis_size("seq")
    parts = math.gcd(windows, BANDS)
    copies = windows // parts
    assert streams == windows and all(count & (count - 1) == 0 for count in (parts, copies, group))
    share = BANDS // parts
    width = 4 * share + 4
    channels = conv1_weight.shape[1]
    features = proj_weight.shape[1]
    head_width = features // group
    local = windows * W
    rows = JS * streams
    n = parts * streams
    outs = 2 * share + 1
    scale = max(1, windows * group // 32)

    route = [(i, i + 1) for i in range(windows * group - 1)]
    rim = lax.ppermute(audio[:, audio.shape[1] - RIM :], ("dp", "seq"), route)

    def to_part(block, step):
        pairs = [(p * copies + c, (p ^ step) * copies + c) for p in range(parts) for c in range(copies)]
        return lax.ppermute(block, "dp", pairs)

    def to_copy(block, step):
        pairs = [(p * copies + c, p * copies + (c ^ step)) for p in range(parts) for c in range(copies)]
        return lax.ppermute(block, "dp", pairs)

    def to_window(block, step):
        return lax.ppermute(block, "dp", [(i, i ^ step) for i in range(windows)])

    def to_plane(block, step):
        return lax.ppermute(block, "seq", [(i, i ^ step) for i in range(group)])

    proj_all = [proj_weight] + [to_copy(proj_weight, step) for step in range(1, copies)]

    table = jnp.asarray(spectrum_table(N_FFT))
    mix_piece = jax.ShapeDtypeStruct((qkv_weight.shape[0], 3 * head_width), BF16)
    *mel_all, mix = pl.pallas_call(
        functools.partial(mel_kernel, parts, group),
        out_shape=tuple([jax.ShapeDtypeStruct((rows, LANES), BF16)] * parts + [mix_piece]),
        in_specs=[smem(), vmem()] + [anywhere()] * 3,
        out_specs=tuple([vmem()] * (parts + 1)),
        scratch_shapes=[
            pltpu.VMEM((streams, RIM + audio.shape[1]), F32),
            pltpu.VMEM(table.shape, F32),
            pltpu.VMEM((parts, rows, LANES), BF16),
            pltpu.SemaphoreType.DMA((5,)),
        ],
        compiler_params=params(60),
        cost_estimate=cost(1e10, 2e6),
        name="log_mel",
    )(slots, rim, audio, table, qkv_weight)
    near = [to_part(out_weight, step) for step in range(1, parts - 1)]
    mel_all, proj_all, near = lax.optimization_barrier((mel_all, proj_all, near))
    mel_all = [mel_all[0]] + [to_part(mel_all[step], step) for step in range(1, parts)]
    mix_all = [mix] + [to_part(mix, step) for step in range(1, parts)]

    block = jax.ShapeDtypeStruct((local, features), BF16)
    partials = pl.pallas_call(
        functools.partial(conv_kernel, parts, width),
        out_shape=tuple([jax.ShapeDtypeStruct((W * parts, features), BF16)] * windows),
        in_specs=[vmem()] + [anywhere()] * 2 + [vmem()] * (parts - 1) + [anywhere()] * copies,
        out_specs=tuple([vmem()] * windows),
        scratch_shapes=[
            pltpu.VMEM((parts, rows, LANES), F32),
            pltpu.VMEM((rows, LANES), BF16),
            pltpu.VMEM((LANES, outs * channels), BF16),
            pltpu.VMEM((JS * n, outs * channels), BF16),
            pltpu.VMEM((W * n, outs * channels), BF16),
            pltpu.VMEM((W * n, share * channels), BF16),
            pltpu.VMEM(conv2_weight.shape, BF16),
            pltpu.VMEM((copies,) + proj_weight.shape, BF16),
            pltpu.VMEM((features // LANES, W * n, LANES), F32),
            pltpu.SemaphoreType.DMA((2 + copies,)),
        ],
        compiler_params=params(min(40 + 4 * scale, 56)),
        cost_estimate=cost(2e9, 4e6),
        name="conv",
    )(conv1_weight, conv2_weight, *mel_all, *proj_all)
    partials = [partials[0]] + [to_window(partials[step], step) for step in range(1, windows)]

    ordered, normed, stack = pl.pallas_call(
        functools.partial(norm_kernel, parts),
        out_shape=(block, block, jax.ShapeDtypeStruct((parts,) + mix_piece.shape, BF16)),
        in_specs=[vmem()] * windows + [anywhere()] * parts,
        out_specs=(vmem(), vmem(), vmem()),
        scratch_shapes=[pltpu.VMEM((local, features), BF16), pltpu.SemaphoreType.DMA((parts,))],
        compiler_params=params(min(12 * scale, 32)),
        cost_estimate=cost(1e8, 1e6),
        name="layer_norm",
    )(*partials, *mix_all)
    mix_stacks = [stack] + [to_copy(stack, step) for step in range(1, copies)]
    regrouped, keys, valid = pl.pallas_call(
        functools.partial(mask_kernel, windows, group),
        out_shape=(
            block,
            jax.ShapeDtypeStruct((group, local), F32),
            jax.ShapeDtypeStruct((local, 1), F32),
        ),
        in_specs=[smem()] * 3 + [vmem()],
        out_specs=(vmem(), vmem(), vmem()),
        compiler_params=params(min(8 * scale, 32)),
        cost_estimate=cost(1e8, 1e6),
        name="mask",
    )(slots, starts, lengths, ordered)
    normed, out_here = lax.optimization_barrier((normed, out_weight))
    normed = [normed] + [to_plane(normed, step) for step in range(1, group)]
    out_all = [out_here] + near + [to_part(out_here, parts - 1)]

    *context, stack = pl.pallas_call(
        functools.partial(attention_kernel, parts, windows, group),
        out_shape=tuple(
            [jax.ShapeDtypeStruct((local, head_width), BF16)] * group
            + [jax.ShapeDtypeStruct((parts,) + out_weight.shape, BF16)]
        ),
        in_specs=[vmem()] * (1 + group + copies) + [anywhere()] * parts,
        out_specs=tuple([vmem()] * (group + 1)),
        scratch_shapes=[
            pltpu.VMEM((windows, group * local, qkv_weight.shape[0]), BF16),
            pltpu.SemaphoreType.DMA((parts,)),
        ],
        compiler_params=params(min(16 * scale, 48)),
        cost_estimate=cost(1e9, 2e6),
        name="attention",
    )(keys, *normed, *mix_stacks, *out_all)
    context = [context[0]] + [to_plane(context[step], step) for step in range(1, group)]
    out_stacks = [stack] + [to_copy(stack, step) for step in range(1, copies)]

    attended = pl.pallas_call(
        functools.partial(output_kernel, parts, windows, group),
        out_shape=block,
        in_specs=[vmem()] * (1 + group + copies),
        out_specs=vmem(),
        scratch_shapes=[
            pltpu.VMEM((local, features), BF16),
            pltpu.VMEM((windows, local, out_weight.shape[1]), F32),
        ],
        compiler_params=params(min(12 * scale, 32)),
        cost_estimate=cost(1e8, 3e6),
        name="output",
    )(valid, *context, *out_stacks)
    shape = (1, windows, 1, W, features)
    return (regrouped.reshape(shape), attended.reshape(shape))


def solution(mesh):
    in_specs = (
        P(None, ("dp", "seq")),
        P(),
        P(),
        P(),
        P(),
        P(),
        P("dp", None),
        P("dp", None),
        P(None, "dp"),
    )
    out_specs = (P("dp", None, "seq", None, None), P("dp", None, "seq", None, None))
    return jax.shard_map(
        on_device, mesh=mesh, in_specs=in_specs, out_specs=out_specs, check_vma=False
    )
```

```python
import functools
import math

import jax
import jax.numpy as jnp
import numpy as np
from jax import lax
from jax.experimental import pallas as pl
from jax.experimental.pallas import tpu as pltpu
from jax.sharding import PartitionSpec as P

HEADS = 8
HEAD_DIM = 128
MELS = 80
BANDS = MELS // 4
N_FFT = 512
HOP = 160
W = 8
RIM = 1024
SPAN = 4 * HOP
JS = W + 1
LANES = 128
SAMPLE_RATE = 16000.0
EPS_LOG = 1e-06
EPS_NORM = 1e-05
MASKED = -1e30
F32 = jnp.float32
BF16 = jnp.bfloat16
MIB = 1 << 20


def mel_table(size, bands):
    count = size // 2 + 1
    highest = 2595.0 * math.log10(1.0 + SAMPLE_RATE / 1400.0)
    points = np.linspace(0.0, highest, bands + 2)
    edges = 700.0 * (10.0 ** (points / 2595.0) - 1.0)
    edges[0] = 0.0
    edges[-1] = SAMPLE_RATE / 2.0
    frequency = np.arange(count) * (SAMPLE_RATE / size)
    lower = edges[:-2][None, :]
    middle = edges[1:-1][None, :]
    upper = edges[2:][None, :]
    rising = (frequency[:, None] - lower) / (middle - lower)
    falling = (upper - frequency[:, None]) / (upper - middle)
    return np.maximum(0.0, np.minimum(rising, falling)).astype(np.float32)


def spectrum_table(size):
    sample = np.arange(size)
    phase = sample[:, None] * np.arange(size // 2)[None, :] % size
    angle = phase * (2.0 * math.pi / size)
    window = 0.5 - 0.5 * np.cos(sample * (2.0 * math.pi / size))
    both = np.concatenate([np.cos(angle), np.sin(angle)], axis=1) * window[:, None]
    filters = np.zeros((size, LANES))
    filters[: size // 2, :MELS] = mel_table(size, MELS)[: size // 2]
    return np.concatenate([both, filters], axis=1).astype(np.float32)


def vmem():
    return pl.BlockSpec(memory_space=pltpu.VMEM)


def smem():
    return pl.BlockSpec(memory_space=pltpu.SMEM)


def anywhere():
    return pl.BlockSpec(memory_space=pl.ANY)


def params(mib):
    return pltpu.CompilerParams(vmem_limit_bytes=mib * MIB)


def cost(flops, moved):
    return pl.CostEstimate(flops=int(flops), bytes_accessed=int(moved), transcendentals=0)


def place(parts):
    mine = lax.axis_index("dp")
    copies = lax.axis_size("dp") // parts
    return mine // copies, mine % copies


def start_all(copies):
    for copy in copies:
        copy.start()


def wait_all(copies):
    for copy in copies:
        copy.wait()


def iota(rows, columns, axis):
    return lax.broadcasted_iota(jnp.int32, (rows, columns), axis)


def quotient(index, step, count):
    result = jnp.zeros_like(index)
    for i in range(1, count):
        result += (index >= i * step).astype(jnp.int32)
    return result


def one_hot(target, count):
    return (iota(target.shape[0], count, 1) == target).astype(F32).astype(BF16)


def frame_order(parts, copies):
    count = parts * copies * W
    row = iota(count, 1, 0)
    k = quotient(row, W, parts * copies)
    p = quotient(k, copies, parts)
    return one_hot((k - p * copies) * W * parts + (row - k * W) * parts + p, count)


def samples(index, windows, group):
    return (index + quotient(index, W, windows) * (group - 1) * W) * SPAN


def mix_columns(group, qkv_ref, mix_out, sems):
    features = qkv_ref.shape[1] // 3
    width = features // group
    first = pl.multiple_of(lax.axis_index("seq") * width, LANES)
    return [
        pltpu.make_async_copy(
            qkv_ref.at[:, pl.ds(kind * features + first, width)],
            mix_out.at[:, pl.ds(kind * width, width)],
            sems.at[kind],
        )
        for kind in range(3)
    ]


def banded_weights(width, conv1_ref, banded_out):
    taps, channels = conv1_ref.shape
    row = lax.broadcasted_iota(jnp.int32, (LANES, taps), 0)
    tap = lax.broadcasted_iota(jnp.int32, (LANES, taps), 1)
    line = (tap >= 3).astype(jnp.int32) + (tap >= 6).astype(jnp.int32)
    target = line * (width - 3) + tap + 1
    weight = conv1_ref[...]
    for g in range(banded_out.shape[1] // channels):
        select = (row == target + 2 * g).astype(F32).astype(BF16)
        banded_out[:, g * channels : (g + 1) * channels] = jnp.dot(
            select, weight, preferred_element_type=F32
        ).astype(BF16)


def mel_kernel(parts, group, slots_here, rim_ref, audio_ref, table_ref, qkv_ref, *refs):
    outs_refs, (mix_out, ext, table, blocks, slots_ref, sems) = refs[:parts], refs[parts:]
    load_slots = pltpu.make_async_copy(slots_here, slots_ref, sems.at[5])
    load_slots.start()
    load_audio = pltpu.make_async_copy(audio_ref, ext.at[:, pl.ds(RIM, audio_ref.shape[1])], sems.at[3])
    load_table = pltpu.make_async_copy(table_ref, table, sems.at[4])
    load_audio.start()
    load_table.start()
    pieces = mix_columns(group, qkv_ref, mix_out, sems)
    start_all(pieces)
    streams = audio_ref.shape[0]
    rows = JS * streams
    ext[:, :RIM] = rim_ref[...]
    load_audio.wait()
    phases = []
    for phase in range(4):
        start = HOP * phase + 32
        base, shift = start // LANES * LANES, start % LANES
        length = N_FFT + (LANES if shift else 0)
        block = jnp.concatenate(
            [ext[:, SPAN * j + base : SPAN * j + base + length] for j in range(JS)], axis=0
        )
        if shift:
            block = pltpu.roll(block, length - shift, 1)[:, :N_FFT]
        phases.append(block)
    frames = jnp.concatenate(phases, axis=0)
    load_table.wait()
    spectrum = jnp.dot(
        frames, table[:, :N_FFT], precision=lax.Precision.HIGHEST, preferred_element_type=F32
    )
    half = N_FFT // 2
    real, imag = spectrum[:, :half], spectrum[:, half:]
    power = real * real + imag * imag
    mel_power = jnp.dot(
        power, table[:half, N_FFT:], precision=lax.Precision.HIGHEST, preferred_element_type=F32
    )
    load_slots.wait()
    column = iota(1, rows, 1)
    early = quotient(column, streams, JS)
    target = jnp.zeros((1, rows), jnp.int32)
    for u in range(streams):
        target = jnp.where(column - early * streams == u, early * streams + slots_ref[u], target)
    routing = (target == iota(rows, rows, 0)).astype(F32).astype(BF16)
    log_mel = jnp.log(mel_power + EPS_LOG)
    share = BANDS // parts
    width = 4 * share + 4
    lane = iota(rows, LANES, 1)
    by_phase = [log_mel[phase * rows : (phase + 1) * rows] for phase in range(4)]

    def next_four(frames):
        return jnp.concatenate([frames[streams:], jnp.zeros((streams, LANES), F32)], axis=0)

    taps = [by_phase[1], by_phase[2], by_phase[3], next_four(by_phase[0]), next_four(by_phase[1])]
    for part in range(parts):
        first = 4 * share * part - 4
        block = jnp.zeros((rows, LANES), F32)
        for delta, frames in enumerate(taps):
            band = lane - width * delta + first
            here = (lane >= width * delta) & (lane < width * (delta + 1)) & (band >= 0) & (band < MELS)
            shift = (width * delta - first) % LANES
            block = jnp.where(here, pltpu.roll(frames, shift, 1) if shift else frames, block)
        blocks[part] = jnp.dot(routing, block.astype(BF16), preferred_element_type=F32).astype(BF16)
    mine, _ = place(parts)
    for step in range(parts):
        outs_refs[step][...] = blocks[mine ^ step]
    wait_all(pieces)


def stacked(parts, pieces, stack_out, sems, base):
    part, _ = place(parts)
    return [
        pltpu.make_async_copy(pieces[step], stack_out.at[part ^ step], sems.at[base + step])
        for step in range(parts)
    ]


def conv_kernel(parts, width, conv1_ref, conv2_ref, *refs):
    part, copy_index = place(parts)
    mine = lax.axis_index("dp")
    windows = lax.axis_size("dp")
    copies = windows // parts
    mel_refs, refs = refs[:parts], refs[parts:]
    proj_refs, refs = refs[:copies], refs[copies:]
    outs_refs, refs = refs[:windows], refs[windows:]
    mel, own, banded_ref, even, odd, second, conv2, proj, partial, sems = refs
    load_own = pltpu.make_async_copy(mel_refs[0], own, sems.at[1 + copies])
    load_own.start()
    load_conv2 = pltpu.make_async_copy(conv2_ref, conv2, sems.at[0])
    load_conv2.start()
    loads = []
    for step in range(copies):
        slot = copy_index ^ step
        loads.append(pltpu.make_async_copy(proj_refs[step], proj.at[slot], sems.at[1 + step]))
    start_all(loads)
    banded_weights(width, conv1_ref, banded_ref)
    streams = mel_refs[0].shape[0] // JS
    n = parts * streams
    load_own.wait()
    mel[part] = own[...].astype(F32)
    for step in range(1, parts):
        mel[part ^ step] = mel_refs[step][...].astype(F32)
    evens = jnp.concatenate(
        [mel[p, j * streams : (j + 1) * streams, :] for j in range(JS) for p in range(parts)], axis=0
    )
    odds = pltpu.roll(evens[: W * n], LANES - 2 * width, 1).astype(BF16)
    evens = evens.astype(BF16)
    channels = conv2.shape[1]
    outs = banded_ref.shape[1] // channels
    for g in range(outs):
        lanes = slice(g * channels, (g + 1) * channels)
        weight = banded_ref[:, lanes]
        even[:, lanes] = jax.nn.relu(jnp.dot(evens, weight, preferred_element_type=F32)).astype(BF16)
        odd[:, lanes] = jax.nn.relu(jnp.dot(odds, weight, preferred_element_type=F32)).astype(BF16)

    load_conv2.wait()
    for h in range((outs - 1) // 2):
        lanes = slice(2 * h * channels, (2 * h + 3) * channels)
        depth = 3 * channels
        total = jnp.dot(even[: W * n, lanes], conv2[:depth], preferred_element_type=F32)
        total += jnp.dot(odd[:, lanes], conv2[depth : 2 * depth], preferred_element_type=F32)
        total += jnp.dot(even[n:, lanes], conv2[2 * depth :], preferred_element_type=F32)
        second[:, h * channels : (h + 1) * channels] = jax.nn.relu(total).astype(BF16)
    wait_all(loads)
    weights = proj[...].reshape(second.shape[1], proj.shape[2])
    sums = jnp.dot(second[...], weights, preferred_element_type=F32)
    for block in range(partial.shape[0]):
        partial[block] = sums[:, block * LANES : (block + 1) * LANES]
    for step in range(windows):
        for block in range(partial.shape[0]):
            rows = partial[block, pl.ds(mine ^ step, W * parts, stride=streams), :]
            outs_refs[step][:, block * LANES : (block + 1) * LANES] = rows.astype(BF16)


def bounds(row, slots_ref, starts_ref, lengths_ref):
    begin, span = jnp.int32(0), jnp.int32(0)
    for u in range(slots_ref.shape[0]):
        chosen = slots_ref[u] == row
        begin = begin + jnp.where(chosen, starts_ref[u], 0)
        span = span + jnp.where(chosen, lengths_ref[u], 0)
    return begin, begin + span


def norm_kernel(parts, *refs):
    _, copy_index = place(parts)
    windows = lax.axis_size("dp")
    copies = windows // parts
    part_refs, refs = refs[:windows][::-1], refs[windows:]
    piece_refs, refs = refs[:parts], refs[parts:]
    rows_out, normed_out, stack_out, encoded, sems = refs
    moves = stacked(parts, piece_refs, stack_out, sems, 0)
    start_all(moves)
    rows = W * parts
    for copy in range(copies):
        total = part_refs[copy][...].astype(F32)
        for step in range(1, parts):
            total += part_refs[step * copies + copy][...].astype(F32)
        at = pl.multiple_of((copy_index ^ copy) * rows, rows)
        encoded[pl.ds(at, rows), :] = total.astype(BF16)
    values = jnp.dot(frame_order(parts, copies), encoded[...], preferred_element_type=F32)
    rows_out[...] = values.astype(BF16)
    mean = jnp.mean(values, axis=-1, keepdims=True)
    centered = values - mean
    variance = jnp.mean(centered * centered, axis=-1, keepdims=True)
    normed_out[...] = (centered * lax.rsqrt(variance + EPS_NORM)).astype(BF16)
    wait_all(moves)


def mask_kernel(windows, group, slots_ref, starts_ref, lengths_ref, rows_ref, rows_out, keys_out, valid_out):
    begin, end = bounds(lax.axis_index("dp"), slots_ref, starts_ref, lengths_ref)
    sample = samples(iota(windows * W, 1, 0), windows, group) + lax.axis_index("seq") * (W * SPAN)
    valid = (sample >= begin) & (sample < end)
    rows_out[...] = jnp.where(valid, rows_ref[...].astype(F32), 0.0).astype(BF16)
    valid_out[...] = valid.astype(F32)
    keys = samples(iota(group, windows * W, 1), windows, group) + iota(group, windows * W, 0) * (W * SPAN)
    keys_out[...] = ((keys >= begin) & (keys < end)).astype(F32)


def attention_kernel(parts, windows, group, keys_ref, *refs):
    _, copy_index = place(parts)
    plane = lax.axis_index("seq")
    copies = windows // parts
    normed_refs, refs = refs[:group], refs[group:]
    stack_refs, refs = refs[:copies], refs[copies:]
    weight_refs, refs = refs[:parts], refs[parts:]
    outs_refs, (stack_out, pieces, sems) = refs[:group], refs[group:]
    moves = stacked(parts, weight_refs, stack_out, sems, 0)
    start_all(moves)
    keys = [keys_ref[pl.ds(plane ^ step, 1), :] for step in range(group)]
    valid = jnp.concatenate(keys, axis=1) > 0.5
    local = normed_refs[0].shape[0]
    depth = pieces.shape[2]
    for step in range(group):
        for piece in range(windows):
            pieces[piece, step * local : (step + 1) * local, :] = normed_refs[step][
                :, piece * depth : (piece + 1) * depth
            ]
    mixed = 0.0
    for step in range(copies):
        slot = copy_index ^ step
        normed = jnp.concatenate([pieces[piece * copies + slot] for piece in range(parts)], axis=1)
        weights = stack_refs[step][...].reshape(parts * depth, stack_refs[step].shape[2])
        mixed += jnp.dot(normed, weights, preferred_element_type=F32)
    mixed = mixed.astype(BF16)
    width = mixed.shape[1] // 3
    scale = HEAD_DIM ** (-0.5)
    for head in range(width // HEAD_DIM):
        at = head * HEAD_DIM
        query = mixed[:, at : at + HEAD_DIM]
        key = mixed[:, width + at : width + at + HEAD_DIM]
        value = mixed[:, 2 * width + at : 2 * width + at + HEAD_DIM]
        scores = lax.dot_general(query, key, (((1,), (1,)), ((), ())), preferred_element_type=F32) * scale
        masked = jnp.where(valid, scores, MASKED)
        peak = jnp.max(masked, axis=1, keepdims=True)
        weight = jnp.where(valid, jnp.exp(masked - peak), 0.0)
        total = jnp.sum(weight, axis=1, keepdims=True)
        summed = jnp.dot(weight.astype(BF16), value, preferred_element_type=F32)
        context = (summed / total).astype(BF16)
        for step in range(group):
            outs_refs[step][:, at : at + HEAD_DIM] = context[step * local : (step + 1) * local]
    wait_all(moves)


def output_kernel(parts, windows, group, valid_ref, *refs):
    context_refs, refs = refs[:group], refs[group:]
    stack_refs, refs = refs[: windows // parts], refs[windows // parts :]
    out_ref, context, pieces = refs
    _, copy_index = place(parts)
    copies = windows // parts
    plane = lax.axis_index("seq")
    head_width = context_refs[0].shape[1]
    for step in range(group):
        at = pl.multiple_of((plane ^ step) * head_width, LANES)
        context[:, pl.ds(at, head_width)] = context_refs[step][...]
    ordered = context[...]
    for step in range(copies):
        slot = copy_index ^ step
        for piece in range(parts):
            pieces[piece * copies + slot] = jnp.dot(
                ordered, stack_refs[step][piece], preferred_element_type=F32
            )
    result = jnp.concatenate([pieces[d] for d in range(windows)], axis=1)
    out_ref[...] = jnp.where(valid_ref[...] > 0.5, result, 0.0).astype(BF16)


def on_device(
    audio, starts, lengths, slots, conv1_weight, conv2_weight, proj_weight, qkv_weight, out_weight
):
    streams = audio.shape[0]
    windows = lax.axis_size("dp")
    group = lax.axis_size("seq")
    parts = math.gcd(windows, BANDS)
    copies = windows // parts
    assert streams == windows and all(count & (count - 1) == 0 for count in (parts, copies, group))
    share = BANDS // parts
    width = 4 * share + 4
    channels = conv1_weight.shape[1]
    features = proj_weight.shape[1]
    head_width = features // group
    local = windows * W
    rows = JS * streams
    n = parts * streams
    outs = 2 * share + 1
    scale = max(1, windows * group // 32)

    route = [(i, i + 1) for i in range(windows * group - 1)]
    rim = lax.ppermute(audio[:, audio.shape[1] - RIM :], ("dp", "seq"), route)

    def to_part(block, step):
        pairs = [(p * copies + c, (p ^ step) * copies + c) for p in range(parts) for c in range(copies)]
        return lax.ppermute(block, "dp", pairs)

    def to_copy(block, step):
        pairs = [(p * copies + c, p * copies + (c ^ step)) for p in range(parts) for c in range(copies)]
        return lax.ppermute(block, "dp", pairs)

    def to_window(block, step):
        return lax.ppermute(block, "dp", [(i, i ^ step) for i in range(windows)])

    def to_plane(block, step):
        return lax.ppermute(block, "seq", [(i, i ^ step) for i in range(group)])

    proj_all = [proj_weight] + [to_copy(proj_weight, step) for step in range(1, copies)]

    table = jnp.asarray(spectrum_table(N_FFT))
    mix_piece = jax.ShapeDtypeStruct((qkv_weight.shape[0], 3 * head_width), BF16)
    *mel_all, mix = pl.pallas_call(
        functools.partial(mel_kernel, parts, group),
        out_shape=tuple([jax.ShapeDtypeStruct((rows, LANES), BF16)] * parts + [mix_piece]),
        in_specs=[anywhere(), vmem()] + [anywhere()] * 3,
        out_specs=tuple([vmem()] * (parts + 1)),
        scratch_shapes=[
            pltpu.VMEM((streams, RIM + audio.shape[1]), F32),
            pltpu.VMEM(table.shape, F32),
            pltpu.VMEM((parts, rows, LANES), BF16),
            pltpu.SMEM((streams,), jnp.int32),
            pltpu.SemaphoreType.DMA((6,)),
        ],
        compiler_params=params(60),
        cost_estimate=cost(1e10, 2e6),
        name="log_mel",
    )(slots, rim, audio, table, qkv_weight)
    near = [to_part(out_weight, step) for step in range(1, parts - 1)]
    mel_all, proj_all, near = lax.optimization_barrier((mel_all, proj_all, near))
    mel_all = [mel_all[0]] + [to_part(mel_all[step], step) for step in range(1, parts)]
    mix_all = [mix] + [to_part(mix, step) for step in range(1, parts)]

    block = jax.ShapeDtypeStruct((local, features), BF16)
    partials = pl.pallas_call(
        functools.partial(conv_kernel, parts, width),
        out_shape=tuple([jax.ShapeDtypeStruct((W * parts, features), BF16)] * windows),
        in_specs=[vmem()] + [anywhere()] * 2 + [vmem()] * (parts - 1) + [anywhere()] * copies,
        out_specs=tuple([vmem()] * windows),
        scratch_shapes=[
            pltpu.VMEM((parts, rows, LANES), F32),
            pltpu.VMEM((rows, LANES), BF16),
            pltpu.VMEM((LANES, outs * channels), BF16),
            pltpu.VMEM((JS * n, outs * channels), BF16),
            pltpu.VMEM((W * n, outs * channels), BF16),
            pltpu.VMEM((W * n, share * channels), BF16),
            pltpu.VMEM(conv2_weight.shape, BF16),
            pltpu.VMEM((copies,) + proj_weight.shape, BF16),
            pltpu.VMEM((features // LANES, W * n, LANES), F32),
            pltpu.SemaphoreType.DMA((2 + copies,)),
        ],
        compiler_params=params(min(40 + 4 * scale, 56)),
        cost_estimate=cost(2e9, 4e6),
        name="conv",
    )(conv1_weight, conv2_weight, *mel_all, *proj_all)
    partials = [to_window(partials[step], step) for step in reversed(range(1, windows))] + [partials[0]]

    ordered, normed, stack = pl.pallas_call(
        functools.partial(norm_kernel, parts),
        out_shape=(block, block, jax.ShapeDtypeStruct((parts,) + mix_piece.shape, BF16)),
        in_specs=[vmem()] * windows + [anywhere()] * parts,
        out_specs=(vmem(), vmem(), vmem()),
        scratch_shapes=[pltpu.VMEM((local, features), BF16), pltpu.SemaphoreType.DMA((parts,))],
        compiler_params=params(min(12 * scale, 32)),
        cost_estimate=cost(1e8, 1e6),
        name="layer_norm",
    )(*partials, *mix_all)
    mix_stacks = [stack] + [to_copy(stack, step) for step in range(1, copies)]
    regrouped, keys, valid = pl.pallas_call(
        functools.partial(mask_kernel, windows, group),
        out_shape=(
            block,
            jax.ShapeDtypeStruct((group, local), F32),
            jax.ShapeDtypeStruct((local, 1), F32),
        ),
        in_specs=[smem()] * 3 + [vmem()],
        out_specs=(vmem(), vmem(), vmem()),
        compiler_params=params(min(8 * scale, 32)),
        cost_estimate=cost(1e8, 1e6),
        name="mask",
    )(slots, starts, lengths, ordered)
    normed, out_here = lax.optimization_barrier((normed, out_weight))
    normed = [normed]
    for step in range(1, group):
        high = 1 << (step.bit_length() - 1)
        normed.append(to_plane(normed[high] if step > high else normed[0], step - high if step > high else high))
    out_all = [out_here] + near + [to_part(out_here, parts - 1)]

    *context, stack = pl.pallas_call(
        functools.partial(attention_kernel, parts, windows, group),
        out_shape=tuple(
            [jax.ShapeDtypeStruct((local, head_width), BF16)] * group
            + [jax.ShapeDtypeStruct((parts,) + out_weight.shape, BF16)]
        ),
        in_specs=[vmem()] * (1 + group + copies) + [anywhere()] * parts,
        out_specs=tuple([vmem()] * (group + 1)),
        scratch_shapes=[
            pltpu.VMEM((windows, group * local, qkv_weight.shape[0]), BF16),
            pltpu.SemaphoreType.DMA((parts,)),
        ],
        compiler_params=params(min(16 * scale, 48)),
        cost_estimate=cost(1e9, 2e6),
        name="attention",
    )(keys, *normed, *mix_stacks, *out_all)
    context = [context[0]] + [to_plane(context[step], step) for step in range(1, group)]
    out_stacks = [stack] + [to_copy(stack, step) for step in range(1, copies)]

    attended = pl.pallas_call(
        functools.partial(output_kernel, parts, windows, group),
        out_shape=block,
        in_specs=[vmem()] * (1 + group + copies),
        out_specs=vmem(),
        scratch_shapes=[
            pltpu.VMEM((local, features), BF16),
            pltpu.VMEM((windows, local, out_weight.shape[1]), F32),
        ],
        compiler_params=params(min(12 * scale, 32)),
        cost_estimate=cost(1e8, 3e6),
        name="output",
    )(valid, *context, *out_stacks)
    shape = (1, windows, 1, W, features)
    return (regrouped.reshape(shape), attended.reshape(shape))


def solution(mesh):
    in_specs = (
        P(None, ("dp", "seq")),
        P(),
        P(),
        P(),
        P(),
        P(),
        P("dp", None),
        P("dp", None),
        P(None, "dp"),
    )
    out_specs = (P("dp", None, "seq", None, None), P("dp", None, "seq", None, None))
    return jax.shard_map(
        on_device, mesh=mesh, in_specs=in_specs, out_specs=out_specs, check_vma=False
    )
```

```python
import functools
import math

import jax
import jax.numpy as jnp
import numpy as np
from jax import lax
from jax.experimental import pallas as pl
from jax.experimental.pallas import tpu as pltpu
from jax.sharding import PartitionSpec as P

HEADS = 8
HEAD_DIM = 128
MELS = 80
BANDS = MELS // 4
N_FFT = 512
HOP = 160
W = 8
RIM = 1024
SPAN = 4 * HOP
JS = W + 1
LANES = 128
SAMPLE_RATE = 16000.0
EPS_LOG = 1e-06
EPS_NORM = 1e-05
MASKED = -1e30
F32 = jnp.float32
BF16 = jnp.bfloat16
MIB = 1 << 20


def mel_table(size, bands):
    count = size // 2 + 1
    highest = 2595.0 * math.log10(1.0 + SAMPLE_RATE / 1400.0)
    points = np.linspace(0.0, highest, bands + 2)
    edges = 700.0 * (10.0 ** (points / 2595.0) - 1.0)
    edges[0] = 0.0
    edges[-1] = SAMPLE_RATE / 2.0
    frequency = np.arange(count) * (SAMPLE_RATE / size)
    lower = edges[:-2][None, :]
    middle = edges[1:-1][None, :]
    upper = edges[2:][None, :]
    rising = (frequency[:, None] - lower) / (middle - lower)
    falling = (upper - frequency[:, None]) / (upper - middle)
    return np.maximum(0.0, np.minimum(rising, falling)).astype(np.float32)


def spectrum_table(size):
    sample = np.arange(size)
    phase = sample[:, None] * np.arange(size // 2)[None, :] % size
    angle = phase * (2.0 * math.pi / size)
    window = 0.5 - 0.5 * np.cos(sample * (2.0 * math.pi / size))
    both = np.concatenate([np.cos(angle), np.sin(angle)], axis=1) * window[:, None]
    filters = np.zeros((size, LANES))
    filters[: size // 2, :MELS] = mel_table(size, MELS)[: size // 2]
    return np.concatenate([both, filters], axis=1).astype(np.float32)


def vmem():
    return pl.BlockSpec(memory_space=pltpu.VMEM)


def smem():
    return pl.BlockSpec(memory_space=pltpu.SMEM)


def anywhere():
    return pl.BlockSpec(memory_space=pl.ANY)


def params(mib):
    return pltpu.CompilerParams(vmem_limit_bytes=mib * MIB)


def cost(flops, moved):
    return pl.CostEstimate(flops=int(flops), bytes_accessed=int(moved), transcendentals=0)


def place(parts):
    mine = lax.axis_index("dp")
    copies = lax.axis_size("dp") // parts
    return mine // copies, mine % copies


def start_all(copies):
    for copy in copies:
        copy.start()


def wait_all(copies):
    for copy in copies:
        copy.wait()


def iota(rows, columns, axis):
    return lax.broadcasted_iota(jnp.int32, (rows, columns), axis)


def quotient(index, step, count):
    result = jnp.zeros_like(index)
    for i in range(1, count):
        result += (index >= i * step).astype(jnp.int32)
    return result


def one_hot(target, count):
    return (iota(target.shape[0], count, 1) == target).astype(F32).astype(BF16)


def frame_order(parts, copies):
    count = parts * copies * W
    row = iota(count, 1, 0)
    k = quotient(row, W, parts * copies)
    p = quotient(k, copies, parts)
    return one_hot((k - p * copies) * W * parts + (row - k * W) * parts + p, count)


def samples(index, windows, group):
    return (index + quotient(index, W, windows) * (group - 1) * W) * SPAN


def mix_columns(group, qkv_ref, mix_out, sems):
    features = qkv_ref.shape[1] // 3
    width = features // group
    first = pl.multiple_of(lax.axis_index("seq") * width, LANES)
    return [
        pltpu.make_async_copy(
            qkv_ref.at[:, pl.ds(kind * features + first, width)],
            mix_out.at[:, pl.ds(kind * width, width)],
            sems.at[kind],
        )
        for kind in range(3)
    ]


def banded_weights(width, conv1_ref, banded_out):
    taps, channels = conv1_ref.shape
    row = lax.broadcasted_iota(jnp.int32, (LANES, taps), 0)
    tap = lax.broadcasted_iota(jnp.int32, (LANES, taps), 1)
    line = (tap >= 3).astype(jnp.int32) + (tap >= 6).astype(jnp.int32)
    target = line * (width - 3) + tap + 1
    weight = conv1_ref[...]
    for g in range(banded_out.shape[1] // channels):
        select = (row == target + 2 * g).astype(F32).astype(BF16)
        banded_out[:, g * channels : (g + 1) * channels] = jnp.dot(
            select, weight, preferred_element_type=F32
        ).astype(BF16)


def mel_kernel(parts, group, slots_here, rim_ref, audio_ref, table_ref, qkv_ref, *refs):
    outs_refs, (mix_out, ext, table, blocks, slots_ref, sems) = refs[:parts], refs[parts:]
    load_slots = pltpu.make_async_copy(slots_here, slots_ref, sems.at[5])
    load_slots.start()
    load_audio = pltpu.make_async_copy(audio_ref, ext.at[:, pl.ds(RIM, audio_ref.shape[1])], sems.at[3])
    load_table = pltpu.make_async_copy(table_ref, table, sems.at[4])
    load_audio.start()
    load_table.start()
    pieces = mix_columns(group, qkv_ref, mix_out, sems)
    start_all(pieces)
    streams = audio_ref.shape[0]
    rows = JS * streams
    ext[:, :RIM] = rim_ref[...]
    load_audio.wait()
    phases = []
    for phase in range(4):
        start = HOP * phase + 32
        base, shift = start // LANES * LANES, start % LANES
        length = N_FFT + (LANES if shift else 0)
        block = jnp.concatenate(
            [ext[:, SPAN * j + base : SPAN * j + base + length] for j in range(JS)], axis=0
        )
        if shift:
            block = pltpu.roll(block, length - shift, 1)[:, :N_FFT]
        phases.append(block)
    frames = jnp.concatenate(phases, axis=0)
    load_table.wait()
    spectrum = jnp.dot(
        frames, table[:, :N_FFT], precision=lax.Precision.HIGHEST, preferred_element_type=F32
    )
    half = N_FFT // 2
    real, imag = spectrum[:, :half], spectrum[:, half:]
    power = real * real + imag * imag
    mel_power = jnp.dot(
        power, table[:half, N_FFT:], precision=lax.Precision.HIGHEST, preferred_element_type=F32
    )
    load_slots.wait()
    column = iota(1, rows, 1)
    early = quotient(column, streams, JS)
    target = jnp.zeros((1, rows), jnp.int32)
    for u in range(streams):
        target = jnp.where(column - early * streams == u, early * streams + slots_ref[u], target)
    routing = (target == iota(rows, rows, 0)).astype(F32).astype(BF16)
    log_mel = jnp.log(mel_power + EPS_LOG)
    share = BANDS // parts
    width = 4 * share + 4
    lane = iota(rows, LANES, 1)
    by_phase = [log_mel[phase * rows : (phase + 1) * rows] for phase in range(4)]

    def next_four(frames):
        return jnp.concatenate([frames[streams:], jnp.zeros((streams, LANES), F32)], axis=0)

    taps = [by_phase[1], by_phase[2], by_phase[3], next_four(by_phase[0]), next_four(by_phase[1])]
    for part in range(parts):
        first = 4 * share * part - 4
        block = jnp.zeros((rows, LANES), F32)
        for delta, frames in enumerate(taps):
            band = lane - width * delta + first
            here = (lane >= width * delta) & (lane < width * (delta + 1)) & (band >= 0) & (band < MELS)
            shift = (width * delta - first) % LANES
            block = jnp.where(here, pltpu.roll(frames, shift, 1) if shift else frames, block)
        blocks[part] = jnp.dot(routing, block.astype(BF16), preferred_element_type=F32).astype(BF16)
    mine, _ = place(parts)
    for step in range(parts):
        outs_refs[step][...] = blocks[mine ^ step]
    wait_all(pieces)


def stacked(parts, pieces, stack_out, sems, base):
    part, _ = place(parts)
    return [
        pltpu.make_async_copy(pieces[step], stack_out.at[part ^ step], sems.at[base + step])
        for step in range(parts)
    ]


def conv_kernel(parts, width, conv1_ref, conv2_ref, *refs):
    part, copy_index = place(parts)
    mine = lax.axis_index("dp")
    windows = lax.axis_size("dp")
    copies = windows // parts
    mel_refs, refs = refs[:parts], refs[parts:]
    proj_refs, refs = refs[:copies], refs[copies:]
    outs_refs, refs = refs[:windows], refs[windows:]
    mel, own, banded_ref, even, odd, second, conv2, proj, partial, sems = refs
    load_own = pltpu.make_async_copy(mel_refs[0], own, sems.at[1 + copies])
    load_own.start()
    load_conv2 = pltpu.make_async_copy(conv2_ref, conv2, sems.at[0])
    load_conv2.start()
    loads = []
    for step in range(copies):
        slot = copy_index ^ step
        loads.append(pltpu.make_async_copy(proj_refs[step], proj.at[slot], sems.at[1 + step]))
    start_all(loads)
    banded_weights(width, conv1_ref, banded_ref)
    streams = mel_refs[0].shape[0] // JS
    n = parts * streams
    load_own.wait()
    mel[part] = own[...].astype(F32)
    for step in range(1, parts):
        mel[part ^ step] = mel_refs[step][...].astype(F32)
    evens = jnp.concatenate(
        [mel[p, j * streams : (j + 1) * streams, :] for j in range(JS) for p in range(parts)], axis=0
    )
    odds = pltpu.roll(evens[: W * n], LANES - 2 * width, 1).astype(BF16)
    evens = evens.astype(BF16)
    channels = conv2.shape[1]
    outs = banded_ref.shape[1] // channels
    for g in range(outs):
        lanes = slice(g * channels, (g + 1) * channels)
        weight = banded_ref[:, lanes]
        even[:, lanes] = jax.nn.relu(jnp.dot(evens, weight, preferred_element_type=F32)).astype(BF16)
        odd[:, lanes] = jax.nn.relu(jnp.dot(odds, weight, preferred_element_type=F32)).astype(BF16)

    load_conv2.wait()
    for h in range((outs - 1) // 2):
        lanes = slice(2 * h * channels, (2 * h + 3) * channels)
        depth = 3 * channels
        total = jnp.dot(even[: W * n, lanes], conv2[:depth], preferred_element_type=F32)
        total += jnp.dot(odd[:, lanes], conv2[depth : 2 * depth], preferred_element_type=F32)
        total += jnp.dot(even[n:, lanes], conv2[2 * depth :], preferred_element_type=F32)
        second[:, h * channels : (h + 1) * channels] = jax.nn.relu(total).astype(BF16)
    wait_all(loads)
    weights = proj[...].reshape(second.shape[1], proj.shape[2])
    sums = jnp.dot(second[...], weights, preferred_element_type=F32)
    for block in range(partial.shape[0]):
        partial[block] = sums[:, block * LANES : (block + 1) * LANES]
    for step in range(windows):
        for block in range(partial.shape[0]):
            rows = partial[block, pl.ds(mine ^ step, W * parts, stride=streams), :]
            outs_refs[step][:, block * LANES : (block + 1) * LANES] = rows.astype(BF16)


def bounds(row, slots_ref, starts_ref, lengths_ref):
    begin, span = jnp.int32(0), jnp.int32(0)
    for u in range(slots_ref.shape[0]):
        chosen = slots_ref[u] == row
        begin = begin + jnp.where(chosen, starts_ref[u], 0)
        span = span + jnp.where(chosen, lengths_ref[u], 0)
    return begin, begin + span


def norm_kernel(parts, *refs):
    _, copy_index = place(parts)
    windows = lax.axis_size("dp")
    copies = windows // parts
    part_refs, refs = refs[:windows][::-1], refs[windows:]
    piece_refs, refs = refs[:parts], refs[parts:]
    rows_out, normed_out, first_out, second_out, stack_out, encoded, sems = refs
    moves = stacked(parts, piece_refs, stack_out, sems, 0)
    start_all(moves)
    rows = W * parts
    for copy in range(copies):
        total = part_refs[copy][...].astype(F32)
        for step in range(1, parts):
            total += part_refs[step * copies + copy][...].astype(F32)
        at = pl.multiple_of((copy_index ^ copy) * rows, rows)
        encoded[pl.ds(at, rows), :] = total.astype(BF16)
    values = jnp.dot(frame_order(parts, copies), encoded[...], preferred_element_type=F32)
    rows_out[...] = values.astype(BF16)
    mean = jnp.mean(values, axis=-1, keepdims=True)
    centered = values - mean
    variance = jnp.mean(centered * centered, axis=-1, keepdims=True)
    normed = (centered * lax.rsqrt(variance + EPS_NORM)).astype(BF16)
    normed_out[...] = normed
    first_out[...] = normed[: normed.shape[0] // 2]
    second_out[...] = normed[normed.shape[0] // 2 :]
    wait_all(moves)


def mask_kernel(windows, group, slots_ref, starts_ref, lengths_ref, rows_ref, rows_out, keys_out, valid_out):
    begin, end = bounds(lax.axis_index("dp"), slots_ref, starts_ref, lengths_ref)
    sample = samples(iota(windows * W, 1, 0), windows, group) + lax.axis_index("seq") * (W * SPAN)
    valid = (sample >= begin) & (sample < end)
    rows_out[...] = jnp.where(valid, rows_ref[...].astype(F32), 0.0).astype(BF16)
    valid_out[...] = valid.astype(F32)
    keys = samples(iota(group, windows * W, 1), windows, group) + iota(group, windows * W, 0) * (W * SPAN)
    keys_out[...] = ((keys >= begin) & (keys < end)).astype(F32)


def attention_kernel(parts, windows, group, keys_ref, *refs):
    _, copy_index = place(parts)
    plane = lax.axis_index("seq")
    copies = windows // parts
    normed_refs, refs = refs[: 2 * group - 2], refs[2 * group - 2 :]
    stack_refs, refs = refs[:copies], refs[copies:]
    weight_refs, refs = refs[:parts], refs[parts:]
    outs_refs, (stack_out, pieces, sems) = refs[:group], refs[group:]
    moves = stacked(parts, weight_refs, stack_out, sems, 0)
    start_all(moves)
    keys = [keys_ref[pl.ds(plane ^ step, 1), :] for step in range(group)]
    valid = jnp.concatenate(keys, axis=1) > 0.5
    local = normed_refs[0].shape[0]
    depth = pieces.shape[2]
    at = 0
    for ref in normed_refs:
        for piece in range(windows):
            pieces[piece, at : at + ref.shape[0], :] = ref[:, piece * depth : (piece + 1) * depth]
        at += ref.shape[0]
    mixed = 0.0
    for step in range(copies):
        slot = copy_index ^ step
        normed = jnp.concatenate([pieces[piece * copies + slot] for piece in range(parts)], axis=1)
        weights = stack_refs[step][...].reshape(parts * depth, stack_refs[step].shape[2])
        mixed += jnp.dot(normed, weights, preferred_element_type=F32)
    mixed = mixed.astype(BF16)
    width = mixed.shape[1] // 3
    scale = HEAD_DIM ** (-0.5)
    for head in range(width // HEAD_DIM):
        at = head * HEAD_DIM
        query = mixed[:, at : at + HEAD_DIM]
        key = mixed[:, width + at : width + at + HEAD_DIM]
        value = mixed[:, 2 * width + at : 2 * width + at + HEAD_DIM]
        scores = lax.dot_general(query, key, (((1,), (1,)), ((), ())), preferred_element_type=F32) * scale
        masked = jnp.where(valid, scores, MASKED)
        peak = jnp.max(masked, axis=1, keepdims=True)
        weight = jnp.where(valid, jnp.exp(masked - peak), 0.0)
        total = jnp.sum(weight, axis=1, keepdims=True)
        summed = jnp.dot(weight.astype(BF16), value, preferred_element_type=F32)
        context = (summed / total).astype(BF16)
        for step in range(group):
            outs_refs[step][:, at : at + HEAD_DIM] = context[step * local : (step + 1) * local]
    wait_all(moves)


def output_kernel(parts, windows, group, valid_ref, *refs):
    context_refs, refs = refs[:group][::-1], refs[group:]
    stack_refs, refs = refs[: windows // parts], refs[windows // parts :]
    out_ref, context, pieces = refs
    _, copy_index = place(parts)
    copies = windows // parts
    plane = lax.axis_index("seq")
    head_width = context_refs[0].shape[1]
    for step in range(group):
        at = pl.multiple_of((plane ^ step) * head_width, LANES)
        context[:, pl.ds(at, head_width)] = context_refs[step][...]
    ordered = context[...]
    for step in range(copies):
        slot = copy_index ^ step
        for piece in range(parts):
            pieces[piece * copies + slot] = jnp.dot(
                ordered, stack_refs[step][piece], preferred_element_type=F32
            )
    result = jnp.concatenate([pieces[d] for d in range(windows)], axis=1)
    out_ref[...] = jnp.where(valid_ref[...] > 0.5, result, 0.0).astype(BF16)


def on_device(
    audio, starts, lengths, slots, conv1_weight, conv2_weight, proj_weight, qkv_weight, out_weight
):
    streams = audio.shape[0]
    windows = lax.axis_size("dp")
    group = lax.axis_size("seq")
    parts = math.gcd(windows, BANDS)
    copies = windows // parts
    assert streams == windows and all(count & (count - 1) == 0 for count in (parts, copies, group))
    share = BANDS // parts
    width = 4 * share + 4
    channels = conv1_weight.shape[1]
    features = proj_weight.shape[1]
    head_width = features // group
    local = windows * W
    rows = JS * streams
    n = parts * streams
    outs = 2 * share + 1
    scale = max(1, windows * group // 32)

    route = [(i, i + 1) for i in range(windows * group - 1)]
    rim = lax.ppermute(audio[:, audio.shape[1] - RIM :], ("dp", "seq"), route)

    def to_part(block, step):
        pairs = [(p * copies + c, (p ^ step) * copies + c) for p in range(parts) for c in range(copies)]
        return lax.ppermute(block, "dp", pairs)

    def to_copy(block, step):
        pairs = [(p * copies + c, p * copies + (c ^ step)) for p in range(parts) for c in range(copies)]
        return lax.ppermute(block, "dp", pairs)

    def to_window(block, step):
        return lax.ppermute(block, "dp", [(i, i ^ step) for i in range(windows)])

    def to_plane(block, step):
        return lax.ppermute(block, "seq", [(i, i ^ step) for i in range(group)])

    proj_all = [proj_weight] + [to_copy(proj_weight, step) for step in range(1, copies)]

    table = jnp.asarray(spectrum_table(N_FFT))
    mix_piece = jax.ShapeDtypeStruct((qkv_weight.shape[0], 3 * head_width), BF16)
    *mel_all, mix = pl.pallas_call(
        functools.partial(mel_kernel, parts, group),
        out_shape=tuple([jax.ShapeDtypeStruct((rows, LANES), BF16)] * parts + [mix_piece]),
        in_specs=[anywhere(), vmem()] + [anywhere()] * 3,
        out_specs=tuple([vmem()] * (parts + 1)),
        scratch_shapes=[
            pltpu.VMEM((streams, RIM + audio.shape[1]), F32),
            pltpu.VMEM(table.shape, F32),
            pltpu.VMEM((parts, rows, LANES), BF16),
            pltpu.SMEM((streams,), jnp.int32),
            pltpu.SemaphoreType.DMA((6,)),
        ],
        compiler_params=params(60),
        cost_estimate=cost(1e10, 2e6),
        name="log_mel",
    )(slots, rim, audio, table, qkv_weight)
    near = [to_part(out_weight, step) for step in range(1, parts - 1)]
    mel_all, proj_all = lax.optimization_barrier((mel_all, proj_all))
    mel_all = [mel_all[0]] + [to_part(mel_all[step], step) for step in range(1, parts)]
    mel_all, near = lax.optimization_barrier((mel_all, near))
    mix_all = [mix] + [to_part(mix, step) for step in range(1, parts)]

    block = jax.ShapeDtypeStruct((local, features), BF16)
    partials = pl.pallas_call(
        functools.partial(conv_kernel, parts, width),
        out_shape=tuple([jax.ShapeDtypeStruct((W * parts, features), BF16)] * windows),
        in_specs=[vmem()] + [anywhere()] * 2 + [vmem()] * (parts - 1) + [anywhere()] * copies,
        out_specs=tuple([vmem()] * windows),
        scratch_shapes=[
            pltpu.VMEM((parts, rows, LANES), F32),
            pltpu.VMEM((rows, LANES), BF16),
            pltpu.VMEM((LANES, outs * channels), BF16),
            pltpu.VMEM((JS * n, outs * channels), BF16),
            pltpu.VMEM((W * n, outs * channels), BF16),
            pltpu.VMEM((W * n, share * channels), BF16),
            pltpu.VMEM(conv2_weight.shape, BF16),
            pltpu.VMEM((copies,) + proj_weight.shape, BF16),
            pltpu.VMEM((features // LANES, W * n, LANES), F32),
            pltpu.SemaphoreType.DMA((2 + copies,)),
        ],
        compiler_params=params(min(40 + 4 * scale, 56)),
        cost_estimate=cost(2e9, 4e6),
        name="conv",
    )(conv1_weight, conv2_weight, *mel_all, *proj_all)
    partials = [to_window(partials[step], step) for step in reversed(range(1, windows))] + [partials[0]]

    half = jax.ShapeDtypeStruct((local // 2, features), BF16)
    ordered, normed, *halves, stack = pl.pallas_call(
        functools.partial(norm_kernel, parts),
        out_shape=(block, block, half, half, jax.ShapeDtypeStruct((parts,) + mix_piece.shape, BF16)),
        in_specs=[vmem()] * windows + [anywhere()] * parts,
        out_specs=tuple([vmem()] * 5),
        scratch_shapes=[pltpu.VMEM((local, features), BF16), pltpu.SemaphoreType.DMA((parts,))],
        compiler_params=params(min(12 * scale, 32)),
        cost_estimate=cost(1e8, 1e6),
        name="layer_norm",
    )(*partials, *mix_all)
    mix_stacks = [stack] + [to_copy(stack, step) for step in range(1, copies)]
    regrouped, keys, valid = pl.pallas_call(
        functools.partial(mask_kernel, windows, group),
        out_shape=(
            block,
            jax.ShapeDtypeStruct((group, local), F32),
            jax.ShapeDtypeStruct((local, 1), F32),
        ),
        in_specs=[smem()] * 3 + [vmem()],
        out_specs=(vmem(), vmem(), vmem()),
        compiler_params=params(min(8 * scale, 32)),
        cost_estimate=cost(1e8, 1e6),
        name="mask",
    )(slots, starts, lengths, ordered)
    normed, out_here = lax.optimization_barrier((normed, out_weight))
    by_plane = {0: [normed], 1: [to_plane(normed, 1)]}
    for step in range(2, group):
        high = 1 << (step.bit_length() - 1)
        source = halves if step == high else by_plane[high]
        by_plane[step] = [to_plane(piece, high if step == high else step - high) for piece in source]
    normed = [piece for step in range(group) for piece in by_plane[step]]
    out_all = [out_here] + near + [to_part(out_here, parts - 1)]

    *context, stack = pl.pallas_call(
        functools.partial(attention_kernel, parts, windows, group),
        out_shape=tuple(
            [jax.ShapeDtypeStruct((local, head_width), BF16)] * group
            + [jax.ShapeDtypeStruct((parts,) + out_weight.shape, BF16)]
        ),
        in_specs=[vmem()] * (1 + len(normed) + copies) + [anywhere()] * parts,
        out_specs=tuple([vmem()] * (group + 1)),
        scratch_shapes=[
            pltpu.VMEM((windows, group * local, qkv_weight.shape[0]), BF16),
            pltpu.SemaphoreType.DMA((parts,)),
        ],
        compiler_params=params(min(16 * scale, 48)),
        cost_estimate=cost(1e9, 2e6),
        name="attention",
    )(keys, *normed, *mix_stacks, *out_all)
    context = [to_plane(context[step], step) for step in reversed(range(1, group))] + [context[0]]
    out_stacks = [stack] + [to_copy(stack, step) for step in range(1, copies)]

    attended = pl.pallas_call(
        functools.partial(output_kernel, parts, windows, group),
        out_shape=block,
        in_specs=[vmem()] * (1 + group + copies),
        out_specs=vmem(),
        scratch_shapes=[
            pltpu.VMEM((local, features), BF16),
            pltpu.VMEM((windows, local, out_weight.shape[1]), F32),
        ],
        compiler_params=params(min(12 * scale, 32)),
        cost_estimate=cost(1e8, 3e6),
        name="output",
    )(valid, *context, *out_stacks)
    shape = (1, windows, 1, W, features)
    return (regrouped.reshape(shape), attended.reshape(shape))


def solution(mesh):
    in_specs = (
        P(None, ("dp", "seq")),
        P(),
        P(),
        P(),
        P(),
        P(),
        P("dp", None),
        P("dp", None),
        P(None, "dp"),
    )
    out_specs = (P("dp", None, "seq", None, None), P("dp", None, "seq", None, None))
    return jax.shard_map(
        on_device, mesh=mesh, in_specs=in_specs, out_specs=out_specs, check_vma=False
    )
```

```python
import functools
import math

import jax
import jax.numpy as jnp
import numpy as np
from jax import lax
from jax.experimental import pallas as pl
from jax.experimental.pallas import tpu as pltpu
from jax.sharding import PartitionSpec as P

HEADS = 8
HEAD_DIM = 128
MELS = 80
BANDS = MELS // 4
N_FFT = 512
HOP = 160
W = 8
RIM = 1024
SPAN = 4 * HOP
JS = W + 1
LANES = 128
SAMPLE_RATE = 16000.0
EPS_LOG = 1e-06
EPS_NORM = 1e-05
MASKED = -1e30
F32 = jnp.float32
BF16 = jnp.bfloat16
MIB = 1 << 20


def mel_table(size, bands):
    count = size // 2 + 1
    highest = 2595.0 * math.log10(1.0 + SAMPLE_RATE / 1400.0)
    points = np.linspace(0.0, highest, bands + 2)
    edges = 700.0 * (10.0 ** (points / 2595.0) - 1.0)
    edges[0] = 0.0
    edges[-1] = SAMPLE_RATE / 2.0
    frequency = np.arange(count) * (SAMPLE_RATE / size)
    lower = edges[:-2][None, :]
    middle = edges[1:-1][None, :]
    upper = edges[2:][None, :]
    rising = (frequency[:, None] - lower) / (middle - lower)
    falling = (upper - frequency[:, None]) / (upper - middle)
    return np.maximum(0.0, np.minimum(rising, falling)).astype(np.float32)


def spectrum_table(size):
    sample = np.arange(size)
    phase = sample[:, None] * np.arange(size // 2)[None, :] % size
    angle = phase * (2.0 * math.pi / size)
    window = 0.5 - 0.5 * np.cos(sample * (2.0 * math.pi / size))
    both = np.concatenate([np.cos(angle), np.sin(angle)], axis=1) * window[:, None]
    filters = np.zeros((size, LANES))
    filters[: size // 2, :MELS] = mel_table(size, MELS)[: size // 2]
    return np.concatenate([both, filters], axis=1).astype(np.float32)


def vmem():
    return pl.BlockSpec(memory_space=pltpu.VMEM)


def smem():
    return pl.BlockSpec(memory_space=pltpu.SMEM)


def anywhere():
    return pl.BlockSpec(memory_space=pl.ANY)


def params(mib):
    return pltpu.CompilerParams(vmem_limit_bytes=mib * MIB)


def cost(flops, moved):
    return pl.CostEstimate(flops=int(flops), bytes_accessed=int(moved), transcendentals=0)


def place(parts):
    mine = lax.axis_index("dp")
    copies = lax.axis_size("dp") // parts
    return mine // copies, mine % copies


def start_all(copies):
    for copy in copies:
        copy.start()


def wait_all(copies):
    for copy in copies:
        copy.wait()


def iota(rows, columns, axis):
    return lax.broadcasted_iota(jnp.int32, (rows, columns), axis)


def quotient(index, step, count):
    result = jnp.zeros_like(index)
    for i in range(1, count):
        result += (index >= i * step).astype(jnp.int32)
    return result


def one_hot(target, count):
    return (iota(target.shape[0], count, 1) == target).astype(F32).astype(BF16)


def frame_order(parts, copies):
    count = parts * copies * W
    row = iota(count, 1, 0)
    k = quotient(row, W, parts * copies)
    p = quotient(k, copies, parts)
    return one_hot((k - p * copies) * W * parts + (row - k * W) * parts + p, count)


def samples(index, windows, group):
    return (index + quotient(index, W, windows) * (group - 1) * W) * SPAN


def mix_columns(group, qkv_ref, mix_out, sems):
    features = qkv_ref.shape[1] // 3
    width = features // group
    first = pl.multiple_of(lax.axis_index("seq") * width, LANES)
    return [
        pltpu.make_async_copy(
            qkv_ref.at[:, pl.ds(kind * features + first, width)],
            mix_out.at[:, pl.ds(kind * width, width)],
            sems.at[kind],
        )
        for kind in range(3)
    ]


def banded_weights(width, conv1_ref, banded_out):
    taps, channels = conv1_ref.shape
    row = lax.broadcasted_iota(jnp.int32, (LANES, taps), 0)
    tap = lax.broadcasted_iota(jnp.int32, (LANES, taps), 1)
    line = (tap >= 3).astype(jnp.int32) + (tap >= 6).astype(jnp.int32)
    target = line * (width - 3) + tap + 1
    weight = conv1_ref[...]
    for g in range(banded_out.shape[1] // channels):
        select = (row == target + 2 * g).astype(F32).astype(BF16)
        banded_out[:, g * channels : (g + 1) * channels] = jnp.dot(
            select, weight, preferred_element_type=F32
        ).astype(BF16)


def mel_kernel(parts, group, slots_here, rim_ref, audio_ref, table_ref, qkv_ref, *refs):
    outs_refs, (mix_out, ext, table, blocks, slots_ref, sems) = refs[:parts], refs[parts:]
    load_slots = pltpu.make_async_copy(slots_here, slots_ref, sems.at[5])
    load_slots.start()
    load_audio = pltpu.make_async_copy(audio_ref, ext.at[:, pl.ds(RIM, audio_ref.shape[1])], sems.at[3])
    load_table = pltpu.make_async_copy(table_ref, table, sems.at[4])
    load_audio.start()
    load_table.start()
    pieces = mix_columns(group, qkv_ref, mix_out, sems)
    start_all(pieces)
    streams = audio_ref.shape[0]
    rows = JS * streams
    ext[:, :RIM] = rim_ref[...]
    load_audio.wait()
    phases = []
    for phase in range(4):
        start = HOP * phase + 32
        base, shift = start // LANES * LANES, start % LANES
        length = N_FFT + (LANES if shift else 0)
        block = jnp.concatenate(
            [ext[:, SPAN * j + base : SPAN * j + base + length] for j in range(JS)], axis=0
        )
        if shift:
            block = pltpu.roll(block, length - shift, 1)[:, :N_FFT]
        phases.append(block)
    frames = jnp.concatenate(phases, axis=0)
    load_table.wait()
    spectrum = jnp.dot(
        frames, table[:, :N_FFT], precision=lax.Precision.HIGHEST, preferred_element_type=F32
    )
    half = N_FFT // 2
    real, imag = spectrum[:, :half], spectrum[:, half:]
    power = real * real + imag * imag
    mel_power = jnp.dot(
        power, table[:half, N_FFT:], precision=lax.Precision.HIGHEST, preferred_element_type=F32
    )
    load_slots.wait()
    column = iota(1, rows, 1)
    early = quotient(column, streams, JS)
    target = jnp.zeros((1, rows), jnp.int32)
    for u in range(streams):
        target = jnp.where(column - early * streams == u, early * streams + slots_ref[u], target)
    routing = (target == iota(rows, rows, 0)).astype(F32).astype(BF16)
    log_mel = jnp.log(mel_power + EPS_LOG)
    share = BANDS // parts
    width = 4 * share + 4
    lane = iota(rows, LANES, 1)
    by_phase = [log_mel[phase * rows : (phase + 1) * rows] for phase in range(4)]

    def next_four(frames):
        return jnp.concatenate([frames[streams:], jnp.zeros((streams, LANES), F32)], axis=0)

    taps = [by_phase[1], by_phase[2], by_phase[3], next_four(by_phase[0]), next_four(by_phase[1])]
    for part in range(parts):
        first = 4 * share * part - 4
        block = jnp.zeros((rows, LANES), F32)
        for delta, frames in enumerate(taps):
            band = lane - width * delta + first
            here = (lane >= width * delta) & (lane < width * (delta + 1)) & (band >= 0) & (band < MELS)
            shift = (width * delta - first) % LANES
            block = jnp.where(here, pltpu.roll(frames, shift, 1) if shift else frames, block)
        blocks[part] = jnp.dot(routing, block.astype(BF16), preferred_element_type=F32).astype(BF16)
    mine, _ = place(parts)
    for step in range(parts):
        outs_refs[step][...] = blocks[mine ^ step]
    wait_all(pieces)


def packed(parts, mix_refs, out_refs, stack_out, sems):
    part, _ = place(parts)
    rows = mix_refs[0].shape[0]
    blocks = mix_refs[0].shape[1] // LANES
    copies = []
    for step in range(parts):
        for block in range(blocks):
            source = mix_refs[step].at[:, pl.ds(block * LANES, LANES)]
            target = stack_out.at[part ^ step, pl.ds(block * rows, rows)]
            copies.append(pltpu.make_async_copy(source, target, sems.at[len(copies)]))
        target = stack_out.at[part ^ step, pl.ds(blocks * rows, out_refs[step].shape[0])]
        copies.append(pltpu.make_async_copy(out_refs[step], target, sems.at[len(copies)]))
    return copies


def conv_kernel(parts, width, conv1_ref, conv2_ref, *refs):
    part, copy_index = place(parts)
    mine = lax.axis_index("dp")
    windows = lax.axis_size("dp")
    copies = windows // parts
    mel_refs, refs = refs[:parts], refs[parts:]
    proj_refs, refs = refs[:copies], refs[copies:]
    outs_refs, refs = refs[:windows], refs[windows:]
    mel, own, banded_ref, even, odd, second, conv2, proj, partial, sems = refs
    load_own = pltpu.make_async_copy(mel_refs[0], own, sems.at[1 + copies])
    load_own.start()
    load_conv2 = pltpu.make_async_copy(conv2_ref, conv2, sems.at[0])
    load_conv2.start()
    loads = []
    for step in range(copies):
        slot = copy_index ^ step
        loads.append(pltpu.make_async_copy(proj_refs[step], proj.at[slot], sems.at[1 + step]))
    start_all(loads)
    banded_weights(width, conv1_ref, banded_ref)
    streams = mel_refs[0].shape[0] // JS
    n = parts * streams
    load_own.wait()
    mel[part] = own[...].astype(F32)
    for step in range(1, parts):
        mel[part ^ step] = mel_refs[step][...].astype(F32)
    evens = jnp.concatenate(
        [mel[p, j * streams : (j + 1) * streams, :] for j in range(JS) for p in range(parts)], axis=0
    )
    odds = pltpu.roll(evens[: W * n], LANES - 2 * width, 1).astype(BF16)
    evens = evens.astype(BF16)
    channels = conv2.shape[1]
    outs = banded_ref.shape[1] // channels
    for g in range(outs):
        lanes = slice(g * channels, (g + 1) * channels)
        weight = banded_ref[:, lanes]
        even[:, lanes] = jax.nn.relu(jnp.dot(evens, weight, preferred_element_type=F32)).astype(BF16)
        odd[:, lanes] = jax.nn.relu(jnp.dot(odds, weight, preferred_element_type=F32)).astype(BF16)

    load_conv2.wait()
    for h in range((outs - 1) // 2):
        lanes = slice(2 * h * channels, (2 * h + 3) * channels)
        depth = 3 * channels
        total = jnp.dot(even[: W * n, lanes], conv2[:depth], preferred_element_type=F32)
        total += jnp.dot(odd[:, lanes], conv2[depth : 2 * depth], preferred_element_type=F32)
        total += jnp.dot(even[n:, lanes], conv2[2 * depth :], preferred_element_type=F32)
        second[:, h * channels : (h + 1) * channels] = jax.nn.relu(total).astype(BF16)
    wait_all(loads)
    weights = proj[...].reshape(second.shape[1], proj.shape[2])
    sums = jnp.dot(second[...], weights, preferred_element_type=F32)
    for block in range(partial.shape[0]):
        partial[block] = sums[:, block * LANES : (block + 1) * LANES]
    for step in range(windows):
        for block in range(partial.shape[0]):
            rows = partial[block, pl.ds(mine ^ step, W * parts, stride=streams), :]
            outs_refs[step][:, block * LANES : (block + 1) * LANES] = rows.astype(BF16)


def bounds(row, slots_ref, starts_ref, lengths_ref):
    begin, span = jnp.int32(0), jnp.int32(0)
    for u in range(slots_ref.shape[0]):
        chosen = slots_ref[u] == row
        begin = begin + jnp.where(chosen, starts_ref[u], 0)
        span = span + jnp.where(chosen, lengths_ref[u], 0)
    return begin, begin + span


def norm_kernel(parts, *refs):
    _, copy_index = place(parts)
    windows = lax.axis_size("dp")
    copies = windows // parts
    part_refs, refs = refs[:windows][::-1], refs[windows:]
    mix_refs, refs = refs[:parts], refs[parts:]
    weight_refs, refs = refs[:parts], refs[parts:]
    rows_out, normed_out, first_out, second_out, stack_out, encoded, sems = refs
    moves = packed(parts, mix_refs, weight_refs, stack_out, sems)
    start_all(moves)
    rows = W * parts
    for copy in range(copies):
        total = part_refs[copy][...].astype(F32)
        for step in range(1, parts):
            total += part_refs[step * copies + copy][...].astype(F32)
        at = pl.multiple_of((copy_index ^ copy) * rows, rows)
        encoded[pl.ds(at, rows), :] = total.astype(BF16)
    values = jnp.dot(frame_order(parts, copies), encoded[...], preferred_element_type=F32)
    rows_out[...] = values.astype(BF16)
    mean = jnp.mean(values, axis=-1, keepdims=True)
    centered = values - mean
    variance = jnp.mean(centered * centered, axis=-1, keepdims=True)
    normed = (centered * lax.rsqrt(variance + EPS_NORM)).astype(BF16)
    normed_out[...] = normed
    first_out[...] = normed[: normed.shape[0] // 2]
    second_out[...] = normed[normed.shape[0] // 2 :]
    wait_all(moves)


def mask_kernel(windows, group, slots_ref, starts_ref, lengths_ref, rows_ref, rows_out, keys_out, valid_out):
    begin, end = bounds(lax.axis_index("dp"), slots_ref, starts_ref, lengths_ref)
    sample = samples(iota(windows * W, 1, 0), windows, group) + lax.axis_index("seq") * (W * SPAN)
    valid = (sample >= begin) & (sample < end)
    rows_out[...] = jnp.where(valid, rows_ref[...].astype(F32), 0.0).astype(BF16)
    valid_out[...] = valid.astype(F32)
    keys = samples(iota(group, windows * W, 1), windows, group) + iota(group, windows * W, 0) * (W * SPAN)
    keys_out[...] = ((keys >= begin) & (keys < end)).astype(F32)


def attention_kernel(parts, windows, group, keys_ref, *refs):
    _, copy_index = place(parts)
    plane = lax.axis_index("seq")
    copies = windows // parts
    normed_refs, refs = refs[: 2 * group - 2], refs[2 * group - 2 :]
    stack_refs, refs = refs[:copies], refs[copies:]
    outs_refs, (pieces,) = refs[:group], refs[group:]
    blocks = 3 * outs_refs[0].shape[1] // LANES
    keys = [keys_ref[pl.ds(plane ^ step, 1), :] for step in range(group)]
    valid = jnp.concatenate(keys, axis=1) > 0.5
    local = normed_refs[0].shape[0]
    depth = pieces.shape[2]
    at = 0
    for ref in normed_refs:
        for piece in range(windows):
            pieces[piece, at : at + ref.shape[0], :] = ref[:, piece * depth : (piece + 1) * depth]
        at += ref.shape[0]
    mixed = 0.0
    for step in range(copies):
        slot = copy_index ^ step
        normed = jnp.concatenate([pieces[piece * copies + slot] for piece in range(parts)], axis=1)
        columns = [
            jnp.concatenate(
                [stack_refs[step][piece, block * depth : (block + 1) * depth, :] for piece in range(parts)], axis=0
            )
            for block in range(blocks)
        ]
        weights = jnp.concatenate(columns, axis=1)
        mixed += jnp.dot(normed, weights, preferred_element_type=F32)
    mixed = mixed.astype(BF16)
    width = mixed.shape[1] // 3
    scale = HEAD_DIM ** (-0.5)
    for head in range(width // HEAD_DIM):
        at = head * HEAD_DIM
        query = mixed[:, at : at + HEAD_DIM]
        key = mixed[:, width + at : width + at + HEAD_DIM]
        value = mixed[:, 2 * width + at : 2 * width + at + HEAD_DIM]
        scores = lax.dot_general(query, key, (((1,), (1,)), ((), ())), preferred_element_type=F32) * scale
        masked = jnp.where(valid, scores, MASKED)
        peak = jnp.max(masked, axis=1, keepdims=True)
        weight = jnp.where(valid, jnp.exp(masked - peak), 0.0)
        total = jnp.sum(weight, axis=1, keepdims=True)
        summed = jnp.dot(weight.astype(BF16), value, preferred_element_type=F32)
        context = (summed / total).astype(BF16)
        for step in range(group):
            outs_refs[step][:, at : at + HEAD_DIM] = context[step * local : (step + 1) * local]


def output_kernel(parts, windows, group, base, valid_ref, *refs):
    context_refs, refs = refs[:group][::-1], refs[group:]
    stack_refs, refs = refs[: windows // parts], refs[windows // parts :]
    out_ref, context, pieces = refs
    _, copy_index = place(parts)
    copies = windows // parts
    plane = lax.axis_index("seq")
    head_width = context_refs[0].shape[1]
    for step in range(group):
        at = pl.multiple_of((plane ^ step) * head_width, LANES)
        context[:, pl.ds(at, head_width)] = context_refs[step][...]
    ordered = context[...]
    for step in range(copies):
        slot = copy_index ^ step
        for piece in range(parts):
            pieces[piece * copies + slot] = jnp.dot(
                ordered, stack_refs[step][piece, base:, :], preferred_element_type=F32
            )
    result = jnp.concatenate([pieces[d] for d in range(windows)], axis=1)
    out_ref[...] = jnp.where(valid_ref[...] > 0.5, result, 0.0).astype(BF16)


def on_device(
    audio, starts, lengths, slots, conv1_weight, conv2_weight, proj_weight, qkv_weight, out_weight
):
    streams = audio.shape[0]
    windows = lax.axis_size("dp")
    group = lax.axis_size("seq")
    parts = math.gcd(windows, BANDS)
    copies = windows // parts
    assert streams == windows and all(count & (count - 1) == 0 for count in (parts, copies, group))
    share = BANDS // parts
    width = 4 * share + 4
    channels = conv1_weight.shape[1]
    features = proj_weight.shape[1]
    head_width = features // group
    local = windows * W
    rows = JS * streams
    n = parts * streams
    outs = 2 * share + 1
    scale = max(1, windows * group // 32)

    route = [(i, i + 1) for i in range(windows * group - 1)]
    rim = lax.ppermute(audio[:, audio.shape[1] - RIM :], ("dp", "seq"), route)

    def to_part(block, step):
        pairs = [(p * copies + c, (p ^ step) * copies + c) for p in range(parts) for c in range(copies)]
        return lax.ppermute(block, "dp", pairs)

    def to_copy(block, step):
        pairs = [(p * copies + c, p * copies + (c ^ step)) for p in range(parts) for c in range(copies)]
        return lax.ppermute(block, "dp", pairs)

    def to_window(block, step):
        return lax.ppermute(block, "dp", [(i, i ^ step) for i in range(windows)])

    def to_plane(block, step):
        return lax.ppermute(block, "seq", [(i, i ^ step) for i in range(group)])

    proj_all = [proj_weight] + [to_copy(proj_weight, step) for step in range(1, copies)]

    table = jnp.asarray(spectrum_table(N_FFT))
    mix_piece = jax.ShapeDtypeStruct((qkv_weight.shape[0], 3 * head_width), BF16)
    *mel_all, mix = pl.pallas_call(
        functools.partial(mel_kernel, parts, group),
        out_shape=tuple([jax.ShapeDtypeStruct((rows, LANES), BF16)] * parts + [mix_piece]),
        in_specs=[anywhere(), vmem()] + [anywhere()] * 3,
        out_specs=tuple([vmem()] * (parts + 1)),
        scratch_shapes=[
            pltpu.VMEM((streams, RIM + audio.shape[1]), F32),
            pltpu.VMEM(table.shape, F32),
            pltpu.VMEM((parts, rows, LANES), BF16),
            pltpu.SMEM((streams,), jnp.int32),
            pltpu.SemaphoreType.DMA((6,)),
        ],
        compiler_params=params(58),
        cost_estimate=cost(1e10, 2e6),
        name="log_mel",
    )(slots, rim, audio, table, qkv_weight)
    near = [to_part(out_weight, step) for step in range(1, parts - 1)]
    mel_all, proj_all = lax.optimization_barrier((mel_all, proj_all))
    mel_all = [mel_all[0]] + [to_part(mel_all[step], step) for step in range(1, parts)]
    mel_all, near = lax.optimization_barrier((mel_all, near))
    out_rows, *near = [piece.reshape(-1, LANES) for piece in [out_weight] + near]
    mix, out_here = lax.optimization_barrier((mix, out_rows))
    out_all = [out_rows] + near + [to_part(out_here, parts - 1)]
    mix_all = [mix] + [to_part(mix, step) for step in range(1, parts)]

    block = jax.ShapeDtypeStruct((local, features), BF16)
    partials = pl.pallas_call(
        functools.partial(conv_kernel, parts, width),
        out_shape=tuple([jax.ShapeDtypeStruct((W * parts, features), BF16)] * windows),
        in_specs=[vmem()] + [anywhere()] * 2 + [vmem()] * (parts - 1) + [anywhere()] * copies,
        out_specs=tuple([vmem()] * windows),
        scratch_shapes=[
            pltpu.VMEM((parts, rows, LANES), F32),
            pltpu.VMEM((rows, LANES), BF16),
            pltpu.VMEM((LANES, outs * channels), BF16),
            pltpu.VMEM((JS * n, outs * channels), BF16),
            pltpu.VMEM((W * n, outs * channels), BF16),
            pltpu.VMEM((W * n, share * channels), BF16),
            pltpu.VMEM(conv2_weight.shape, BF16),
            pltpu.VMEM((copies,) + proj_weight.shape, BF16),
            pltpu.VMEM((features // LANES, W * n, LANES), F32),
            pltpu.SemaphoreType.DMA((2 + copies,)),
        ],
        compiler_params=params(min(40 + 4 * scale, 56)),
        cost_estimate=cost(2e9, 4e6),
        name="conv",
    )(conv1_weight, conv2_weight, *mel_all, *proj_all)
    partials = [to_window(partials[step], step) for step in reversed(range(1, windows))] + [partials[0]]

    half = jax.ShapeDtypeStruct((local // 2, features), BF16)
    blocks = 3 * head_width // LANES
    mix_rows = blocks * qkv_weight.shape[0]
    pack = jax.ShapeDtypeStruct((parts, mix_rows + out_rows.shape[0], LANES), BF16)
    ordered, normed, *halves, stack = pl.pallas_call(
        functools.partial(norm_kernel, parts),
        out_shape=(block, block, half, half, pack),
        in_specs=[vmem()] * windows + [anywhere()] * (2 * parts),
        out_specs=tuple([vmem()] * 5),
        scratch_shapes=[pltpu.VMEM((local, features), BF16), pltpu.SemaphoreType.DMA((parts * (blocks + 1),))],
        compiler_params=params(min(12 * scale, 32)),
        cost_estimate=cost(1e8, 1e6),
        name="layer_norm",
    )(*partials, *mix_all, *out_all)
    stacks = [stack] + [to_copy(stack, step) for step in range(1, copies)]
    regrouped, keys, valid = pl.pallas_call(
        functools.partial(mask_kernel, windows, group),
        out_shape=(
            block,
            jax.ShapeDtypeStruct((group, local), F32),
            jax.ShapeDtypeStruct((local, 1), F32),
        ),
        in_specs=[smem()] * 3 + [vmem()],
        out_specs=(vmem(), vmem(), vmem()),
        compiler_params=params(min(8 * scale, 32)),
        cost_estimate=cost(1e8, 1e6),
        name="mask",
    )(slots, starts, lengths, ordered)
    by_plane = {0: [normed], 1: [to_plane(normed, 1)]}
    for step in range(2, group):
        high = 1 << (step.bit_length() - 1)
        source = halves if step == high else by_plane[high]
        by_plane[step] = [to_plane(piece, high if step == high else step - high) for piece in source]
    normed = [piece for step in range(group) for piece in by_plane[step]]

    context = pl.pallas_call(
        functools.partial(attention_kernel, parts, windows, group),
        out_shape=tuple([jax.ShapeDtypeStruct((local, head_width), BF16)] * group),
        in_specs=[vmem()] * (1 + len(normed) + copies),
        out_specs=tuple([vmem()] * group),
        scratch_shapes=[pltpu.VMEM((windows, group * local, qkv_weight.shape[0]), BF16)],
        compiler_params=params(min(16 * scale, 48)),
        cost_estimate=cost(1e9, 2e6),
        name="attention",
    )(keys, *normed, *stacks)
    context = [to_plane(context[step], step) for step in reversed(range(1, group))] + [context[0]]
    if out_rows.shape != out_weight.shape:
        stacks = [stack[:, mix_rows:].reshape((parts,) + out_weight.shape) for stack in stacks]
        mix_rows = 0

    attended = pl.pallas_call(
        functools.partial(output_kernel, parts, windows, group, mix_rows),
        out_shape=block,
        in_specs=[vmem()] * (1 + group + copies),
        out_specs=vmem(),
        scratch_shapes=[
            pltpu.VMEM((local, features), BF16),
            pltpu.VMEM((windows, local, out_weight.shape[1]), F32),
        ],
        compiler_params=params(min(12 * scale, 32)),
        cost_estimate=cost(1e8, 3e6),
        name="output",
    )(valid, *context, *stacks)
    shape = (1, windows, 1, W, features)
    return (regrouped.reshape(shape), attended.reshape(shape))


def solution(mesh):
    in_specs = (
        P(None, ("dp", "seq")),
        P(),
        P(),
        P(),
        P(),
        P(),
        P("dp", None),
        P("dp", None),
        P(None, "dp"),
    )
    out_specs = (P("dp", None, "seq", None, None), P("dp", None, "seq", None, None))
    return jax.shard_map(
        on_device, mesh=mesh, in_specs=in_specs, out_specs=out_specs, check_vma=False
    )
```

```python
import functools
import math

import jax
import jax.numpy as jnp
import numpy as np
from jax import lax
from jax.experimental import pallas as pl
from jax.experimental.pallas import tpu as pltpu
from jax.sharding import PartitionSpec as P

HEADS = 8
HEAD_DIM = 128
MELS = 80
BANDS = MELS // 4
N_FFT = 512
HOP = 160
W = 8
RIM = 1024
SPAN = 4 * HOP
JS = W + 1
LANES = 128
SAMPLE_RATE = 16000.0
EPS_LOG = 1e-06
EPS_NORM = 1e-05
MASKED = -1e30
F32 = jnp.float32
BF16 = jnp.bfloat16
MIB = 1 << 20


def mel_table(size, bands):
    count = size // 2 + 1
    highest = 2595.0 * math.log10(1.0 + SAMPLE_RATE / 1400.0)
    points = np.linspace(0.0, highest, bands + 2)
    edges = 700.0 * (10.0 ** (points / 2595.0) - 1.0)
    edges[0] = 0.0
    edges[-1] = SAMPLE_RATE / 2.0
    frequency = np.arange(count) * (SAMPLE_RATE / size)
    lower = edges[:-2][None, :]
    middle = edges[1:-1][None, :]
    upper = edges[2:][None, :]
    rising = (frequency[:, None] - lower) / (middle - lower)
    falling = (upper - frequency[:, None]) / (upper - middle)
    return np.maximum(0.0, np.minimum(rising, falling)).astype(np.float32)


def spectrum_table(size):
    half = size // 2
    sample = np.arange(half)
    bins = np.concatenate([np.arange(0, half, 2), np.arange(1, half, 2)])
    angle = sample[:, None] * bins[None, :] % size * (2.0 * math.pi / size)
    table = np.zeros((half + 8, size + LANES))
    for odd in range(2):
        part = angle[:, odd * half // 2 : (odd + 1) * half // 2]
        table[:half, odd * half : (odd + 1) * half] = np.concatenate([np.cos(part), np.sin(part)], axis=1)
    table[:half, size : size + MELS] = mel_table(size, MELS)[bins]
    table[half, :size] = 0.5 - 0.5 * np.cos(np.arange(size) * (2.0 * math.pi / size))
    return table.astype(np.float32)


def vmem():
    return pl.BlockSpec(memory_space=pltpu.VMEM)


def smem():
    return pl.BlockSpec(memory_space=pltpu.SMEM)


def anywhere():
    return pl.BlockSpec(memory_space=pl.ANY)


def params(mib):
    return pltpu.CompilerParams(vmem_limit_bytes=mib * MIB)


def cost(flops, moved):
    return pl.CostEstimate(flops=int(flops), bytes_accessed=int(moved), transcendentals=0)


def place(parts):
    mine = lax.axis_index("dp")
    copies = lax.axis_size("dp") // parts
    return mine // copies, mine % copies


def start_all(copies):
    for copy in copies:
        copy.start()


def wait_all(copies):
    for copy in copies:
        copy.wait()


def iota(rows, columns, axis):
    return lax.broadcasted_iota(jnp.int32, (rows, columns), axis)


def quotient(index, step, count):
    result = jnp.zeros_like(index)
    for i in range(1, count):
        result += (index >= i * step).astype(jnp.int32)
    return result


def one_hot(target, count):
    return (iota(target.shape[0], count, 1) == target).astype(F32).astype(BF16)


def frame_order(parts, copies):
    count = parts * copies * W
    row = iota(count, 1, 0)
    k = quotient(row, W, parts * copies)
    p = quotient(k, copies, parts)
    return one_hot((k - p * copies) * W * parts + (row - k * W) * parts + p, count)


def samples(index, windows, group):
    return (index + quotient(index, W, windows) * (group - 1) * W) * SPAN


def mix_columns(group, qkv_ref, mix_out, sems):
    features = qkv_ref.shape[1] // 3
    width = features // group
    first = pl.multiple_of(lax.axis_index("seq") * width, LANES)
    return [
        pltpu.make_async_copy(
            qkv_ref.at[:, pl.ds(kind * features + first, width)],
            mix_out.at[:, pl.ds(kind * width, width)],
            sems.at[kind],
        )
        for kind in range(3)
    ]


def banded_weights(width, conv1_ref, banded_out):
    taps, channels = conv1_ref.shape
    row = lax.broadcasted_iota(jnp.int32, (LANES, taps), 0)
    tap = lax.broadcasted_iota(jnp.int32, (LANES, taps), 1)
    line = (tap >= 3).astype(jnp.int32) + (tap >= 6).astype(jnp.int32)
    target = line * (width - 3) + tap + 1
    weight = conv1_ref[...]
    for g in range(banded_out.shape[1] // channels):
        select = (row == target + 2 * g).astype(F32).astype(BF16)
        banded_out[:, g * channels : (g + 1) * channels] = jnp.dot(
            select, weight, preferred_element_type=F32
        ).astype(BF16)


def mel_kernel(parts, group, slots_here, rim_ref, audio_ref, table_ref, qkv_ref, *refs):
    outs_refs, (mix_out, ext, table, blocks, slots_ref, sems) = refs[:parts], refs[parts:]
    load_slots = pltpu.make_async_copy(slots_here, slots_ref, sems.at[5])
    load_slots.start()
    load_audio = pltpu.make_async_copy(audio_ref, ext.at[:, pl.ds(RIM, audio_ref.shape[1])], sems.at[3])
    load_table = pltpu.make_async_copy(table_ref, table, sems.at[4])
    load_audio.start()
    load_table.start()
    pieces = mix_columns(group, qkv_ref, mix_out, sems)
    start_all(pieces)
    streams = audio_ref.shape[0]
    rows = JS * streams
    ext[:, :RIM] = rim_ref[...]
    load_audio.wait()
    phases = []
    for phase in range(4):
        start = HOP * phase + 32
        base, shift = start // LANES * LANES, start % LANES
        length = N_FFT + (LANES if shift else 0)
        block = jnp.concatenate(
            [ext[:, SPAN * j + base : SPAN * j + base + length] for j in range(JS)], axis=0
        )
        if shift:
            block = pltpu.roll(block, length - shift, 1)[:, :N_FFT]
        phases.append(block)
    frames = jnp.concatenate(phases, axis=0)
    load_table.wait()
    half = N_FFT // 2
    frames = frames * table[half : half + 1, :N_FFT]
    low, high = frames[:, :half], frames[:, half:]
    powers = []
    for odd in range(2):
        spectrum = jnp.dot(
            low - high if odd else low + high,
            table[:half, odd * half : (odd + 1) * half],
            precision=lax.Precision.HIGHEST,
            preferred_element_type=F32,
        )
        real, imag = spectrum[:, : half // 2], spectrum[:, half // 2 :]
        powers.append(real * real + imag * imag)
    mel_power = jnp.dot(
        jnp.concatenate(powers, axis=1),
        table[:half, N_FFT:],
        precision=lax.Precision.HIGHEST,
        preferred_element_type=F32,
    )
    load_slots.wait()
    column = iota(1, rows, 1)
    early = quotient(column, streams, JS)
    target = jnp.zeros((1, rows), jnp.int32)
    for u in range(streams):
        target = jnp.where(column - early * streams == u, early * streams + slots_ref[u], target)
    routing = (target == iota(rows, rows, 0)).astype(F32).astype(BF16)
    log_mel = jnp.log(mel_power + EPS_LOG)
    share = BANDS // parts
    width = 4 * share + 4
    lane = iota(rows, LANES, 1)
    by_phase = [log_mel[phase * rows : (phase + 1) * rows] for phase in range(4)]

    def next_four(frames):
        return jnp.concatenate([frames[streams:], jnp.zeros((streams, LANES), F32)], axis=0)

    taps = [by_phase[1], by_phase[2], by_phase[3], next_four(by_phase[0]), next_four(by_phase[1])]
    for part in range(parts):
        first = 4 * share * part - 4
        block = jnp.zeros((rows, LANES), F32)
        for delta, frames in enumerate(taps):
            band = lane - width * delta + first
            here = (lane >= width * delta) & (lane < width * (delta + 1)) & (band >= 0) & (band < MELS)
            shift = (width * delta - first) % LANES
            block = jnp.where(here, pltpu.roll(frames, shift, 1) if shift else frames, block)
        blocks[part] = jnp.dot(routing, block.astype(BF16), preferred_element_type=F32).astype(BF16)
    mine, _ = place(parts)
    for step in range(parts):
        outs_refs[step][...] = blocks[mine ^ step]
    wait_all(pieces)


def stacked(parts, pieces, stack_out, sems, base):
    part, _ = place(parts)
    return [
        pltpu.make_async_copy(pieces[step], stack_out.at[part ^ step], sems.at[base + step])
        for step in range(parts)
    ]


def conv_kernel(parts, width, conv1_ref, conv2_ref, *refs):
    part, copy_index = place(parts)
    mine = lax.axis_index("dp")
    windows = lax.axis_size("dp")
    copies = windows // parts
    mel_refs, refs = refs[:parts], refs[parts:]
    proj_refs, refs = refs[:copies], refs[copies:]
    outs_refs, refs = refs[:windows], refs[windows:]
    mel, own, banded_ref, even, odd, second, conv2, proj, partial, sems = refs
    load_own = pltpu.make_async_copy(mel_refs[0], own, sems.at[1 + copies])
    load_own.start()
    load_conv2 = pltpu.make_async_copy(conv2_ref, conv2, sems.at[0])
    load_conv2.start()
    loads = []
    for step in range(copies):
        slot = copy_index ^ step
        loads.append(pltpu.make_async_copy(proj_refs[step], proj.at[slot], sems.at[1 + step]))
    start_all(loads)
    banded_weights(width, conv1_ref, banded_ref)
    streams = mel_refs[0].shape[0] // JS
    n = parts * streams
    load_own.wait()
    mel[part] = own[...].astype(F32)
    for step in range(1, parts):
        mel[part ^ step] = mel_refs[step][...].astype(F32)
    evens = jnp.concatenate(
        [mel[p, j * streams : (j + 1) * streams, :] for j in range(JS) for p in range(parts)], axis=0
    )
    odds = pltpu.roll(evens[: W * n], LANES - 2 * width, 1).astype(BF16)
    evens = evens.astype(BF16)
    channels = conv2.shape[1]
    outs = banded_ref.shape[1] // channels
    for g in range(outs):
        lanes = slice(g * channels, (g + 1) * channels)
        weight = banded_ref[:, lanes]
        even[:, lanes] = jax.nn.relu(jnp.dot(evens, weight, preferred_element_type=F32)).astype(BF16)
        odd[:, lanes] = jax.nn.relu(jnp.dot(odds, weight, preferred_element_type=F32)).astype(BF16)

    load_conv2.wait()
    for h in range((outs - 1) // 2):
        lanes = slice(2 * h * channels, (2 * h + 3) * channels)
        taps = jnp.concatenate([even[: W * n, lanes], odd[:, lanes], even[n:, lanes]], axis=1)
        total = jnp.dot(taps, conv2[...], preferred_element_type=F32)
        second[:, h * channels : (h + 1) * channels] = jax.nn.relu(total).astype(BF16)
    wait_all(loads)
    weights = proj[...].reshape(second.shape[1], proj.shape[2])
    sums = jnp.dot(second[...], weights, preferred_element_type=F32)
    for block in range(partial.shape[0]):
        partial[block] = sums[:, block * LANES : (block + 1) * LANES]
    for step in range(windows):
        for block in range(partial.shape[0]):
            rows = partial[block, pl.ds(mine ^ step, W * parts, stride=streams), :]
            outs_refs[step][:, block * LANES : (block + 1) * LANES] = rows.astype(BF16)


def bounds(row, slots_ref, starts_ref, lengths_ref):
    begin, span = jnp.int32(0), jnp.int32(0)
    for u in range(slots_ref.shape[0]):
        chosen = slots_ref[u] == row
        begin = begin + jnp.where(chosen, starts_ref[u], 0)
        span = span + jnp.where(chosen, lengths_ref[u], 0)
    return begin, begin + span


def norm_kernel(parts, *refs):
    _, copy_index = place(parts)
    windows = lax.axis_size("dp")
    copies = windows // parts
    part_refs, refs = refs[:windows][::-1], refs[windows:]
    piece_refs, refs = refs[:parts], refs[parts:]
    rows_out, normed_out, stack_out, encoded, sems = refs
    moves = stacked(parts, piece_refs, stack_out, sems, 0)
    start_all(moves)
    rows = W * parts
    for copy in range(copies):
        total = part_refs[copy][...].astype(F32)
        for step in range(1, parts):
            total += part_refs[step * copies + copy][...].astype(F32)
        at = pl.multiple_of((copy_index ^ copy) * rows, rows)
        encoded[pl.ds(at, rows), :] = total.astype(BF16)
    values = jnp.dot(frame_order(parts, copies), encoded[...], preferred_element_type=F32)
    rows_out[...] = values.astype(BF16)
    mean = jnp.mean(values, axis=-1, keepdims=True)
    centered = values - mean
    variance = jnp.mean(centered * centered, axis=-1, keepdims=True)
    normed_out[...] = (centered * lax.rsqrt(variance + EPS_NORM)).astype(BF16)
    wait_all(moves)


def mask_kernel(windows, group, slots_ref, starts_ref, lengths_ref, rows_ref, rows_out, keys_out, valid_out):
    begin, end = bounds(lax.axis_index("dp"), slots_ref, starts_ref, lengths_ref)
    sample = samples(iota(windows * W, 1, 0), windows, group) + lax.axis_index("seq") * (W * SPAN)
    valid = (sample >= begin) & (sample < end)
    rows_out[...] = jnp.where(valid, rows_ref[...].astype(F32), 0.0).astype(BF16)
    valid_out[...] = valid.astype(F32)
    keys = samples(iota(group, windows * W, 1), windows, group) + iota(group, windows * W, 0) * (W * SPAN)
    keys_out[...] = ((keys >= begin) & (keys < end)).astype(F32)


def attention_kernel(parts, windows, group, keys_ref, *refs):
    _, copy_index = place(parts)
    plane = lax.axis_index("seq")
    copies = windows // parts
    normed_refs, refs = refs[:group], refs[group:]
    stack_refs, refs = refs[:copies], refs[copies:]
    weight_refs, refs = refs[:parts], refs[parts:]
    outs_refs, (stack_out, pieces, sems) = refs[:group], refs[group:]
    moves = stacked(parts, weight_refs, stack_out, sems, 0)
    start_all(moves)
    keys = [keys_ref[pl.ds(plane ^ step, 1), :] for step in range(group)]
    valid = jnp.concatenate(keys, axis=1) > 0.5
    local = normed_refs[0].shape[0]
    depth = pieces.shape[2]
    for step in range(group):
        for piece in range(windows):
            pieces[piece, step * local : (step + 1) * local, :] = normed_refs[step][
                :, piece * depth : (piece + 1) * depth
            ]
    mixed = 0.0
    for step in range(copies):
        slot = copy_index ^ step
        normed = jnp.concatenate([pieces[piece * copies + slot] for piece in range(parts)], axis=1)
        weights = stack_refs[step][...].reshape(parts * depth, stack_refs[step].shape[2])
        mixed += jnp.dot(normed, weights, preferred_element_type=F32)
    mixed = mixed.astype(BF16)
    width = mixed.shape[1] // 3
    scale = HEAD_DIM ** (-0.5)
    for head in range(width // HEAD_DIM):
        at = head * HEAD_DIM
        query = mixed[:, at : at + HEAD_DIM]
        key = mixed[:, width + at : width + at + HEAD_DIM]
        value = mixed[:, 2 * width + at : 2 * width + at + HEAD_DIM]
        scores = lax.dot_general(query, key, (((1,), (1,)), ((), ())), preferred_element_type=F32) * scale
        masked = jnp.where(valid, scores, MASKED)
        peak = jnp.max(masked, axis=1, keepdims=True)
        weight = jnp.where(valid, jnp.exp(masked - peak), 0.0)
        total = jnp.sum(weight, axis=1, keepdims=True)
        summed = jnp.dot(weight.astype(BF16), value, preferred_element_type=F32)
        context = (summed / total).astype(BF16)
        for step in range(group):
            outs_refs[step][:, at : at + HEAD_DIM] = context[step * local : (step + 1) * local]
    wait_all(moves)


def output_kernel(parts, windows, group, valid_ref, *refs):
    context_refs, refs = refs[:group], refs[group:]
    stack_refs, refs = refs[: windows // parts], refs[windows // parts :]
    out_ref, context, pieces = refs
    _, copy_index = place(parts)
    copies = windows // parts
    plane = lax.axis_index("seq")
    head_width = context_refs[0].shape[1]
    for step in range(group):
        at = pl.multiple_of((plane ^ step) * head_width, LANES)
        context[:, pl.ds(at, head_width)] = context_refs[step][...]
    ordered = context[...]
    for step in range(copies):
        slot = copy_index ^ step
        for piece in range(parts):
            pieces[piece * copies + slot] = jnp.dot(
                ordered, stack_refs[step][piece], preferred_element_type=F32
            )
    result = jnp.concatenate([pieces[d] for d in range(windows)], axis=1)
    out_ref[...] = jnp.where(valid_ref[...] > 0.5, result, 0.0).astype(BF16)


def on_device(
    audio, starts, lengths, slots, conv1_weight, conv2_weight, proj_weight, qkv_weight, out_weight
):
    streams = audio.shape[0]
    windows = lax.axis_size("dp")
    group = lax.axis_size("seq")
    parts = math.gcd(windows, BANDS)
    copies = windows // parts
    assert streams == windows and all(count & (count - 1) == 0 for count in (parts, copies, group))
    share = BANDS // parts
    width = 4 * share + 4
    channels = conv1_weight.shape[1]
    features = proj_weight.shape[1]
    head_width = features // group
    local = windows * W
    rows = JS * streams
    n = parts * streams
    outs = 2 * share + 1
    scale = max(1, windows * group // 32)

    route = [(i, i + 1) for i in range(windows * group - 1)]
    rim = lax.ppermute(audio[:, audio.shape[1] - RIM :], ("dp", "seq"), route)

    def to_part(block, step):
        pairs = [(p * copies + c, (p ^ step) * copies + c) for p in range(parts) for c in range(copies)]
        return lax.ppermute(block, "dp", pairs)

    def to_copy(block, step):
        pairs = [(p * copies + c, p * copies + (c ^ step)) for p in range(parts) for c in range(copies)]
        return lax.ppermute(block, "dp", pairs)

    def to_window(block, step):
        return lax.ppermute(block, "dp", [(i, i ^ step) for i in range(windows)])

    def to_plane(block, step):
        return lax.ppermute(block, "seq", [(i, i ^ step) for i in range(group)])

    proj_all = [proj_weight] + [to_copy(proj_weight, step) for step in range(1, copies)]

    table = jnp.asarray(spectrum_table(N_FFT))
    mix_piece = jax.ShapeDtypeStruct((qkv_weight.shape[0], 3 * head_width), BF16)
    *mel_all, mix = pl.pallas_call(
        functools.partial(mel_kernel, parts, group),
        out_shape=tuple([jax.ShapeDtypeStruct((rows, LANES), BF16)] * parts + [mix_piece]),
        in_specs=[anywhere(), vmem()] + [anywhere()] * 3,
        out_specs=tuple([vmem()] * (parts + 1)),
        scratch_shapes=[
            pltpu.VMEM((streams, RIM + audio.shape[1]), F32),
            pltpu.VMEM(table.shape, F32),
            pltpu.VMEM((parts, rows, LANES), BF16),
            pltpu.SMEM((streams,), jnp.int32),
            pltpu.SemaphoreType.DMA((6,)),
        ],
        compiler_params=params(60),
        cost_estimate=cost(1e10, 2e6),
        name="log_mel",
    )(slots, rim, audio, table, qkv_weight)
    near = [to_part(out_weight, step) for step in range(1, parts - 1)]
    mel_all, proj_all = lax.optimization_barrier((mel_all, proj_all))
    mel_all = [mel_all[0]] + [to_part(mel_all[step], step) for step in range(1, parts)]
    mel_all, near = lax.optimization_barrier((mel_all, near))
    mix_all = [mix] + [to_part(mix, step) for step in range(1, parts)]

    block = jax.ShapeDtypeStruct((local, features), BF16)
    partials = pl.pallas_call(
        functools.partial(conv_kernel, parts, width),
        out_shape=tuple([jax.ShapeDtypeStruct((W * parts, features), BF16)] * windows),
        in_specs=[vmem()] + [anywhere()] * 2 + [vmem()] * (parts - 1) + [anywhere()] * copies,
        out_specs=tuple([vmem()] * windows),
        scratch_shapes=[
            pltpu.VMEM((parts, rows, LANES), F32),
            pltpu.VMEM((rows, LANES), BF16),
            pltpu.VMEM((LANES, outs * channels), BF16),
            pltpu.VMEM((JS * n, outs * channels), BF16),
            pltpu.VMEM((W * n, outs * channels), BF16),
            pltpu.VMEM((W * n, share * channels), BF16),
            pltpu.VMEM(conv2_weight.shape, BF16),
            pltpu.VMEM((copies,) + proj_weight.shape, BF16),
            pltpu.VMEM((features // LANES, W * n, LANES), F32),
            pltpu.SemaphoreType.DMA((2 + copies,)),
        ],
        compiler_params=params(min(40 + 4 * scale, 56)),
        cost_estimate=cost(2e9, 4e6),
        name="conv",
    )(conv1_weight, conv2_weight, *mel_all, *proj_all)
    partials = [to_window(partials[step], step) for step in reversed(range(1, windows))] + [partials[0]]

    ordered, normed, stack = pl.pallas_call(
        functools.partial(norm_kernel, parts),
        out_shape=(block, block, jax.ShapeDtypeStruct((parts,) + mix_piece.shape, BF16)),
        in_specs=[vmem()] * windows + [anywhere()] * parts,
        out_specs=(vmem(), vmem(), vmem()),
        scratch_shapes=[pltpu.VMEM((local, features), BF16), pltpu.SemaphoreType.DMA((parts,))],
        compiler_params=params(min(12 * scale, 32)),
        cost_estimate=cost(1e8, 1e6),
        name="layer_norm",
    )(*partials, *mix_all)
    mix_stacks = [stack] + [to_copy(stack, step) for step in range(1, copies)]
    regrouped, keys, valid = pl.pallas_call(
        functools.partial(mask_kernel, windows, group),
        out_shape=(
            block,
            jax.ShapeDtypeStruct((group, local), F32),
            jax.ShapeDtypeStruct((local, 1), F32),
        ),
        in_specs=[smem()] * 3 + [vmem()],
        out_specs=(vmem(), vmem(), vmem()),
        compiler_params=params(min(8 * scale, 32)),
        cost_estimate=cost(1e8, 1e6),
        name="mask",
    )(slots, starts, lengths, ordered)
    normed, out_here = lax.optimization_barrier((normed, out_weight))
    normed = [normed]
    for step in range(1, group):
        high = 1 << (step.bit_length() - 1)
        normed.append(to_plane(normed[high] if step > high else normed[0], step - high if step > high else high))
    out_all = [out_here] + near + [to_part(out_here, parts - 1)]

    *context, stack = pl.pallas_call(
        functools.partial(attention_kernel, parts, windows, group),
        out_shape=tuple(
            [jax.ShapeDtypeStruct((local, head_width), BF16)] * group
            + [jax.ShapeDtypeStruct((parts,) + out_weight.shape, BF16)]
        ),
        in_specs=[vmem()] * (1 + group + copies) + [anywhere()] * parts,
        out_specs=tuple([vmem()] * (group + 1)),
        scratch_shapes=[
            pltpu.VMEM((windows, group * local, qkv_weight.shape[0]), BF16),
            pltpu.SemaphoreType.DMA((parts,)),
        ],
        compiler_params=params(min(16 * scale, 48)),
        cost_estimate=cost(1e9, 2e6),
        name="attention",
    )(keys, *normed, *mix_stacks, *out_all)
    context = [context[0]] + [to_plane(context[step], step) for step in range(1, group)]
    out_stacks = [stack] + [to_copy(stack, step) for step in range(1, copies)]

    attended = pl.pallas_call(
        functools.partial(output_kernel, parts, windows, group),
        out_shape=block,
        in_specs=[vmem()] * (1 + group + copies),
        out_specs=vmem(),
        scratch_shapes=[
            pltpu.VMEM((local, features), BF16),
            pltpu.VMEM((windows, local, out_weight.shape[1]), F32),
        ],
        compiler_params=params(min(12 * scale, 32)),
        cost_estimate=cost(1e8, 3e6),
        name="output",
    )(valid, *context, *out_stacks)
    shape = (1, windows, 1, W, features)
    return (regrouped.reshape(shape), attended.reshape(shape))


def solution(mesh):
    in_specs = (
        P(None, ("dp", "seq")),
        P(),
        P(),
        P(),
        P(),
        P(),
        P("dp", None),
        P("dp", None),
        P(None, "dp"),
    )
    out_specs = (P("dp", None, "seq", None, None), P("dp", None, "seq", None, None))
    return jax.shard_map(
        on_device, mesh=mesh, in_specs=in_specs, out_specs=out_specs, check_vma=False
    )
```

```python
import functools
import math

import jax
import jax.numpy as jnp
import numpy as np
from jax import lax
from jax.experimental import pallas as pl
from jax.experimental.pallas import tpu as pltpu
from jax.sharding import PartitionSpec as P

HEADS = 8
HEAD_DIM = 128
MELS = 80
BANDS = MELS // 4
N_FFT = 512
HOP = 160
W = 8
RIM = 1024
SPAN = 4 * HOP
JS = W + 1
LANES = 128
CUTS = 2
SAMPLE_RATE = 16000.0
EPS_LOG = 1e-06
EPS_NORM = 1e-05
MASKED = -1e30
F32 = jnp.float32
BF16 = jnp.bfloat16
MIB = 1 << 20


def mel_table(size, bands):
    count = size // 2 + 1
    highest = 2595.0 * math.log10(1.0 + SAMPLE_RATE / 1400.0)
    points = np.linspace(0.0, highest, bands + 2)
    edges = 700.0 * (10.0 ** (points / 2595.0) - 1.0)
    edges[0] = 0.0
    edges[-1] = SAMPLE_RATE / 2.0
    frequency = np.arange(count) * (SAMPLE_RATE / size)
    lower = edges[:-2][None, :]
    middle = edges[1:-1][None, :]
    upper = edges[2:][None, :]
    rising = (frequency[:, None] - lower) / (middle - lower)
    falling = (upper - frequency[:, None]) / (upper - middle)
    return np.maximum(0.0, np.minimum(rising, falling)).astype(np.float32)


def spectrum_table(size):
    half = size // 2
    sample = np.arange(half)
    bins = np.concatenate([np.arange(0, half, 2), np.arange(1, half, 2)])
    angle = sample[:, None] * bins[None, :] % size * (2.0 * math.pi / size)
    table = np.zeros((half + 8, size + LANES))
    for odd in range(2):
        part = angle[:, odd * half // 2 : (odd + 1) * half // 2]
        table[:half, odd * half : (odd + 1) * half] = np.concatenate([np.cos(part), np.sin(part)], axis=1)
    table[:half, size : size + MELS] = mel_table(size, MELS)[bins]
    table[half, :size] = 0.5 - 0.5 * np.cos(np.arange(size) * (2.0 * math.pi / size))
    return table.astype(np.float32)


def vmem():
    return pl.BlockSpec(memory_space=pltpu.VMEM)


def smem():
    return pl.BlockSpec(memory_space=pltpu.SMEM)


def anywhere():
    return pl.BlockSpec(memory_space=pl.ANY)


def params(mib):
    return pltpu.CompilerParams(vmem_limit_bytes=mib * MIB)


def cost(flops, moved):
    return pl.CostEstimate(flops=int(flops), bytes_accessed=int(moved), transcendentals=0)


def place(parts):
    mine = lax.axis_index("dp")
    copies = lax.axis_size("dp") // parts
    return mine // copies, mine % copies


def start_all(copies):
    for copy in copies:
        copy.start()


def wait_all(copies):
    for copy in copies:
        copy.wait()


def iota(rows, columns, axis):
    return lax.broadcasted_iota(jnp.int32, (rows, columns), axis)


def quotient(index, step, count):
    result = jnp.zeros_like(index)
    for i in range(1, count):
        result += (index >= i * step).astype(jnp.int32)
    return result


def one_hot(target, count):
    return (iota(target.shape[0], count, 1) == target).astype(F32).astype(BF16)


def frame_order(parts, copies):
    count = parts * copies * W
    row = iota(count, 1, 0)
    k = quotient(row, W, parts * copies)
    p = quotient(k, copies, parts)
    return one_hot((k - p * copies) * W * parts + (row - k * W) * parts + p, count)


def samples(index, windows, group):
    return (index + quotient(index, W, windows) * (group - 1) * W) * SPAN


def mix_columns(group, qkv_ref, mix_out, sems):
    features = qkv_ref.shape[1] // 3
    width = features // group
    first = pl.multiple_of(lax.axis_index("seq") * width, LANES)
    return [
        pltpu.make_async_copy(
            qkv_ref.at[:, pl.ds(kind * features + first, width)],
            mix_out.at[:, pl.ds(kind * width, width)],
            sems.at[kind],
        )
        for kind in range(3)
    ]


def banded_weights(width, conv1_ref, banded_out):
    taps, channels = conv1_ref.shape
    row = lax.broadcasted_iota(jnp.int32, (LANES, taps), 0)
    tap = lax.broadcasted_iota(jnp.int32, (LANES, taps), 1)
    line = (tap >= 3).astype(jnp.int32) + (tap >= 6).astype(jnp.int32)
    target = line * (width - 3) + tap + 1
    weight = conv1_ref[...]
    for g in range(banded_out.shape[1] // channels):
        select = (row == target + 2 * g).astype(F32).astype(BF16)
        banded_out[:, g * channels : (g + 1) * channels] = jnp.dot(
            select, weight, preferred_element_type=F32
        ).astype(BF16)


def mel_kernel(parts, group, slots_here, rim_ref, audio_ref, table_ref, qkv_ref, *refs):
    outs_refs, (mix_out, ext, table, blocks, slots_ref, sems) = refs[:parts], refs[parts:]
    load_slots = pltpu.make_async_copy(slots_here, slots_ref, sems.at[5])
    load_slots.start()
    load_audio = pltpu.make_async_copy(audio_ref, ext.at[:, pl.ds(RIM, audio_ref.shape[1])], sems.at[3])
    third = table_ref.shape[0] // 3
    load_table = [
        pltpu.make_async_copy(table_ref.at[pl.ds(i * third, third)], table.at[pl.ds(i * third, third)], sems.at[6 + i])
        for i in range(3)
    ]
    load_audio.start()
    start_all(load_table)
    pieces = mix_columns(group, qkv_ref, mix_out, sems)
    start_all(pieces)
    streams = audio_ref.shape[0]
    rows = JS * streams
    ext[:, :RIM] = rim_ref[...]
    load_audio.wait()
    phases = []
    for phase in range(4):
        start = HOP * phase + 32
        base, shift = start // LANES * LANES, start % LANES
        length = N_FFT + (LANES if shift else 0)
        block = jnp.concatenate(
            [ext[:, SPAN * j + base : SPAN * j + base + length] for j in range(JS)], axis=0
        )
        if shift:
            block = pltpu.roll(block, length - shift, 1)[:, :N_FFT]
        phases.append(block)
    frames = jnp.concatenate(phases, axis=0)
    wait_all(load_table)
    half = N_FFT // 2
    frames = frames * table[half : half + 1, :N_FFT]
    low, high = frames[:, :half], frames[:, half:]
    powers = []
    for odd in range(2):
        spectrum = jnp.dot(
            low - high if odd else low + high,
            table[:half, odd * half : (odd + 1) * half],
            precision=lax.Precision.HIGHEST,
            preferred_element_type=F32,
        )
        real, imag = spectrum[:, : half // 2], spectrum[:, half // 2 :]
        powers.append(real * real + imag * imag)
    mel_power = jnp.dot(
        jnp.concatenate(powers, axis=1),
        table[:half, N_FFT:],
        precision=lax.Precision.HIGHEST,
        preferred_element_type=F32,
    )
    load_slots.wait()
    column = iota(1, rows, 1)
    early = quotient(column, streams, JS)
    target = jnp.zeros((1, rows), jnp.int32)
    for u in range(streams):
        target = jnp.where(column - early * streams == u, early * streams + slots_ref[u], target)
    routing = (target == iota(rows, rows, 0)).astype(F32).astype(BF16)
    log_mel = jnp.log(mel_power + EPS_LOG)
    share = BANDS // parts
    width = 4 * share + 4
    lane = iota(rows, LANES, 1)
    by_phase = [log_mel[phase * rows : (phase + 1) * rows] for phase in range(4)]

    def next_four(frames):
        return jnp.concatenate([frames[streams:], jnp.zeros((streams, LANES), F32)], axis=0)

    taps = [by_phase[1], by_phase[2], by_phase[3], next_four(by_phase[0]), next_four(by_phase[1])]
    for part in range(parts):
        first = 4 * share * part - 4
        block = jnp.zeros((rows, LANES), F32)
        for delta, frames in enumerate(taps):
            band = lane - width * delta + first
            here = (lane >= width * delta) & (lane < width * (delta + 1)) & (band >= 0) & (band < MELS)
            shift = (width * delta - first) % LANES
            block = jnp.where(here, pltpu.roll(frames, shift, 1) if shift else frames, block)
        blocks[part] = jnp.dot(routing, block.astype(BF16), preferred_element_type=F32).astype(BF16)
    mine, _ = place(parts)
    for step in range(parts):
        outs_refs[step][...] = blocks[mine ^ step]
    wait_all(pieces)


def stacked(parts, pieces, stack_out, sems, base):
    part, _ = place(parts)
    rows = stack_out.shape[1] // CUTS
    copies = []
    for step in range(parts):
        for cut in range(CUTS):
            at = pl.ds(cut * rows, rows)
            copies.append(
                pltpu.make_async_copy(
                    pieces[step].at[at], stack_out.at[part ^ step, at], sems.at[base + len(copies)]
                )
            )
    return copies


def conv_kernel(parts, width, conv1_ref, conv2_ref, *refs):
    part, copy_index = place(parts)
    mine = lax.axis_index("dp")
    windows = lax.axis_size("dp")
    copies = windows // parts
    mel_refs, refs = refs[:parts], refs[parts:]
    proj_refs, refs = refs[:copies], refs[copies:]
    outs_refs, refs = refs[:windows], refs[windows:]
    mel, banded_ref, even, odd, second, by_slot, partial = refs
    banded_weights(width, conv1_ref, banded_ref)
    streams = mel_refs[0].shape[0] // JS
    n = parts * streams
    for step in range(parts):
        mel[part ^ step] = mel_refs[step][...].astype(F32)
    evens = jnp.concatenate(
        [mel[p, j * streams : (j + 1) * streams, :] for j in range(JS) for p in range(parts)], axis=0
    )
    odds = pltpu.roll(evens[: W * n], LANES - 2 * width, 1).astype(BF16)
    evens = evens.astype(BF16)
    channels = conv2_ref.shape[1]
    outs = banded_ref.shape[1] // channels
    for g in range(outs):
        lanes = slice(g * channels, (g + 1) * channels)
        weight = banded_ref[:, lanes]
        even[:, lanes] = jax.nn.relu(jnp.dot(evens, weight, preferred_element_type=F32)).astype(BF16)
        odd[:, lanes] = jax.nn.relu(jnp.dot(odds, weight, preferred_element_type=F32)).astype(BF16)

    for h in range((outs - 1) // 2):
        lanes = slice(2 * h * channels, (2 * h + 3) * channels)
        taps = jnp.concatenate([even[: W * n, lanes], odd[:, lanes], even[n:, lanes]], axis=1)
        total = jnp.dot(taps, conv2_ref[...], preferred_element_type=F32)
        second[:, h * channels : (h + 1) * channels] = jax.nn.relu(total).astype(BF16)
    depth = by_slot.shape[2]
    for slot in range(copies):
        by_slot[slot] = second[:, slot * depth : (slot + 1) * depth]
    sums = jnp.dot(by_slot[copy_index], proj_refs[0][...], preferred_element_type=F32)
    for step in range(1, copies):
        sums += jnp.dot(by_slot[copy_index ^ step], proj_refs[step][...], preferred_element_type=F32)
    for block in range(partial.shape[0]):
        partial[block] = sums[:, block * LANES : (block + 1) * LANES]
    for step in range(windows):
        for block in range(partial.shape[0]):
            rows = partial[block, pl.ds(mine ^ step, W * parts, stride=streams), :]
            outs_refs[step][:, block * LANES : (block + 1) * LANES] = rows.astype(BF16)


def bounds(row, slots_ref, starts_ref, lengths_ref):
    begin, span = jnp.int32(0), jnp.int32(0)
    for u in range(slots_ref.shape[0]):
        chosen = slots_ref[u] == row
        begin = begin + jnp.where(chosen, starts_ref[u], 0)
        span = span + jnp.where(chosen, lengths_ref[u], 0)
    return begin, begin + span


def norm_kernel(parts, *refs):
    _, copy_index = place(parts)
    windows = lax.axis_size("dp")
    copies = windows // parts
    part_refs, refs = refs[:windows][::-1], refs[windows:]
    piece_refs, refs = refs[:parts], refs[parts:]
    rows_out, normed_out, stack_out, encoded, sems = refs
    moves = stacked(parts, piece_refs, stack_out, sems, 0)
    start_all(moves)
    rows = W * parts
    for copy in range(copies):
        total = part_refs[copy][...].astype(F32)
        for step in range(1, parts):
            total += part_refs[step * copies + copy][...].astype(F32)
        at = pl.multiple_of((copy_index ^ copy) * rows, rows)
        encoded[pl.ds(at, rows), :] = total.astype(BF16)
    values = jnp.dot(frame_order(parts, copies), encoded[...], preferred_element_type=F32)
    rows_out[...] = values.astype(BF16)
    mean = jnp.mean(values, axis=-1, keepdims=True)
    centered = values - mean
    variance = jnp.mean(centered * centered, axis=-1, keepdims=True)
    normed_out[...] = (centered * lax.rsqrt(variance + EPS_NORM)).astype(BF16)
    wait_all(moves)


def mask_kernel(windows, group, slots_ref, starts_ref, lengths_ref, rows_ref, rows_out, keys_out, valid_out):
    begin, end = bounds(lax.axis_index("dp"), slots_ref, starts_ref, lengths_ref)
    sample = samples(iota(windows * W, 1, 0), windows, group) + lax.axis_index("seq") * (W * SPAN)
    valid = (sample >= begin) & (sample < end)
    rows_out[...] = jnp.where(valid, rows_ref[...].astype(F32), 0.0).astype(BF16)
    valid_out[...] = valid.astype(F32)
    keys = samples(iota(group, windows * W, 1), windows, group) + iota(group, windows * W, 0) * (W * SPAN)
    keys_out[...] = ((keys >= begin) & (keys < end)).astype(F32)


def attention_kernel(parts, windows, group, keys_ref, *refs):
    _, copy_index = place(parts)
    plane = lax.axis_index("seq")
    copies = windows // parts
    normed_refs, refs = refs[:group], refs[group:]
    stack_refs, refs = refs[:copies], refs[copies:]
    weight_refs, refs = refs[:parts], refs[parts:]
    outs_refs, (stack_out, pieces, sems) = refs[:group], refs[group:]
    moves = stacked(parts, weight_refs, stack_out, sems, 0)
    start_all(moves)
    keys = [keys_ref[pl.ds(plane ^ step, 1), :] for step in range(group)]
    valid = jnp.concatenate(keys, axis=1) > 0.5
    local = normed_refs[0].shape[0]
    depth = pieces.shape[2]
    for step in range(group):
        for piece in range(windows):
            pieces[piece, step * local : (step + 1) * local, :] = normed_refs[step][
                :, piece * depth : (piece + 1) * depth
            ]
    mixed = 0.0
    for step in range(copies):
        slot = copy_index ^ step
        normed = jnp.concatenate([pieces[piece * copies + slot] for piece in range(parts)], axis=1)
        weights = stack_refs[step][...].reshape(parts * depth, stack_refs[step].shape[2])
        mixed += jnp.dot(normed, weights, preferred_element_type=F32)
    mixed = mixed.astype(BF16)
    width = mixed.shape[1] // 3
    scale = HEAD_DIM ** (-0.5)
    for head in range(width // HEAD_DIM):
        at = head * HEAD_DIM
        query = mixed[:, at : at + HEAD_DIM]
        key = mixed[:, width + at : width + at + HEAD_DIM]
        value = mixed[:, 2 * width + at : 2 * width + at + HEAD_DIM]
        scores = lax.dot_general(query, key, (((1,), (1,)), ((), ())), preferred_element_type=F32) * scale
        masked = jnp.where(valid, scores, MASKED)
        peak = jnp.max(masked, axis=1, keepdims=True)
        weight = jnp.where(valid, jnp.exp(masked - peak), 0.0)
        total = jnp.sum(weight, axis=1, keepdims=True)
        summed = jnp.dot(weight.astype(BF16), value, preferred_element_type=F32)
        context = (summed / total).astype(BF16)
        for step in range(group):
            outs_refs[step][:, at : at + HEAD_DIM] = context[step * local : (step + 1) * local]
    wait_all(moves)


def output_kernel(parts, windows, group, valid_ref, *refs):
    context_refs, refs = refs[:group], refs[group:]
    stack_refs, refs = refs[: windows // parts], refs[windows // parts :]
    out_ref, context, pieces = refs
    _, copy_index = place(parts)
    copies = windows // parts
    plane = lax.axis_index("seq")
    head_width = context_refs[0].shape[1]
    for step in range(group):
        at = pl.multiple_of((plane ^ step) * head_width, LANES)
        context[:, pl.ds(at, head_width)] = context_refs[step][...]
    ordered = context[...]
    for step in range(copies):
        slot = copy_index ^ step
        for piece in range(parts):
            pieces[piece * copies + slot] = jnp.dot(
                ordered, stack_refs[step][piece], preferred_element_type=F32
            )
    result = jnp.concatenate([pieces[d] for d in range(windows)], axis=1)
    out_ref[...] = jnp.where(valid_ref[...] > 0.5, result, 0.0).astype(BF16)


def on_device(
    audio, starts, lengths, slots, conv1_weight, conv2_weight, proj_weight, qkv_weight, out_weight
):
    streams = audio.shape[0]
    windows = lax.axis_size("dp")
    group = lax.axis_size("seq")
    parts = math.gcd(windows, BANDS)
    copies = windows // parts
    assert streams == windows and all(count & (count - 1) == 0 for count in (parts, copies, group))
    share = BANDS // parts
    width = 4 * share + 4
    channels = conv1_weight.shape[1]
    features = proj_weight.shape[1]
    head_width = features // group
    local = windows * W
    rows = JS * streams
    n = parts * streams
    outs = 2 * share + 1
    scale = max(1, windows * group // 32)

    route = [(i, i + 1) for i in range(windows * group - 1)]
    rim = lax.ppermute(audio[:, audio.shape[1] - RIM :], ("dp", "seq"), route)

    def to_part(block, step):
        pairs = [(p * copies + c, (p ^ step) * copies + c) for p in range(parts) for c in range(copies)]
        return lax.ppermute(block, "dp", pairs)

    def to_copy(block, step):
        pairs = [(p * copies + c, p * copies + (c ^ step)) for p in range(parts) for c in range(copies)]
        return lax.ppermute(block, "dp", pairs)

    def to_window(block, step):
        return lax.ppermute(block, "dp", [(i, i ^ step) for i in range(windows)])

    def to_plane(block, step):
        return lax.ppermute(block, "seq", [(i, i ^ step) for i in range(group)])

    proj_all = [proj_weight] + [to_copy(proj_weight, step) for step in range(1, copies)]

    table = jnp.asarray(spectrum_table(N_FFT))
    mix_piece = jax.ShapeDtypeStruct((qkv_weight.shape[0], 3 * head_width), BF16)
    *mel_all, mix = pl.pallas_call(
        functools.partial(mel_kernel, parts, group),
        out_shape=tuple([jax.ShapeDtypeStruct((rows, LANES), BF16)] * parts + [mix_piece]),
        in_specs=[anywhere(), vmem()] + [anywhere()] * 3,
        out_specs=tuple([vmem()] * (parts + 1)),
        scratch_shapes=[
            pltpu.VMEM((streams, RIM + audio.shape[1]), F32),
            pltpu.VMEM(table.shape, F32),
            pltpu.VMEM((parts, rows, LANES), BF16),
            pltpu.SMEM((streams,), jnp.int32),
            pltpu.SemaphoreType.DMA((9,)),
        ],
        compiler_params=params(60),
        cost_estimate=cost(1e10, 2e6),
        name="log_mel",
    )(slots, rim, audio, table, qkv_weight)
    near = [to_part(out_weight, step) for step in range(1, parts - 1)]
    mel_all, proj_all = lax.optimization_barrier((mel_all, proj_all))
    mel_all = [mel_all[0]] + [to_part(mel_all[step], step) for step in range(1, parts)]
    mel_all, near = lax.optimization_barrier((mel_all, near))
    mix_all = [mix] + [to_part(mix, step) for step in range(1, parts)]

    block = jax.ShapeDtypeStruct((local, features), BF16)
    partials = pl.pallas_call(
        functools.partial(conv_kernel, parts, width),
        out_shape=tuple([jax.ShapeDtypeStruct((W * parts, features), BF16)] * windows),
        in_specs=[vmem()] * (2 + parts + copies),
        out_specs=tuple([vmem()] * windows),
        scratch_shapes=[
            pltpu.VMEM((parts, rows, LANES), F32),
            pltpu.VMEM((LANES, outs * channels), BF16),
            pltpu.VMEM((JS * n, outs * channels), BF16),
            pltpu.VMEM((W * n, outs * channels), BF16),
            pltpu.VMEM((W * n, share * channels), BF16),
            pltpu.VMEM((copies, W * n, proj_weight.shape[0]), BF16),
            pltpu.VMEM((features // LANES, W * n, LANES), F32),
        ],
        compiler_params=params(min(40 + 4 * scale, 56)),
        cost_estimate=cost(2e9, 4e6),
        name="conv",
    )(conv1_weight, conv2_weight, *mel_all, *proj_all)
    partials = [to_window(partials[step], step) for step in reversed(range(1, windows))] + [partials[0]]

    ordered, normed, stack = pl.pallas_call(
        functools.partial(norm_kernel, parts),
        out_shape=(block, block, jax.ShapeDtypeStruct((parts,) + mix_piece.shape, BF16)),
        in_specs=[vmem()] * windows + [anywhere()] * parts,
        out_specs=(vmem(), vmem(), vmem()),
        scratch_shapes=[pltpu.VMEM((local, features), BF16), pltpu.SemaphoreType.DMA((CUTS * parts,))],
        compiler_params=params(min(12 * scale, 32)),
        cost_estimate=cost(1e8, 1e6),
        name="layer_norm",
    )(*partials, *mix_all)
    mix_stacks = [stack] + [to_copy(stack, step) for step in range(1, copies)]
    regrouped, keys, valid = pl.pallas_call(
        functools.partial(mask_kernel, windows, group),
        out_shape=(
            block,
            jax.ShapeDtypeStruct((group, local), F32),
            jax.ShapeDtypeStruct((local, 1), F32),
        ),
        in_specs=[smem()] * 3 + [vmem()],
        out_specs=(vmem(), vmem(), vmem()),
        compiler_params=params(min(8 * scale, 32)),
        cost_estimate=cost(1e8, 1e6),
        name="mask",
    )(slots, starts, lengths, ordered)
    normed, out_here = lax.optimization_barrier((normed, out_weight))
    normed = [normed]
    for step in range(1, group):
        high = 1 << (step.bit_length() - 1)
        normed.append(to_plane(normed[high] if step > high else normed[0], step - high if step > high else high))
    out_all = [out_here] + near + [to_part(out_here, parts - 1)]

    *context, stack = pl.pallas_call(
        functools.partial(attention_kernel, parts, windows, group),
        out_shape=tuple(
            [jax.ShapeDtypeStruct((local, head_width), BF16)] * group
            + [jax.ShapeDtypeStruct((parts,) + out_weight.shape, BF16)]
        ),
        in_specs=[vmem()] * (1 + group + copies) + [anywhere()] * parts,
        out_specs=tuple([vmem()] * (group + 1)),
        scratch_shapes=[
            pltpu.VMEM((windows, group * local, qkv_weight.shape[0]), BF16),
            pltpu.SemaphoreType.DMA((CUTS * parts,)),
        ],
        compiler_params=params(min(16 * scale, 48)),
        cost_estimate=cost(1e9, 2e6),
        name="attention",
    )(keys, *normed, *mix_stacks, *out_all)
    context = [context[0]] + [to_plane(context[step], step) for step in range(1, group)]
    out_stacks = [stack] + [to_copy(stack, step) for step in range(1, copies)]

    attended = pl.pallas_call(
        functools.partial(output_kernel, parts, windows, group),
        out_shape=block,
        in_specs=[vmem()] * (1 + group + copies),
        out_specs=vmem(),
        scratch_shapes=[
            pltpu.VMEM((local, features), BF16),
            pltpu.VMEM((windows, local, out_weight.shape[1]), F32),
        ],
        compiler_params=params(min(12 * scale, 32)),
        cost_estimate=cost(1e8, 3e6),
        name="output",
    )(valid, *context, *out_stacks)
    shape = (1, windows, 1, W, features)
    return (regrouped.reshape(shape), attended.reshape(shape))


def solution(mesh):
    in_specs = (
        P(None, ("dp", "seq")),
        P(),
        P(),
        P(),
        P(),
        P(),
        P("dp", None),
        P("dp", None),
        P(None, "dp"),
    )
    out_specs = (P("dp", None, "seq", None, None), P("dp", None, "seq", None, None))
    return jax.shard_map(
        on_device, mesh=mesh, in_specs=in_specs, out_specs=out_specs, check_vma=False
    )
```

```python
import functools
import math

import jax
import jax.numpy as jnp
import numpy as np
from jax import lax
from jax.experimental import pallas as pl
from jax.experimental.pallas import tpu as pltpu
from jax.sharding import PartitionSpec as P

HEADS = 8
HEAD_DIM = 128
MELS = 80
BANDS = MELS // 4
N_FFT = 512
HOP = 160
W = 8
RIM = 1024
SPAN = 4 * HOP
JS = W + 1
LANES = 128
SAMPLE_RATE = 16000.0
EPS_LOG = 1e-06
EPS_NORM = 1e-05
MASKED = -1e30
F32 = jnp.float32
BF16 = jnp.bfloat16
MIB = 1 << 20


def mel_table(size, bands):
    count = size // 2 + 1
    highest = 2595.0 * math.log10(1.0 + SAMPLE_RATE / 1400.0)
    points = np.linspace(0.0, highest, bands + 2)
    edges = 700.0 * (10.0 ** (points / 2595.0) - 1.0)
    edges[0] = 0.0
    edges[-1] = SAMPLE_RATE / 2.0
    frequency = np.arange(count) * (SAMPLE_RATE / size)
    lower = edges[:-2][None, :]
    middle = edges[1:-1][None, :]
    upper = edges[2:][None, :]
    rising = (frequency[:, None] - lower) / (middle - lower)
    falling = (upper - frequency[:, None]) / (upper - middle)
    return np.maximum(0.0, np.minimum(rising, falling)).astype(np.float32)


def spectrum_table(size):
    half = size // 2
    sample = np.arange(half)
    bins = np.concatenate([np.arange(0, half, 2), np.arange(1, half, 2)])
    angle = sample[:, None] * bins[None, :] % size * (2.0 * math.pi / size)
    table = np.zeros((half + 8, size + LANES))
    for odd in range(2):
        part = angle[:, odd * half // 2 : (odd + 1) * half // 2]
        table[:half, odd * half : (odd + 1) * half] = np.concatenate([np.cos(part), np.sin(part)], axis=1)
    table[:half, size : size + MELS] = mel_table(size, MELS)[bins]
    table[half, :size] = 0.5 - 0.5 * np.cos(np.arange(size) * (2.0 * math.pi / size))
    return table.astype(np.float32)


def vmem():
    return pl.BlockSpec(memory_space=pltpu.VMEM)


def smem():
    return pl.BlockSpec(memory_space=pltpu.SMEM)


def anywhere():
    return pl.BlockSpec(memory_space=pl.ANY)


def params(mib):
    return pltpu.CompilerParams(vmem_limit_bytes=mib * MIB)


def cost(flops, moved):
    return pl.CostEstimate(flops=int(flops), bytes_accessed=int(moved), transcendentals=0)


def place(parts):
    mine = lax.axis_index("dp")
    copies = lax.axis_size("dp") // parts
    return mine // copies, mine % copies


def start_all(copies):
    for copy in copies:
        copy.start()


def wait_all(copies):
    for copy in copies:
        copy.wait()


def iota(rows, columns, axis):
    return lax.broadcasted_iota(jnp.int32, (rows, columns), axis)


def quotient(index, step, count):
    result = jnp.zeros_like(index)
    for i in range(1, count):
        result += (index >= i * step).astype(jnp.int32)
    return result


def one_hot(target, count):
    return (iota(target.shape[0], count, 1) == target).astype(F32).astype(BF16)


def frame_order(parts, copies):
    count = parts * copies * W
    row = iota(count, 1, 0)
    k = quotient(row, W, parts * copies)
    p = quotient(k, copies, parts)
    return one_hot((k - p * copies) * W * parts + (row - k * W) * parts + p, count)


def samples(index, windows, group):
    return (index + quotient(index, W, windows) * (group - 1) * W) * SPAN


def mix_columns(group, qkv_ref, mix_out, sems):
    features = qkv_ref.shape[1] // 3
    width = features // group
    first = pl.multiple_of(lax.axis_index("seq") * width, LANES)
    return [
        pltpu.make_async_copy(
            qkv_ref.at[:, pl.ds(kind * features + first, width)],
            mix_out.at[:, pl.ds(kind * width, width)],
            sems.at[kind],
        )
        for kind in range(3)
    ]


def banded_weights(width, conv1_ref, banded_out):
    taps, channels = conv1_ref.shape
    row = lax.broadcasted_iota(jnp.int32, (LANES, taps), 0)
    tap = lax.broadcasted_iota(jnp.int32, (LANES, taps), 1)
    line = (tap >= 3).astype(jnp.int32) + (tap >= 6).astype(jnp.int32)
    target = line * (width - 3) + tap + 1
    weight = conv1_ref[...]
    for g in range(banded_out.shape[1] // channels):
        select = (row == target + 2 * g).astype(F32).astype(BF16)
        banded_out[:, g * channels : (g + 1) * channels] = jnp.dot(
            select, weight, preferred_element_type=F32
        ).astype(BF16)


def mel_kernel(parts, group, slots_here, rim_ref, audio_ref, table_ref, qkv_ref, *refs):
    outs_refs, (mix_out, ext, table, blocks, slots_ref, sems) = refs[:parts], refs[parts:]
    load_slots = pltpu.make_async_copy(slots_here, slots_ref, sems.at[5])
    load_slots.start()
    load_audio = pltpu.make_async_copy(audio_ref, ext.at[:, pl.ds(RIM, audio_ref.shape[1])], sems.at[3])
    load_table = pltpu.make_async_copy(table_ref, table, sems.at[4])
    load_audio.start()
    load_table.start()
    pieces = mix_columns(group, qkv_ref, mix_out, sems)
    start_all(pieces)
    streams = audio_ref.shape[0]
    rows = JS * streams
    ext[:, :RIM] = rim_ref[...]
    load_audio.wait()
    phases = []
    for phase in range(4):
        start = HOP * phase + 32
        base, shift = start // LANES * LANES, start % LANES
        length = N_FFT + (LANES if shift else 0)
        block = jnp.concatenate(
            [ext[:, SPAN * j + base : SPAN * j + base + length] for j in range(JS)], axis=0
        )
        if shift:
            block = pltpu.roll(block, length - shift, 1)[:, :N_FFT]
        phases.append(block)
    frames = jnp.concatenate(phases, axis=0)
    load_table.wait()
    half = N_FFT // 2
    frames = frames * table[half : half + 1, :N_FFT]
    low, high = frames[:, :half], frames[:, half:]
    powers = []
    for odd in range(2):
        spectrum = jnp.dot(
            low - high if odd else low + high,
            table[:half, odd * half : (odd + 1) * half],
            precision=lax.Precision.HIGHEST,
            preferred_element_type=F32,
        )
        real, imag = spectrum[:, : half // 2], spectrum[:, half // 2 :]
        powers.append(real * real + imag * imag)
    mel_power = jnp.dot(
        jnp.concatenate(powers, axis=1),
        table[:half, N_FFT:],
        precision=lax.Precision.HIGHEST,
        preferred_element_type=F32,
    )
    load_slots.wait()
    column = iota(1, rows, 1)
    early = quotient(column, streams, JS)
    target = jnp.zeros((1, rows), jnp.int32)
    for u in range(streams):
        target = jnp.where(column - early * streams == u, early * streams + slots_ref[u], target)
    routing = (target == iota(rows, rows, 0)).astype(F32).astype(BF16)
    log_mel = jnp.log(mel_power + EPS_LOG)
    share = BANDS // parts
    width = 4 * share + 4
    lane = iota(rows, LANES, 1)
    by_phase = [log_mel[phase * rows : (phase + 1) * rows] for phase in range(4)]

    def next_four(frames):
        return jnp.concatenate([frames[streams:], jnp.zeros((streams, LANES), F32)], axis=0)

    taps = [by_phase[1], by_phase[2], by_phase[3], next_four(by_phase[0]), next_four(by_phase[1])]
    for part in range(parts):
        first = 4 * share * part - 4
        block = jnp.zeros((rows, LANES), F32)
        for delta, frames in enumerate(taps):
            band = lane - width * delta + first
            here = (lane >= width * delta) & (lane < width * (delta + 1)) & (band >= 0) & (band < MELS)
            shift = (width * delta - first) % LANES
            block = jnp.where(here, pltpu.roll(frames, shift, 1) if shift else frames, block)
        blocks[part] = jnp.dot(routing, block.astype(BF16), preferred_element_type=F32).astype(BF16)
    mine, _ = place(parts)
    for step in range(parts):
        outs_refs[step][...] = blocks[mine ^ step]
    wait_all(pieces)


def stacked(parts, pieces, stack_out, sems, base):
    part, _ = place(parts)
    return [
        pltpu.make_async_copy(pieces[step], stack_out.at[part ^ step], sems.at[base + step])
        for step in range(parts)
    ]


def conv_kernel(parts, width, conv1_ref, conv2_ref, *refs):
    part, copy_index = place(parts)
    mine = lax.axis_index("dp")
    windows = lax.axis_size("dp")
    copies = windows // parts
    mel_refs, refs = refs[:parts], refs[parts:]
    proj_refs, refs = refs[:copies], refs[copies:]
    outs_refs, refs = refs[:windows], refs[windows:]
    mel, banded_ref, even, odd, second, by_slot, partial = refs
    banded_weights(width, conv1_ref, banded_ref)
    streams = mel_refs[0].shape[0] // JS
    n = parts * streams
    for step in range(parts):
        mel[part ^ step] = mel_refs[step][...].astype(F32)
    evens = jnp.concatenate(
        [mel[p, j * streams : (j + 1) * streams, :] for j in range(JS) for p in range(parts)], axis=0
    )
    odds = pltpu.roll(evens[: W * n], LANES - 2 * width, 1).astype(BF16)
    evens = evens.astype(BF16)
    channels = conv2_ref.shape[1]
    outs = banded_ref.shape[1] // channels
    for g in range(outs):
        lanes = slice(g * channels, (g + 1) * channels)
        weight = banded_ref[:, lanes]
        even[:, lanes] = jax.nn.relu(jnp.dot(evens, weight, preferred_element_type=F32)).astype(BF16)
        odd[:, lanes] = jax.nn.relu(jnp.dot(odds, weight, preferred_element_type=F32)).astype(BF16)

    for h in range((outs - 1) // 2):
        lanes = slice(2 * h * channels, (2 * h + 3) * channels)
        taps = jnp.concatenate([even[: W * n, lanes], odd[:, lanes], even[n:, lanes]], axis=1)
        total = jnp.dot(taps, conv2_ref[...], preferred_element_type=F32)
        second[:, h * channels : (h + 1) * channels] = jax.nn.relu(total).astype(BF16)
    depth = by_slot.shape[2]
    for slot in range(copies):
        by_slot[slot] = second[:, slot * depth : (slot + 1) * depth]
    sums = jnp.dot(by_slot[copy_index], proj_refs[0][...], preferred_element_type=F32)
    for step in range(1, copies):
        sums += jnp.dot(by_slot[copy_index ^ step], proj_refs[step][...], preferred_element_type=F32)
    for block in range(partial.shape[0]):
        partial[block] = sums[:, block * LANES : (block + 1) * LANES]
    for step in range(windows):
        for block in range(partial.shape[0]):
            rows = partial[block, pl.ds(mine ^ step, W * parts, stride=streams), :]
            outs_refs[step][:, block * LANES : (block + 1) * LANES] = rows.astype(BF16)


def bounds(row, slots_ref, starts_ref, lengths_ref):
    begin, span = jnp.int32(0), jnp.int32(0)
    for u in range(slots_ref.shape[0]):
        chosen = slots_ref[u] == row
        begin = begin + jnp.where(chosen, starts_ref[u], 0)
        span = span + jnp.where(chosen, lengths_ref[u], 0)
    return begin, begin + span


def norm_kernel(parts, *refs):
    part, copy_index = place(parts)
    windows = lax.axis_size("dp")
    copies = windows // parts
    part_refs, refs = refs[:windows][::-1], refs[windows:]
    piece_refs, refs = refs[:parts], refs[parts:]
    rows_out, normed_out, stack_out, encoded = refs
    for step in range(parts):
        stack_out[part ^ step] = piece_refs[step][...]
    rows = W * parts
    for copy in range(copies):
        total = part_refs[copy][...].astype(F32)
        for step in range(1, parts):
            total += part_refs[step * copies + copy][...].astype(F32)
        at = pl.multiple_of((copy_index ^ copy) * rows, rows)
        encoded[pl.ds(at, rows), :] = total.astype(BF16)
    values = jnp.dot(frame_order(parts, copies), encoded[...], preferred_element_type=F32)
    rows_out[...] = values.astype(BF16)
    mean = jnp.mean(values, axis=-1, keepdims=True)
    centered = values - mean
    variance = jnp.mean(centered * centered, axis=-1, keepdims=True)
    normed_out[...] = (centered * lax.rsqrt(variance + EPS_NORM)).astype(BF16)


def mask_kernel(windows, group, slots_ref, starts_ref, lengths_ref, rows_ref, rows_out, keys_out, valid_out):
    begin, end = bounds(lax.axis_index("dp"), slots_ref, starts_ref, lengths_ref)
    sample = samples(iota(windows * W, 1, 0), windows, group) + lax.axis_index("seq") * (W * SPAN)
    valid = (sample >= begin) & (sample < end)
    rows_out[...] = jnp.where(valid, rows_ref[...].astype(F32), 0.0).astype(BF16)
    valid_out[...] = valid.astype(F32)
    keys = samples(iota(group, windows * W, 1), windows, group) + iota(group, windows * W, 0) * (W * SPAN)
    keys_out[...] = ((keys >= begin) & (keys < end)).astype(F32)


def attention_kernel(parts, windows, group, keys_ref, *refs):
    _, copy_index = place(parts)
    plane = lax.axis_index("seq")
    copies = windows // parts
    normed_refs, refs = refs[:group], refs[group:]
    stack_refs, refs = refs[:copies], refs[copies:]
    weight_refs, refs = refs[:parts], refs[parts:]
    outs_refs, (stack_out, pieces, sems) = refs[:group], refs[group:]
    moves = stacked(parts, weight_refs, stack_out, sems, 0)
    start_all(moves)
    keys = [keys_ref[pl.ds(plane ^ step, 1), :] for step in range(group)]
    valid = jnp.concatenate(keys, axis=1) > 0.5
    local = normed_refs[0].shape[0]
    depth = pieces.shape[2]
    for step in range(group):
        for piece in range(windows):
            pieces[piece, step * local : (step + 1) * local, :] = normed_refs[step][
                :, piece * depth : (piece + 1) * depth
            ]
    mixed = 0.0
    for step in range(copies):
        slot = copy_index ^ step
        normed = jnp.concatenate([pieces[piece * copies + slot] for piece in range(parts)], axis=1)
        weights = stack_refs[step][...].reshape(parts * depth, stack_refs[step].shape[2])
        mixed += jnp.dot(normed, weights, preferred_element_type=F32)
    mixed = mixed.astype(BF16)
    width = mixed.shape[1] // 3
    scale = HEAD_DIM ** (-0.5)
    for head in range(width // HEAD_DIM):
        at = head * HEAD_DIM
        query = mixed[:, at : at + HEAD_DIM]
        key = mixed[:, width + at : width + at + HEAD_DIM]
        value = mixed[:, 2 * width + at : 2 * width + at + HEAD_DIM]
        scores = lax.dot_general(query, key, (((1,), (1,)), ((), ())), preferred_element_type=F32) * scale
        masked = jnp.where(valid, scores, MASKED)
        peak = jnp.max(masked, axis=1, keepdims=True)
        weight = jnp.where(valid, jnp.exp(masked - peak), 0.0)
        total = jnp.sum(weight, axis=1, keepdims=True)
        summed = jnp.dot(weight.astype(BF16), value, preferred_element_type=F32)
        context = (summed / total).astype(BF16)
        for step in range(group):
            outs_refs[step][:, at : at + HEAD_DIM] = context[step * local : (step + 1) * local]
    wait_all(moves)


def output_kernel(parts, windows, group, valid_ref, *refs):
    context_refs, refs = refs[:group], refs[group:]
    stack_refs, refs = refs[: windows // parts], refs[windows // parts :]
    out_ref, context, pieces = refs
    _, copy_index = place(parts)
    copies = windows // parts
    plane = lax.axis_index("seq")
    head_width = context_refs[0].shape[1]
    for step in range(group):
        at = pl.multiple_of((plane ^ step) * head_width, LANES)
        context[:, pl.ds(at, head_width)] = context_refs[step][...]
    ordered = context[...]
    for step in range(copies):
        slot = copy_index ^ step
        for piece in range(parts):
            pieces[piece * copies + slot] = jnp.dot(
                ordered, stack_refs[step][piece], preferred_element_type=F32
            )
    result = jnp.concatenate([pieces[d] for d in range(windows)], axis=1)
    out_ref[...] = jnp.where(valid_ref[...] > 0.5, result, 0.0).astype(BF16)


def on_device(
    audio, starts, lengths, slots, conv1_weight, conv2_weight, proj_weight, qkv_weight, out_weight
):
    streams = audio.shape[0]
    windows = lax.axis_size("dp")
    group = lax.axis_size("seq")
    parts = math.gcd(windows, BANDS)
    copies = windows // parts
    assert streams == windows and all(count & (count - 1) == 0 for count in (parts, copies, group))
    share = BANDS // parts
    width = 4 * share + 4
    channels = conv1_weight.shape[1]
    features = proj_weight.shape[1]
    head_width = features // group
    local = windows * W
    rows = JS * streams
    n = parts * streams
    outs = 2 * share + 1
    scale = max(1, windows * group // 32)

    route = [(i, i + 1) for i in range(windows * group - 1)]
    rim = lax.ppermute(audio[:, audio.shape[1] - RIM :], ("dp", "seq"), route)

    def to_part(block, step):
        pairs = [(p * copies + c, (p ^ step) * copies + c) for p in range(parts) for c in range(copies)]
        return lax.ppermute(block, "dp", pairs)

    def to_copy(block, step):
        pairs = [(p * copies + c, p * copies + (c ^ step)) for p in range(parts) for c in range(copies)]
        return lax.ppermute(block, "dp", pairs)

    def to_window(block, step):
        return lax.ppermute(block, "dp", [(i, i ^ step) for i in range(windows)])

    def to_plane(block, step):
        return lax.ppermute(block, "seq", [(i, i ^ step) for i in range(group)])

    proj_all = [proj_weight] + [to_copy(proj_weight, step) for step in range(1, copies)]

    table = jnp.asarray(spectrum_table(N_FFT))
    mix_piece = jax.ShapeDtypeStruct((qkv_weight.shape[0], 3 * head_width), BF16)
    *mel_all, mix = pl.pallas_call(
        functools.partial(mel_kernel, parts, group),
        out_shape=tuple([jax.ShapeDtypeStruct((rows, LANES), BF16)] * parts + [mix_piece]),
        in_specs=[anywhere(), vmem()] + [anywhere()] * 3,
        out_specs=tuple([vmem()] * (parts + 1)),
        scratch_shapes=[
            pltpu.VMEM((streams, RIM + audio.shape[1]), F32),
            pltpu.VMEM(table.shape, F32),
            pltpu.VMEM((parts, rows, LANES), BF16),
            pltpu.SMEM((streams,), jnp.int32),
            pltpu.SemaphoreType.DMA((6,)),
        ],
        compiler_params=params(60),
        cost_estimate=cost(1e10, 2e6),
        name="log_mel",
    )(slots, rim, audio, table, qkv_weight)
    near = [to_part(out_weight, step) for step in range(1, parts - 1)]
    mel_all, proj_all = lax.optimization_barrier((mel_all, proj_all))
    mel_all = [mel_all[0]] + [to_part(mel_all[step], step) for step in range(1, parts)]
    mel_all, near = lax.optimization_barrier((mel_all, near))
    mix_all = [mix] + [to_part(mix, step) for step in range(1, parts)]

    block = jax.ShapeDtypeStruct((local, features), BF16)
    partials = pl.pallas_call(
        functools.partial(conv_kernel, parts, width),
        out_shape=tuple([jax.ShapeDtypeStruct((W * parts, features), BF16)] * windows),
        in_specs=[vmem()] * (2 + parts + copies),
        out_specs=tuple([vmem()] * windows),
        scratch_shapes=[
            pltpu.VMEM((parts, rows, LANES), F32),
            pltpu.VMEM((LANES, outs * channels), BF16),
            pltpu.VMEM((JS * n, outs * channels), BF16),
            pltpu.VMEM((W * n, outs * channels), BF16),
            pltpu.VMEM((W * n, share * channels), BF16),
            pltpu.VMEM((copies, W * n, proj_weight.shape[0]), BF16),
            pltpu.VMEM((features // LANES, W * n, LANES), F32),
        ],
        compiler_params=params(min(40 + 4 * scale, 56)),
        cost_estimate=cost(2e9, 4e6),
        name="conv",
    )(conv1_weight, conv2_weight, *mel_all, *proj_all)
    partials = [to_window(partials[step], step) for step in reversed(range(1, windows))] + [partials[0]]

    ordered, normed, stack = pl.pallas_call(
        functools.partial(norm_kernel, parts),
        out_shape=(block, block, jax.ShapeDtypeStruct((parts,) + mix_piece.shape, BF16)),
        in_specs=[vmem()] * (windows + parts),
        out_specs=(vmem(), vmem(), vmem()),
        scratch_shapes=[pltpu.VMEM((local, features), BF16)],
        compiler_params=params(min(12 * scale, 32)),
        cost_estimate=cost(1e8, 1e6),
        name="layer_norm",
    )(*partials, *mix_all)
    mix_stacks = [stack] + [to_copy(stack, step) for step in range(1, copies)]
    regrouped, keys, valid = pl.pallas_call(
        functools.partial(mask_kernel, windows, group),
        out_shape=(
            block,
            jax.ShapeDtypeStruct((group, local), F32),
            jax.ShapeDtypeStruct((local, 1), F32),
        ),
        in_specs=[smem()] * 3 + [vmem()],
        out_specs=(vmem(), vmem(), vmem()),
        compiler_params=params(min(8 * scale, 32)),
        cost_estimate=cost(1e8, 1e6),
        name="mask",
    )(slots, starts, lengths, ordered)
    normed, out_here = lax.optimization_barrier((normed, out_weight))
    normed = [normed]
    for step in range(1, group):
        high = 1 << (step.bit_length() - 1)
        normed.append(to_plane(normed[high] if step > high else normed[0], step - high if step > high else high))
    out_all = [out_here] + near + [to_part(out_here, parts - 1)]

    *context, stack = pl.pallas_call(
        functools.partial(attention_kernel, parts, windows, group),
        out_shape=tuple(
            [jax.ShapeDtypeStruct((local, head_width), BF16)] * group
            + [jax.ShapeDtypeStruct((parts,) + out_weight.shape, BF16)]
        ),
        in_specs=[vmem()] * (1 + group + copies) + [anywhere()] * parts,
        out_specs=tuple([vmem()] * (group + 1)),
        scratch_shapes=[
            pltpu.VMEM((windows, group * local, qkv_weight.shape[0]), BF16),
            pltpu.SemaphoreType.DMA((parts,)),
        ],
        compiler_params=params(min(16 * scale, 48)),
        cost_estimate=cost(1e9, 2e6),
        name="attention",
    )(keys, *normed, *mix_stacks, *out_all)
    context = [context[0]] + [to_plane(context[step], step) for step in range(1, group)]
    out_stacks = [stack] + [to_copy(stack, step) for step in range(1, copies)]

    attended = pl.pallas_call(
        functools.partial(output_kernel, parts, windows, group),
        out_shape=block,
        in_specs=[vmem()] * (1 + group + copies),
        out_specs=vmem(),
        scratch_shapes=[
            pltpu.VMEM((local, features), BF16),
            pltpu.VMEM((windows, local, out_weight.shape[1]), F32),
        ],
        compiler_params=params(min(12 * scale, 32)),
        cost_estimate=cost(1e8, 3e6),
        name="output",
    )(valid, *context, *out_stacks)
    shape = (1, windows, 1, W, features)
    return (regrouped.reshape(shape), attended.reshape(shape))


def solution(mesh):
    in_specs = (
        P(None, ("dp", "seq")),
        P(),
        P(),
        P(),
        P(),
        P(),
        P("dp", None),
        P("dp", None),
        P(None, "dp"),
    )
    out_specs = (P("dp", None, "seq", None, None), P("dp", None, "seq", None, None))
    return jax.shard_map(
        on_device, mesh=mesh, in_specs=in_specs, out_specs=out_specs, check_vma=False
    )
```

```python
import functools
import math

import jax
import jax.numpy as jnp
import numpy as np
from jax import lax
from jax.experimental import pallas as pl
from jax.experimental.pallas import tpu as pltpu
from jax.sharding import PartitionSpec as P

HEADS = 8
HEAD_DIM = 128
MELS = 80
BANDS = MELS // 4
N_FFT = 512
HOP = 160
W = 8
RIM = 1024
SPAN = 4 * HOP
JS = W + 1
LANES = 128
SAMPLE_RATE = 16000.0
EPS_LOG = 1e-06
EPS_NORM = 1e-05
MASKED = -1e30
F32 = jnp.float32
BF16 = jnp.bfloat16
MIB = 1 << 20


def mel_table(size, bands):
    count = size // 2 + 1
    highest = 2595.0 * math.log10(1.0 + SAMPLE_RATE / 1400.0)
    points = np.linspace(0.0, highest, bands + 2)
    edges = 700.0 * (10.0 ** (points / 2595.0) - 1.0)
    edges[0] = 0.0
    edges[-1] = SAMPLE_RATE / 2.0
    frequency = np.arange(count) * (SAMPLE_RATE / size)
    lower = edges[:-2][None, :]
    middle = edges[1:-1][None, :]
    upper = edges[2:][None, :]
    rising = (frequency[:, None] - lower) / (middle - lower)
    falling = (upper - frequency[:, None]) / (upper - middle)
    return np.maximum(0.0, np.minimum(rising, falling)).astype(np.float32)


def spectrum_table(size):
    half = size // 2
    sample = np.arange(half)
    bins = np.concatenate([np.arange(0, half, 2), np.arange(1, half, 2)])
    angle = sample[:, None] * bins[None, :] % size * (2.0 * math.pi / size)
    table = np.zeros((half + 8, size + LANES))
    for odd in range(2):
        part = angle[:, odd * half // 2 : (odd + 1) * half // 2]
        table[:half, odd * half : (odd + 1) * half] = np.concatenate([np.cos(part), np.sin(part)], axis=1)
    table[:half, size : size + MELS] = mel_table(size, MELS)[bins]
    table[half, :size] = 0.5 - 0.5 * np.cos(np.arange(size) * (2.0 * math.pi / size))
    return table.astype(np.float32)


def vmem():
    return pl.BlockSpec(memory_space=pltpu.VMEM)


def smem():
    return pl.BlockSpec(memory_space=pltpu.SMEM)


def anywhere():
    return pl.BlockSpec(memory_space=pl.ANY)


def params(mib):
    return pltpu.CompilerParams(vmem_limit_bytes=mib * MIB)


def cost(flops, moved):
    return pl.CostEstimate(flops=int(flops), bytes_accessed=int(moved), transcendentals=0)


def place(parts):
    mine = lax.axis_index("dp")
    copies = lax.axis_size("dp") // parts
    return mine // copies, mine % copies


def start_all(copies):
    for copy in copies:
        copy.start()


def wait_all(copies):
    for copy in copies:
        copy.wait()


def iota(rows, columns, axis):
    return lax.broadcasted_iota(jnp.int32, (rows, columns), axis)


def quotient(index, step, count):
    result = jnp.zeros_like(index)
    for i in range(1, count):
        result += (index >= i * step).astype(jnp.int32)
    return result


def one_hot(target, count):
    return (iota(target.shape[0], count, 1) == target).astype(F32).astype(BF16)


def frame_order(parts, copies):
    count = parts * copies * W
    row = iota(count, 1, 0)
    k = quotient(row, W, parts * copies)
    p = quotient(k, copies, parts)
    return one_hot((k - p * copies) * W * parts + (row - k * W) * parts + p, count)


def samples(index, windows, group):
    return (index + quotient(index, W, windows) * (group - 1) * W) * SPAN


def mix_columns(group, qkv_ref, mix_out, sems):
    features = qkv_ref.shape[1] // 3
    width = features // group
    first = pl.multiple_of(lax.axis_index("seq") * width, LANES)
    return [
        pltpu.make_async_copy(
            qkv_ref.at[:, pl.ds(kind * features + first, width)],
            mix_out.at[:, pl.ds(kind * width, width)],
            sems.at[kind],
        )
        for kind in range(3)
    ]


def banded_weights(width, conv1_ref, banded_out):
    taps, channels = conv1_ref.shape
    row = lax.broadcasted_iota(jnp.int32, (LANES, taps), 0)
    tap = lax.broadcasted_iota(jnp.int32, (LANES, taps), 1)
    line = (tap >= 3).astype(jnp.int32) + (tap >= 6).astype(jnp.int32)
    target = line * (width - 3) + tap + 1
    weight = conv1_ref[...]
    for g in range(banded_out.shape[1] // channels):
        select = (row == target + 2 * g).astype(F32).astype(BF16)
        banded_out[:, g * channels : (g + 1) * channels] = jnp.dot(
            select, weight, preferred_element_type=F32
        ).astype(BF16)


def mel_kernel(parts, group, slots_here, rim_ref, audio_ref, table_ref, qkv_ref, *refs):
    outs_refs, (mix_out, ext, table, blocks, slots_ref, sems) = refs[:parts], refs[parts:]
    load_slots = pltpu.make_async_copy(slots_here, slots_ref, sems.at[5])
    load_slots.start()
    load_audio = pltpu.make_async_copy(audio_ref, ext.at[:, pl.ds(RIM, audio_ref.shape[1])], sems.at[3])
    load_table = pltpu.make_async_copy(table_ref, table, sems.at[4])
    load_audio.start()
    load_table.start()
    pieces = mix_columns(group, qkv_ref, mix_out, sems)
    start_all(pieces)
    streams = audio_ref.shape[0]
    rows = JS * streams
    ext[:, :RIM] = rim_ref[...]
    load_audio.wait()
    phases = []
    for phase in range(4):
        start = HOP * phase + 32
        base, shift = start // LANES * LANES, start % LANES
        length = N_FFT + (LANES if shift else 0)
        block = jnp.concatenate(
            [ext[:, SPAN * j + base : SPAN * j + base + length] for j in range(JS)], axis=0
        )
        if shift:
            block = pltpu.roll(block, length - shift, 1)[:, :N_FFT]
        phases.append(block)
    frames = jnp.concatenate(phases, axis=0)
    load_table.wait()
    half = N_FFT // 2
    frames = frames * table[half : half + 1, :N_FFT]
    low, high = frames[:, :half], frames[:, half:]
    powers = []
    for odd in range(2):
        spectrum = jnp.dot(
            low - high if odd else low + high,
            table[:half, odd * half : (odd + 1) * half],
            precision=lax.Precision.HIGHEST,
            preferred_element_type=F32,
        )
        real, imag = spectrum[:, : half // 2], spectrum[:, half // 2 :]
        powers.append(real * real + imag * imag)
    mel_power = jnp.dot(
        jnp.concatenate(powers, axis=1),
        table[:half, N_FFT:],
        precision=lax.Precision.HIGHEST,
        preferred_element_type=F32,
    )
    load_slots.wait()
    column = iota(1, rows, 1)
    early = quotient(column, streams, JS)
    target = jnp.zeros((1, rows), jnp.int32)
    for u in range(streams):
        target = jnp.where(column - early * streams == u, early * streams + slots_ref[u], target)
    routing = (target == iota(rows, rows, 0)).astype(F32).astype(BF16)
    log_mel = jnp.log(mel_power + EPS_LOG)
    share = BANDS // parts
    width = 4 * share + 4
    lane = iota(rows, LANES, 1)
    by_phase = [log_mel[phase * rows : (phase + 1) * rows] for phase in range(4)]

    def next_four(frames):
        return jnp.concatenate([frames[streams:], jnp.zeros((streams, LANES), F32)], axis=0)

    taps = [by_phase[1], by_phase[2], by_phase[3], next_four(by_phase[0]), next_four(by_phase[1])]
    for part in range(parts):
        first = 4 * share * part - 4
        block = jnp.zeros((rows, LANES), F32)
        for delta, frames in enumerate(taps):
            band = lane - width * delta + first
            here = (lane >= width * delta) & (lane < width * (delta + 1)) & (band >= 0) & (band < MELS)
            shift = (width * delta - first) % LANES
            block = jnp.where(here, pltpu.roll(frames, shift, 1) if shift else frames, block)
        blocks[part] = jnp.dot(routing, block.astype(BF16), preferred_element_type=F32).astype(BF16)
    mine, _ = place(parts)
    for step in range(parts):
        outs_refs[step][...] = blocks[mine ^ step]
    wait_all(pieces)


def conv_kernel(parts, width, conv1_ref, conv2_ref, *refs):
    part, copy_index = place(parts)
    mine = lax.axis_index("dp")
    windows = lax.axis_size("dp")
    copies = windows // parts
    mel_refs, refs = refs[:parts], refs[parts:]
    proj_refs, refs = refs[:copies], refs[copies:]
    outs_refs, refs = refs[:windows], refs[windows:]
    mel, banded_ref, even, odd, second, by_slot, partial = refs
    banded_weights(width, conv1_ref, banded_ref)
    streams = mel_refs[0].shape[0] // JS
    n = parts * streams
    for step in range(parts):
        mel[part ^ step] = mel_refs[step][...].astype(F32)
    evens = jnp.concatenate(
        [mel[p, j * streams : (j + 1) * streams, :] for j in range(JS) for p in range(parts)], axis=0
    )
    odds = pltpu.roll(evens[: W * n], LANES - 2 * width, 1).astype(BF16)
    evens = evens.astype(BF16)
    channels = conv2_ref.shape[1]
    outs = banded_ref.shape[1] // channels
    for g in range(outs):
        lanes = slice(g * channels, (g + 1) * channels)
        weight = banded_ref[:, lanes]
        even[:, lanes] = jax.nn.relu(jnp.dot(evens, weight, preferred_element_type=F32)).astype(BF16)
        odd[:, lanes] = jax.nn.relu(jnp.dot(odds, weight, preferred_element_type=F32)).astype(BF16)

    for h in range((outs - 1) // 2):
        lanes = slice(2 * h * channels, (2 * h + 3) * channels)
        taps = jnp.concatenate([even[: W * n, lanes], odd[:, lanes], even[n:, lanes]], axis=1)
        total = jnp.dot(taps, conv2_ref[...], preferred_element_type=F32)
        second[:, h * channels : (h + 1) * channels] = jax.nn.relu(total).astype(BF16)
    depth = by_slot.shape[2]
    for slot in range(copies):
        by_slot[slot] = second[:, slot * depth : (slot + 1) * depth]
    sums = jnp.dot(by_slot[copy_index], proj_refs[0][...], preferred_element_type=F32)
    for step in range(1, copies):
        sums += jnp.dot(by_slot[copy_index ^ step], proj_refs[step][...], preferred_element_type=F32)
    for block in range(partial.shape[0]):
        partial[block] = sums[:, block * LANES : (block + 1) * LANES]
    for step in range(windows):
        for block in range(partial.shape[0]):
            rows = partial[block, pl.ds(mine ^ step, W * parts, stride=streams), :]
            outs_refs[step][:, block * LANES : (block + 1) * LANES] = rows.astype(BF16)


def bounds(row, slots_ref, starts_ref, lengths_ref):
    begin, span = jnp.int32(0), jnp.int32(0)
    for u in range(slots_ref.shape[0]):
        chosen = slots_ref[u] == row
        begin = begin + jnp.where(chosen, starts_ref[u], 0)
        span = span + jnp.where(chosen, lengths_ref[u], 0)
    return begin, begin + span


def norm_kernel(parts, *refs):
    part, copy_index = place(parts)
    windows = lax.axis_size("dp")
    copies = windows // parts
    part_refs, refs = refs[:windows][::-1], refs[windows:]
    piece_refs, refs = refs[:parts], refs[parts:]
    rows_out, normed_out, stack_out, encoded = refs
    for step in range(parts):
        stack_out[part ^ step] = piece_refs[step][...]
    rows = W * parts
    for copy in range(copies):
        total = part_refs[copy][...].astype(F32)
        for step in range(1, parts):
            total += part_refs[step * copies + copy][...].astype(F32)
        at = pl.multiple_of((copy_index ^ copy) * rows, rows)
        encoded[pl.ds(at, rows), :] = total.astype(BF16)
    values = jnp.dot(frame_order(parts, copies), encoded[...], preferred_element_type=F32)
    rows_out[...] = values.astype(BF16)
    mean = jnp.mean(values, axis=-1, keepdims=True)
    centered = values - mean
    variance = jnp.mean(centered * centered, axis=-1, keepdims=True)
    normed_out[...] = (centered * lax.rsqrt(variance + EPS_NORM)).astype(BF16)


def mask_kernel(windows, group, slots_ref, starts_ref, lengths_ref, rows_ref, rows_out, keys_out, valid_out):
    begin, end = bounds(lax.axis_index("dp"), slots_ref, starts_ref, lengths_ref)
    sample = samples(iota(windows * W, 1, 0), windows, group) + lax.axis_index("seq") * (W * SPAN)
    valid = (sample >= begin) & (sample < end)
    rows_out[...] = jnp.where(valid, rows_ref[...].astype(F32), 0.0).astype(BF16)
    valid_out[...] = valid.astype(F32)
    keys = samples(iota(group, windows * W, 1), windows, group) + iota(group, windows * W, 0) * (W * SPAN)
    keys_out[...] = ((keys >= begin) & (keys < end)).astype(F32)


def attention_kernel(parts, windows, group, keys_ref, *refs):
    part, copy_index = place(parts)
    plane = lax.axis_index("seq")
    copies = windows // parts
    normed_refs, refs = refs[:group], refs[group:]
    stack_refs, refs = refs[:copies], refs[copies:]
    weight_refs, refs = refs[:parts], refs[parts:]
    outs_refs, (stack_out, pieces) = refs[:group], refs[group:]
    for step in range(parts):
        stack_out[part ^ step] = weight_refs[step][...]
    keys = [keys_ref[pl.ds(plane ^ step, 1), :] for step in range(group)]
    valid = jnp.concatenate(keys, axis=1) > 0.5
    local = normed_refs[0].shape[0]
    depth = pieces.shape[2]
    for step in range(group):
        for piece in range(windows):
            pieces[piece, step * local : (step + 1) * local, :] = normed_refs[step][
                :, piece * depth : (piece + 1) * depth
            ]
    mixed = 0.0
    for step in range(copies):
        slot = copy_index ^ step
        normed = jnp.concatenate([pieces[piece * copies + slot] for piece in range(parts)], axis=1)
        weights = stack_refs[step][...].reshape(parts * depth, stack_refs[step].shape[2])
        mixed += jnp.dot(normed, weights, preferred_element_type=F32)
    mixed = mixed.astype(BF16)
    width = mixed.shape[1] // 3
    scale = HEAD_DIM ** (-0.5)
    for head in range(width // HEAD_DIM):
        at = head * HEAD_DIM
        query = mixed[:, at : at + HEAD_DIM]
        key = mixed[:, width + at : width + at + HEAD_DIM]
        value = mixed[:, 2 * width + at : 2 * width + at + HEAD_DIM]
        scores = lax.dot_general(query, key, (((1,), (1,)), ((), ())), preferred_element_type=F32) * scale
        masked = jnp.where(valid, scores, MASKED)
        peak = jnp.max(masked, axis=1, keepdims=True)
        weight = jnp.where(valid, jnp.exp(masked - peak), 0.0)
        total = jnp.sum(weight, axis=1, keepdims=True)
        summed = jnp.dot(weight.astype(BF16), value, preferred_element_type=F32)
        context = (summed / total).astype(BF16)
        for step in range(group):
            outs_refs[step][:, at : at + HEAD_DIM] = context[step * local : (step + 1) * local]


def output_kernel(parts, windows, group, valid_ref, *refs):
    context_refs, refs = refs[:group], refs[group:]
    stack_refs, refs = refs[: windows // parts], refs[windows // parts :]
    out_ref, context, pieces = refs
    _, copy_index = place(parts)
    copies = windows // parts
    plane = lax.axis_index("seq")
    head_width = context_refs[0].shape[1]
    for step in range(group):
        at = pl.multiple_of((plane ^ step) * head_width, LANES)
        context[:, pl.ds(at, head_width)] = context_refs[step][...]
    ordered = context[...]
    for step in range(copies):
        slot = copy_index ^ step
        for piece in range(parts):
            pieces[piece * copies + slot] = jnp.dot(
                ordered, stack_refs[step][piece], preferred_element_type=F32
            )
    result = jnp.concatenate([pieces[d] for d in range(windows)], axis=1)
    out_ref[...] = jnp.where(valid_ref[...] > 0.5, result, 0.0).astype(BF16)


def on_device(
    audio, starts, lengths, slots, conv1_weight, conv2_weight, proj_weight, qkv_weight, out_weight
):
    streams = audio.shape[0]
    windows = lax.axis_size("dp")
    group = lax.axis_size("seq")
    parts = math.gcd(windows, BANDS)
    copies = windows // parts
    assert streams == windows and all(count & (count - 1) == 0 for count in (parts, copies, group))
    share = BANDS // parts
    width = 4 * share + 4
    channels = conv1_weight.shape[1]
    features = proj_weight.shape[1]
    head_width = features // group
    local = windows * W
    rows = JS * streams
    n = parts * streams
    outs = 2 * share + 1
    scale = max(1, windows * group // 32)

    route = [(i, i + 1) for i in range(windows * group - 1)]
    rim = lax.ppermute(audio[:, audio.shape[1] - RIM :], ("dp", "seq"), route)

    def to_part(block, step):
        pairs = [(p * copies + c, (p ^ step) * copies + c) for p in range(parts) for c in range(copies)]
        return lax.ppermute(block, "dp", pairs)

    def to_copy(block, step):
        pairs = [(p * copies + c, p * copies + (c ^ step)) for p in range(parts) for c in range(copies)]
        return lax.ppermute(block, "dp", pairs)

    def to_window(block, step):
        return lax.ppermute(block, "dp", [(i, i ^ step) for i in range(windows)])

    def to_plane(block, step):
        return lax.ppermute(block, "seq", [(i, i ^ step) for i in range(group)])

    proj_all = [proj_weight] + [to_copy(proj_weight, step) for step in range(1, copies)]

    table = jnp.asarray(spectrum_table(N_FFT))
    mix_piece = jax.ShapeDtypeStruct((qkv_weight.shape[0], 3 * head_width), BF16)
    *mel_all, mix = pl.pallas_call(
        functools.partial(mel_kernel, parts, group),
        out_shape=tuple([jax.ShapeDtypeStruct((rows, LANES), BF16)] * parts + [mix_piece]),
        in_specs=[anywhere(), vmem()] + [anywhere()] * 3,
        out_specs=tuple([vmem()] * (parts + 1)),
        scratch_shapes=[
            pltpu.VMEM((streams, RIM + audio.shape[1]), F32),
            pltpu.VMEM(table.shape, F32),
            pltpu.VMEM((parts, rows, LANES), BF16),
            pltpu.SMEM((streams,), jnp.int32),
            pltpu.SemaphoreType.DMA((6,)),
        ],
        compiler_params=params(60),
        cost_estimate=cost(1e10, 2e6),
        name="log_mel",
    )(slots, rim, audio, table, qkv_weight)
    near = [to_part(out_weight, step) for step in range(1, parts - 1)]
    mel_all, proj_all = lax.optimization_barrier((mel_all, proj_all))
    mel_all = [mel_all[0]] + [to_part(mel_all[step], step) for step in range(1, parts)]
    mel_all, near = lax.optimization_barrier((mel_all, near))
    mix_all = [mix] + [to_part(mix, step) for step in range(1, parts)]

    block = jax.ShapeDtypeStruct((local, features), BF16)
    partials = pl.pallas_call(
        functools.partial(conv_kernel, parts, width),
        out_shape=tuple([jax.ShapeDtypeStruct((W * parts, features), BF16)] * windows),
        in_specs=[vmem()] * (2 + parts + copies),
        out_specs=tuple([vmem()] * windows),
        scratch_shapes=[
            pltpu.VMEM((parts, rows, LANES), F32),
            pltpu.VMEM((LANES, outs * channels), BF16),
            pltpu.VMEM((JS * n, outs * channels), BF16),
            pltpu.VMEM((W * n, outs * channels), BF16),
            pltpu.VMEM((W * n, share * channels), BF16),
            pltpu.VMEM((copies, W * n, proj_weight.shape[0]), BF16),
            pltpu.VMEM((features // LANES, W * n, LANES), F32),
        ],
        compiler_params=params(min(40 + 4 * scale, 56)),
        cost_estimate=cost(2e9, 4e6),
        name="conv",
    )(conv1_weight, conv2_weight, *mel_all, *proj_all)
    partials = [to_window(partials[step], step) for step in reversed(range(1, windows))] + [partials[0]]

    ordered, normed, stack = pl.pallas_call(
        functools.partial(norm_kernel, parts),
        out_shape=(block, block, jax.ShapeDtypeStruct((parts,) + mix_piece.shape, BF16)),
        in_specs=[vmem()] * (windows + parts),
        out_specs=(vmem(), vmem(), vmem()),
        scratch_shapes=[pltpu.VMEM((local, features), BF16)],
        compiler_params=params(min(12 * scale, 32)),
        cost_estimate=cost(1e8, 1e6),
        name="layer_norm",
    )(*partials, *mix_all)
    mix_stacks = [stack] + [to_copy(stack, step) for step in range(1, copies)]
    regrouped, keys, valid = pl.pallas_call(
        functools.partial(mask_kernel, windows, group),
        out_shape=(
            block,
            jax.ShapeDtypeStruct((group, local), F32),
            jax.ShapeDtypeStruct((local, 1), F32),
        ),
        in_specs=[smem()] * 3 + [vmem()],
        out_specs=(vmem(), vmem(), vmem()),
        compiler_params=params(min(8 * scale, 32)),
        cost_estimate=cost(1e8, 1e6),
        name="mask",
    )(slots, starts, lengths, ordered)
    normed, out_here = lax.optimization_barrier((normed, out_weight))
    normed = [normed]
    for step in range(1, group):
        high = 1 << (step.bit_length() - 1)
        normed.append(to_plane(normed[high] if step > high else normed[0], step - high if step > high else high))
    out_all = [out_here] + near + [to_part(out_here, parts - 1)]

    *context, stack = pl.pallas_call(
        functools.partial(attention_kernel, parts, windows, group),
        out_shape=tuple(
            [jax.ShapeDtypeStruct((local, head_width), BF16)] * group
            + [jax.ShapeDtypeStruct((parts,) + out_weight.shape, BF16)]
        ),
        in_specs=[vmem()] * (1 + group + copies + parts),
        out_specs=tuple([vmem()] * (group + 1)),
        scratch_shapes=[pltpu.VMEM((windows, group * local, qkv_weight.shape[0]), BF16)],
        compiler_params=params(min(16 * scale, 48)),
        cost_estimate=cost(1e9, 2e6),
        name="attention",
    )(keys, *normed, *mix_stacks, *out_all)
    context = [context[0]] + [to_plane(context[step], step) for step in range(1, group)]
    out_stacks = [stack] + [to_copy(stack, step) for step in range(1, copies)]

    attended = pl.pallas_call(
        functools.partial(output_kernel, parts, windows, group),
        out_shape=block,
        in_specs=[vmem()] * (1 + group + copies),
        out_specs=vmem(),
        scratch_shapes=[
            pltpu.VMEM((local, features), BF16),
            pltpu.VMEM((windows, local, out_weight.shape[1]), F32),
        ],
        compiler_params=params(min(12 * scale, 32)),
        cost_estimate=cost(1e8, 3e6),
        name="output",
    )(valid, *context, *out_stacks)
    shape = (1, windows, 1, W, features)
    return (regrouped.reshape(shape), attended.reshape(shape))


def solution(mesh):
    in_specs = (
        P(None, ("dp", "seq")),
        P(),
        P(),
        P(),
        P(),
        P(),
        P("dp", None),
        P("dp", None),
        P(None, "dp"),
    )
    out_specs = (P("dp", None, "seq", None, None), P("dp", None, "seq", None, None))
    return jax.shard_map(
        on_device, mesh=mesh, in_specs=in_specs, out_specs=out_specs, check_vma=False
    )
```

```python
import functools
import math

import jax
import jax.numpy as jnp
import numpy as np
from jax import lax
from jax.experimental import pallas as pl
from jax.experimental.pallas import tpu as pltpu
from jax.sharding import PartitionSpec as P

HEADS = 8
HEAD_DIM = 128
MELS = 80
BANDS = MELS // 4
N_FFT = 512
HOP = 160
W = 8
RIM = 1024
SPAN = 4 * HOP
JS = W + 1
LANES = 128
SAMPLE_RATE = 16000.0
EPS_LOG = 1e-06
EPS_NORM = 1e-05
MASKED = -1e30
F32 = jnp.float32
BF16 = jnp.bfloat16
MIB = 1 << 20


def mel_table(size, bands):
    count = size // 2 + 1
    highest = 2595.0 * math.log10(1.0 + SAMPLE_RATE / 1400.0)
    points = np.linspace(0.0, highest, bands + 2)
    edges = 700.0 * (10.0 ** (points / 2595.0) - 1.0)
    edges[0] = 0.0
    edges[-1] = SAMPLE_RATE / 2.0
    frequency = np.arange(count) * (SAMPLE_RATE / size)
    lower = edges[:-2][None, :]
    middle = edges[1:-1][None, :]
    upper = edges[2:][None, :]
    rising = (frequency[:, None] - lower) / (middle - lower)
    falling = (upper - frequency[:, None]) / (upper - middle)
    return np.maximum(0.0, np.minimum(rising, falling)).astype(np.float32)


def spectrum_table(size):
    half = size // 2
    sample = np.arange(half)
    bins = np.concatenate([np.arange(0, half, 2), np.arange(1, half, 2)])
    angle = sample[:, None] * bins[None, :] % size * (2.0 * math.pi / size)
    table = np.zeros((half + 8, size + LANES))
    for odd in range(2):
        part = angle[:, odd * half // 2 : (odd + 1) * half // 2]
        table[:half, odd * half : (odd + 1) * half] = np.concatenate([np.cos(part), np.sin(part)], axis=1)
    table[:half, size : size + MELS] = mel_table(size, MELS)[bins]
    table[half, :size] = 0.5 - 0.5 * np.cos(np.arange(size) * (2.0 * math.pi / size))
    return table.astype(np.float32)


def vmem():
    return pl.BlockSpec(memory_space=pltpu.VMEM)


def smem():
    return pl.BlockSpec(memory_space=pltpu.SMEM)


def anywhere():
    return pl.BlockSpec(memory_space=pl.ANY)


def params(mib):
    return pltpu.CompilerParams(vmem_limit_bytes=mib * MIB)


def cost(flops, moved):
    return pl.CostEstimate(flops=int(flops), bytes_accessed=int(moved), transcendentals=0)


def place(parts):
    mine = lax.axis_index("dp")
    copies = lax.axis_size("dp") // parts
    return mine // copies, mine % copies


def start_all(copies):
    for copy in copies:
        copy.start()


def wait_all(copies):
    for copy in copies:
        copy.wait()


def iota(rows, columns, axis):
    return lax.broadcasted_iota(jnp.int32, (rows, columns), axis)


def quotient(index, step, count):
    result = jnp.zeros_like(index)
    for i in range(1, count):
        result += (index >= i * step).astype(jnp.int32)
    return result


def one_hot(target, count):
    return (iota(target.shape[0], count, 1) == target).astype(F32).astype(BF16)


def frame_order(parts, copies):
    count = parts * copies * W
    row = iota(count, 1, 0)
    k = quotient(row, W, parts * copies)
    p = quotient(k, copies, parts)
    return one_hot((k - p * copies) * W * parts + (row - k * W) * parts + p, count)


def samples(index, windows, group):
    return (index + quotient(index, W, windows) * (group - 1) * W) * SPAN


def mix_columns(group, qkv_ref, mix_out, sems):
    features = qkv_ref.shape[1] // 3
    width = features // group
    first = pl.multiple_of(lax.axis_index("seq") * width, LANES)
    return [
        pltpu.make_async_copy(
            qkv_ref.at[:, pl.ds(kind * features + first, width)],
            mix_out.at[:, pl.ds(kind * width, width)],
            sems.at[kind],
        )
        for kind in range(3)
    ]


def banded_weights(width, conv1_ref, banded_out):
    taps, channels = conv1_ref.shape
    row = lax.broadcasted_iota(jnp.int32, (LANES, taps), 0)
    tap = lax.broadcasted_iota(jnp.int32, (LANES, taps), 1)
    line = (tap >= 3).astype(jnp.int32) + (tap >= 6).astype(jnp.int32)
    target = line * (width - 3) + tap + 1
    weight = conv1_ref[...]
    for g in range(banded_out.shape[1] // channels):
        select = (row == target + 2 * g).astype(F32).astype(BF16)
        banded_out[:, g * channels : (g + 1) * channels] = jnp.dot(
            select, weight, preferred_element_type=F32
        ).astype(BF16)


def mel_kernel(parts, group, slots_here, rim_ref, audio_ref, table_ref, qkv_ref, *refs):
    outs_refs, (mix_out, ext, table, blocks, slots_ref, sems) = refs[:parts], refs[parts:]
    load_slots = pltpu.make_async_copy(slots_here, slots_ref, sems.at[5])
    load_slots.start()
    load_audio = pltpu.make_async_copy(audio_ref, ext.at[:, pl.ds(RIM, audio_ref.shape[1])], sems.at[3])
    load_table = pltpu.make_async_copy(table_ref, table, sems.at[4])
    load_rim = pltpu.make_async_copy(rim_ref, ext.at[:, pl.ds(0, RIM)], sems.at[6])
    load_rim.start()
    load_audio.start()
    load_table.start()
    pieces = mix_columns(group, qkv_ref, mix_out, sems)
    start_all(pieces)
    streams = audio_ref.shape[0]
    rows = JS * streams
    load_rim.wait()
    load_audio.wait()
    phases = []
    for phase in range(4):
        start = HOP * phase + 32
        base, shift = start // LANES * LANES, start % LANES
        length = N_FFT + (LANES if shift else 0)
        block = jnp.concatenate(
            [ext[:, SPAN * j + base : SPAN * j + base + length] for j in range(JS)], axis=0
        )
        if shift:
            block = pltpu.roll(block, length - shift, 1)[:, :N_FFT]
        phases.append(block)
    frames = jnp.concatenate(phases, axis=0)
    load_table.wait()
    half = N_FFT // 2
    frames = frames * table[half : half + 1, :N_FFT]
    low, high = frames[:, :half], frames[:, half:]
    powers = []
    for odd in range(2):
        spectrum = jnp.dot(
            low - high if odd else low + high,
            table[:half, odd * half : (odd + 1) * half],
            precision=lax.Precision.HIGHEST,
            preferred_element_type=F32,
        )
        real, imag = spectrum[:, : half // 2], spectrum[:, half // 2 :]
        powers.append(real * real + imag * imag)
    mel_power = jnp.dot(
        jnp.concatenate(powers, axis=1),
        table[:half, N_FFT:],
        precision=lax.Precision.HIGHEST,
        preferred_element_type=F32,
    )
    load_slots.wait()
    column = iota(1, rows, 1)
    early = quotient(column, streams, JS)
    target = jnp.zeros((1, rows), jnp.int32)
    for u in range(streams):
        target = jnp.where(column - early * streams == u, early * streams + slots_ref[u], target)
    routing = (target == iota(rows, rows, 0)).astype(F32).astype(BF16)
    log_mel = jnp.log(mel_power + EPS_LOG)
    share = BANDS // parts
    width = 4 * share + 4
    lane = iota(rows, LANES, 1)
    by_phase = [log_mel[phase * rows : (phase + 1) * rows] for phase in range(4)]

    def next_four(frames):
        return jnp.concatenate([frames[streams:], jnp.zeros((streams, LANES), F32)], axis=0)

    taps = [by_phase[1], by_phase[2], by_phase[3], next_four(by_phase[0]), next_four(by_phase[1])]
    for part in range(parts):
        first = 4 * share * part - 4
        block = jnp.zeros((rows, LANES), F32)
        for delta, frames in enumerate(taps):
            band = lane - width * delta + first
            here = (lane >= width * delta) & (lane < width * (delta + 1)) & (band >= 0) & (band < MELS)
            shift = (width * delta - first) % LANES
            block = jnp.where(here, pltpu.roll(frames, shift, 1) if shift else frames, block)
        blocks[part] = jnp.dot(routing, block.astype(BF16), preferred_element_type=F32).astype(BF16)
    mine, _ = place(parts)
    for step in range(parts):
        outs_refs[step][...] = blocks[mine ^ step]
    wait_all(pieces)


def stacked(parts, pieces, stack_out, sems, base):
    part, _ = place(parts)
    return [
        pltpu.make_async_copy(pieces[step], stack_out.at[part ^ step], sems.at[base + step])
        for step in range(parts)
    ]


def conv_kernel(parts, width, conv1_ref, conv2_ref, *refs):
    part, copy_index = place(parts)
    mine = lax.axis_index("dp")
    windows = lax.axis_size("dp")
    copies = windows // parts
    mel_refs, refs = refs[:parts], refs[parts:]
    proj_refs, refs = refs[:copies], refs[copies:]
    outs_refs, refs = refs[:windows], refs[windows:]
    mel, banded_ref, even, odd, second, by_slot, partial = refs
    banded_weights(width, conv1_ref, banded_ref)
    streams = mel_refs[0].shape[0] // JS
    n = parts * streams
    for step in range(parts):
        mel[part ^ step] = mel_refs[step][...].astype(F32)
    evens = jnp.concatenate(
        [mel[p, j * streams : (j + 1) * streams, :] for j in range(JS) for p in range(parts)], axis=0
    )
    odds = pltpu.roll(evens[: W * n], LANES - 2 * width, 1).astype(BF16)
    evens = evens.astype(BF16)
    channels = conv2_ref.shape[1]
    outs = banded_ref.shape[1] // channels
    for g in range(outs):
        lanes = slice(g * channels, (g + 1) * channels)
        weight = banded_ref[:, lanes]
        even[:, lanes] = jax.nn.relu(jnp.dot(evens, weight, preferred_element_type=F32)).astype(BF16)
        odd[:, lanes] = jax.nn.relu(jnp.dot(odds, weight, preferred_element_type=F32)).astype(BF16)

    for h in range((outs - 1) // 2):
        lanes = slice(2 * h * channels, (2 * h + 3) * channels)
        taps = jnp.concatenate([even[: W * n, lanes], odd[:, lanes], even[n:, lanes]], axis=1)
        total = jnp.dot(taps, conv2_ref[...], preferred_element_type=F32)
        second[:, h * channels : (h + 1) * channels] = jax.nn.relu(total).astype(BF16)
    depth = by_slot.shape[2]
    for slot in range(copies):
        by_slot[slot] = second[:, slot * depth : (slot + 1) * depth]
    sums = jnp.dot(by_slot[copy_index], proj_refs[0][...], preferred_element_type=F32)
    for step in range(1, copies):
        sums += jnp.dot(by_slot[copy_index ^ step], proj_refs[step][...], preferred_element_type=F32)
    for block in range(partial.shape[0]):
        partial[block] = sums[:, block * LANES : (block + 1) * LANES]
    for step in range(windows):
        for block in range(partial.shape[0]):
            rows = partial[block, pl.ds(mine ^ step, W * parts, stride=streams), :]
            outs_refs[step][:, block * LANES : (block + 1) * LANES] = rows.astype(BF16)


def bounds(row, slots_ref, starts_ref, lengths_ref):
    begin, span = jnp.int32(0), jnp.int32(0)
    for u in range(slots_ref.shape[0]):
        chosen = slots_ref[u] == row
        begin = begin + jnp.where(chosen, starts_ref[u], 0)
        span = span + jnp.where(chosen, lengths_ref[u], 0)
    return begin, begin + span


def norm_kernel(parts, *refs):
    part, copy_index = place(parts)
    windows = lax.axis_size("dp")
    copies = windows // parts
    part_refs, refs = refs[:windows][::-1], refs[windows:]
    piece_refs, refs = refs[:parts], refs[parts:]
    rows_out, normed_out, stack_out, encoded = refs
    for step in range(parts):
        stack_out[part ^ step] = piece_refs[step][...]
    rows = W * parts
    for copy in range(copies):
        total = part_refs[copy][...].astype(F32)
        for step in range(1, parts):
            total += part_refs[step * copies + copy][...].astype(F32)
        at = pl.multiple_of((copy_index ^ copy) * rows, rows)
        encoded[pl.ds(at, rows), :] = total.astype(BF16)
    values = jnp.dot(frame_order(parts, copies), encoded[...], preferred_element_type=F32)
    rows_out[...] = values.astype(BF16)
    mean = jnp.mean(values, axis=-1, keepdims=True)
    centered = values - mean
    variance = jnp.mean(centered * centered, axis=-1, keepdims=True)
    normed_out[...] = (centered * lax.rsqrt(variance + EPS_NORM)).astype(BF16)


def mask_kernel(windows, group, slots_ref, starts_ref, lengths_ref, rows_ref, rows_out, keys_out, valid_out):
    begin, end = bounds(lax.axis_index("dp"), slots_ref, starts_ref, lengths_ref)
    sample = samples(iota(windows * W, 1, 0), windows, group) + lax.axis_index("seq") * (W * SPAN)
    valid = (sample >= begin) & (sample < end)
    rows_out[...] = jnp.where(valid, rows_ref[...].astype(F32), 0.0).astype(BF16)
    valid_out[...] = valid.astype(F32)
    keys = samples(iota(group, windows * W, 1), windows, group) + iota(group, windows * W, 0) * (W * SPAN)
    keys_out[...] = ((keys >= begin) & (keys < end)).astype(F32)


def attention_kernel(parts, windows, group, keys_ref, *refs):
    _, copy_index = place(parts)
    plane = lax.axis_index("seq")
    copies = windows // parts
    normed_refs, refs = refs[:group], refs[group:]
    stack_refs, refs = refs[:copies], refs[copies:]
    weight_refs, refs = refs[:parts], refs[parts:]
    outs_refs, (stack_out, pieces, sems) = refs[:group], refs[group:]
    moves = stacked(parts, weight_refs, stack_out, sems, 0)
    start_all(moves)
    keys = [keys_ref[pl.ds(plane ^ step, 1), :] for step in range(group)]
    valid = jnp.concatenate(keys, axis=1) > 0.5
    local = normed_refs[0].shape[0]
    depth = pieces.shape[2]
    for step in range(group):
        for piece in range(windows):
            pieces[piece, step * local : (step + 1) * local, :] = normed_refs[step][
                :, piece * depth : (piece + 1) * depth
            ]
    mixed = 0.0
    for step in range(copies):
        slot = copy_index ^ step
        normed = jnp.concatenate([pieces[piece * copies + slot] for piece in range(parts)], axis=1)
        weights = stack_refs[step][...].reshape(parts * depth, stack_refs[step].shape[2])
        mixed += jnp.dot(normed, weights, preferred_element_type=F32)
    mixed = mixed.astype(BF16)
    width = mixed.shape[1] // 3
    scale = HEAD_DIM ** (-0.5)
    for head in range(width // HEAD_DIM):
        at = head * HEAD_DIM
        query = mixed[:, at : at + HEAD_DIM]
        key = mixed[:, width + at : width + at + HEAD_DIM]
        value = mixed[:, 2 * width + at : 2 * width + at + HEAD_DIM]
        scores = lax.dot_general(query, key, (((1,), (1,)), ((), ())), preferred_element_type=F32) * scale
        masked = jnp.where(valid, scores, MASKED)
        peak = jnp.max(masked, axis=1, keepdims=True)
        weight = jnp.where(valid, jnp.exp(masked - peak), 0.0)
        total = jnp.sum(weight, axis=1, keepdims=True)
        summed = jnp.dot(weight.astype(BF16), value, preferred_element_type=F32)
        context = (summed / total).astype(BF16)
        for step in range(group):
            outs_refs[step][:, at : at + HEAD_DIM] = context[step * local : (step + 1) * local]
    wait_all(moves)


def output_kernel(parts, windows, group, valid_ref, *refs):
    context_refs, refs = refs[:group], refs[group:]
    stack_refs, refs = refs[: windows // parts], refs[windows // parts :]
    out_ref, context, pieces = refs
    _, copy_index = place(parts)
    copies = windows // parts
    plane = lax.axis_index("seq")
    head_width = context_refs[0].shape[1]
    for step in range(group):
        at = pl.multiple_of((plane ^ step) * head_width, LANES)
        context[:, pl.ds(at, head_width)] = context_refs[step][...]
    ordered = context[...]
    for step in range(copies):
        slot = copy_index ^ step
        for piece in range(parts):
            pieces[piece * copies + slot] = jnp.dot(
                ordered, stack_refs[step][piece], preferred_element_type=F32
            )
    result = jnp.concatenate([pieces[d] for d in range(windows)], axis=1)
    out_ref[...] = jnp.where(valid_ref[...] > 0.5, result, 0.0).astype(BF16)


def on_device(
    audio, starts, lengths, slots, conv1_weight, conv2_weight, proj_weight, qkv_weight, out_weight
):
    streams = audio.shape[0]
    windows = lax.axis_size("dp")
    group = lax.axis_size("seq")
    parts = math.gcd(windows, BANDS)
    copies = windows // parts
    assert streams == windows and all(count & (count - 1) == 0 for count in (parts, copies, group))
    share = BANDS // parts
    width = 4 * share + 4
    channels = conv1_weight.shape[1]
    features = proj_weight.shape[1]
    head_width = features // group
    local = windows * W
    rows = JS * streams
    n = parts * streams
    outs = 2 * share + 1
    scale = max(1, windows * group // 32)

    route = [(i, i + 1) for i in range(windows * group - 1)]
    rim = lax.ppermute(audio[:, audio.shape[1] - RIM :], ("dp", "seq"), route)

    def to_part(block, step):
        pairs = [(p * copies + c, (p ^ step) * copies + c) for p in range(parts) for c in range(copies)]
        return lax.ppermute(block, "dp", pairs)

    def to_copy(block, step):
        pairs = [(p * copies + c, p * copies + (c ^ step)) for p in range(parts) for c in range(copies)]
        return lax.ppermute(block, "dp", pairs)

    def to_window(block, step):
        return lax.ppermute(block, "dp", [(i, i ^ step) for i in range(windows)])

    def to_plane(block, step):
        return lax.ppermute(block, "seq", [(i, i ^ step) for i in range(group)])

    proj_all = [proj_weight] + [to_copy(proj_weight, step) for step in range(1, copies)]

    table = jnp.asarray(spectrum_table(N_FFT))
    mix_piece = jax.ShapeDtypeStruct((qkv_weight.shape[0], 3 * head_width), BF16)
    *mel_all, mix = pl.pallas_call(
        functools.partial(mel_kernel, parts, group),
        out_shape=tuple([jax.ShapeDtypeStruct((rows, LANES), BF16)] * parts + [mix_piece]),
        in_specs=[anywhere()] * 5,
        out_specs=tuple([vmem()] * (parts + 1)),
        scratch_shapes=[
            pltpu.VMEM((streams, RIM + audio.shape[1]), F32),
            pltpu.VMEM(table.shape, F32),
            pltpu.VMEM((parts, rows, LANES), BF16),
            pltpu.SMEM((streams,), jnp.int32),
            pltpu.SemaphoreType.DMA((7,)),
        ],
        compiler_params=params(60),
        cost_estimate=cost(1e10, 2e6),
        name="log_mel",
    )(slots, rim, audio, table, qkv_weight)
    near = [to_part(out_weight, step) for step in range(1, parts - 1)]
    mel_all, proj_all = lax.optimization_barrier((mel_all, proj_all))
    mel_all = [mel_all[0]] + [to_part(mel_all[step], step) for step in range(1, parts)]
    mel_all, near = lax.optimization_barrier((mel_all, near))
    mix_all = [mix] + [to_part(mix, step) for step in range(1, parts)]

    block = jax.ShapeDtypeStruct((local, features), BF16)
    partials = pl.pallas_call(
        functools.partial(conv_kernel, parts, width),
        out_shape=tuple([jax.ShapeDtypeStruct((W * parts, features), BF16)] * windows),
        in_specs=[vmem()] * (2 + parts + copies),
        out_specs=tuple([vmem()] * windows),
        scratch_shapes=[
            pltpu.VMEM((parts, rows, LANES), F32),
            pltpu.VMEM((LANES, outs * channels), BF16),
            pltpu.VMEM((JS * n, outs * channels), BF16),
            pltpu.VMEM((W * n, outs * channels), BF16),
            pltpu.VMEM((W * n, share * channels), BF16),
            pltpu.VMEM((copies, W * n, proj_weight.shape[0]), BF16),
            pltpu.VMEM((features // LANES, W * n, LANES), F32),
        ],
        compiler_params=params(min(40 + 4 * scale, 56)),
        cost_estimate=cost(2e9, 4e6),
        name="conv",
    )(conv1_weight, conv2_weight, *mel_all, *proj_all)
    partials = [to_window(partials[step], step) for step in reversed(range(1, windows))] + [partials[0]]

    ordered, normed, stack = pl.pallas_call(
        functools.partial(norm_kernel, parts),
        out_shape=(block, block, jax.ShapeDtypeStruct((parts,) + mix_piece.shape, BF16)),
        in_specs=[vmem()] * (windows + parts),
        out_specs=(vmem(), vmem(), vmem()),
        scratch_shapes=[pltpu.VMEM((local, features), BF16)],
        compiler_params=params(min(12 * scale, 32)),
        cost_estimate=cost(1e8, 1e6),
        name="layer_norm",
    )(*partials, *mix_all)
    mix_stacks = [stack] + [to_copy(stack, step) for step in range(1, copies)]
    regrouped, keys, valid = pl.pallas_call(
        functools.partial(mask_kernel, windows, group),
        out_shape=(
            block,
            jax.ShapeDtypeStruct((group, local), F32),
            jax.ShapeDtypeStruct((local, 1), F32),
        ),
        in_specs=[smem()] * 3 + [vmem()],
        out_specs=(vmem(), vmem(), vmem()),
        compiler_params=params(min(8 * scale, 32)),
        cost_estimate=cost(1e8, 1e6),
        name="mask",
    )(slots, starts, lengths, ordered)
    normed, out_here = lax.optimization_barrier((normed, out_weight))
    normed = [normed]
    for step in range(1, group):
        high = 1 << (step.bit_length() - 1)
        normed.append(to_plane(normed[high] if step > high else normed[0], step - high if step > high else high))
    out_all = [out_here] + near + [to_part(out_here, parts - 1)]

    *context, stack = pl.pallas_call(
        functools.partial(attention_kernel, parts, windows, group),
        out_shape=tuple(
            [jax.ShapeDtypeStruct((local, head_width), BF16)] * group
            + [jax.ShapeDtypeStruct((parts,) + out_weight.shape, BF16)]
        ),
        in_specs=[vmem()] * (1 + group + copies) + [anywhere()] * parts,
        out_specs=tuple([vmem()] * (group + 1)),
        scratch_shapes=[
            pltpu.VMEM((windows, group * local, qkv_weight.shape[0]), BF16),
            pltpu.SemaphoreType.DMA((parts,)),
        ],
        compiler_params=params(min(16 * scale, 48)),
        cost_estimate=cost(1e9, 2e6),
        name="attention",
    )(keys, *normed, *mix_stacks, *out_all)
    context = [context[0]] + [to_plane(context[step], step) for step in range(1, group)]
    out_stacks = [stack] + [to_copy(stack, step) for step in range(1, copies)]

    attended = pl.pallas_call(
        functools.partial(output_kernel, parts, windows, group),
        out_shape=block,
        in_specs=[vmem()] * (1 + group + copies),
        out_specs=vmem(),
        scratch_shapes=[
            pltpu.VMEM((local, features), BF16),
            pltpu.VMEM((windows, local, out_weight.shape[1]), F32),
        ],
        compiler_params=params(min(12 * scale, 32)),
        cost_estimate=cost(1e8, 3e6),
        name="output",
    )(valid, *context, *out_stacks)
    shape = (1, windows, 1, W, features)
    return (regrouped.reshape(shape), attended.reshape(shape))


def solution(mesh):
    in_specs = (
        P(None, ("dp", "seq")),
        P(),
        P(),
        P(),
        P(),
        P(),
        P("dp", None),
        P("dp", None),
        P(None, "dp"),
    )
    out_specs = (P("dp", None, "seq", None, None), P("dp", None, "seq", None, None))
    return jax.shard_map(
        on_device, mesh=mesh, in_specs=in_specs, out_specs=out_specs, check_vma=False
    )
```

```python
import functools
import math

import jax
import jax.numpy as jnp
import numpy as np
from jax import lax
from jax.experimental import pallas as pl
from jax.experimental.pallas import tpu as pltpu
from jax.sharding import PartitionSpec as P

HEADS = 8
HEAD_DIM = 128
MELS = 80
BANDS = MELS // 4
N_FFT = 512
HOP = 160
W = 8
RIM = 1024
SPAN = 4 * HOP
JS = W + 1
LANES = 128
SAMPLE_RATE = 16000.0
EPS_LOG = 1e-06
EPS_NORM = 1e-05
MASKED = -1e30
F32 = jnp.float32
BF16 = jnp.bfloat16
MIB = 1 << 20


def mel_table(size, bands):
    count = size // 2 + 1
    highest = 2595.0 * math.log10(1.0 + SAMPLE_RATE / 1400.0)
    points = np.linspace(0.0, highest, bands + 2)
    edges = 700.0 * (10.0 ** (points / 2595.0) - 1.0)
    edges[0] = 0.0
    edges[-1] = SAMPLE_RATE / 2.0
    frequency = np.arange(count) * (SAMPLE_RATE / size)
    lower = edges[:-2][None, :]
    middle = edges[1:-1][None, :]
    upper = edges[2:][None, :]
    rising = (frequency[:, None] - lower) / (middle - lower)
    falling = (upper - frequency[:, None]) / (upper - middle)
    return np.maximum(0.0, np.minimum(rising, falling)).astype(np.float32)


def spectrum_table(size):
    half = size // 2
    sample = np.arange(half)
    bins = np.concatenate([np.arange(0, half, 2), np.arange(1, half, 2)])
    angle = sample[:, None] * bins[None, :] % size * (2.0 * math.pi / size)
    table = np.zeros((half + 8, size + LANES))
    for odd in range(2):
        part = angle[:, odd * half // 2 : (odd + 1) * half // 2]
        table[:half, odd * half : (odd + 1) * half] = np.concatenate([np.cos(part), np.sin(part)], axis=1)
    table[:half, size : size + MELS] = mel_table(size, MELS)[bins]
    table[half, :size] = 0.5 - 0.5 * np.cos(np.arange(size) * (2.0 * math.pi / size))
    return table.astype(np.float32)


def vmem():
    return pl.BlockSpec(memory_space=pltpu.VMEM)


def smem():
    return pl.BlockSpec(memory_space=pltpu.SMEM)


def anywhere():
    return pl.BlockSpec(memory_space=pl.ANY)


def params(mib):
    return pltpu.CompilerParams(vmem_limit_bytes=mib * MIB)


def cost(flops, moved):
    return pl.CostEstimate(flops=int(flops), bytes_accessed=int(moved), transcendentals=0)


def place(parts):
    mine = lax.axis_index("dp")
    copies = lax.axis_size("dp") // parts
    return mine // copies, mine % copies


def start_all(copies):
    for copy in copies:
        copy.start()


def wait_all(copies):
    for copy in copies:
        copy.wait()


def iota(rows, columns, axis):
    return lax.broadcasted_iota(jnp.int32, (rows, columns), axis)


def quotient(index, step, count):
    result = jnp.zeros_like(index)
    for i in range(1, count):
        result += (index >= i * step).astype(jnp.int32)
    return result


def one_hot(target, count):
    return (iota(target.shape[0], count, 1) == target).astype(F32).astype(BF16)


def frame_order(parts, copies):
    count = parts * copies * W
    row = iota(count, 1, 0)
    k = quotient(row, W, parts * copies)
    p = quotient(k, copies, parts)
    return one_hot((k - p * copies) * W * parts + (row - k * W) * parts + p, count)


def samples(index, windows, group):
    return (index + quotient(index, W, windows) * (group - 1) * W) * SPAN


def mix_columns(group, qkv_ref, mix_out, sems):
    features = qkv_ref.shape[1] // 3
    width = features // group
    first = pl.multiple_of(lax.axis_index("seq") * width, LANES)
    return [
        pltpu.make_async_copy(
            qkv_ref.at[:, pl.ds(kind * features + first, width)],
            mix_out.at[:, pl.ds(kind * width, width)],
            sems.at[kind],
        )
        for kind in range(3)
    ]


def banded_weights(width, conv1_ref, banded_out):
    taps, channels = conv1_ref.shape
    row = lax.broadcasted_iota(jnp.int32, (LANES, taps), 0)
    tap = lax.broadcasted_iota(jnp.int32, (LANES, taps), 1)
    line = (tap >= 3).astype(jnp.int32) + (tap >= 6).astype(jnp.int32)
    target = line * (width - 3) + tap + 1
    weight = conv1_ref[...]
    for g in range(banded_out.shape[1] // channels):
        select = (row == target + 2 * g).astype(F32).astype(BF16)
        banded_out[:, g * channels : (g + 1) * channels] = jnp.dot(
            select, weight, preferred_element_type=F32
        ).astype(BF16)


def mel_kernel(parts, group, slots_here, rim_ref, audio_ref, table_ref, qkv_ref, *refs):
    outs_refs, (mix_out, ext, table, blocks, slots_ref, sems) = refs[:parts], refs[parts:]
    load_slots = pltpu.make_async_copy(slots_here, slots_ref, sems.at[5])
    load_audio = pltpu.make_async_copy(audio_ref, ext.at[:, pl.ds(RIM, audio_ref.shape[1])], sems.at[3])
    load_table = pltpu.make_async_copy(table_ref, table, sems.at[4])
    load_table.start()
    load_rim = pltpu.make_async_copy(rim_ref, ext.at[:, pl.ds(0, RIM)], sems.at[6])
    load_rim.start()
    load_audio.start()
    load_slots.start()
    pieces = mix_columns(group, qkv_ref, mix_out, sems)
    start_all(pieces)
    streams = audio_ref.shape[0]
    rows = JS * streams
    load_rim.wait()
    load_audio.wait()
    phases = []
    for phase in range(4):
        start = HOP * phase + 32
        base, shift = start // LANES * LANES, start % LANES
        length = N_FFT + (LANES if shift else 0)
        block = jnp.concatenate(
            [ext[:, SPAN * j + base : SPAN * j + base + length] for j in range(JS)], axis=0
        )
        if shift:
            block = pltpu.roll(block, length - shift, 1)[:, :N_FFT]
        phases.append(block)
    frames = jnp.concatenate(phases, axis=0)
    load_table.wait()
    half = N_FFT // 2
    frames = frames * table[half : half + 1, :N_FFT]
    low, high = frames[:, :half], frames[:, half:]
    powers = []
    for odd in range(2):
        spectrum = jnp.dot(
            low - high if odd else low + high,
            table[:half, odd * half : (odd + 1) * half],
            precision=lax.Precision.HIGHEST,
            preferred_element_type=F32,
        )
        real, imag = spectrum[:, : half // 2], spectrum[:, half // 2 :]
        powers.append(real * real + imag * imag)
    mel_power = jnp.dot(
        jnp.concatenate(powers, axis=1),
        table[:half, N_FFT:],
        precision=lax.Precision.HIGHEST,
        preferred_element_type=F32,
    )
    load_slots.wait()
    column = iota(1, rows, 1)
    early = quotient(column, streams, JS)
    target = jnp.zeros((1, rows), jnp.int32)
    for u in range(streams):
        target = jnp.where(column - early * streams == u, early * streams + slots_ref[u], target)
    routing = (target == iota(rows, rows, 0)).astype(F32).astype(BF16)
    log_mel = jnp.log(mel_power + EPS_LOG)
    share = BANDS // parts
    width = 4 * share + 4
    lane = iota(rows, LANES, 1)
    by_phase = [log_mel[phase * rows : (phase + 1) * rows] for phase in range(4)]

    def next_four(frames):
        return jnp.concatenate([frames[streams:], jnp.zeros((streams, LANES), F32)], axis=0)

    taps = [by_phase[1], by_phase[2], by_phase[3], next_four(by_phase[0]), next_four(by_phase[1])]
    for part in range(parts):
        first = 4 * share * part - 4
        block = jnp.zeros((rows, LANES), F32)
        for delta, frames in enumerate(taps):
            band = lane - width * delta + first
            here = (lane >= width * delta) & (lane < width * (delta + 1)) & (band >= 0) & (band < MELS)
            shift = (width * delta - first) % LANES
            block = jnp.where(here, pltpu.roll(frames, shift, 1) if shift else frames, block)
        blocks[part] = jnp.dot(routing, block.astype(BF16), preferred_element_type=F32).astype(BF16)
    mine, _ = place(parts)
    for step in range(parts):
        outs_refs[step][...] = blocks[mine ^ step]
    wait_all(pieces)


def stacked(parts, pieces, stack_out, sems, base):
    part, _ = place(parts)
    return [
        pltpu.make_async_copy(pieces[step], stack_out.at[part ^ step], sems.at[base + step])
        for step in range(parts)
    ]


def conv_kernel(parts, width, conv1_ref, conv2_ref, *refs):
    part, copy_index = place(parts)
    mine = lax.axis_index("dp")
    windows = lax.axis_size("dp")
    copies = windows // parts
    mel_refs, refs = refs[:parts], refs[parts:]
    proj_refs, refs = refs[:copies], refs[copies:]
    outs_refs, refs = refs[:windows], refs[windows:]
    mel, banded_ref, even, odd, second, by_slot, partial = refs
    banded_weights(width, conv1_ref, banded_ref)
    streams = mel_refs[0].shape[0] // JS
    n = parts * streams
    for step in range(parts):
        mel[part ^ step] = mel_refs[step][...].astype(F32)
    evens = jnp.concatenate(
        [mel[p, j * streams : (j + 1) * streams, :] for j in range(JS) for p in range(parts)], axis=0
    )
    odds = pltpu.roll(evens[: W * n], LANES - 2 * width, 1).astype(BF16)
    evens = evens.astype(BF16)
    channels = conv2_ref.shape[1]
    outs = banded_ref.shape[1] // channels
    for g in range(outs):
        lanes = slice(g * channels, (g + 1) * channels)
        weight = banded_ref[:, lanes]
        even[:, lanes] = jax.nn.relu(jnp.dot(evens, weight, preferred_element_type=F32)).astype(BF16)
        odd[:, lanes] = jax.nn.relu(jnp.dot(odds, weight, preferred_element_type=F32)).astype(BF16)

    for h in range((outs - 1) // 2):
        lanes = slice(2 * h * channels, (2 * h + 3) * channels)
        taps = jnp.concatenate([even[: W * n, lanes], odd[:, lanes], even[n:, lanes]], axis=1)
        total = jnp.dot(taps, conv2_ref[...], preferred_element_type=F32)
        second[:, h * channels : (h + 1) * channels] = jax.nn.relu(total).astype(BF16)
    depth = by_slot.shape[2]
    for slot in range(copies):
        by_slot[slot] = second[:, slot * depth : (slot + 1) * depth]
    sums = jnp.dot(by_slot[copy_index], proj_refs[0][...], preferred_element_type=F32)
    for step in range(1, copies):
        sums += jnp.dot(by_slot[copy_index ^ step], proj_refs[step][...], preferred_element_type=F32)
    for block in range(partial.shape[0]):
        partial[block] = sums[:, block * LANES : (block + 1) * LANES]
    for step in range(windows):
        for block in range(partial.shape[0]):
            rows = partial[block, pl.ds(mine ^ step, W * parts, stride=streams), :]
            outs_refs[step][:, block * LANES : (block + 1) * LANES] = rows.astype(BF16)


def bounds(row, slots_ref, starts_ref, lengths_ref):
    begin, span = jnp.int32(0), jnp.int32(0)
    for u in range(slots_ref.shape[0]):
        chosen = slots_ref[u] == row
        begin = begin + jnp.where(chosen, starts_ref[u], 0)
        span = span + jnp.where(chosen, lengths_ref[u], 0)
    return begin, begin + span


def norm_kernel(parts, *refs):
    part, copy_index = place(parts)
    windows = lax.axis_size("dp")
    copies = windows // parts
    part_refs, refs = refs[:windows][::-1], refs[windows:]
    piece_refs, refs = refs[:parts], refs[parts:]
    rows_out, normed_out, stack_out, encoded = refs
    for step in range(parts):
        stack_out[part ^ step] = piece_refs[step][...]
    rows = W * parts
    for copy in range(copies):
        total = part_refs[copy][...].astype(F32)
        for step in range(1, parts):
            total += part_refs[step * copies + copy][...].astype(F32)
        at = pl.multiple_of((copy_index ^ copy) * rows, rows)
        encoded[pl.ds(at, rows), :] = total.astype(BF16)
    values = jnp.dot(frame_order(parts, copies), encoded[...], preferred_element_type=F32)
    rows_out[...] = values.astype(BF16)
    mean = jnp.mean(values, axis=-1, keepdims=True)
    centered = values - mean
    variance = jnp.mean(centered * centered, axis=-1, keepdims=True)
    normed_out[...] = (centered * lax.rsqrt(variance + EPS_NORM)).astype(BF16)


def mask_kernel(windows, group, slots_ref, starts_ref, lengths_ref, rows_ref, rows_out, keys_out, valid_out):
    begin, end = bounds(lax.axis_index("dp"), slots_ref, starts_ref, lengths_ref)
    sample = samples(iota(windows * W, 1, 0), windows, group) + lax.axis_index("seq") * (W * SPAN)
    valid = (sample >= begin) & (sample < end)
    rows_out[...] = jnp.where(valid, rows_ref[...].astype(F32), 0.0).astype(BF16)
    valid_out[...] = valid.astype(F32)
    keys = samples(iota(group, windows * W, 1), windows, group) + iota(group, windows * W, 0) * (W * SPAN)
    keys_out[...] = ((keys >= begin) & (keys < end)).astype(F32)


def attention_kernel(parts, windows, group, keys_ref, *refs):
    _, copy_index = place(parts)
    plane = lax.axis_index("seq")
    copies = windows // parts
    normed_refs, refs = refs[:group], refs[group:]
    stack_refs, refs = refs[:copies], refs[copies:]
    weight_refs, refs = refs[:parts], refs[parts:]
    outs_refs, (stack_out, pieces, sems) = refs[:group], refs[group:]
    moves = stacked(parts, weight_refs, stack_out, sems, 0)
    start_all(moves)
    keys = [keys_ref[pl.ds(plane ^ step, 1), :] for step in range(group)]
    valid = jnp.concatenate(keys, axis=1) > 0.5
    local = normed_refs[0].shape[0]
    depth = pieces.shape[2]
    for step in range(group):
        for piece in range(windows):
            pieces[piece, step * local : (step + 1) * local, :] = normed_refs[step][
                :, piece * depth : (piece + 1) * depth
            ]
    mixed = 0.0
    for step in range(copies):
        slot = copy_index ^ step
        normed = jnp.concatenate([pieces[piece * copies + slot] for piece in range(parts)], axis=1)
        weights = stack_refs[step][...].reshape(parts * depth, stack_refs[step].shape[2])
        mixed += jnp.dot(normed, weights, preferred_element_type=F32)
    mixed = mixed.astype(BF16)
    width = mixed.shape[1] // 3
    scale = HEAD_DIM ** (-0.5)
    for head in range(width // HEAD_DIM):
        at = head * HEAD_DIM
        query = mixed[:, at : at + HEAD_DIM]
        key = mixed[:, width + at : width + at + HEAD_DIM]
        value = mixed[:, 2 * width + at : 2 * width + at + HEAD_DIM]
        scores = lax.dot_general(query, key, (((1,), (1,)), ((), ())), preferred_element_type=F32) * scale
        masked = jnp.where(valid, scores, MASKED)
        peak = jnp.max(masked, axis=1, keepdims=True)
        weight = jnp.where(valid, jnp.exp(masked - peak), 0.0)
        total = jnp.sum(weight, axis=1, keepdims=True)
        summed = jnp.dot(weight.astype(BF16), value, preferred_element_type=F32)
        context = (summed / total).astype(BF16)
        for step in range(group):
            outs_refs[step][:, at : at + HEAD_DIM] = context[step * local : (step + 1) * local]
    wait_all(moves)


def output_kernel(parts, windows, group, valid_ref, *refs):
    context_refs, refs = refs[:group], refs[group:]
    stack_refs, refs = refs[: windows // parts], refs[windows // parts :]
    out_ref, context, pieces = refs
    _, copy_index = place(parts)
    copies = windows // parts
    plane = lax.axis_index("seq")
    head_width = context_refs[0].shape[1]
    for step in range(group):
        at = pl.multiple_of((plane ^ step) * head_width, LANES)
        context[:, pl.ds(at, head_width)] = context_refs[step][...]
    ordered = context[...]
    for step in range(copies):
        slot = copy_index ^ step
        for piece in range(parts):
            pieces[piece * copies + slot] = jnp.dot(
                ordered, stack_refs[step][piece], preferred_element_type=F32
            )
    result = jnp.concatenate([pieces[d] for d in range(windows)], axis=1)
    out_ref[...] = jnp.where(valid_ref[...] > 0.5, result, 0.0).astype(BF16)


def on_device(
    audio, starts, lengths, slots, conv1_weight, conv2_weight, proj_weight, qkv_weight, out_weight
):
    streams = audio.shape[0]
    windows = lax.axis_size("dp")
    group = lax.axis_size("seq")
    parts = math.gcd(windows, BANDS)
    copies = windows // parts
    assert streams == windows and all(count & (count - 1) == 0 for count in (parts, copies, group))
    share = BANDS // parts
    width = 4 * share + 4
    channels = conv1_weight.shape[1]
    features = proj_weight.shape[1]
    head_width = features // group
    local = windows * W
    rows = JS * streams
    n = parts * streams
    outs = 2 * share + 1
    scale = max(1, windows * group // 32)

    route = [(i, i + 1) for i in range(windows * group - 1)]
    edge, proj_weight = lax.optimization_barrier((audio[:, audio.shape[1] - RIM :], proj_weight))
    rim = lax.ppermute(edge, ("dp", "seq"), route)

    def to_part(block, step):
        pairs = [(p * copies + c, (p ^ step) * copies + c) for p in range(parts) for c in range(copies)]
        return lax.ppermute(block, "dp", pairs)

    def to_copy(block, step):
        pairs = [(p * copies + c, p * copies + (c ^ step)) for p in range(parts) for c in range(copies)]
        return lax.ppermute(block, "dp", pairs)

    def to_window(block, step):
        return lax.ppermute(block, "dp", [(i, i ^ step) for i in range(windows)])

    def to_plane(block, step):
        return lax.ppermute(block, "seq", [(i, i ^ step) for i in range(group)])

    proj_all = [proj_weight] + [to_copy(proj_weight, step) for step in range(1, copies)]

    table = jnp.asarray(spectrum_table(N_FFT))
    mix_piece = jax.ShapeDtypeStruct((qkv_weight.shape[0], 3 * head_width), BF16)
    *mel_all, mix = pl.pallas_call(
        functools.partial(mel_kernel, parts, group),
        out_shape=tuple([jax.ShapeDtypeStruct((rows, LANES), BF16)] * parts + [mix_piece]),
        in_specs=[anywhere()] * 5,
        out_specs=tuple([vmem()] * (parts + 1)),
        scratch_shapes=[
            pltpu.VMEM((streams, RIM + audio.shape[1]), F32),
            pltpu.VMEM(table.shape, F32),
            pltpu.VMEM((parts, rows, LANES), BF16),
            pltpu.SMEM((streams,), jnp.int32),
            pltpu.SemaphoreType.DMA((7,)),
        ],
        compiler_params=params(60),
        cost_estimate=cost(1e10, 2e6),
        name="log_mel",
    )(slots, rim, audio, table, qkv_weight)
    near = [to_part(out_weight, step) for step in range(1, parts - 1)]
    mel_all, proj_all = lax.optimization_barrier((mel_all, proj_all))
    mel_all = [mel_all[0]] + [to_part(mel_all[step], step) for step in range(1, parts)]
    mel_all, near = lax.optimization_barrier((mel_all, near))
    mix_all = [mix] + [to_part(mix, step) for step in range(1, parts)]

    block = jax.ShapeDtypeStruct((local, features), BF16)
    partials = pl.pallas_call(
        functools.partial(conv_kernel, parts, width),
        out_shape=tuple([jax.ShapeDtypeStruct((W * parts, features), BF16)] * windows),
        in_specs=[vmem()] * (2 + parts + copies),
        out_specs=tuple([vmem()] * windows),
        scratch_shapes=[
            pltpu.VMEM((parts, rows, LANES), F32),
            pltpu.VMEM((LANES, outs * channels), BF16),
            pltpu.VMEM((JS * n, outs * channels), BF16),
            pltpu.VMEM((W * n, outs * channels), BF16),
            pltpu.VMEM((W * n, share * channels), BF16),
            pltpu.VMEM((copies, W * n, proj_weight.shape[0]), BF16),
            pltpu.VMEM((features // LANES, W * n, LANES), F32),
        ],
        compiler_params=params(min(40 + 4 * scale, 56)),
        cost_estimate=cost(2e9, 4e6),
        name="conv",
    )(conv1_weight, conv2_weight, *mel_all, *proj_all)
    partials = [to_window(partials[step], step) for step in reversed(range(1, windows))] + [partials[0]]

    ordered, normed, stack = pl.pallas_call(
        functools.partial(norm_kernel, parts),
        out_shape=(block, block, jax.ShapeDtypeStruct((parts,) + mix_piece.shape, BF16)),
        in_specs=[vmem()] * (windows + parts),
        out_specs=(vmem(), vmem(), vmem()),
        scratch_shapes=[pltpu.VMEM((local, features), BF16)],
        compiler_params=params(min(12 * scale, 32)),
        cost_estimate=cost(1e8, 1e6),
        name="layer_norm",
    )(*partials, *mix_all)
    mix_stacks = [stack] + [to_copy(stack, step) for step in range(1, copies)]
    regrouped, keys, valid = pl.pallas_call(
        functools.partial(mask_kernel, windows, group),
        out_shape=(
            block,
            jax.ShapeDtypeStruct((group, local), F32),
            jax.ShapeDtypeStruct((local, 1), F32),
        ),
        in_specs=[smem()] * 3 + [vmem()],
        out_specs=(vmem(), vmem(), vmem()),
        compiler_params=params(min(8 * scale, 32)),
        cost_estimate=cost(1e8, 1e6),
        name="mask",
    )(slots, starts, lengths, ordered)
    normed, out_here = lax.optimization_barrier((normed, out_weight))
    normed = [normed]
    for step in range(1, group):
        high = 1 << (step.bit_length() - 1)
        normed.append(to_plane(normed[high] if step > high else normed[0], step - high if step > high else high))
    out_all = [out_here] + near + [to_part(out_here, parts - 1)]

    *context, stack = pl.pallas_call(
        functools.partial(attention_kernel, parts, windows, group),
        out_shape=tuple(
            [jax.ShapeDtypeStruct((local, head_width), BF16)] * group
            + [jax.ShapeDtypeStruct((parts,) + out_weight.shape, BF16)]
        ),
        in_specs=[vmem()] * (1 + group + copies) + [anywhere()] * parts,
        out_specs=tuple([vmem()] * (group + 1)),
        scratch_shapes=[
            pltpu.VMEM((windows, group * local, qkv_weight.shape[0]), BF16),
            pltpu.SemaphoreType.DMA((parts,)),
        ],
        compiler_params=params(min(16 * scale, 48)),
        cost_estimate=cost(1e9, 2e6),
        name="attention",
    )(keys, *normed, *mix_stacks, *out_all)
    context = [context[0]] + [to_plane(context[step], step) for step in range(1, group)]
    out_stacks = [stack] + [to_copy(stack, step) for step in range(1, copies)]

    attended = pl.pallas_call(
        functools.partial(output_kernel, parts, windows, group),
        out_shape=block,
        in_specs=[vmem()] * (1 + group + copies),
        out_specs=vmem(),
        scratch_shapes=[
            pltpu.VMEM((local, features), BF16),
            pltpu.VMEM((windows, local, out_weight.shape[1]), F32),
        ],
        compiler_params=params(min(12 * scale, 32)),
        cost_estimate=cost(1e8, 3e6),
        name="output",
    )(valid, *context, *out_stacks)
    shape = (1, windows, 1, W, features)
    return (regrouped.reshape(shape), attended.reshape(shape))


def solution(mesh):
    in_specs = (
        P(None, ("dp", "seq")),
        P(),
        P(),
        P(),
        P(),
        P(),
        P("dp", None),
        P("dp", None),
        P(None, "dp"),
    )
    out_specs = (P("dp", None, "seq", None, None), P("dp", None, "seq", None, None))
    return jax.shard_map(
        on_device, mesh=mesh, in_specs=in_specs, out_specs=out_specs, check_vma=False
    )
```

```python
import functools
import math

import jax
import jax.numpy as jnp
import numpy as np
from jax import lax
from jax.experimental import pallas as pl
from jax.experimental.pallas import tpu as pltpu
from jax.sharding import PartitionSpec as P

HEADS = 8
HEAD_DIM = 128
MELS = 80
BANDS = MELS // 4
N_FFT = 512
HOP = 160
W = 8
RIM = 1024
SPAN = 4 * HOP
JS = W + 1
LANES = 128
SAMPLE_RATE = 16000.0
EPS_LOG = 1e-06
EPS_NORM = 1e-05
MASKED = -1e30
F32 = jnp.float32
BF16 = jnp.bfloat16
MIB = 1 << 20


def mel_table(size, bands):
    count = size // 2 + 1
    highest = 2595.0 * math.log10(1.0 + SAMPLE_RATE / 1400.0)
    points = np.linspace(0.0, highest, bands + 2)
    edges = 700.0 * (10.0 ** (points / 2595.0) - 1.0)
    edges[0] = 0.0
    edges[-1] = SAMPLE_RATE / 2.0
    frequency = np.arange(count) * (SAMPLE_RATE / size)
    lower = edges[:-2][None, :]
    middle = edges[1:-1][None, :]
    upper = edges[2:][None, :]
    rising = (frequency[:, None] - lower) / (middle - lower)
    falling = (upper - frequency[:, None]) / (upper - middle)
    return np.maximum(0.0, np.minimum(rising, falling)).astype(np.float32)


def spectrum_table(size):
    half = size // 2
    sample = np.arange(half)
    bins = np.concatenate([np.arange(0, half, 2), np.arange(1, half, 2)])
    angle = sample[:, None] * bins[None, :] % size * (2.0 * math.pi / size)
    table = np.zeros((half + 8, size + LANES))
    for odd in range(2):
        part = angle[:, odd * half // 2 : (odd + 1) * half // 2]
        table[:half, odd * half : (odd + 1) * half] = np.concatenate([np.cos(part), np.sin(part)], axis=1)
    table[:half, size : size + MELS] = mel_table(size, MELS)[bins]
    table[half, :size] = 0.5 - 0.5 * np.cos(np.arange(size) * (2.0 * math.pi / size))
    return table.astype(np.float32)


def vmem():
    return pl.BlockSpec(memory_space=pltpu.VMEM)


def smem():
    return pl.BlockSpec(memory_space=pltpu.SMEM)


def anywhere():
    return pl.BlockSpec(memory_space=pl.ANY)


def params(mib):
    return pltpu.CompilerParams(vmem_limit_bytes=mib * MIB)


def cost(flops, moved):
    return pl.CostEstimate(flops=int(flops), bytes_accessed=int(moved), transcendentals=0)


def place(parts):
    mine = lax.axis_index("dp")
    copies = lax.axis_size("dp") // parts
    return mine // copies, mine % copies


def start_all(copies):
    for copy in copies:
        copy.start()


def wait_all(copies):
    for copy in copies:
        copy.wait()


def iota(rows, columns, axis):
    return lax.broadcasted_iota(jnp.int32, (rows, columns), axis)


def quotient(index, step, count):
    result = jnp.zeros_like(index)
    for i in range(1, count):
        result += (index >= i * step).astype(jnp.int32)
    return result


def one_hot(target, count):
    return (iota(target.shape[0], count, 1) == target).astype(F32).astype(BF16)


def frame_order(parts, copies):
    count = parts * copies * W
    row = iota(count, 1, 0)
    k = quotient(row, W, parts * copies)
    p = quotient(k, copies, parts)
    return one_hot((k - p * copies) * W * parts + (row - k * W) * parts + p, count)


def samples(index, windows, group):
    return (index + quotient(index, W, windows) * (group - 1) * W) * SPAN


def mix_columns(group, qkv_ref, mix_out, sems):
    features = qkv_ref.shape[1] // 3
    width = features // group
    first = pl.multiple_of(lax.axis_index("seq") * width, LANES)
    return [
        pltpu.make_async_copy(
            qkv_ref.at[:, pl.ds(kind * features + first, width)],
            mix_out.at[:, pl.ds(kind * width, width)],
            sems.at[kind],
        )
        for kind in range(3)
    ]


def banded_weights(width, conv1_ref, banded_out):
    taps, channels = conv1_ref.shape
    row = lax.broadcasted_iota(jnp.int32, (LANES, taps), 0)
    tap = lax.broadcasted_iota(jnp.int32, (LANES, taps), 1)
    line = (tap >= 3).astype(jnp.int32) + (tap >= 6).astype(jnp.int32)
    target = line * (width - 3) + tap + 1
    weight = conv1_ref[...]
    for g in range(banded_out.shape[1] // channels):
        select = (row == target + 2 * g).astype(F32).astype(BF16)
        banded_out[:, g * channels : (g + 1) * channels] = jnp.dot(
            select, weight, preferred_element_type=F32
        ).astype(BF16)


def mel_kernel(parts, group, slots_here, rim_ref, audio_ref, table_ref, qkv_ref, *refs):
    outs_refs, (mix_out, ext, table, blocks, slots_ref, sems) = refs[:parts], refs[parts:]
    load_slots = pltpu.make_async_copy(slots_here, slots_ref, sems.at[5])
    load_slots.start()
    load_audio = pltpu.make_async_copy(audio_ref, ext.at[:, pl.ds(RIM, audio_ref.shape[1])], sems.at[3])
    load_table = pltpu.make_async_copy(table_ref, table, sems.at[4])
    load_rim = pltpu.make_async_copy(rim_ref, ext.at[:, pl.ds(0, RIM)], sems.at[6])
    load_rim.start()
    load_audio.start()
    load_table.start()
    pieces = mix_columns(group, qkv_ref, mix_out, sems)
    start_all(pieces)
    streams = audio_ref.shape[0]
    rows = JS * streams
    load_rim.wait()
    load_audio.wait()
    phases = []
    for phase in range(4):
        start = HOP * phase + 32
        base, shift = start // LANES * LANES, start % LANES
        length = N_FFT + (LANES if shift else 0)
        block = jnp.concatenate(
            [ext[:, SPAN * j + base : SPAN * j + base + length] for j in range(JS)], axis=0
        )
        if shift:
            block = pltpu.roll(block, length - shift, 1)[:, :N_FFT]
        phases.append(block)
    frames = jnp.concatenate(phases, axis=0)
    load_table.wait()
    half = N_FFT // 2
    frames = frames * table[half : half + 1, :N_FFT]
    low, high = frames[:, :half], frames[:, half:]
    powers = []
    for odd in range(2):
        spectrum = jnp.dot(
            low - high if odd else low + high,
            table[:half, odd * half : (odd + 1) * half],
            precision=lax.Precision.HIGHEST,
            preferred_element_type=F32,
        )
        real, imag = spectrum[:, : half // 2], spectrum[:, half // 2 :]
        powers.append(real * real + imag * imag)
    mel_power = jnp.dot(
        jnp.concatenate(powers, axis=1),
        table[:half, N_FFT:],
        precision=lax.Precision.HIGHEST,
        preferred_element_type=F32,
    )
    load_slots.wait()
    column = iota(1, rows, 1)
    early = quotient(column, streams, JS)
    target = jnp.zeros((1, rows), jnp.int32)
    for u in range(streams):
        target = jnp.where(column - early * streams == u, early * streams + slots_ref[u], target)
    routing = (target == iota(rows, rows, 0)).astype(F32).astype(BF16)
    log_mel = jnp.log(mel_power + EPS_LOG)
    share = BANDS // parts
    width = 4 * share + 4
    lane = iota(rows, LANES, 1)
    by_phase = [log_mel[phase * rows : (phase + 1) * rows] for phase in range(4)]

    def next_four(frames):
        return jnp.concatenate([frames[streams:], jnp.zeros((streams, LANES), F32)], axis=0)

    taps = [by_phase[1], by_phase[2], by_phase[3], next_four(by_phase[0]), next_four(by_phase[1])]
    by_part = []
    for part in range(parts):
        first = 4 * share * part - 4
        block = jnp.zeros((rows, LANES), F32)
        for delta, frames in enumerate(taps):
            band = lane - width * delta + first
            here = (lane >= width * delta) & (lane < width * (delta + 1)) & (band >= 0) & (band < MELS)
            shift = (width * delta - first) % LANES
            block = jnp.where(here, pltpu.roll(frames, shift, 1) if shift else frames, block)
        by_part.append(block.astype(BF16))
    routed = jnp.dot(routing, jnp.concatenate(by_part, axis=1), preferred_element_type=F32).astype(BF16)
    for part in range(parts):
        blocks[part] = routed[:, part * LANES : (part + 1) * LANES]
    mine, _ = place(parts)
    for step in range(parts):
        outs_refs[step][...] = blocks[mine ^ step]
    wait_all(pieces)


def stacked(parts, pieces, stack_out, sems, base):
    part, _ = place(parts)
    return [
        pltpu.make_async_copy(pieces[step], stack_out.at[part ^ step], sems.at[base + step])
        for step in range(parts)
    ]


def conv_kernel(parts, width, conv1_ref, conv2_ref, *refs):
    part, copy_index = place(parts)
    mine = lax.axis_index("dp")
    windows = lax.axis_size("dp")
    copies = windows // parts
    mel_refs, refs = refs[:parts], refs[parts:]
    proj_refs, refs = refs[:copies], refs[copies:]
    outs_refs, refs = refs[:windows], refs[windows:]
    mel, banded_ref, even, odd, second, by_slot, partial = refs
    banded_weights(width, conv1_ref, banded_ref)
    streams = mel_refs[0].shape[0] // JS
    n = parts * streams
    for step in range(parts):
        mel[part ^ step] = mel_refs[step][...].astype(F32)
    evens = jnp.concatenate(
        [mel[p, j * streams : (j + 1) * streams, :] for j in range(JS) for p in range(parts)], axis=0
    )
    odds = pltpu.roll(evens[: W * n], LANES - 2 * width, 1).astype(BF16)
    both = jnp.concatenate([evens.astype(BF16), odds], axis=0)
    channels = conv2_ref.shape[1]
    outs = banded_ref.shape[1] // channels
    for g in range(outs):
        lanes = slice(g * channels, (g + 1) * channels)
        weight = banded_ref[:, lanes]
        first = jax.nn.relu(jnp.dot(both, weight, preferred_element_type=F32)).astype(BF16)
        even[:, lanes] = first[: JS * n]
        odd[:, lanes] = first[JS * n :]

    for h in range((outs - 1) // 2):
        lanes = slice(2 * h * channels, (2 * h + 3) * channels)
        taps = jnp.concatenate([even[: W * n, lanes], odd[:, lanes], even[n:, lanes]], axis=1)
        total = jnp.dot(taps, conv2_ref[...], preferred_element_type=F32)
        second[:, h * channels : (h + 1) * channels] = jax.nn.relu(total).astype(BF16)
    depth = by_slot.shape[2]
    for slot in range(copies):
        by_slot[slot] = second[:, slot * depth : (slot + 1) * depth]
    sums = jnp.dot(by_slot[copy_index], proj_refs[0][...], preferred_element_type=F32)
    for step in range(1, copies):
        sums += jnp.dot(by_slot[copy_index ^ step], proj_refs[step][...], preferred_element_type=F32)
    for block in range(partial.shape[0]):
        partial[block] = sums[:, block * LANES : (block + 1) * LANES]
    for step in range(windows):
        for block in range(partial.shape[0]):
            rows = partial[block, pl.ds(mine ^ step, W * parts, stride=streams), :]
            outs_refs[step][:, block * LANES : (block + 1) * LANES] = rows.astype(BF16)


def bounds(row, slots_ref, starts_ref, lengths_ref):
    begin, span = jnp.int32(0), jnp.int32(0)
    for u in range(slots_ref.shape[0]):
        chosen = slots_ref[u] == row
        begin = begin + jnp.where(chosen, starts_ref[u], 0)
        span = span + jnp.where(chosen, lengths_ref[u], 0)
    return begin, begin + span


def norm_kernel(parts, *refs):
    part, copy_index = place(parts)
    windows = lax.axis_size("dp")
    copies = windows // parts
    part_refs, refs = refs[:windows][::-1], refs[windows:]
    piece_refs, refs = refs[:parts], refs[parts:]
    rows_out, normed_out, stack_out, encoded = refs
    for step in range(parts):
        stack_out[part ^ step] = piece_refs[step][...]
    rows = W * parts
    for copy in range(copies):
        total = part_refs[copy][...].astype(F32)
        for step in range(1, parts):
            total += part_refs[step * copies + copy][...].astype(F32)
        at = pl.multiple_of((copy_index ^ copy) * rows, rows)
        encoded[pl.ds(at, rows), :] = total.astype(BF16)
    values = jnp.dot(frame_order(parts, copies), encoded[...], preferred_element_type=F32)
    rows_out[...] = values.astype(BF16)
    mean = jnp.mean(values, axis=-1, keepdims=True)
    centered = values - mean
    variance = jnp.mean(centered * centered, axis=-1, keepdims=True)
    normed_out[...] = (centered * lax.rsqrt(variance + EPS_NORM)).astype(BF16)


def mask_kernel(windows, group, slots_ref, starts_ref, lengths_ref, rows_ref, rows_out, keys_out, valid_out):
    begin, end = bounds(lax.axis_index("dp"), slots_ref, starts_ref, lengths_ref)
    sample = samples(iota(windows * W, 1, 0), windows, group) + lax.axis_index("seq") * (W * SPAN)
    valid = (sample >= begin) & (sample < end)
    rows_out[...] = jnp.where(valid, rows_ref[...].astype(F32), 0.0).astype(BF16)
    valid_out[...] = valid.astype(F32)
    keys = samples(iota(group, windows * W, 1), windows, group) + iota(group, windows * W, 0) * (W * SPAN)
    keys_out[...] = ((keys >= begin) & (keys < end)).astype(F32)


def attention_kernel(parts, windows, group, keys_ref, *refs):
    _, copy_index = place(parts)
    plane = lax.axis_index("seq")
    copies = windows // parts
    normed_refs, refs = refs[:group], refs[group:]
    stack_refs, refs = refs[:copies], refs[copies:]
    weight_refs, refs = refs[:parts], refs[parts:]
    outs_refs, (stack_out, pieces, sems) = refs[:group], refs[group:]
    moves = stacked(parts, weight_refs, stack_out, sems, 0)
    start_all(moves)
    keys = [keys_ref[pl.ds(plane ^ step, 1), :] for step in range(group)]
    valid = jnp.concatenate(keys, axis=1) > 0.5
    local = normed_refs[0].shape[0]
    depth = pieces.shape[2]
    for step in range(group):
        for piece in range(windows):
            pieces[piece, step * local : (step + 1) * local, :] = normed_refs[step][
                :, piece * depth : (piece + 1) * depth
            ]
    mixed = 0.0
    for step in range(copies):
        slot = copy_index ^ step
        normed = jnp.concatenate([pieces[piece * copies + slot] for piece in range(parts)], axis=1)
        weights = stack_refs[step][...].reshape(parts * depth, stack_refs[step].shape[2])
        mixed += jnp.dot(normed, weights, preferred_element_type=F32)
    mixed = mixed.astype(BF16)
    width = mixed.shape[1] // 3
    scale = HEAD_DIM ** (-0.5)
    for head in range(width // HEAD_DIM):
        at = head * HEAD_DIM
        query = mixed[:, at : at + HEAD_DIM]
        key = mixed[:, width + at : width + at + HEAD_DIM]
        value = mixed[:, 2 * width + at : 2 * width + at + HEAD_DIM]
        scores = lax.dot_general(query, key, (((1,), (1,)), ((), ())), preferred_element_type=F32) * scale
        masked = jnp.where(valid, scores, MASKED)
        peak = jnp.max(masked, axis=1, keepdims=True)
        weight = jnp.where(valid, jnp.exp(masked - peak), 0.0)
        total = jnp.sum(weight, axis=1, keepdims=True)
        summed = jnp.dot(weight.astype(BF16), value, preferred_element_type=F32)
        context = (summed / total).astype(BF16)
        for step in range(group):
            outs_refs[step][:, at : at + HEAD_DIM] = context[step * local : (step + 1) * local]
    wait_all(moves)


def output_kernel(parts, windows, group, valid_ref, *refs):
    context_refs, refs = refs[:group], refs[group:]
    stack_refs, refs = refs[: windows // parts], refs[windows // parts :]
    out_ref, context, pieces = refs
    _, copy_index = place(parts)
    copies = windows // parts
    plane = lax.axis_index("seq")
    head_width = context_refs[0].shape[1]
    for step in range(group):
        at = pl.multiple_of((plane ^ step) * head_width, LANES)
        context[:, pl.ds(at, head_width)] = context_refs[step][...]
    ordered = context[...]
    for step in range(copies):
        slot = copy_index ^ step
        for piece in range(parts):
            pieces[piece * copies + slot] = jnp.dot(
                ordered, stack_refs[step][piece], preferred_element_type=F32
            )
    result = jnp.concatenate([pieces[d] for d in range(windows)], axis=1)
    out_ref[...] = jnp.where(valid_ref[...] > 0.5, result, 0.0).astype(BF16)


def on_device(
    audio, starts, lengths, slots, conv1_weight, conv2_weight, proj_weight, qkv_weight, out_weight
):
    streams = audio.shape[0]
    windows = lax.axis_size("dp")
    group = lax.axis_size("seq")
    parts = math.gcd(windows, BANDS)
    copies = windows // parts
    assert streams == windows and all(count & (count - 1) == 0 for count in (parts, copies, group))
    share = BANDS // parts
    width = 4 * share + 4
    channels = conv1_weight.shape[1]
    features = proj_weight.shape[1]
    head_width = features // group
    local = windows * W
    rows = JS * streams
    n = parts * streams
    outs = 2 * share + 1
    scale = max(1, windows * group // 32)

    route = [(i, i + 1) for i in range(windows * group - 1)]
    rim = lax.ppermute(audio[:, audio.shape[1] - RIM :], ("dp", "seq"), route)

    def to_part(block, step):
        pairs = [(p * copies + c, (p ^ step) * copies + c) for p in range(parts) for c in range(copies)]
        return lax.ppermute(block, "dp", pairs)

    def to_copy(block, step):
        pairs = [(p * copies + c, p * copies + (c ^ step)) for p in range(parts) for c in range(copies)]
        return lax.ppermute(block, "dp", pairs)

    def to_window(block, step):
        return lax.ppermute(block, "dp", [(i, i ^ step) for i in range(windows)])

    def to_plane(block, step):
        return lax.ppermute(block, "seq", [(i, i ^ step) for i in range(group)])

    proj_all = [proj_weight] + [to_copy(proj_weight, step) for step in range(1, copies)]

    table = jnp.asarray(spectrum_table(N_FFT))
    mix_piece = jax.ShapeDtypeStruct((qkv_weight.shape[0], 3 * head_width), BF16)
    *mel_all, mix = pl.pallas_call(
        functools.partial(mel_kernel, parts, group),
        out_shape=tuple([jax.ShapeDtypeStruct((rows, LANES), BF16)] * parts + [mix_piece]),
        in_specs=[anywhere()] * 5,
        out_specs=tuple([vmem()] * (parts + 1)),
        scratch_shapes=[
            pltpu.VMEM((streams, RIM + audio.shape[1]), F32),
            pltpu.VMEM(table.shape, F32),
            pltpu.VMEM((parts, rows, LANES), BF16),
            pltpu.SMEM((streams,), jnp.int32),
            pltpu.SemaphoreType.DMA((7,)),
        ],
        compiler_params=params(60),
        cost_estimate=cost(1e10, 2e6),
        name="log_mel",
    )(slots, rim, audio, table, qkv_weight)
    near = [to_part(out_weight, step) for step in range(1, parts - 1)]
    mel_all, proj_all = lax.optimization_barrier((mel_all, proj_all))
    mel_all = [mel_all[0]] + [to_part(mel_all[step], step) for step in range(1, parts)]
    mel_all, near = lax.optimization_barrier((mel_all, near))
    mix_all = [mix] + [to_part(mix, step) for step in range(1, parts)]

    block = jax.ShapeDtypeStruct((local, features), BF16)
    partials = pl.pallas_call(
        functools.partial(conv_kernel, parts, width),
        out_shape=tuple([jax.ShapeDtypeStruct((W * parts, features), BF16)] * windows),
        in_specs=[vmem()] * (2 + parts + copies),
        out_specs=tuple([vmem()] * windows),
        scratch_shapes=[
            pltpu.VMEM((parts, rows, LANES), F32),
            pltpu.VMEM((LANES, outs * channels), BF16),
            pltpu.VMEM((JS * n, outs * channels), BF16),
            pltpu.VMEM((W * n, outs * channels), BF16),
            pltpu.VMEM((W * n, share * channels), BF16),
            pltpu.VMEM((copies, W * n, proj_weight.shape[0]), BF16),
            pltpu.VMEM((features // LANES, W * n, LANES), F32),
        ],
        compiler_params=params(min(40 + 4 * scale, 56)),
        cost_estimate=cost(2e9, 4e6),
        name="conv",
    )(conv1_weight, conv2_weight, *mel_all, *proj_all)
    partials = [to_window(partials[step], step) for step in reversed(range(1, windows))] + [partials[0]]

    ordered, normed, stack = pl.pallas_call(
        functools.partial(norm_kernel, parts),
        out_shape=(block, block, jax.ShapeDtypeStruct((parts,) + mix_piece.shape, BF16)),
        in_specs=[vmem()] * (windows + parts),
        out_specs=(vmem(), vmem(), vmem()),
        scratch_shapes=[pltpu.VMEM((local, features), BF16)],
        compiler_params=params(min(12 * scale, 32)),
        cost_estimate=cost(1e8, 1e6),
        name="layer_norm",
    )(*partials, *mix_all)
    mix_stacks = [stack] + [to_copy(stack, step) for step in range(1, copies)]
    regrouped, keys, valid = pl.pallas_call(
        functools.partial(mask_kernel, windows, group),
        out_shape=(
            block,
            jax.ShapeDtypeStruct((group, local), F32),
            jax.ShapeDtypeStruct((local, 1), F32),
        ),
        in_specs=[smem()] * 3 + [vmem()],
        out_specs=(vmem(), vmem(), vmem()),
        compiler_params=params(min(8 * scale, 32)),
        cost_estimate=cost(1e8, 1e6),
        name="mask",
    )(slots, starts, lengths, ordered)
    normed, out_here = lax.optimization_barrier((normed, out_weight))
    normed = [normed]
    for step in range(1, group):
        high = 1 << (step.bit_length() - 1)
        normed.append(to_plane(normed[high] if step > high else normed[0], step - high if step > high else high))
    out_all = [out_here] + near + [to_part(out_here, parts - 1)]

    *context, stack = pl.pallas_call(
        functools.partial(attention_kernel, parts, windows, group),
        out_shape=tuple(
            [jax.ShapeDtypeStruct((local, head_width), BF16)] * group
            + [jax.ShapeDtypeStruct((parts,) + out_weight.shape, BF16)]
        ),
        in_specs=[vmem()] * (1 + group + copies) + [anywhere()] * parts,
        out_specs=tuple([vmem()] * (group + 1)),
        scratch_shapes=[
            pltpu.VMEM((windows, group * local, qkv_weight.shape[0]), BF16),
            pltpu.SemaphoreType.DMA((parts,)),
        ],
        compiler_params=params(min(16 * scale, 48)),
        cost_estimate=cost(1e9, 2e6),
        name="attention",
    )(keys, *normed, *mix_stacks, *out_all)
    context = [context[0]] + [to_plane(context[step], step) for step in range(1, group)]
    out_stacks = [stack] + [to_copy(stack, step) for step in range(1, copies)]

    attended = pl.pallas_call(
        functools.partial(output_kernel, parts, windows, group),
        out_shape=block,
        in_specs=[vmem()] * (1 + group + copies),
        out_specs=vmem(),
        scratch_shapes=[
            pltpu.VMEM((local, features), BF16),
            pltpu.VMEM((windows, local, out_weight.shape[1]), F32),
        ],
        compiler_params=params(min(12 * scale, 32)),
        cost_estimate=cost(1e8, 3e6),
        name="output",
    )(valid, *context, *out_stacks)
    shape = (1, windows, 1, W, features)
    return (regrouped.reshape(shape), attended.reshape(shape))


def solution(mesh):
    in_specs = (
        P(None, ("dp", "seq")),
        P(),
        P(),
        P(),
        P(),
        P(),
        P("dp", None),
        P("dp", None),
        P(None, "dp"),
    )
    out_specs = (P("dp", None, "seq", None, None), P("dp", None, "seq", None, None))
    return jax.shard_map(
        on_device, mesh=mesh, in_specs=in_specs, out_specs=out_specs, check_vma=False
    )
```

```python
import functools
import math

import jax
import jax.numpy as jnp
import numpy as np
from jax import lax
from jax.experimental import pallas as pl
from jax.experimental.pallas import tpu as pltpu
from jax.sharding import PartitionSpec as P

HEADS = 8
HEAD_DIM = 128
MELS = 80
BANDS = MELS // 4
N_FFT = 512
HOP = 160
W = 8
RIM = 1024
SPAN = 4 * HOP
JS = W + 1
LANES = 128
SAMPLE_RATE = 16000.0
EPS_LOG = 1e-06
EPS_NORM = 1e-05
MASKED = -1e30
F32 = jnp.float32
BF16 = jnp.bfloat16
MIB = 1 << 20


def mel_table(size, bands):
    count = size // 2 + 1
    highest = 2595.0 * math.log10(1.0 + SAMPLE_RATE / 1400.0)
    points = np.linspace(0.0, highest, bands + 2)
    edges = 700.0 * (10.0 ** (points / 2595.0) - 1.0)
    edges[0] = 0.0
    edges[-1] = SAMPLE_RATE / 2.0
    frequency = np.arange(count) * (SAMPLE_RATE / size)
    lower = edges[:-2][None, :]
    middle = edges[1:-1][None, :]
    upper = edges[2:][None, :]
    rising = (frequency[:, None] - lower) / (middle - lower)
    falling = (upper - frequency[:, None]) / (upper - middle)
    return np.maximum(0.0, np.minimum(rising, falling)).astype(np.float32)


def spectrum_table(size):
    half = size // 2
    sample = np.arange(half)
    bins = np.concatenate([np.arange(0, half, 2), np.arange(1, half, 2)])
    angle = sample[:, None] * bins[None, :] % size * (2.0 * math.pi / size)
    table = np.zeros((half + 8, size + LANES))
    for odd in range(2):
        part = angle[:, odd * half // 2 : (odd + 1) * half // 2]
        table[:half, odd * half : (odd + 1) * half] = np.concatenate([np.cos(part), np.sin(part)], axis=1)
    table[:half, size : size + MELS] = mel_table(size, MELS)[bins]
    table[half, :size] = 0.5 - 0.5 * np.cos(np.arange(size) * (2.0 * math.pi / size))
    return table.astype(np.float32)


def vmem():
    return pl.BlockSpec(memory_space=pltpu.VMEM)


def smem():
    return pl.BlockSpec(memory_space=pltpu.SMEM)


def anywhere():
    return pl.BlockSpec(memory_space=pl.ANY)


def params(mib):
    return pltpu.CompilerParams(vmem_limit_bytes=mib * MIB)


def cost(flops, moved):
    return pl.CostEstimate(flops=int(flops), bytes_accessed=int(moved), transcendentals=0)


def place(parts):
    mine = lax.axis_index("dp")
    copies = lax.axis_size("dp") // parts
    return mine // copies, mine % copies


def start_all(copies):
    for copy in copies:
        copy.start()


def wait_all(copies):
    for copy in copies:
        copy.wait()


def iota(rows, columns, axis):
    return lax.broadcasted_iota(jnp.int32, (rows, columns), axis)


def quotient(index, step, count):
    result = jnp.zeros_like(index)
    for i in range(1, count):
        result += (index >= i * step).astype(jnp.int32)
    return result


def one_hot(target, count):
    return (iota(target.shape[0], count, 1) == target).astype(F32).astype(BF16)


def frame_order(parts, copies):
    count = parts * copies * W
    row = iota(count, 1, 0)
    k = quotient(row, W, parts * copies)
    p = quotient(k, copies, parts)
    return one_hot((k - p * copies) * W * parts + (row - k * W) * parts + p, count)


def samples(index, windows, group):
    return (index + quotient(index, W, windows) * (group - 1) * W) * SPAN


def mix_columns(group, qkv_ref, mix_out, sems):
    features = qkv_ref.shape[1] // 3
    width = features // group
    first = pl.multiple_of(lax.axis_index("seq") * width, LANES)
    return [
        pltpu.make_async_copy(
            qkv_ref.at[:, pl.ds(kind * features + first, width)],
            mix_out.at[:, pl.ds(kind * width, width)],
            sems.at[kind],
        )
        for kind in range(3)
    ]


def banded_weights(width, conv1_ref, banded_out):
    taps, channels = conv1_ref.shape
    row = lax.broadcasted_iota(jnp.int32, (LANES, taps), 0)
    tap = lax.broadcasted_iota(jnp.int32, (LANES, taps), 1)
    line = (tap >= 3).astype(jnp.int32) + (tap >= 6).astype(jnp.int32)
    target = line * (width - 3) + tap + 1
    weight = conv1_ref[...]
    for g in range(banded_out.shape[1] // channels):
        select = (row == target + 2 * g).astype(F32).astype(BF16)
        banded_out[:, g * channels : (g + 1) * channels] = jnp.dot(
            select, weight, preferred_element_type=F32
        ).astype(BF16)


def mel_kernel(parts, group, slots_here, rim_ref, audio_ref, table_ref, qkv_ref, *refs):
    outs_refs, (mix_out, ext, table, blocks, slots_ref, sems) = refs[:parts], refs[parts:]
    load_slots = pltpu.make_async_copy(slots_here, slots_ref, sems.at[5])
    load_slots.start()
    load_audio = pltpu.make_async_copy(audio_ref, ext.at[:, pl.ds(RIM, audio_ref.shape[1])], sems.at[3])
    load_table = pltpu.make_async_copy(table_ref, table, sems.at[4])
    load_rim = pltpu.make_async_copy(rim_ref, ext.at[:, pl.ds(0, RIM)], sems.at[6])
    load_rim.start()
    load_audio.start()
    load_table.start()
    pieces = mix_columns(group, qkv_ref, mix_out, sems)
    start_all(pieces)
    streams = audio_ref.shape[0]
    rows = JS * streams
    load_rim.wait()
    load_audio.wait()
    phases = []
    for phase in range(4):
        start = HOP * phase + 32
        base, shift = start // LANES * LANES, start % LANES
        length = N_FFT + (LANES if shift else 0)
        block = jnp.concatenate(
            [ext[:, SPAN * j + base : SPAN * j + base + length] for j in range(JS)], axis=0
        )
        if shift:
            block = pltpu.roll(block, length - shift, 1)[:, :N_FFT]
        phases.append(block)
    frames = jnp.concatenate(phases, axis=0)
    load_table.wait()
    half = N_FFT // 2
    frames = frames * table[half : half + 1, :N_FFT]
    low, high = frames[:, :half], frames[:, half:]
    powers = []
    for odd in range(2):
        spectrum = jnp.dot(
            low - high if odd else low + high,
            table[:half, odd * half : (odd + 1) * half],
            precision=lax.Precision.HIGHEST,
            preferred_element_type=F32,
        )
        real, imag = spectrum[:, : half // 2], spectrum[:, half // 2 :]
        powers.append(real * real + imag * imag)
    mel_power = jnp.dot(
        jnp.concatenate(powers, axis=1),
        table[:half, N_FFT:],
        precision=lax.Precision.HIGHEST,
        preferred_element_type=F32,
    )
    load_slots.wait()
    column = iota(1, rows, 1)
    early = quotient(column, streams, JS)
    target = jnp.zeros((1, rows), jnp.int32)
    for u in range(streams):
        target = jnp.where(column - early * streams == u, early * streams + slots_ref[u], target)
    routing = (target == iota(rows, rows, 0)).astype(F32).astype(BF16)
    log_mel = jnp.log(mel_power + EPS_LOG)
    share = BANDS // parts
    width = 4 * share + 4
    lane = iota(rows, LANES, 1)
    by_phase = [log_mel[phase * rows : (phase + 1) * rows] for phase in range(4)]

    def next_four(frames):
        return jnp.concatenate([frames[streams:], jnp.zeros((streams, LANES), F32)], axis=0)

    taps = [by_phase[1], by_phase[2], by_phase[3], next_four(by_phase[0]), next_four(by_phase[1])]
    by_part = []
    for part in range(parts):
        first = 4 * share * part - 4
        block = jnp.zeros((rows, LANES), F32)
        for delta, frames in enumerate(taps):
            band = lane - width * delta + first
            here = (lane >= width * delta) & (lane < width * (delta + 1)) & (band >= 0) & (band < MELS)
            shift = (width * delta - first) % LANES
            block = jnp.where(here, pltpu.roll(frames, shift, 1) if shift else frames, block)
        by_part.append(block.astype(BF16))
    routed = jnp.dot(routing, jnp.concatenate(by_part, axis=1), preferred_element_type=F32).astype(BF16)
    for part in range(parts):
        blocks[part] = routed[:, part * LANES : (part + 1) * LANES]
    mine, _ = place(parts)
    for step in range(parts):
        outs_refs[step][...] = blocks[mine ^ step]
    wait_all(pieces)


def stacked(parts, pieces, stack_out, sems, base):
    part, _ = place(parts)
    return [
        pltpu.make_async_copy(pieces[step], stack_out.at[part ^ step], sems.at[base + step])
        for step in range(parts)
    ]


def conv_kernel(parts, width, conv1_ref, conv2_ref, *refs):
    part, copy_index = place(parts)
    mine = lax.axis_index("dp")
    windows = lax.axis_size("dp")
    copies = windows // parts
    mel_refs, refs = refs[:parts], refs[parts:]
    proj_refs, refs = refs[:copies], refs[copies:]
    outs_refs, refs = refs[:windows], refs[windows:]
    mel, banded_ref, even, odd, second, by_slot, partial = refs
    banded_weights(width, conv1_ref, banded_ref)
    streams = mel_refs[0].shape[0] // JS
    n = parts * streams
    for step in range(parts):
        mel[part ^ step] = mel_refs[step][...].astype(F32)
    evens = jnp.concatenate(
        [mel[p, j * streams : (j + 1) * streams, :] for j in range(JS) for p in range(parts)], axis=0
    )
    odds = pltpu.roll(evens[: W * n], LANES - 2 * width, 1).astype(BF16)
    both = jnp.concatenate([evens.astype(BF16), odds], axis=0)
    channels = conv2_ref.shape[1]
    outs = banded_ref.shape[1] // channels
    for g in range(outs):
        lanes = slice(g * channels, (g + 1) * channels)
        weight = banded_ref[:, lanes]
        first = jax.nn.relu(jnp.dot(both, weight, preferred_element_type=F32)).astype(BF16)
        even[:, lanes] = first[: JS * n]
        odd[:, lanes] = first[JS * n :]

    for h in range((outs - 1) // 2):
        lanes = slice(2 * h * channels, (2 * h + 3) * channels)
        taps = jnp.concatenate([even[: W * n, lanes], odd[:, lanes], even[n:, lanes]], axis=1)
        total = jnp.dot(taps, conv2_ref[...], preferred_element_type=F32)
        second[:, h * channels : (h + 1) * channels] = jax.nn.relu(total).astype(BF16)
    depth = by_slot.shape[2]
    for slot in range(copies):
        by_slot[slot] = second[:, slot * depth : (slot + 1) * depth]
    sums = jnp.dot(by_slot[copy_index], proj_refs[0][...], preferred_element_type=F32)
    for step in range(1, copies):
        sums += jnp.dot(by_slot[copy_index ^ step], proj_refs[step][...], preferred_element_type=F32)
    for block in range(partial.shape[0]):
        partial[block] = sums[:, block * LANES : (block + 1) * LANES]
    for step in range(windows):
        for block in range(partial.shape[0]):
            rows = partial[block, pl.ds(mine ^ step, W * parts, stride=streams), :]
            outs_refs[step][:, block * LANES : (block + 1) * LANES] = rows.astype(BF16)


def bounds(row, slots_ref, starts_ref, lengths_ref):
    begin, span = jnp.int32(0), jnp.int32(0)
    for u in range(slots_ref.shape[0]):
        chosen = slots_ref[u] == row
        begin = begin + jnp.where(chosen, starts_ref[u], 0)
        span = span + jnp.where(chosen, lengths_ref[u], 0)
    return begin, begin + span


def norm_kernel(parts, *refs):
    part, copy_index = place(parts)
    windows = lax.axis_size("dp")
    copies = windows // parts
    part_refs, refs = refs[:windows][::-1], refs[windows:]
    piece_refs, refs = refs[:parts], refs[parts:]
    rows_out, normed_out, stack_out, encoded = refs
    for step in range(parts):
        stack_out[part ^ step] = piece_refs[step][...]
    rows = W * parts
    for copy in range(copies):
        total = part_refs[copy][...].astype(F32)
        for step in range(1, parts):
            total += part_refs[step * copies + copy][...].astype(F32)
        at = pl.multiple_of((copy_index ^ copy) * rows, rows)
        encoded[pl.ds(at, rows), :] = total.astype(BF16)
    values = jnp.dot(frame_order(parts, copies), encoded[...], preferred_element_type=F32)
    rows_out[...] = values.astype(BF16)
    mean = jnp.mean(values, axis=-1, keepdims=True)
    centered = values - mean
    variance = jnp.mean(centered * centered, axis=-1, keepdims=True)
    normed_out[...] = (centered * lax.rsqrt(variance + EPS_NORM)).astype(BF16)


def mask_kernel(windows, group, slots_ref, starts_ref, lengths_ref, rows_ref, rows_out, keys_out, valid_out):
    begin, end = bounds(lax.axis_index("dp"), slots_ref, starts_ref, lengths_ref)
    sample = samples(iota(windows * W, 1, 0), windows, group) + lax.axis_index("seq") * (W * SPAN)
    valid = (sample >= begin) & (sample < end)
    rows_out[...] = jnp.where(valid, rows_ref[...].astype(F32), 0.0).astype(BF16)
    valid_out[...] = valid.astype(F32)
    keys = samples(iota(group, windows * W, 1), windows, group) + iota(group, windows * W, 0) * (W * SPAN)
    keys_out[...] = ((keys >= begin) & (keys < end)).astype(F32)


def attention_kernel(parts, windows, group, keys_ref, *refs):
    _, copy_index = place(parts)
    plane = lax.axis_index("seq")
    copies = windows // parts
    normed_refs, refs = refs[:group], refs[group:]
    stack_refs, refs = refs[:copies], refs[copies:]
    weight_refs, refs = refs[:parts], refs[parts:]
    outs_refs, (stack_out, pieces, sems) = refs[:group], refs[group:]
    moves = stacked(parts, weight_refs, stack_out, sems, 0)
    start_all(moves)
    keys = [keys_ref[pl.ds(plane ^ step, 1), :] for step in range(group)]
    valid = jnp.concatenate(keys, axis=1) > 0.5
    local = normed_refs[0].shape[0]
    depth = pieces.shape[2]
    for step in range(group):
        for piece in range(windows if depth % LANES else 0):
            pieces[piece, step * local : (step + 1) * local, :] = normed_refs[step][
                :, piece * depth : (piece + 1) * depth
            ]
    mixed = 0.0
    for step in range(copies):
        slot = copy_index ^ step
        if depth % LANES:
            normed = jnp.concatenate([pieces[piece * copies + slot] for piece in range(parts)], axis=1)
        else:
            places = [pl.multiple_of((piece * copies + slot) * depth, LANES) for piece in range(parts)]
            columns = [[ref[:, pl.ds(at, depth)] for at in places] for ref in normed_refs]
            normed = jnp.concatenate([jnp.concatenate(row, axis=1) for row in columns], axis=0)
        weights = stack_refs[step][...].reshape(parts * depth, stack_refs[step].shape[2])
        mixed += jnp.dot(normed, weights, preferred_element_type=F32)
    mixed = mixed.astype(BF16)
    width = mixed.shape[1] // 3
    scale = HEAD_DIM ** (-0.5)
    for head in range(width // HEAD_DIM):
        at = head * HEAD_DIM
        query = mixed[:, at : at + HEAD_DIM]
        key = mixed[:, width + at : width + at + HEAD_DIM]
        value = mixed[:, 2 * width + at : 2 * width + at + HEAD_DIM]
        scores = lax.dot_general(query, key, (((1,), (1,)), ((), ())), preferred_element_type=F32) * scale
        masked = jnp.where(valid, scores, MASKED)
        peak = jnp.max(masked, axis=1, keepdims=True)
        weight = jnp.where(valid, jnp.exp(masked - peak), 0.0)
        total = jnp.sum(weight, axis=1, keepdims=True)
        summed = jnp.dot(weight.astype(BF16), value, preferred_element_type=F32)
        context = (summed / total).astype(BF16)
        for step in range(group):
            outs_refs[step][:, at : at + HEAD_DIM] = context[step * local : (step + 1) * local]
    wait_all(moves)


def output_kernel(parts, windows, group, valid_ref, *refs):
    context_refs, refs = refs[:group], refs[group:]
    stack_refs, refs = refs[: windows // parts], refs[windows // parts :]
    out_ref, context, pieces = refs
    _, copy_index = place(parts)
    copies = windows // parts
    plane = lax.axis_index("seq")
    head_width = context_refs[0].shape[1]
    for step in range(group):
        at = pl.multiple_of((plane ^ step) * head_width, LANES)
        context[:, pl.ds(at, head_width)] = context_refs[step][...]
    ordered = context[...]
    for step in range(copies):
        slot = copy_index ^ step
        for piece in range(parts):
            pieces[piece * copies + slot] = jnp.dot(
                ordered, stack_refs[step][piece], preferred_element_type=F32
            )
    result = jnp.concatenate([pieces[d] for d in range(windows)], axis=1)
    out_ref[...] = jnp.where(valid_ref[...] > 0.5, result, 0.0).astype(BF16)


def on_device(
    audio, starts, lengths, slots, conv1_weight, conv2_weight, proj_weight, qkv_weight, out_weight
):
    streams = audio.shape[0]
    windows = lax.axis_size("dp")
    group = lax.axis_size("seq")
    parts = math.gcd(windows, BANDS)
    copies = windows // parts
    assert streams == windows and all(count & (count - 1) == 0 for count in (parts, copies, group))
    share = BANDS // parts
    width = 4 * share + 4
    channels = conv1_weight.shape[1]
    features = proj_weight.shape[1]
    head_width = features // group
    local = windows * W
    rows = JS * streams
    n = parts * streams
    outs = 2 * share + 1
    scale = max(1, windows * group // 32)

    route = [(i, i + 1) for i in range(windows * group - 1)]
    rim = lax.ppermute(audio[:, audio.shape[1] - RIM :], ("dp", "seq"), route)

    def to_part(block, step):
        pairs = [(p * copies + c, (p ^ step) * copies + c) for p in range(parts) for c in range(copies)]
        return lax.ppermute(block, "dp", pairs)

    def to_copy(block, step):
        pairs = [(p * copies + c, p * copies + (c ^ step)) for p in range(parts) for c in range(copies)]
        return lax.ppermute(block, "dp", pairs)

    def to_window(block, step):
        return lax.ppermute(block, "dp", [(i, i ^ step) for i in range(windows)])

    def to_plane(block, step):
        return lax.ppermute(block, "seq", [(i, i ^ step) for i in range(group)])

    proj_all = [proj_weight] + [to_copy(proj_weight, step) for step in range(1, copies)]

    table = jnp.asarray(spectrum_table(N_FFT))
    mix_piece = jax.ShapeDtypeStruct((qkv_weight.shape[0], 3 * head_width), BF16)
    *mel_all, mix = pl.pallas_call(
        functools.partial(mel_kernel, parts, group),
        out_shape=tuple([jax.ShapeDtypeStruct((rows, LANES), BF16)] * parts + [mix_piece]),
        in_specs=[anywhere()] * 5,
        out_specs=tuple([vmem()] * (parts + 1)),
        scratch_shapes=[
            pltpu.VMEM((streams, RIM + audio.shape[1]), F32),
            pltpu.VMEM(table.shape, F32),
            pltpu.VMEM((parts, rows, LANES), BF16),
            pltpu.SMEM((streams,), jnp.int32),
            pltpu.SemaphoreType.DMA((7,)),
        ],
        compiler_params=params(60),
        cost_estimate=cost(1e10, 2e6),
        name="log_mel",
    )(slots, rim, audio, table, qkv_weight)
    near = [to_part(out_weight, step) for step in range(1, parts - 1)]
    mel_all, proj_all = lax.optimization_barrier((mel_all, proj_all))
    mel_all = [mel_all[0]] + [to_part(mel_all[step], step) for step in range(1, parts)]
    mel_all, near = lax.optimization_barrier((mel_all, near))
    mix_all = [mix] + [to_part(mix, step) for step in range(1, parts)]

    block = jax.ShapeDtypeStruct((local, features), BF16)
    partials = pl.pallas_call(
        functools.partial(conv_kernel, parts, width),
        out_shape=tuple([jax.ShapeDtypeStruct((W * parts, features), BF16)] * windows),
        in_specs=[vmem()] * (2 + parts + copies),
        out_specs=tuple([vmem()] * windows),
        scratch_shapes=[
            pltpu.VMEM((parts, rows, LANES), F32),
            pltpu.VMEM((LANES, outs * channels), BF16),
            pltpu.VMEM((JS * n, outs * channels), BF16),
            pltpu.VMEM((W * n, outs * channels), BF16),
            pltpu.VMEM((W * n, share * channels), BF16),
            pltpu.VMEM((copies, W * n, proj_weight.shape[0]), BF16),
            pltpu.VMEM((features // LANES, W * n, LANES), F32),
        ],
        compiler_params=params(min(40 + 4 * scale, 56)),
        cost_estimate=cost(2e9, 4e6),
        name="conv",
    )(conv1_weight, conv2_weight, *mel_all, *proj_all)
    partials = [to_window(partials[step], step) for step in reversed(range(1, windows))] + [partials[0]]

    ordered, normed, stack = pl.pallas_call(
        functools.partial(norm_kernel, parts),
        out_shape=(block, block, jax.ShapeDtypeStruct((parts,) + mix_piece.shape, BF16)),
        in_specs=[vmem()] * (windows + parts),
        out_specs=(vmem(), vmem(), vmem()),
        scratch_shapes=[pltpu.VMEM((local, features), BF16)],
        compiler_params=params(min(12 * scale, 32)),
        cost_estimate=cost(1e8, 1e6),
        name="layer_norm",
    )(*partials, *mix_all)
    mix_stacks = [stack] + [to_copy(stack, step) for step in range(1, copies)]
    regrouped, keys, valid = pl.pallas_call(
        functools.partial(mask_kernel, windows, group),
        out_shape=(
            block,
            jax.ShapeDtypeStruct((group, local), F32),
            jax.ShapeDtypeStruct((local, 1), F32),
        ),
        in_specs=[smem()] * 3 + [vmem()],
        out_specs=(vmem(), vmem(), vmem()),
        compiler_params=params(min(8 * scale, 32)),
        cost_estimate=cost(1e8, 1e6),
        name="mask",
    )(slots, starts, lengths, ordered)
    normed, out_here = lax.optimization_barrier((normed, out_weight))
    normed = [normed]
    for step in range(1, group):
        high = 1 << (step.bit_length() - 1)
        normed.append(to_plane(normed[high] if step > high else normed[0], step - high if step > high else high))
    out_all = [out_here] + near + [to_part(out_here, parts - 1)]

    *context, stack = pl.pallas_call(
        functools.partial(attention_kernel, parts, windows, group),
        out_shape=tuple(
            [jax.ShapeDtypeStruct((local, head_width), BF16)] * group
            + [jax.ShapeDtypeStruct((parts,) + out_weight.shape, BF16)]
        ),
        in_specs=[vmem()] * (1 + group + copies) + [anywhere()] * parts,
        out_specs=tuple([vmem()] * (group + 1)),
        scratch_shapes=[
            pltpu.VMEM((windows, group * local, qkv_weight.shape[0]), BF16),
            pltpu.SemaphoreType.DMA((parts,)),
        ],
        compiler_params=params(min(16 * scale, 48)),
        cost_estimate=cost(1e9, 2e6),
        name="attention",
    )(keys, *normed, *mix_stacks, *out_all)
    context = [context[0]] + [to_plane(context[step], step) for step in range(1, group)]
    out_stacks = [stack] + [to_copy(stack, step) for step in range(1, copies)]

    attended = pl.pallas_call(
        functools.partial(output_kernel, parts, windows, group),
        out_shape=block,
        in_specs=[vmem()] * (1 + group + copies),
        out_specs=vmem(),
        scratch_shapes=[
            pltpu.VMEM((local, features), BF16),
            pltpu.VMEM((windows, local, out_weight.shape[1]), F32),
        ],
        compiler_params=params(min(12 * scale, 32)),
        cost_estimate=cost(1e8, 3e6),
        name="output",
    )(valid, *context, *out_stacks)
    shape = (1, windows, 1, W, features)
    return (regrouped.reshape(shape), attended.reshape(shape))


def solution(mesh):
    in_specs = (
        P(None, ("dp", "seq")),
        P(),
        P(),
        P(),
        P(),
        P(),
        P("dp", None),
        P("dp", None),
        P(None, "dp"),
    )
    out_specs = (P("dp", None, "seq", None, None), P("dp", None, "seq", None, None))
    return jax.shard_map(
        on_device, mesh=mesh, in_specs=in_specs, out_specs=out_specs, check_vma=False
    )
```
